32 devices in a mesh: dp: 4 (over y, x), fsdp: 8 (over z, core).
Axes of the slice: x: 2, y: 2, z: 4, core: 2. Of those that a mesh axis runs over, the one named last changes fastest.
Arguments:
- tokens: bfloat16 [64, 512, 768], P(('dp', 'fsdp')), may hold values from -6 to 6
- w_query: float32 [768, 768], P(('dp', 'fsdp')), may hold values from -0.21875 to 0.21875
- b_query: float32 [768], P(('dp', 'fsdp')), may hold values from -4 to 4
- w_key: float32 [768, 768], P(('dp', 'fsdp')), may hold values from -0.21875 to 0.21875
- w_value: float32 [768, 768], P(('dp', 'fsdp')), may hold values from -0.21875 to 0.21875
- b_value: float32 [768], P(('dp', 'fsdp')), may hold values from -4 to 4
- w_out: float32 [768, 768], P(('dp', 'fsdp')), may hold values from -1.75 to 1.75
- b_out: float32 [768], P(('dp', 'fsdp')), may hold values from -4 to 4
- gain_one: float32 [768], P(('dp', 'fsdp')), may hold values from 0.5 to 1.5
- shift_one: float32 [768], P(('dp', 'fsdp')), may hold values from -4 to 4
- w_up: float32 [768, 3072], P(('dp', 'fsdp')), may hold values from -0.21875 to 0.21875
- b_up: float32 [3072], P(('dp', 'fsdp')), may hold values from -4 to 4
- w_down: float32 [3072, 768], P(('dp', 'fsdp')), may hold values from -0.109375 to 0.109375
- b_down: float32 [768], P(('dp', 'fsdp')), may hold values from -4 to 4
- gain_two: float32 [768], P(('dp', 'fsdp')), may hold values from 0.5 to 1.5
- shift_two: float32 [768], P(('dp', 'fsdp')), may hold values from -4 to 4
- w_proj: float32 [768, 128], P(('dp', 'fsdp')), may hold values from -0.21875 to 0.21875
- segment_ids: int32 [64, 512], P(('dp', 'fsdp')), may hold values from 0 to 8, as said below
- row_lengths: int32 [64], P(('dp', 'fsdp')), may hold values from 490 to 512, as said below
- teacher_index: int32 [64, 8], P(('dp', 'fsdp')), may hold values from 0 to 1023
- teacher_table: float32 [1024], replicated, may hold values from -6 to 6
Outputs:
- losses: float32 [64], P(('dp', 'fsdp'))
- embeddings: float32 [64, 512, 128], P(('dp', 'fsdp'))
- grad_tokens: float32 [64, 512, 768], P(('dp', 'fsdp'))
- grad_w_query: float32 [768, 768], P(('dp', 'fsdp'))
- grad_b_query: float32 [768], P(('dp', 'fsdp'))
- grad_w_key: float32 [768, 768], P(('dp', 'fsdp'))
- grad_w_value: float32 [768, 768], P(('dp', 'fsdp'))
- grad_b_value: float32 [768], P(('dp', 'fsdp'))
- grad_w_out: float32 [768, 768], P(('dp', 'fsdp'))
- grad_b_out: float32 [768], P(('dp', 'fsdp'))
- grad_gain_one: float32 [768], P(('dp', 'fsdp'))
- grad_shift_one: float32 [768], P(('dp', 'fsdp'))
- grad_w_up: float32 [768, 3072], P(('dp', 'fsdp'))
- grad_b_up: float32 [3072], P(('dp', 'fsdp'))
- grad_w_down: float32 [3072, 768], P(('dp', 'fsdp'))
- grad_b_down: float32 [768], P(('dp', 'fsdp'))
- grad_gain_two: float32 [768], P(('dp', 'fsdp'))
- grad_shift_two: float32 [768], P(('dp', 'fsdp'))
- grad_w_proj: float32 [768, 128], P(('dp', 'fsdp'))
The draws below stay inside these ranges and needn't reach their ends.
Inputs may be any that keep to these rules, and one draw needn't show every extreme that they name: `segment_ids`: positions below 32 hold 0, the query; the other positions hold the passage numbers 1 to 8 in rising order, each passage a run of consecutive positions. `row_lengths`: padding lies inside a row's last passage, which keeps at least half of its positions live; the first row has no padding.
All inputs are finite; a program needn't handle non-finite values.
Results may differ from the reference program's by a relative error of at most 0.024.
Values may be sent and summed in bfloat16 or wider, within the bound.
A program may use at most 192 MiB of HBM per device.

```python
import math
import jax
import jax.numpy as jnp
from jax import lax

D = 768
HEADS = 12
HEAD = 64
FF = 3072
DIM_OUT = 128
SEQ = 512
QLEN = 32
NPASS = 8
TABLE = 1024
ROWS = 64


def draw_bounds(key):
    spacing = (SEQ - QLEN) // NPASS
    jitter = spacing // 4
    offsets = jax.random.randint(key, (ROWS, NPASS - 1), -jitter, jitter + 1)
    return QLEN + spacing * jnp.arange(1, NPASS, dtype=jnp.int32)[None, :] + offsets


def draw_segment_ids(key, part):
    places = draw_bounds(key)
    positions = jnp.arange(SEQ, dtype=jnp.int32)
    passed = jnp.sum((positions[None, None, :] >= places[:, :, None]).astype(jnp.int32), axis=1)
    return jnp.where(positions[None, :] < QLEN, 0, 1 + passed).astype(jnp.int32)


def draw_row_lengths(key, part):
    key = jax.random.fold_in(key, 23)
    spacing = (SEQ - QLEN) // NPASS
    jitter = spacing // 4
    shortest = SEQ - QLEN - spacing * (NPASS - 1) - jitter
    ceiling = shortest // 2
    padding = jax.random.randint(key, (ROWS,), 0, ceiling + 1)
    chosen = jax.random.randint(jax.random.fold_in(key, 5), (), 1, ROWS)
    row_numbers = jnp.arange(ROWS, dtype=jnp.int32)
    padding = jnp.where(row_numbers == chosen, ceiling, padding)
    lengths = SEQ - padding
    return jnp.where(row_numbers == 0, SEQ, lengths).astype(jnp.int32)


def with_ends(drawn, key, least, largest):
    longest = drawn.shape.index(max(drawn.shape))
    spots = []
    for shift in (0, 1):
        where = [jax.random.randint(jax.random.fold_in(key, axis), (), 0, length) for axis, length in enumerate(drawn.shape)]
        where[longest] = (where[longest] + shift) % drawn.shape[longest]
        spots.append(tuple(where))
    return drawn.at[spots[0]].set(least).at[spots[1]].set(largest)


def block_scale(stream_key, shape, shards, least, top_value):
    def one(dim, blocks):
        draws = jax.random.uniform(jax.random.fold_in(jax.random.fold_in(stream_key, 6), dim), (blocks,), jnp.float32, least / len(shards), top_value / len(shards))
        return jnp.repeat(jnp.exp(draws), shape[dim] // blocks).reshape((-1,) + (1,) * (len(shape) - dim - 1))

    level = one(*shards[0])
    for cut in shards[1:]:
        level = level * one(*cut)
    return level


def noise(rng, shape, scale, bound, split=(), kind=jnp.bfloat16):
    drawn = scale * jax.random.normal(rng, shape, jnp.float32)
    if split:
        drawn = drawn * block_scale(rng, shape, split, -0.22, 0.18)
    return jnp.clip(drawn, -bound, bound).astype(kind)


def setup_inputs(seed: int = 0) -> dict:
    arg_keys = jax.random.split(jax.random.key(seed), 22)
    return {
        "tokens": noise(arg_keys[0], (ROWS, SEQ, D), 1.0, 6.0, ((0, 32),)),
        "w_query": noise(arg_keys[1], (D, D), D ** -0.5, 0.21875, ((0, 32),), jnp.float32),
        "b_query": noise(arg_keys[2], (D,), 0.3, 4.0, ((0, 32),), jnp.float32),
        "w_key": noise(arg_keys[3], (D, D), D ** -0.5, 0.21875, ((0, 32),), jnp.float32),
        "w_value": noise(arg_keys[4], (D, D), D ** -0.5, 0.21875, ((0, 32),), jnp.float32),
        "b_value": noise(arg_keys[5], (D,), 0.3, 4.0, ((0, 32),), jnp.float32),
        "w_out": noise(arg_keys[6], (D, D), (D // 64) ** -0.5, 1.75, ((0, 32),), jnp.float32),
        "b_out": noise(arg_keys[7], (D,), 0.3, 4.0, ((0, 32),), jnp.float32),
        "gain_one": jnp.clip(1.0 + 0.1 * jax.random.normal(arg_keys[8], (D,), jnp.float32), 0.5, 1.5),
        "shift_one": noise(arg_keys[9], (D,), 0.3, 4.0, ((0, 32),), jnp.float32),
        "w_up": noise(arg_keys[10], (D, FF), D ** -0.5, 0.21875, ((0, 32),), jnp.float32),
        "b_up": noise(arg_keys[11], (FF,), 0.3, 4.0, ((0, 32),), jnp.float32),
        "w_down": noise(arg_keys[12], (FF, D), FF ** -0.5, 0.109375, ((0, 32),), jnp.float32),
        "b_down": noise(arg_keys[13], (D,), 0.3, 4.0, ((0, 32),), jnp.float32),
        "gain_two": jnp.clip(1.0 + 0.1 * jax.random.normal(arg_keys[14], (D,), jnp.float32), 0.5, 1.5),
        "shift_two": noise(arg_keys[15], (D,), 0.3, 4.0, ((0, 32),), jnp.float32),
        "w_proj": noise(arg_keys[16], (D, DIM_OUT), D ** -0.5, 0.21875, ((0, 32),), jnp.float32),
        "segment_ids": draw_segment_ids(jax.random.fold_in(arg_keys[21], 71), 0),
        "row_lengths": draw_row_lengths(jax.random.fold_in(arg_keys[21], 71), 0),
        "teacher_index": with_ends(jax.random.randint(arg_keys[19], (ROWS, NPASS), 0, TABLE), jax.random.fold_in(arg_keys[19], 1), 0, TABLE - 1).astype(jnp.int32),
        "teacher_table": noise(arg_keys[20], (TABLE,), 2.0, 6.0, (), jnp.float32),
    }


NORM_EPS = 1e-12
UNIT_EPS = 1e-12
SOFTNESS = 0.1
MASK_FILL = -1000000000.0
HIGHEST = lax.Precision.HIGHEST

@jax.custom_vjp
def low(v):
    return lax.optimization_barrier(v.astype(jnp.bfloat16)).astype(jnp.float32)

@jax.custom_vjp
def low_back(v):
    return v

def low_keep(v):
    return (low(v), None)

def low_pass(kept, grad):
    return (grad,)

def back_keep(v):
    return (v, None)

def back_low(kept, grad):
    return (low(grad),)
low.defvjp(low_keep, low_pass)
low_back.defvjp(back_keep, back_low)

def dense(left, right):
    return jnp.dot(left, right, precision=HIGHEST, preferred_element_type=jnp.float32)

def layer_norm(mixed, gain, shift):
    centred = mixed - lax.optimization_barrier(jnp.mean(mixed, -1, keepdims=True))
    scaled = lax.rsqrt(lax.optimization_barrier(jnp.mean(centred * centred, -1, keepdims=True)) + NORM_EPS)
    return centred * scaled * gain + shift

def attention_row(queries, keys_all, values, visible):
    scale = 1.0 / math.sqrt(HEAD)
    query_heads = queries.reshape(SEQ, HEADS, HEAD)
    key_heads = keys_all.reshape(SEQ, HEADS, HEAD)
    value_heads = values.reshape(SEQ, HEADS, HEAD)
    scores = low_back(jnp.einsum('qhd,khd->hqk', query_heads, key_heads, precision=HIGHEST) * scale)
    scores = jnp.where(visible[None], scores, MASK_FILL)
    chances = low(jax.nn.softmax(scores, axis=-1))
    context = jnp.einsum('hqk,khd->qhd', chances, value_heads, precision=HIGHEST)
    return context.reshape(SEQ, HEADS * HEAD)

def row_forward(lowered, tokens_row, segment_row, length_row, index_row, teacher_table):
    w_query, b_query, w_key, w_value, b_value, w_out, b_out, gain_one, shift_one, w_up, b_up, w_down, b_down, gain_two, shift_two, w_proj = lowered
    positions = jnp.arange(SEQ, dtype=jnp.int32)
    live = positions < length_row
    visible = (segment_row[:, None] == segment_row[None, :]) & live[None, :]
    queries = low(low_back(dense(tokens_row, w_query) + b_query))
    keys_all = low(low_back(dense(tokens_row, w_key)))
    values = low(low_back(dense(tokens_row, w_value) + b_value))
    context = low(low_back(attention_row(queries, keys_all, values, visible)))
    branch_one = low_back(dense(context, w_out) + b_out)
    hidden_one = layer_norm(tokens_row + branch_one, gain_one, shift_one)
    upward = low_back(dense(low(hidden_one), w_up) + b_up)
    activated = low(jax.nn.gelu(upward, approximate=False))
    branch_two = low_back(dense(activated, w_down) + b_down)
    hidden_two = layer_norm(hidden_one + branch_two, gain_two, shift_two)
    raw_embed = low_back(dense(low(hidden_two), w_proj))
    embeddings = raw_embed * lax.rsqrt(lax.optimization_barrier(jnp.sum(raw_embed * raw_embed, -1, keepdims=True)) + UNIT_EPS)
    embed_low = low(embeddings)
    similar = low_back(dense(embed_low[:QLEN], embed_low.T))
    passages = jnp.arange(1, NPASS + 1, dtype=jnp.int32)
    member = (segment_row[None, :] == passages[:, None]) & live[None, :]
    masked = jnp.where(member[None], similar[:, None, :] / SOFTNESS, MASK_FILL)
    student = SOFTNESS * lax.optimization_barrier(jnp.sum(jax.nn.logsumexp(masked, axis=-1), 0))
    teacher = teacher_table[index_row]
    loss_row = jnp.sum(jax.nn.softmax(teacher) * (jax.nn.log_softmax(teacher) - jax.nn.log_softmax(student)))
    return (loss_row, embeddings)

def reference(tokens, w_query, b_query, w_key, w_value, b_value, w_out, b_out, gain_one, shift_one, w_up, b_up, w_down, b_down, gain_two, shift_two, w_proj, segment_ids, row_lengths, teacher_index, teacher_table):
    params = (w_query, b_query, w_key, w_value, b_value, w_out, b_out, gain_one, shift_one, w_up, b_up, w_down, b_down, gain_two, shift_two, w_proj)
    tokens_wide = tokens.astype(jnp.float32)

    def forward(params, tokens_wide):
        lowered = tuple((low(member) for member in params))
        row_step = jax.checkpoint(row_forward)

        def scan_row(running, inputs):
            tokens_row, segment_row, length_row, index_row = inputs
            loss_row, embed_row = row_step(lowered, tokens_row, segment_row, length_row, index_row, teacher_table)
            return (running, (loss_row, embed_row))
        running, outputs = lax.scan(scan_row, jnp.zeros((), jnp.float32), (tokens_wide, segment_ids, row_lengths, teacher_index))
        return outputs
    outputs, pullback = jax.vjp(forward, params, tokens_wide)
    losses, embeddings = outputs
    param_grads, grad_tokens = pullback((jnp.ones_like(losses), jnp.zeros_like(embeddings)))
    grad_w_query, grad_b_query, grad_w_key, grad_w_value, grad_b_value, grad_w_out, grad_b_out, grad_gain_one, grad_shift_one, grad_w_up, grad_b_up, grad_w_down, grad_b_down, grad_gain_two, grad_shift_two, grad_w_proj = param_grads
    return (losses, embeddings, grad_tokens, grad_w_query, grad_b_query, grad_w_key, grad_w_value, grad_b_value, grad_w_out, grad_b_out, grad_gain_one, grad_shift_one, grad_w_up, grad_b_up, grad_w_down, grad_b_down, grad_gain_two, grad_shift_two, grad_w_proj)
```

```python
import functools
import math

import jax
import jax.numpy as jnp
from jax import lax
from jax.experimental import pallas as pl
from jax.experimental.pallas import tpu as pltpu
from jax.sharding import PartitionSpec as P

HEADS = 12
HEAD = 64
SEQ = 512
QLEN = 32
NPASS = 8
TABLE = 1024


NORM_EPS = 1e-12
UNIT_EPS = 1e-12
SOFTNESS = 0.1
MASK_FILL = -1000000000.0
ROOT_HALF = 0.7071067811865476
DENSITY_SCALE = 0.3989422804014327


def matmul(left, right):
    return jnp.dot(left, right, preferred_element_type=jnp.float32)


def over_rows(left, right):
    return lax.dot_general(
        left, right, (((0,), (0,)), ((), ())), preferred_element_type=jnp.float32
    )


def against(left, right):
    return lax.dot_general(
        left, right, (((1,), (1,)), ((), ())), preferred_element_type=jnp.float32
    )


def normalise(mixed, gain, shift):
    centred = mixed - jnp.mean(mixed, -1, keepdims=True)
    scaled = lax.rsqrt(jnp.mean(centred * centred, -1, keepdims=True) + NORM_EPS)
    normed = centred * scaled
    return (normed * gain + shift, normed, scaled)


def normalise_back(grad_out, normed, scaled, gain):
    inner = grad_out * gain
    grad_in = scaled * (
        inner
        - jnp.mean(inner, -1, keepdims=True)
        - normed * jnp.mean(inner * normed, -1, keepdims=True)
    )
    return (grad_in, jnp.sum(grad_out * normed, 0), jnp.sum(grad_out, 0))


def gelu_exact(upward):
    return 0.5 * upward * (1.0 + lax.erf(upward * ROOT_HALF))


def gelu_slope(upward):
    return (
        0.5 * (1.0 + lax.erf(upward * ROOT_HALF))
        + upward * jnp.exp(-0.5 * upward * upward) * DENSITY_SCALE
    )


def split_heads(matrix, rows_dev):
    return (
        matrix.reshape(rows_dev, SEQ, HEADS, HEAD)
        .transpose(0, 2, 1, 3)
        .reshape(rows_dev * HEADS, SEQ, HEAD)
    )


def join_heads(stacked, rows_dev):
    return (
        stacked.reshape(rows_dev, HEADS, SEQ, HEAD)
        .transpose(0, 2, 1, 3)
        .reshape(rows_dev * SEQ, HEADS * HEAD)
    )


def collect(sent):
    return (
        lax.all_gather(sent[0], ("dp", "fsdp"), axis=0, tiled=True),
        lax.all_gather(sent[1], ("dp", "fsdp"), axis=0, tiled=True),
        lax.all_gather(sent[2], ("dp", "fsdp"), axis=0, tiled=True),
        lax.all_gather(sent[3], ("dp", "fsdp"), axis=0, tiled=True),
        lax.all_gather(sent[4], ("dp", "fsdp"), axis=0, tiled=True),
        lax.all_gather(sent[5], ("dp", "fsdp"), axis=0, tiled=True),
        lax.all_gather(sent[6], ("dp", "fsdp"), axis=0, tiled=True),
        lax.all_gather(sent[7], ("dp", "fsdp"), axis=0, tiled=True),
        lax.all_gather(sent[8], ("dp", "fsdp"), axis=0, tiled=True),
        lax.all_gather(sent[9], ("dp", "fsdp"), axis=0, tiled=True),
        lax.all_gather(sent[10], ("dp", "fsdp"), axis=0, tiled=True),
        lax.all_gather(sent[11], ("dp", "fsdp"), axis=0, tiled=True),
        lax.all_gather(sent[12], ("dp", "fsdp"), axis=0, tiled=True),
        lax.all_gather(sent[13], ("dp", "fsdp"), axis=0, tiled=True),
        lax.all_gather(sent[14], ("dp", "fsdp"), axis=0, tiled=True),
        lax.all_gather(sent[15], ("dp", "fsdp"), axis=0, tiled=True),
    )


def spread_grads(terms):
    return (
        lax.psum_scatter(terms[0], ("dp", "fsdp"), scatter_dimension=0, tiled=True),
        lax.psum_scatter(terms[1], ("dp", "fsdp"), scatter_dimension=0, tiled=True),
        lax.psum_scatter(terms[2], ("dp", "fsdp"), scatter_dimension=0, tiled=True),
        lax.psum_scatter(terms[3], ("dp", "fsdp"), scatter_dimension=0, tiled=True),
        lax.psum_scatter(terms[4], ("dp", "fsdp"), scatter_dimension=0, tiled=True),
        lax.psum_scatter(terms[5], ("dp", "fsdp"), scatter_dimension=0, tiled=True),
        lax.psum_scatter(terms[6], ("dp", "fsdp"), scatter_dimension=0, tiled=True),
        lax.psum_scatter(terms[7], ("dp", "fsdp"), scatter_dimension=0, tiled=True),
        lax.psum_scatter(terms[8], ("dp", "fsdp"), scatter_dimension=0, tiled=True),
        lax.psum_scatter(terms[9], ("dp", "fsdp"), scatter_dimension=0, tiled=True),
        lax.psum_scatter(terms[10], ("dp", "fsdp"), scatter_dimension=0, tiled=True),
        lax.psum_scatter(terms[11], ("dp", "fsdp"), scatter_dimension=0, tiled=True),
        lax.psum_scatter(terms[12], ("dp", "fsdp"), scatter_dimension=0, tiled=True),
        lax.psum_scatter(terms[13], ("dp", "fsdp"), scatter_dimension=0, tiled=True),
        lax.psum_scatter(terms[14], ("dp", "fsdp"), scatter_dimension=0, tiled=True),
        lax.psum_scatter(terms[15], ("dp", "fsdp"), scatter_dimension=0, tiled=True),
    )


def body_whole(
    tokens,
    w_query,
    b_query,
    w_key,
    w_value,
    b_value,
    w_out,
    b_out,
    gain_one,
    shift_one,
    w_up,
    b_up,
    w_down,
    b_down,
    gain_two,
    shift_two,
    w_proj,
    segment_ids,
    row_lengths,
    teacher_index,
    teacher_table,
):
    rows_dev = tokens.shape[0]
    width = tokens.shape[2]
    scale = 1.0 / math.sqrt(HEAD)
    shards = (
        w_query,
        b_query,
        w_key,
        w_value,
        b_value,
        w_out,
        b_out,
        gain_one,
        shift_one,
        w_up,
        b_up,
        w_down,
        b_down,
        gain_two,
        shift_two,
        w_proj,
    )
    sent = tuple((member.astype(jnp.bfloat16) for member in shards))
    gathered = collect(sent)
    (
        query_mat,
        query_bias,
        key_mat,
        value_mat,
        value_bias,
        out_mat,
        out_bias,
        gain_first,
        shift_first,
        up_mat,
        up_bias,
        down_mat,
        down_bias,
        gain_second,
        shift_second,
        proj_mat,
    ) = gathered

    def visibility(item_index):
        row_index = item_index // HEADS
        segment_row = lax.dynamic_index_in_dim(segment_ids, row_index, 0, keepdims=False)
        length_row = lax.dynamic_index_in_dim(row_lengths, row_index, 0, keepdims=False)
        positions = jnp.arange(SEQ, dtype=jnp.int32)
        return (segment_row[:, None] == segment_row[None, :]) & (positions[None, :] < length_row)

    def attend(inputs):
        query_h, key_h, value_h, item_index = inputs
        scores = jnp.where(visibility(item_index), against(query_h, key_h) * scale, MASK_FILL)
        peak = jnp.max(scores, -1, keepdims=True)
        shifted = jnp.exp(scores - peak)
        totals = jnp.sum(shifted, -1, keepdims=True)
        chances = (shifted / totals).astype(jnp.bfloat16)
        context_h = matmul(chances, value_h).astype(jnp.bfloat16)
        return (context_h, (peak + jnp.log(totals))[:, 0])

    def attend_back(inputs):
        query_h, key_h, value_h, grad_h, logsum, item_index = inputs
        scores = jnp.where(visibility(item_index), against(query_h, key_h) * scale, MASK_FILL)
        chances = jnp.exp(scores - logsum[:, None])
        d_chances = against(grad_h, value_h)
        rowdot = jnp.sum(chances * d_chances, -1, keepdims=True)
        d_scores = (chances * (d_chances - rowdot)).astype(jnp.bfloat16)
        d_query_h = (matmul(d_scores, key_h) * scale).astype(jnp.bfloat16)
        d_key_h = (over_rows(d_scores, query_h) * scale).astype(jnp.bfloat16)
        d_value_h = over_rows(chances.astype(jnp.bfloat16), grad_h).astype(jnp.bfloat16)
        return (d_query_h, d_key_h, d_value_h)

    flat = tokens.reshape(rows_dev * SEQ, width)
    queries = (matmul(flat, query_mat) + query_bias.astype(jnp.float32)).astype(jnp.bfloat16)
    keys_all = matmul(flat, key_mat).astype(jnp.bfloat16)
    values = (matmul(flat, value_mat) + value_bias.astype(jnp.float32)).astype(jnp.bfloat16)
    query_heads = split_heads(queries, rows_dev)
    key_heads = split_heads(keys_all, rows_dev)
    value_heads = split_heads(values, rows_dev)
    items = jnp.arange(rows_dev * HEADS, dtype=jnp.int32)
    context_heads, logsums = lax.map(attend, (query_heads, key_heads, value_heads, items))
    context_low = join_heads(context_heads, rows_dev)
    branch_one = matmul(context_low, out_mat) + out_bias.astype(jnp.float32)
    mid_one = flat.astype(jnp.float32) + branch_one
    hidden_one, normed_one, scaled_one = normalise(
        mid_one, gain_first.astype(jnp.float32), shift_first.astype(jnp.float32)
    )
    hidden_one_low = hidden_one.astype(jnp.bfloat16)
    upward = matmul(hidden_one_low, up_mat) + up_bias.astype(jnp.float32)
    activated = gelu_exact(upward).astype(jnp.bfloat16)
    branch_two = matmul(activated, down_mat) + down_bias.astype(jnp.float32)
    hidden_two, normed_two, scaled_two = normalise(
        hidden_one + branch_two, gain_second.astype(jnp.float32), shift_second.astype(jnp.float32)
    )
    hidden_two_low = hidden_two.astype(jnp.bfloat16)
    raw_embed = matmul(hidden_two_low, proj_mat)
    inverse = lax.rsqrt(jnp.sum(raw_embed * raw_embed, -1, keepdims=True) + UNIT_EPS)
    embeddings = raw_embed * inverse
    embed_dim = embeddings.shape[1]
    embed_low = embeddings.astype(jnp.bfloat16).reshape(rows_dev, SEQ, embed_dim)
    query_low = embed_low[:, :QLEN]
    similar = jnp.einsum("rqc,rsc->rqs", query_low, embed_low, preferred_element_type=jnp.float32)
    positions = jnp.arange(SEQ, dtype=jnp.int32)
    live = positions[None, :] < row_lengths[:, None]
    passages = jnp.arange(1, NPASS + 1, dtype=jnp.int32)
    member = (segment_ids[:, None, :] == passages[None, :, None]) & live[:, None, :]
    masked = jnp.where(member[:, None], similar[:, :, None, :] / SOFTNESS, MASK_FILL)
    peak = jnp.max(masked, -1, keepdims=True)
    shifted = jnp.exp(masked - peak)
    totals = jnp.sum(shifted, -1, keepdims=True)
    student = SOFTNESS * jnp.sum(peak[..., 0] + jnp.log(totals[..., 0]), axis=1)
    choose = teacher_index[..., None] == jnp.arange(TABLE, dtype=jnp.int32)
    teacher = jnp.sum(jnp.where(choose, teacher_table, 0.0), -1)
    teacher_logp = jax.nn.log_softmax(teacher, axis=-1)
    student_logp = jax.nn.log_softmax(student, axis=-1)
    losses = jnp.sum(jnp.exp(teacher_logp) * (teacher_logp - student_logp), -1)
    again = collect(sent)
    (
        query_back,
        query_bias_back,
        key_back,
        value_back,
        value_bias_back,
        out_back,
        out_bias_back,
        gain_first_back,
        shift_first_back,
        up_back,
        up_bias_back,
        down_back,
        down_bias_back,
        gain_second_back,
        shift_second_back,
        proj_back,
    ) = again
    d_student = jnp.exp(student_logp) - jnp.exp(teacher_logp)
    spread_weights = shifted / totals
    d_similar = jnp.einsum("rp,rqps->rqs", d_student, spread_weights).astype(jnp.bfloat16)
    d_embed = jnp.einsum("rqs,rqc->rsc", d_similar, query_low, preferred_element_type=jnp.float32)
    d_query_part = jnp.einsum(
        "rqs,rsc->rqc", d_similar, embed_low, preferred_element_type=jnp.float32
    )
    d_embed = jnp.concatenate([d_embed[:, :QLEN] + d_query_part, d_embed[:, QLEN:]], 1).reshape(
        rows_dev * SEQ, embed_dim
    )
    d_raw = (
        inverse * (d_embed - embeddings * jnp.sum(d_embed * embeddings, -1, keepdims=True))
    ).astype(jnp.bfloat16)
    grad_proj = over_rows(hidden_two_low, d_raw)
    d_hidden_two = against(d_raw, proj_back)
    d_mid_two, grad_gain_second, grad_shift_second = normalise_back(
        d_hidden_two, normed_two, scaled_two, gain_second_back.astype(jnp.float32)
    )
    d_branch_two = d_mid_two.astype(jnp.bfloat16)
    grad_down = over_rows(activated, d_branch_two)
    grad_down_bias = jnp.sum(d_branch_two, 0, dtype=jnp.float32)
    d_upward = (against(d_branch_two, down_back) * gelu_slope(upward)).astype(jnp.bfloat16)
    grad_up = over_rows(hidden_one_low, d_upward)
    grad_up_bias = jnp.sum(d_upward, 0, dtype=jnp.float32)
    d_hidden_one = d_mid_two + against(d_upward, up_back)
    d_mid_one, grad_gain_first, grad_shift_first = normalise_back(
        d_hidden_one, normed_one, scaled_one, gain_first_back.astype(jnp.float32)
    )
    d_branch_one = d_mid_one.astype(jnp.bfloat16)
    grad_out = over_rows(context_low, d_branch_one)
    grad_out_bias = jnp.sum(d_branch_one, 0, dtype=jnp.float32)
    d_context = against(d_branch_one, out_back).astype(jnp.bfloat16)
    d_context_heads = split_heads(d_context, rows_dev)
    d_query_heads, d_key_heads, d_value_heads = lax.map(
        attend_back, (query_heads, key_heads, value_heads, d_context_heads, logsums, items)
    )
    d_queries = join_heads(d_query_heads, rows_dev)
    d_keys = join_heads(d_key_heads, rows_dev)
    d_values = join_heads(d_value_heads, rows_dev)
    grad_query = over_rows(flat, d_queries)
    grad_query_bias = jnp.sum(d_queries, 0, dtype=jnp.float32)
    grad_key = over_rows(flat, d_keys)
    grad_value = over_rows(flat, d_values)
    grad_value_bias = jnp.sum(d_values, 0, dtype=jnp.float32)
    grad_input = (
        d_mid_one
        + against(d_queries, query_back)
        + against(d_keys, key_back)
        + against(d_values, value_back)
    )
    terms = (
        grad_query,
        grad_query_bias,
        grad_key,
        grad_value,
        grad_value_bias,
        grad_out,
        grad_out_bias,
        grad_gain_first,
        grad_shift_first,
        grad_up,
        grad_up_bias,
        grad_down,
        grad_down_bias,
        grad_gain_second,
        grad_shift_second,
        grad_proj,
    )
    owned = spread_grads(terms)
    return (
        losses,
        embeddings.reshape(rows_dev, SEQ, embed_dim),
        grad_input.reshape(rows_dev, SEQ, width),
        owned[0],
        owned[1],
        owned[2],
        owned[3],
        owned[4],
        owned[5],
        owned[6],
        owned[7],
        owned[8],
        owned[9],
        owned[10],
        owned[11],
        owned[12],
        owned[13],
        owned[14],
        owned[15],
    )


MESH = pl.DeviceIdType.MESH
EXP2_SCALE = 1.4426950408889634 / math.sqrt(HEAD)
SHARDS = 32
CHIPS = 16
WIDTH = 768
HIDDEN = 3072
EMBED = 128
SMALL = 40


def fits(mesh):
    return dict(mesh.shape) == {"dp": 4, "fsdp": 8}


def dotted(left, right, left_dim, right_dim):
    return lax.dot_general(
        left,
        right,
        (((left_dim,), (right_dim,)), ((), ())),
        preferred_element_type=jnp.float32,
    )


def place():
    outer = lax.axis_index("dp")
    inner = lax.axis_index("fsdp")
    return lax.rem(outer, 2), lax.div(outer, 2), lax.div(inner, 2), lax.rem(inner, 2)


def device(x, y, z, c):
    return (y * 2 + x, z * 2 + c)


class Links:
    def __init__(self):
        x, y, z, c = place()
        self.c = c
        self.z = z
        self.chip_own = (y * 2 + x) * 4
        self.chip_x = (y * 2 + 1 - x) * 4
        self.chip_y = ((1 - y) * 2 + x) * 4
        self.chip_d = ((1 - y) * 2 + 1 - x) * 4
        self.to_core = device(x, y, z, 1 - c)
        self.to_x = device(1 - x, y, z, c)
        self.to_y = device(x, 1 - y, z, c)
        self.to_z = [None] + [device(x, y, lax.rem(z + k, 4), c) for k in (1, 2, 3)]
        self.started = []

    def greet(self):
        barrier = pltpu.get_barrier_semaphore()
        partners = [self.to_core, self.to_x, self.to_y] + self.to_z[1:]
        for partner in partners:
            pl.semaphore_signal(barrier, inc=1, device_id=partner, device_id_type=MESH)
        pl.semaphore_wait(barrier, len(partners))

    def level(self, k):
        return lax.rem(self.z + k, 4)

    def send(self, src, dst, send_sem, recv_sem, target):
        copy = pltpu.make_async_remote_copy(
            src_ref=src,
            dst_ref=dst,
            send_sem=send_sem,
            recv_sem=recv_sem,
            device_id=target,
            device_id_type=MESH,
        )
        copy.start()
        self.started.append(copy)

    def arrived(self, ref, send_sem, recv_sem, source):
        pltpu.make_async_remote_copy(
            src_ref=ref,
            dst_ref=ref,
            send_sem=send_sem,
            recv_sem=recv_sem,
            device_id=source,
            device_id_type=MESH,
        ).wait_recv()

    def finish(self):
        for copy in self.started:
            copy.wait_send()
        self.started = []


class Gather:
    Z, X, Y, FX, FY, C = 0, 3, 7, 11, 13, 15

    def __init__(self, links, block, sends, recvs, group):
        self.links = links
        self.block = block
        self.sends = sends
        self.recvs = recvs
        self.group = group

    def sems(self, index):
        return self.sends.at[self.group, index], self.recvs.at[self.group, index]

    def ship(self, ref, index, target):
        send_sem, recv_sem = self.sems(index)
        self.links.send(ref, ref, send_sem, recv_sem, target)

    def take(self, ref, index, source):
        send_sem, recv_sem = self.sems(index)
        self.links.arrived(ref, send_sem, recv_sem, source)

    def first(self):
        n = self.links
        own = self.block(n.c, n.chip_own + n.z, 1)
        for j in (1, 2, 3):
            send_sem = self.sends.at[self.group, self.Z + j - 1]
            recv_sem = self.recvs.at[self.group, self.Z + 3 - j]
            n.send(own, own, send_sem, recv_sem, n.to_z[j])
        self.ship(own, self.X, n.to_x)
        self.ship(own, self.Y, n.to_y)

    def second(self):
        n = self.links
        for k in (1, 2, 3):
            block = self.block(n.c, n.chip_own + n.level(k), 1)
            self.take(block, self.Z + k - 1, n.to_z[k])
            self.ship(block, self.X + k, n.to_x)
            self.ship(block, self.Y + k, n.to_y)
        self.ship(self.block(n.c, n.chip_own, 4), self.C, n.to_core)

    def third(self):
        n = self.links
        for k in (0, 1):
            block = self.block(n.c, n.chip_x + n.level(k), 1)
            self.take(block, self.X + k, n.to_x)
            self.ship(block, self.FY + k, n.to_y)
        for k in (2, 3):
            block = self.block(n.c, n.chip_y + n.level(k), 1)
            self.take(block, self.Y + k, n.to_y)
            self.ship(block, self.FX + k - 2, n.to_x)
        for k in (2, 3):
            self.take(self.block(n.c, n.chip_x + n.level(k), 1), self.X + k, n.to_x)
        self.ship(self.block(n.c, n.chip_x, 4), self.C + 1, n.to_core)
        for k in (0, 1):
            self.take(self.block(n.c, n.chip_y + n.level(k), 1), self.Y + k, n.to_y)
        self.ship(self.block(n.c, n.chip_y, 4), self.C + 2, n.to_core)

    def fourth(self):
        n = self.links
        for k in (0, 1):
            self.take(self.block(n.c, n.chip_d + n.level(k), 1), self.FY + k, n.to_y)
        for k in (2, 3):
            self.take(self.block(n.c, n.chip_d + n.level(k), 1), self.FX + k - 2, n.to_x)
        self.ship(self.block(n.c, n.chip_d, 4), self.C + 3, n.to_core)

    def last(self):
        n = self.links
        for index, chip in enumerate((n.chip_own, n.chip_x, n.chip_y, n.chip_d)):
            self.take(self.block(1 - n.c, chip, 4), self.C + index, n.to_core)


def rows_block(ref, rows, columns):
    def block(core, chip, count):
        return ref.at[
            pl.ds(pl.multiple_of(chip * rows, rows), count * rows),
            pl.ds(pl.multiple_of(core * columns, columns), columns),
        ]

    return block


def lead_block(ref):
    def block(core, chip, count):
        return ref.at[core, pl.ds(chip, count)]

    return block


def spread_lanes(parts, step):
    lane = lax.broadcasted_iota(jnp.int32, (8, 128), 1)
    tiles = [None] * (len(parts) * step // 128)

    def add(index, value):
        tiles[index] = value if tiles[index] is None else tiles[index] + value

    for i, part in enumerate(parts):
        part = jnp.where(lane < step, part, 0.0)
        index, shift = i * step // 128, i * step % 128
        rolled = pltpu.roll(part, shift, 1) if shift else part
        if shift + step <= 128:
            add(index, rolled)
        else:
            add(index, jnp.where(lane >= shift, rolled, 0.0))
            add(index + 1, jnp.where(lane < shift, rolled, 0.0))
    return tiles


def mask_bias(own_segment, other_segment, bias):
    for r in range(bias.shape[0]):
        bias[r] = jnp.where(
            own_segment[r * SEQ : (r + 1) * SEQ, :] == other_segment[r], 0.0, MASK_FILL
        )


def attend_pair(item, qkv, context, logsums, bias):
    r = lax.div(item, HEADS // 2)
    p = lax.rem(item, HEADS // 2)
    rows = pl.ds(pl.multiple_of(r * SEQ, SEQ), SEQ)
    columns = pl.multiple_of(p * 128, 128)
    query = qkv[rows, pl.ds(columns, 128)]
    key = qkv[rows, pl.ds(columns + WIDTH, 128)]
    value = qkv[rows, pl.ds(columns + 2 * WIDTH, 128)]
    low = lax.broadcasted_iota(jnp.int32, (SEQ, 128), 1) < HEAD
    zero = jnp.zeros_like(key)
    outs, sums = [], []
    for j in range(2):
        key_j = jnp.where(low, key, zero) if j == 0 else jnp.where(low, zero, key)
        scores = dotted(query, key_j, 1, 1) * EXP2_SCALE + bias[r]
        peak = jnp.max(scores, -1, keepdims=True)
        shifted = jnp.exp2(scores - peak)
        total = jnp.sum(shifted, -1, keepdims=True)
        out = dotted(shifted.astype(jnp.bfloat16), value, 1, 0)
        outs.append(out * (1.0 / total))
        sums.append(peak + jnp.log2(total))
    context[rows, pl.ds(columns, 128)] = jnp.where(low, outs[0], outs[1]).astype(jnp.bfloat16)
    turned = jnp.where(low, sums[0], sums[1]).T
    logsums[r, p, 0:1] = turned[0:1]
    logsums[r, p, 1:2] = turned[HEAD : HEAD + 1]


def attend_back_pair(item, qkv, d_context, logsums, rowdots, d_qkv, bias):
    r = lax.div(item, HEADS // 2)
    p = lax.rem(item, HEADS // 2)
    rows = pl.ds(pl.multiple_of(r * SEQ, SEQ), SEQ)
    columns = pl.multiple_of(p * 128, 128)
    query = qkv[rows, pl.ds(columns, 128)]
    key = qkv[rows, pl.ds(columns + WIDTH, 128)]
    value = qkv[rows, pl.ds(columns + 2 * WIDTH, 128)]
    grad = d_context[rows, pl.ds(columns, 128)]
    low = lax.broadcasted_iota(jnp.int32, (SEQ, 128), 1) < HEAD
    zero = jnp.zeros_like(key)
    d_query, d_key, d_value = None, [], []
    for j in range(2):
        pick = (lambda a: jnp.where(low, a, zero)) if j == 0 else (lambda a: jnp.where(low, zero, a))
        key_j = pick(key)
        scores = dotted(key_j, query, 1, 1) * EXP2_SCALE + bias[r]
        chances = jnp.exp2(scores - logsums[r, p, j : j + 1, :])
        d_chances = dotted(pick(value), grad, 1, 1)
        d_scores = (chances * (d_chances - rowdots[r, p, j : j + 1, :])).astype(jnp.bfloat16)
        d_value.append(dotted(chances.astype(jnp.bfloat16), grad, 1, 0))
        d_key.append(dotted(d_scores, query, 1, 0))
        term = dotted(d_scores, key_j, 0, 0)
        d_query = term if d_query is None else d_query + term
    scale = 1.0 / math.sqrt(HEAD)
    d_qkv[rows, pl.ds(columns, 128)] = (d_query * scale).astype(jnp.bfloat16)
    d_qkv[rows, pl.ds(columns + WIDTH, 128)] = (
        jnp.where(low, d_key[0], d_key[1]) * scale
    ).astype(jnp.bfloat16)
    d_qkv[rows, pl.ds(columns + 2 * WIDTH, 128)] = jnp.where(low, d_value[0], d_value[1]).astype(
        jnp.bfloat16
    )


def row_dots(context, d_context, rowdots, rows_dev):
    shape = (8, 128)
    head = lax.broadcasted_iota(jnp.int32, shape, 1) // HEAD
    pick = (head == lax.broadcasted_iota(jnp.int32, shape, 0)).astype(jnp.float32)
    for r in range(rows_dev):
        for p in range(HEADS // 2):
            part = (slice(r * SEQ, (r + 1) * SEQ), slice(p * 128, (p + 1) * 128))
            both = context[part].astype(jnp.float32) * d_context[part].astype(jnp.float32)
            rowdots[r, p] = lax.dot_general(
                pick,
                both,
                (((1,), (1,)), ((), ())),
                precision=lax.Precision.HIGHEST,
                preferred_element_type=jnp.float32,
            )


def halves(links, src, stage, sends, recvs, index):
    rows, width = src.shape
    columns = width // 2
    theirs = src.at[:, pl.ds(pl.multiple_of((1 - links.c) * columns, columns), columns)]
    there = stage.at[pl.ds(pl.multiple_of(links.c * rows, rows), rows), :]
    links.send(theirs, there, sends.at[index], recvs.at[index], links.to_core)
    stage[pl.ds(pl.multiple_of(links.c * rows, rows), rows), :] = src[
        :, pl.ds(pl.multiple_of(links.c * columns, columns), columns)
    ]


def joined(links, stage, sends, recvs, index):
    rows = stage.shape[0] // 2
    here = stage.at[pl.ds(pl.multiple_of((1 - links.c) * rows, rows), rows), :]
    links.arrived(here, sends.at[index], recvs.at[index], links.to_core)
    return stage[...].astype(jnp.bfloat16)


def first_kernel(
    tokens,
    w_query,
    w_key,
    w_value,
    w_out,
    w_up,
    w_down,
    small,
    own_segment,
    live_segment,
    attn_hbm,
    up_hbm,
    down_hbm,
    proj_out,
    vectors_out,
    up_bias_out,
    qkv,
    context,
    logsums,
    attn_mat,
    up_mat,
    down_mat,
    small_all,
    cat_attn,
    stage_attn,
    stage_up,
    stage_down,
    bias,
    sends,
    recvs,
    half_sends,
    half_recvs,
    local_sems,
):
    links = Links()
    attn = Gather(links, rows_block(attn_mat, 48, 1536), sends, recvs, 0)
    up = Gather(links, rows_block(up_mat, 48, 1536), sends, recvs, 1)
    down = Gather(links, rows_block(down_mat, 192, 384), sends, recvs, 2)
    tiny = Gather(links, lead_block(small_all), sends, recvs, 3)
    chip = links.chip_own + links.z

    for index, ref in enumerate((w_query, w_key, w_value, w_out)):
        cat_attn[:, index * WIDTH : (index + 1) * WIDTH] = ref[...]
    small_all[links.c, chip] = small[...]
    links.greet()
    halves(links, cat_attn, stage_attn, half_sends, half_recvs, 0)
    tiny.first()
    halves(links, w_up, stage_up, half_sends, half_recvs, 1)
    halves(links, w_down, stage_down, half_sends, half_recvs, 2)

    def own(ref, rows, columns):
        return (
            pl.ds(pl.multiple_of(chip * rows, rows), rows),
            pl.ds(pl.multiple_of(links.c * columns, columns), columns),
        )

    where = own(attn_mat, 48, 1536)
    attn_mat[where[0], where[1]] = joined(links, stage_attn, half_sends, half_recvs, 0)
    attn.first()
    where = own(up_mat, 48, 1536)
    up_mat[where[0], where[1]] = joined(links, stage_up, half_sends, half_recvs, 1)
    where = own(down_mat, 192, 384)
    down_mat[where[0], where[1]] = joined(links, stage_down, half_sends, half_recvs, 2)
    mask_bias(own_segment, live_segment, bias)
    tiny.second()
    attn.second()
    up.first()
    tiny.third()
    attn.third()
    up.second()
    tiny.fourth()
    attn.fourth()
    tiny.last()
    attn.last()
    down.first()

    cores = [(i % 2, i // 2) for i in range(SHARDS)]
    vectors = spread_lanes([small_all[c, n, 24:32, :] for c, n in cores], 24)
    for index, tile in enumerate(vectors):
        vectors_out[:, index * 128 : (index + 1) * 128] = tile.astype(jnp.bfloat16).astype(jnp.float32)
    up_bias = spread_lanes([small_all[c, n, 32:40, :] for c, n in cores], 96)
    for index, tile in enumerate(up_bias):
        up_bias_out[:, index * 128 : (index + 1) * 128] = tile.astype(jnp.bfloat16).astype(jnp.float32)
    for c, n in cores:
        part = small_all[c, n, 0:24, :]
        proj_out[(n * 2 + c) * 24 : (n * 2 + c + 1) * 24, :] = part

    def project(step, carry):
        rows = pl.ds(pl.multiple_of(step * 256, 256), 256)
        part = tokens[rows, :]
        for index in range(3):
            columns = slice(index * WIDTH, (index + 1) * WIDTH)
            out = dotted(part, attn_mat[:, columns], 1, 0)
            if index != 1:
                out = out + vectors_out[index // 2 : index // 2 + 1, :]
            qkv[rows, columns] = out.astype(jnp.bfloat16)
        return carry

    lax.fori_loop(0, tokens.shape[0] // 256, project, 0)

    def attend(item, carry):
        attend_pair(item, qkv, context, logsums, bias)
        return carry

    lax.fori_loop(0, 3, attend, 0)
    up.third()
    down.second()
    lax.fori_loop(3, 6, attend, 0)
    up.fourth()
    lax.fori_loop(6, 9, attend, 0)
    down.third()
    up.last()
    lax.fori_loop(9, 12, attend, 0)
    down.fourth()
    down.last()
    copies = [
        pltpu.make_async_copy(attn_mat, attn_hbm, local_sems.at[0]),
        pltpu.make_async_copy(up_mat, up_hbm, local_sems.at[1]),
        pltpu.make_async_copy(down_mat, down_hbm, local_sems.at[2]),
    ]
    for copy in copies:
        copy.start()
    links.finish()
    for copy in copies:
        copy.wait()


def run_first(tokens, weights, small, own_segment, live_segment):
    count = tokens.shape[0]
    rows_dev = count // SEQ
    vmem = pl.BlockSpec(memory_space=pltpu.VMEM)
    anywhere = pl.BlockSpec(memory_space=pl.ANY)
    low = jnp.bfloat16
    wide = jnp.float32
    return pl.pallas_call(
        first_kernel,
        out_shape=[
            jax.ShapeDtypeStruct((WIDTH, HIDDEN), low),
            jax.ShapeDtypeStruct((WIDTH, HIDDEN), low),
            jax.ShapeDtypeStruct((HIDDEN, WIDTH), low),
            jax.ShapeDtypeStruct((WIDTH, EMBED), wide),
            jax.ShapeDtypeStruct((8, WIDTH), wide),
            jax.ShapeDtypeStruct((8, HIDDEN), wide),
            jax.ShapeDtypeStruct((count, 3 * WIDTH), low),
            jax.ShapeDtypeStruct((count, WIDTH), low),
            jax.ShapeDtypeStruct((rows_dev, HEADS // 2, 8, SEQ), wide),
        ],
        in_specs=[vmem] * 10,
        out_specs=[anywhere] * 3 + [vmem] * 6,
        scratch_shapes=[
            pltpu.VMEM((WIDTH, HIDDEN), low),
            pltpu.VMEM((WIDTH, HIDDEN), low),
            pltpu.VMEM((HIDDEN, WIDTH), low),
            pltpu.VMEM((2, CHIPS, SMALL, 128), wide),
            pltpu.VMEM((24, HIDDEN), wide),
            pltpu.VMEM((48, HIDDEN // 2), wide),
            pltpu.VMEM((48, HIDDEN // 2), wide),
            pltpu.VMEM((192, WIDTH // 2), wide),
            pltpu.VMEM((rows_dev, SEQ, SEQ), wide),
            pltpu.SemaphoreType.DMA((4, 19)),
            pltpu.SemaphoreType.DMA((4, 19)),
            pltpu.SemaphoreType.DMA((3,)),
            pltpu.SemaphoreType.DMA((3,)),
            pltpu.SemaphoreType.DMA((3,)),
        ],
        compiler_params=pltpu.CompilerParams(
            collective_id=0, has_side_effects=True, vmem_limit_bytes=60 * 2**20
        ),
        name="gather_attend",
    )(tokens, *weights, small, own_segment, live_segment)


class Scatter:
    C, DY, DX, OX, OY, Z, F = 0, 4, 5, 6, 8, 10, 13

    def __init__(self, links, block, rows, held, sends, recvs, local_sems, group):
        self.links = links
        self.block = block
        self.rows = rows
        self.part, self.core_in, self.d_y, self.d_x, self.o_x, self.o_y, self.z_in = held
        self.sends = sends
        self.recvs = recvs
        self.local_sems = local_sems
        self.group = group
        n = links
        self.columns = (n.chip_d, n.chip_x, n.chip_y, n.chip_own)

    def at(self, ref, start, count):
        if isinstance(start, int):
            return ref.at[pl.ds(start * self.rows, count * self.rows)]
        return ref.at[pl.ds(pl.multiple_of(start * self.rows, self.rows), count * self.rows)]

    def sems(self, index):
        return self.sends.at[self.group, index], self.recvs.at[self.group, index]

    def ship(self, src, dst, index, target):
        send_sem, recv_sem = self.sems(index)
        self.links.send(src, dst, send_sem, recv_sem, target)

    def take(self, ref, index, source):
        send_sem, recv_sem = self.sems(index)
        self.links.arrived(ref, send_sem, recv_sem, source)

    def own_copy(self, index):
        chip = self.columns[index]
        return pltpu.make_async_copy(
            self.block(self.links.c, chip, 4),
            self.at(self.part, chip, 4),
            self.local_sems.at[self.group, index],
        )

    def add(self, count, target, *others):
        def step(i, carry):
            def here(ref, start):
                return self.at(ref, start + i, 1)

            total = here(*target)[...].astype(jnp.float32)
            for other in others:
                total = total + here(*other)[...].astype(jnp.float32)
            here(*target)[...] = total.astype(target[0].dtype)
            return carry

        lax.fori_loop(0, count, step, 0)

    def first(self):
        n = self.links
        for index, chip in enumerate(self.columns):
            self.ship(
                self.block(1 - n.c, chip, 4), self.at(self.core_in, chip, 4), self.C + index, n.to_core
            )
            self.own_copy(index).start()

    def second(self):
        n = self.links
        for index, chip in enumerate(self.columns):
            self.take(self.at(self.core_in, chip, 4), self.C + index, n.to_core)
            self.own_copy(index).wait()
            self.add(4, (self.part, chip), (self.core_in, chip))
            if index == 0:
                self.ship(self.at(self.part, chip, 2), self.at(self.d_y, 0, 2), self.DY, n.to_y)
                self.ship(self.at(self.part, chip + 2, 2), self.at(self.d_x, 0, 2), self.DX, n.to_x)
            elif index == 1:
                self.ship(
                    self.at(self.part, chip + 2, 2), self.at(self.o_x, 2, 2), self.OX + 1, n.to_x
                )
            elif index == 2:
                self.ship(self.at(self.part, chip, 2), self.at(self.o_y, 0, 2), self.OY, n.to_y)

    def third(self):
        n = self.links
        self.take(self.at(self.d_y, 0, 2), self.DY, n.to_y)
        self.add(2, (self.part, n.chip_x), (self.d_y, 0))
        self.ship(self.at(self.part, n.chip_x, 2), self.at(self.o_x, 0, 2), self.OX, n.to_x)
        self.take(self.at(self.d_x, 0, 2), self.DX, n.to_x)
        self.add(2, (self.part, n.chip_y + 2), (self.d_x, 0))
        self.ship(self.at(self.part, n.chip_y + 2, 2), self.at(self.o_y, 2, 2), self.OY + 1, n.to_y)

    def fourth(self):
        n = self.links
        self.take(self.at(self.o_x, 2, 2), self.OX + 1, n.to_x)
        self.take(self.at(self.o_y, 0, 2), self.OY, n.to_y)
        self.take(self.at(self.o_x, 0, 2), self.OX, n.to_x)
        self.take(self.at(self.o_y, 2, 2), self.OY + 1, n.to_y)
        self.add(4, (self.part, n.chip_own), (self.o_x, 0), (self.o_y, 0))
        for j in (1, 2, 3):
            n.send(
                self.at(self.part, n.chip_own + n.level(j), 1),
                self.at(self.z_in, 3 - j, 1),
                self.sends.at[self.group, self.Z + j - 1],
                self.recvs.at[self.group, self.Z + 3 - j],
                n.to_z[j],
            )

    def fifth(self):
        n = self.links
        total = self.at(self.part, n.chip_own + n.z, 1)[...].astype(jnp.float32)
        for k in (1, 2, 3):
            ref = self.at(self.z_in, k - 1, 1)
            self.take(ref, self.Z + k - 1, n.to_z[k])
            total = total + ref[...].astype(jnp.float32)
        return total

    def trade(self, total, fin, fin_in):
        n = self.links
        rows = self.rows // 2
        fin[...] = total
        theirs = fin.at[pl.ds(pl.multiple_of((1 - n.c) * rows, rows), rows)]
        self.ship(theirs, fin_in, self.F, n.to_core)

    def whole(self, fin, fin_in):
        n = self.links
        rows = self.rows // 2
        self.take(fin_in, self.F, n.to_core)
        mine = fin[pl.ds(pl.multiple_of(n.c * rows, rows), rows), :]
        theirs = fin_in[...]
        return jnp.where(n.c == 0, mine, theirs), jnp.where(n.c == 0, theirs, mine)


def pick_lanes(tiles, step, count):
    parts = []
    lane = lax.broadcasted_iota(jnp.int32, (8, 128), 1)
    for i in range(count):
        index, shift = i * step // 128, i * step % 128
        part = pltpu.roll(tiles[index], 128 - shift, 1) if shift else tiles[index]
        if shift + step > 128:
            after = pltpu.roll(tiles[index + 1], 128 - shift, 1)
            part = jnp.where(lane < 128 - shift, part, after)
        parts.append(jnp.where(lane < step, part, 0.0))
    return parts


def last_kernel(
    tokens_hbm,
    attn_hbm,
    d_mid_hbm,
    grad_up,
    grad_down,
    grad_out,
    grad_proj,
    grad_vectors,
    grad_up_bias,
    qkv,
    context,
    d_context,
    logsums,
    live_segment_column,
    segment_row,
    grad_tokens,
    own_query,
    own_key,
    own_value,
    own_out,
    own_up,
    own_down,
    own_small,
    tokens,
    attn_mat,
    d_mid,
    grad_attn,
    small_all,
    d_qkv,
    rowdots,
    bias,
    *rest,
):
    held = [rest[7 * i : 7 * i + 7] for i in range(4)]
    fins = rest[28:34]
    sends, recvs, own_sems, local_sems = rest[34:]
    links = Links()
    down = Scatter(links, rows_block(grad_down, 192, 384), 192, held[0], sends, recvs, own_sems, 0)
    up = Scatter(links, rows_block(grad_up, 48, 1536), 48, held[1], sends, recvs, own_sems, 1)
    attn = Scatter(links, rows_block(grad_attn, 48, 1536), 48, held[2], sends, recvs, own_sems, 2)
    tiny = Scatter(links, lead_block(small_all), 1, held[3], sends, recvs, own_sems, 3)
    loads = [
        pltpu.make_async_copy(tokens_hbm, tokens, local_sems.at[0]),
        pltpu.make_async_copy(attn_hbm, attn_mat, local_sems.at[1]),
        pltpu.make_async_copy(d_mid_hbm, d_mid, local_sems.at[2]),
    ]
    links.greet()
    down.first()
    up.first()
    rows_dev = bias.shape[0]
    row_dots(context, d_context, rowdots, rows_dev)
    mask_bias(live_segment_column, segment_row, bias)
    down.second()
    up.second()
    for load in loads:
        load.start()

    def attend(item, carry):
        attend_back_pair(item, qkv, d_context, logsums, rowdots, d_qkv, bias)
        return carry

    lax.fori_loop(0, 3, attend, 0)
    down.third()
    lax.fori_loop(3, 6, attend, 0)
    up.third()
    lax.fori_loop(6, 8, attend, 0)
    down.fourth()
    lax.fori_loop(8, 12, attend, 0)
    for load in loads:
        load.wait()
    up.fourth()

    grad_attn[:, 3 * WIDTH :] = grad_out[...]

    def weigh(step, carry):
        rows = pl.ds(pl.multiple_of(step * 256, 256), 256)
        for index in range(3):
            columns = slice(index * WIDTH, (index + 1) * WIDTH)
            grad_attn[rows, columns] = dotted(tokens[:, rows], d_qkv[:, columns], 0, 0).astype(
                jnp.bfloat16
            )
        return carry

    lax.fori_loop(0, WIDTH // 256, weigh, 0)
    attn.first()

    ones = jnp.ones((8, tokens.shape[0]), jnp.bfloat16)
    row = lax.broadcasted_iota(jnp.int32, (8, WIDTH), 0)
    vectors = grad_vectors[...]
    vectors = jnp.where(row == 0, dotted(ones, d_qkv[:, 0:WIDTH], 1, 0), vectors)
    vectors = jnp.where(row == 1, dotted(ones, d_qkv[:, 2 * WIDTH : 3 * WIDTH], 1, 0), vectors)
    parts = pick_lanes([vectors[:, i * 128 : (i + 1) * 128] for i in range(WIDTH // 128)], 24, SHARDS)
    for i, part in enumerate(parts):
        small_all[i % 2, i // 2, 24:32, :] = part
    parts = pick_lanes(
        [grad_up_bias[:, i * 128 : (i + 1) * 128] for i in range(HIDDEN // 128)], 96, SHARDS
    )
    for i, part in enumerate(parts):
        small_all[i % 2, i // 2, 32:40, :] = part
        small_all[i % 2, i // 2, 0:24, :] = grad_proj[i * 24 : (i + 1) * 24, :]
    tiny.first()
    attn.second()
    tiny.second()

    def back(step, carry):
        rows = pl.ds(pl.multiple_of(step * 256, 256), 256)
        out = dotted(d_qkv[rows, :], attn_mat[:, 0 : 3 * WIDTH], 1, 1)
        grad_tokens[rows, :] = out + d_mid[rows, :]
        return carry

    lax.fori_loop(0, 2, back, 0)
    down.trade(down.fifth(), fins[0], fins[1])
    attn.third()
    tiny.third()
    lax.fori_loop(2, 4, back, 0)
    up.trade(up.fifth(), fins[2], fins[3])
    tiny.fourth()
    attn.fourth()
    first, second = down.whole(fins[0], fins[1])
    own_down[:, : WIDTH // 2] = first
    own_down[:, WIDTH // 2 :] = second
    first, second = up.whole(fins[2], fins[3])
    own_up[:, : HIDDEN // 2] = first
    own_up[:, HIDDEN // 2 :] = second
    own_small[...] = tiny.fifth()[0]
    attn.trade(attn.fifth(), fins[4], fins[5])
    first, second = attn.whole(fins[4], fins[5])
    own_query[...] = first[:, :WIDTH]
    own_key[...] = first[:, WIDTH:]
    own_value[...] = second[:, :WIDTH]
    own_out[...] = second[:, WIDTH:]
    links.finish()


def run_last(
    tokens,
    attn_mat,
    d_mid,
    grad_up,
    grad_down,
    grad_out,
    grad_proj,
    grad_vectors,
    grad_up_bias,
    qkv,
    context,
    d_context,
    logsums,
    live_segment_column,
    segment_row,
):
    count = tokens.shape[0]
    rows_dev = count // SEQ
    vmem = pl.BlockSpec(memory_space=pltpu.VMEM)
    anywhere = pl.BlockSpec(memory_space=pl.ANY)
    low = jnp.bfloat16
    wide = jnp.float32

    def held(unit, kind):
        def buffer(units):
            return pltpu.VMEM((units * unit[0],) + unit[1:], kind)

        return [buffer(n) for n in (16, 16, 2, 2, 4, 4, 3)]

    fins = []
    for rows, columns in ((192, 384), (48, 1536), (48, 1536)):
        fins += [pltpu.VMEM((rows, columns), wide), pltpu.VMEM((rows // 2, columns), wide)]
    return pl.pallas_call(
        last_kernel,
        out_shape=[
            jax.ShapeDtypeStruct((count, WIDTH), wide),
            jax.ShapeDtypeStruct((24, WIDTH), wide),
            jax.ShapeDtypeStruct((24, WIDTH), wide),
            jax.ShapeDtypeStruct((24, WIDTH), wide),
            jax.ShapeDtypeStruct((24, WIDTH), wide),
            jax.ShapeDtypeStruct((24, HIDDEN), wide),
            jax.ShapeDtypeStruct((96, WIDTH), wide),
            jax.ShapeDtypeStruct((SMALL, 128), wide),
        ],
        in_specs=[anywhere] * 5 + [vmem] * 10,
        out_specs=[vmem] * 8,
        scratch_shapes=[
            pltpu.VMEM((count, WIDTH), low),
            pltpu.VMEM((WIDTH, HIDDEN), low),
            pltpu.VMEM((count, WIDTH), wide),
            pltpu.VMEM((WIDTH, HIDDEN), low),
            pltpu.VMEM((2, CHIPS, SMALL, 128), wide),
            pltpu.VMEM((count, 3 * WIDTH), low),
            pltpu.VMEM((rows_dev, HEADS // 2, 8, SEQ), wide),
            pltpu.VMEM((rows_dev, SEQ, SEQ), wide),
        ]
        + held((192, 384), low)
        + held((48, 1536), low)
        + held((48, 1536), low)
        + held((1, SMALL, 128), wide)
        + fins
        + [
            pltpu.SemaphoreType.DMA((4, 14)),
            pltpu.SemaphoreType.DMA((4, 14)),
            pltpu.SemaphoreType.DMA((4, 4)),
            pltpu.SemaphoreType.DMA((3,)),
        ],
        compiler_params=pltpu.CompilerParams(
            collective_id=1, has_side_effects=True, vmem_limit_bytes=62 * 2**20
        ),
        name="attend_back_scatter",
    )(
        tokens,
        attn_mat,
        d_mid,
        grad_up,
        grad_down,
        grad_out,
        grad_proj,
        grad_vectors,
        grad_up_bias,
        qkv,
        context,
        d_context,
        logsums,
        live_segment_column,
        segment_row,
    )


def body_tiles(
    tokens,
    w_query,
    b_query,
    w_key,
    w_value,
    b_value,
    w_out,
    b_out,
    gain_one,
    shift_one,
    w_up,
    b_up,
    w_down,
    b_down,
    gain_two,
    shift_two,
    w_proj,
    segment_ids,
    row_lengths,
    teacher_index,
    teacher_table,
):
    rows_dev = tokens.shape[0]
    width = tokens.shape[2]
    flat = tokens.reshape(rows_dev * SEQ, width)
    positions = jnp.arange(SEQ, dtype=jnp.int32)
    live = positions[None, :] < row_lengths[:, None]
    live_segment = jnp.where(live, segment_ids, -1)
    vectors = jnp.stack([b_query, b_value, b_out, gain_one, shift_one, b_down, gain_two, shift_two])
    small = jnp.concatenate(
        [
            w_proj,
            jnp.pad(vectors, ((0, 0), (0, 128 - vectors.shape[1]))),
            jnp.pad(b_up[None, :], ((0, 7), (0, 128 - b_up.shape[0]))),
        ]
    )
    attn_mat, up_mat, down_mat, proj, vectors_all, up_bias, qkv, context_low, logsums = run_first(
        flat,
        (w_query, w_key, w_value, w_out, w_up, w_down),
        small,
        segment_ids.reshape(rows_dev * SEQ, 1),
        live_segment.reshape(rows_dev, 1, SEQ),
    )
    out_bias, gain_first, shift_first, down_bias, gain_second, shift_second = (
        vectors_all[i : i + 1] for i in range(2, 8)
    )
    proj_mat = proj.astype(jnp.bfloat16)
    out_mat = attn_mat[:, 3 * width :]
    branch_one = matmul(context_low, out_mat) + out_bias
    mid_one = flat.astype(jnp.float32) + branch_one
    hidden_one, normed_one, scaled_one = normalise(mid_one, gain_first, shift_first)
    hidden_one_low = hidden_one.astype(jnp.bfloat16)
    upward = matmul(hidden_one_low, up_mat) + up_bias[0:1]
    activated = gelu_exact(upward).astype(jnp.bfloat16)
    branch_two = matmul(activated, down_mat) + down_bias
    hidden_two, normed_two, scaled_two = normalise(
        hidden_one + branch_two, gain_second, shift_second
    )
    hidden_two_low = hidden_two.astype(jnp.bfloat16)
    raw_embed = matmul(hidden_two_low, proj_mat)
    inverse = lax.rsqrt(jnp.sum(raw_embed * raw_embed, -1, keepdims=True) + UNIT_EPS)
    embeddings = raw_embed * inverse
    embed_dim = embeddings.shape[1]
    embed_low = embeddings.astype(jnp.bfloat16).reshape(rows_dev, SEQ, embed_dim)
    query_low = embed_low[:, :QLEN]
    similar = jnp.einsum("rqc,rsc->rqs", query_low, embed_low, preferred_element_type=jnp.float32)
    passages = jnp.arange(1, NPASS + 1, dtype=jnp.int32)
    member = (segment_ids[:, None, :] == passages[None, :, None]) & live[:, None, :]
    masked = jnp.where(member[:, None], similar[:, :, None, :] / SOFTNESS, MASK_FILL)
    peak = jnp.max(masked, -1, keepdims=True)
    shifted = jnp.exp(masked - peak)
    totals = jnp.sum(shifted, -1, keepdims=True)
    student = SOFTNESS * jnp.sum(peak[..., 0] + jnp.log(totals[..., 0]), axis=1)
    choose = teacher_index[..., None] == jnp.arange(TABLE, dtype=jnp.int32)
    teacher = jnp.sum(jnp.where(choose, teacher_table, 0.0), -1)
    teacher_logp = jax.nn.log_softmax(teacher, axis=-1)
    student_logp = jax.nn.log_softmax(student, axis=-1)
    losses = jnp.sum(jnp.exp(teacher_logp) * (teacher_logp - student_logp), -1)
    d_student = jnp.exp(student_logp) - jnp.exp(teacher_logp)
    spread_weights = shifted / totals
    d_similar = jnp.einsum("rp,rqps->rqs", d_student, spread_weights).astype(jnp.bfloat16)
    d_embed = jnp.einsum("rqs,rqc->rsc", d_similar, query_low, preferred_element_type=jnp.float32)
    d_query_part = jnp.einsum(
        "rqs,rsc->rqc", d_similar, embed_low, preferred_element_type=jnp.float32
    )
    d_embed = jnp.concatenate([d_embed[:, :QLEN] + d_query_part, d_embed[:, QLEN:]], 1).reshape(
        rows_dev * SEQ, embed_dim
    )
    d_raw = (
        inverse * (d_embed - embeddings * jnp.sum(d_embed * embeddings, -1, keepdims=True))
    ).astype(jnp.bfloat16)
    grad_proj = over_rows(hidden_two_low, d_raw)
    d_hidden_two = against(d_raw, proj_mat)
    d_mid_two, grad_gain_second, grad_shift_second = normalise_back(
        d_hidden_two, normed_two, scaled_two, gain_second
    )
    d_branch_two = d_mid_two.astype(jnp.bfloat16)
    grad_down = over_rows(activated, d_branch_two)
    grad_down_bias = jnp.sum(d_branch_two, 0, dtype=jnp.float32)
    d_upward = (against(d_branch_two, down_mat) * gelu_slope(upward)).astype(jnp.bfloat16)
    grad_up = over_rows(hidden_one_low, d_upward)
    grad_up_bias = jnp.sum(d_upward, 0, dtype=jnp.float32)
    d_hidden_one = d_mid_two + against(d_upward, up_mat)
    d_mid_one, grad_gain_first, grad_shift_first = normalise_back(
        d_hidden_one, normed_one, scaled_one, gain_first
    )
    d_branch_one = d_mid_one.astype(jnp.bfloat16)
    grad_out = over_rows(context_low, d_branch_one)
    grad_out_bias = jnp.sum(d_branch_one, 0, dtype=jnp.float32)
    d_context = against(d_branch_one, out_mat).astype(jnp.bfloat16)
    nothing = jnp.zeros_like(grad_out_bias)
    grad_vectors = jnp.stack(
        [
            nothing,
            nothing,
            grad_out_bias,
            grad_gain_first,
            grad_shift_first,
            grad_down_bias,
            grad_gain_second,
            grad_shift_second,
        ]
    )
    grad_input, own_query, own_key, own_value, own_out, own_up, own_down, own_small = run_last(
        flat,
        attn_mat,
        d_mid_one,
        grad_up.astype(jnp.bfloat16),
        grad_down.astype(jnp.bfloat16),
        grad_out.astype(jnp.bfloat16),
        grad_proj,
        grad_vectors,
        jnp.pad(grad_up_bias[None, :], ((0, 7), (0, 0))),
        qkv,
        context_low,
        d_context,
        logsums,
        live_segment.reshape(rows_dev * SEQ, 1),
        segment_ids.reshape(rows_dev, 1, SEQ),
    )
    owned = [own_small[24 + i, :24] for i in range(8)]
    return (
        losses,
        embeddings.reshape(rows_dev, SEQ, embed_dim),
        grad_input.reshape(rows_dev, SEQ, width),
        own_query,
        owned[0],
        own_key,
        own_value,
        owned[1],
        own_out,
        owned[2],
        owned[3],
        owned[4],
        own_up,
        own_small[32, :96],
        own_down,
        owned[5],
        owned[6],
        owned[7],
        own_small[:24],
    )


def solution(mesh):
    in_specs = (
        P(("dp", "fsdp"), None, None),
        P(("dp", "fsdp"), None),
        P(("dp", "fsdp")),
        P(("dp", "fsdp"), None),
        P(("dp", "fsdp"), None),
        P(("dp", "fsdp")),
        P(("dp", "fsdp"), None),
        P(("dp", "fsdp")),
        P(("dp", "fsdp")),
        P(("dp", "fsdp")),
        P(("dp", "fsdp"), None),
        P(("dp", "fsdp")),
        P(("dp", "fsdp"), None),
        P(("dp", "fsdp")),
        P(("dp", "fsdp")),
        P(("dp", "fsdp")),
        P(("dp", "fsdp"), None),
        P(("dp", "fsdp"), None),
        P(("dp", "fsdp")),
        P(("dp", "fsdp"), None),
        P(),
    )
    out_specs = (
        P(("dp", "fsdp")),
        P(("dp", "fsdp"), None, None),
        P(("dp", "fsdp"), None, None),
        P(("dp", "fsdp"), None),
        P(("dp", "fsdp")),
        P(("dp", "fsdp"), None),
        P(("dp", "fsdp"), None),
        P(("dp", "fsdp")),
        P(("dp", "fsdp"), None),
        P(("dp", "fsdp")),
        P(("dp", "fsdp")),
        P(("dp", "fsdp")),
        P(("dp", "fsdp"), None),
        P(("dp", "fsdp")),
        P(("dp", "fsdp"), None),
        P(("dp", "fsdp")),
        P(("dp", "fsdp")),
        P(("dp", "fsdp")),
        P(("dp", "fsdp"), None),
    )
    body = body_tiles if fits(mesh) else body_whole
    return jax.shard_map(body, mesh=mesh, in_specs=in_specs, out_specs=out_specs, check_vma=False)
```

```python
import functools
import math

import jax
import jax.numpy as jnp
from jax import lax
from jax.experimental import pallas as pl
from jax.experimental.pallas import tpu as pltpu
from jax.sharding import PartitionSpec as P

HEADS = 12
HEAD = 64
SEQ = 512
QLEN = 32
NPASS = 8
TABLE = 1024


NORM_EPS = 1e-12
UNIT_EPS = 1e-12
SOFTNESS = 0.1
MASK_FILL = -1000000000.0
ROOT_HALF = 0.7071067811865476
DENSITY_SCALE = 0.3989422804014327


def matmul(left, right):
    return jnp.dot(left, right, preferred_element_type=jnp.float32)


def over_rows(left, right):
    return lax.dot_general(
        left, right, (((0,), (0,)), ((), ())), preferred_element_type=jnp.float32
    )


def against(left, right):
    return lax.dot_general(
        left, right, (((1,), (1,)), ((), ())), preferred_element_type=jnp.float32
    )


def normalise(mixed, gain, shift):
    centred = mixed - jnp.mean(mixed, -1, keepdims=True)
    scaled = lax.rsqrt(jnp.mean(centred * centred, -1, keepdims=True) + NORM_EPS)
    normed = centred * scaled
    return (normed * gain + shift, normed, scaled)


def normalise_back(grad_out, normed, scaled, gain):
    inner = grad_out * gain
    grad_in = scaled * (
        inner
        - jnp.mean(inner, -1, keepdims=True)
        - normed * jnp.mean(inner * normed, -1, keepdims=True)
    )
    return (grad_in, jnp.sum(grad_out * normed, 0), jnp.sum(grad_out, 0))


def gelu_exact(upward):
    return 0.5 * upward * (1.0 + lax.erf(upward * ROOT_HALF))


def gelu_slope(upward):
    return (
        0.5 * (1.0 + lax.erf(upward * ROOT_HALF))
        + upward * jnp.exp(-0.5 * upward * upward) * DENSITY_SCALE
    )


def split_heads(matrix, rows_dev):
    return (
        matrix.reshape(rows_dev, SEQ, HEADS, HEAD)
        .transpose(0, 2, 1, 3)
        .reshape(rows_dev * HEADS, SEQ, HEAD)
    )


def join_heads(stacked, rows_dev):
    return (
        stacked.reshape(rows_dev, HEADS, SEQ, HEAD)
        .transpose(0, 2, 1, 3)
        .reshape(rows_dev * SEQ, HEADS * HEAD)
    )


def collect(sent):
    return (
        lax.all_gather(sent[0], ("dp", "fsdp"), axis=0, tiled=True),
        lax.all_gather(sent[1], ("dp", "fsdp"), axis=0, tiled=True),
        lax.all_gather(sent[2], ("dp", "fsdp"), axis=0, tiled=True),
        lax.all_gather(sent[3], ("dp", "fsdp"), axis=0, tiled=True),
        lax.all_gather(sent[4], ("dp", "fsdp"), axis=0, tiled=True),
        lax.all_gather(sent[5], ("dp", "fsdp"), axis=0, tiled=True),
        lax.all_gather(sent[6], ("dp", "fsdp"), axis=0, tiled=True),
        lax.all_gather(sent[7], ("dp", "fsdp"), axis=0, tiled=True),
        lax.all_gather(sent[8], ("dp", "fsdp"), axis=0, tiled=True),
        lax.all_gather(sent[9], ("dp", "fsdp"), axis=0, tiled=True),
        lax.all_gather(sent[10], ("dp", "fsdp"), axis=0, tiled=True),
        lax.all_gather(sent[11], ("dp", "fsdp"), axis=0, tiled=True),
        lax.all_gather(sent[12], ("dp", "fsdp"), axis=0, tiled=True),
        lax.all_gather(sent[13], ("dp", "fsdp"), axis=0, tiled=True),
        lax.all_gather(sent[14], ("dp", "fsdp"), axis=0, tiled=True),
        lax.all_gather(sent[15], ("dp", "fsdp"), axis=0, tiled=True),
    )


def spread_grads(terms):
    return (
        lax.psum_scatter(terms[0], ("dp", "fsdp"), scatter_dimension=0, tiled=True),
        lax.psum_scatter(terms[1], ("dp", "fsdp"), scatter_dimension=0, tiled=True),
        lax.psum_scatter(terms[2], ("dp", "fsdp"), scatter_dimension=0, tiled=True),
        lax.psum_scatter(terms[3], ("dp", "fsdp"), scatter_dimension=0, tiled=True),
        lax.psum_scatter(terms[4], ("dp", "fsdp"), scatter_dimension=0, tiled=True),
        lax.psum_scatter(terms[5], ("dp", "fsdp"), scatter_dimension=0, tiled=True),
        lax.psum_scatter(terms[6], ("dp", "fsdp"), scatter_dimension=0, tiled=True),
        lax.psum_scatter(terms[7], ("dp", "fsdp"), scatter_dimension=0, tiled=True),
        lax.psum_scatter(terms[8], ("dp", "fsdp"), scatter_dimension=0, tiled=True),
        lax.psum_scatter(terms[9], ("dp", "fsdp"), scatter_dimension=0, tiled=True),
        lax.psum_scatter(terms[10], ("dp", "fsdp"), scatter_dimension=0, tiled=True),
        lax.psum_scatter(terms[11], ("dp", "fsdp"), scatter_dimension=0, tiled=True),
        lax.psum_scatter(terms[12], ("dp", "fsdp"), scatter_dimension=0, tiled=True),
        lax.psum_scatter(terms[13], ("dp", "fsdp"), scatter_dimension=0, tiled=True),
        lax.psum_scatter(terms[14], ("dp", "fsdp"), scatter_dimension=0, tiled=True),
        lax.psum_scatter(terms[15], ("dp", "fsdp"), scatter_dimension=0, tiled=True),
    )


def body_whole(
    tokens,
    w_query,
    b_query,
    w_key,
    w_value,
    b_value,
    w_out,
    b_out,
    gain_one,
    shift_one,
    w_up,
    b_up,
    w_down,
    b_down,
    gain_two,
    shift_two,
    w_proj,
    segment_ids,
    row_lengths,
    teacher_index,
    teacher_table,
):
    rows_dev = tokens.shape[0]
    width = tokens.shape[2]
    scale = 1.0 / math.sqrt(HEAD)
    shards = (
        w_query,
        b_query,
        w_key,
        w_value,
        b_value,
        w_out,
        b_out,
        gain_one,
        shift_one,
        w_up,
        b_up,
        w_down,
        b_down,
        gain_two,
        shift_two,
        w_proj,
    )
    sent = tuple((member.astype(jnp.bfloat16) for member in shards))
    gathered = collect(sent)
    (
        query_mat,
        query_bias,
        key_mat,
        value_mat,
        value_bias,
        out_mat,
        out_bias,
        gain_first,
        shift_first,
        up_mat,
        up_bias,
        down_mat,
        down_bias,
        gain_second,
        shift_second,
        proj_mat,
    ) = gathered

    def visibility(item_index):
        row_index = item_index // HEADS
        segment_row = lax.dynamic_index_in_dim(segment_ids, row_index, 0, keepdims=False)
        length_row = lax.dynamic_index_in_dim(row_lengths, row_index, 0, keepdims=False)
        positions = jnp.arange(SEQ, dtype=jnp.int32)
        return (segment_row[:, None] == segment_row[None, :]) & (positions[None, :] < length_row)

    def attend(inputs):
        query_h, key_h, value_h, item_index = inputs
        scores = jnp.where(visibility(item_index), against(query_h, key_h) * scale, MASK_FILL)
        peak = jnp.max(scores, -1, keepdims=True)
        shifted = jnp.exp(scores - peak)
        totals = jnp.sum(shifted, -1, keepdims=True)
        chances = (shifted / totals).astype(jnp.bfloat16)
        context_h = matmul(chances, value_h).astype(jnp.bfloat16)
        return (context_h, (peak + jnp.log(totals))[:, 0])

    def attend_back(inputs):
        query_h, key_h, value_h, grad_h, logsum, item_index = inputs
        scores = jnp.where(visibility(item_index), against(query_h, key_h) * scale, MASK_FILL)
        chances = jnp.exp(scores - logsum[:, None])
        d_chances = against(grad_h, value_h)
        rowdot = jnp.sum(chances * d_chances, -1, keepdims=True)
        d_scores = (chances * (d_chances - rowdot)).astype(jnp.bfloat16)
        d_query_h = (matmul(d_scores, key_h) * scale).astype(jnp.bfloat16)
        d_key_h = (over_rows(d_scores, query_h) * scale).astype(jnp.bfloat16)
        d_value_h = over_rows(chances.astype(jnp.bfloat16), grad_h).astype(jnp.bfloat16)
        return (d_query_h, d_key_h, d_value_h)

    flat = tokens.reshape(rows_dev * SEQ, width)
    queries = (matmul(flat, query_mat) + query_bias.astype(jnp.float32)).astype(jnp.bfloat16)
    keys_all = matmul(flat, key_mat).astype(jnp.bfloat16)
    values = (matmul(flat, value_mat) + value_bias.astype(jnp.float32)).astype(jnp.bfloat16)
    query_heads = split_heads(queries, rows_dev)
    key_heads = split_heads(keys_all, rows_dev)
    value_heads = split_heads(values, rows_dev)
    items = jnp.arange(rows_dev * HEADS, dtype=jnp.int32)
    context_heads, logsums = lax.map(attend, (query_heads, key_heads, value_heads, items))
    context_low = join_heads(context_heads, rows_dev)
    branch_one = matmul(context_low, out_mat) + out_bias.astype(jnp.float32)
    mid_one = flat.astype(jnp.float32) + branch_one
    hidden_one, normed_one, scaled_one = normalise(
        mid_one, gain_first.astype(jnp.float32), shift_first.astype(jnp.float32)
    )
    hidden_one_low = hidden_one.astype(jnp.bfloat16)
    upward = matmul(hidden_one_low, up_mat) + up_bias.astype(jnp.float32)
    activated = gelu_exact(upward).astype(jnp.bfloat16)
    branch_two = matmul(activated, down_mat) + down_bias.astype(jnp.float32)
    hidden_two, normed_two, scaled_two = normalise(
        hidden_one + branch_two, gain_second.astype(jnp.float32), shift_second.astype(jnp.float32)
    )
    hidden_two_low = hidden_two.astype(jnp.bfloat16)
    raw_embed = matmul(hidden_two_low, proj_mat)
    inverse = lax.rsqrt(jnp.sum(raw_embed * raw_embed, -1, keepdims=True) + UNIT_EPS)
    embeddings = raw_embed * inverse
    embed_dim = embeddings.shape[1]
    embed_low = embeddings.astype(jnp.bfloat16).reshape(rows_dev, SEQ, embed_dim)
    query_low = embed_low[:, :QLEN]
    similar = jnp.einsum("rqc,rsc->rqs", query_low, embed_low, preferred_element_type=jnp.float32)
    positions = jnp.arange(SEQ, dtype=jnp.int32)
    live = positions[None, :] < row_lengths[:, None]
    passages = jnp.arange(1, NPASS + 1, dtype=jnp.int32)
    member = (segment_ids[:, None, :] == passages[None, :, None]) & live[:, None, :]
    masked = jnp.where(member[:, None], similar[:, :, None, :] / SOFTNESS, MASK_FILL)
    peak = jnp.max(masked, -1, keepdims=True)
    shifted = jnp.exp(masked - peak)
    totals = jnp.sum(shifted, -1, keepdims=True)
    student = SOFTNESS * jnp.sum(peak[..., 0] + jnp.log(totals[..., 0]), axis=1)
    choose = teacher_index[..., None] == jnp.arange(TABLE, dtype=jnp.int32)
    teacher = jnp.sum(jnp.where(choose, teacher_table, 0.0), -1)
    teacher_logp = jax.nn.log_softmax(teacher, axis=-1)
    student_logp = jax.nn.log_softmax(student, axis=-1)
    losses = jnp.sum(jnp.exp(teacher_logp) * (teacher_logp - student_logp), -1)
    again = collect(sent)
    (
        query_back,
        query_bias_back,
        key_back,
        value_back,
        value_bias_back,
        out_back,
        out_bias_back,
        gain_first_back,
        shift_first_back,
        up_back,
        up_bias_back,
        down_back,
        down_bias_back,
        gain_second_back,
        shift_second_back,
        proj_back,
    ) = again
    d_student = jnp.exp(student_logp) - jnp.exp(teacher_logp)
    spread_weights = shifted / totals
    d_similar = jnp.einsum("rp,rqps->rqs", d_student, spread_weights).astype(jnp.bfloat16)
    d_embed = jnp.einsum("rqs,rqc->rsc", d_similar, query_low, preferred_element_type=jnp.float32)
    d_query_part = jnp.einsum(
        "rqs,rsc->rqc", d_similar, embed_low, preferred_element_type=jnp.float32
    )
    d_embed = jnp.concatenate([d_embed[:, :QLEN] + d_query_part, d_embed[:, QLEN:]], 1).reshape(
        rows_dev * SEQ, embed_dim
    )
    d_raw = (
        inverse * (d_embed - embeddings * jnp.sum(d_embed * embeddings, -1, keepdims=True))
    ).astype(jnp.bfloat16)
    grad_proj = over_rows(hidden_two_low, d_raw)
    d_hidden_two = against(d_raw, proj_back)
    d_mid_two, grad_gain_second, grad_shift_second = normalise_back(
        d_hidden_two, normed_two, scaled_two, gain_second_back.astype(jnp.float32)
    )
    d_branch_two = d_mid_two.astype(jnp.bfloat16)
    grad_down = over_rows(activated, d_branch_two)
    grad_down_bias = jnp.sum(d_branch_two, 0, dtype=jnp.float32)
    d_upward = (against(d_branch_two, down_back) * gelu_slope(upward)).astype(jnp.bfloat16)
    grad_up = over_rows(hidden_one_low, d_upward)
    grad_up_bias = jnp.sum(d_upward, 0, dtype=jnp.float32)
    d_hidden_one = d_mid_two + against(d_upward, up_back)
    d_mid_one, grad_gain_first, grad_shift_first = normalise_back(
        d_hidden_one, normed_one, scaled_one, gain_first_back.astype(jnp.float32)
    )
    d_branch_one = d_mid_one.astype(jnp.bfloat16)
    grad_out = over_rows(context_low, d_branch_one)
    grad_out_bias = jnp.sum(d_branch_one, 0, dtype=jnp.float32)
    d_context = against(d_branch_one, out_back).astype(jnp.bfloat16)
    d_context_heads = split_heads(d_context, rows_dev)
    d_query_heads, d_key_heads, d_value_heads = lax.map(
        attend_back, (query_heads, key_heads, value_heads, d_context_heads, logsums, items)
    )
    d_queries = join_heads(d_query_heads, rows_dev)
    d_keys = join_heads(d_key_heads, rows_dev)
    d_values = join_heads(d_value_heads, rows_dev)
    grad_query = over_rows(flat, d_queries)
    grad_query_bias = jnp.sum(d_queries, 0, dtype=jnp.float32)
    grad_key = over_rows(flat, d_keys)
    grad_value = over_rows(flat, d_values)
    grad_value_bias = jnp.sum(d_values, 0, dtype=jnp.float32)
    grad_input = (
        d_mid_one
        + against(d_queries, query_back)
        + against(d_keys, key_back)
        + against(d_values, value_back)
    )
    terms = (
        grad_query,
        grad_query_bias,
        grad_key,
        grad_value,
        grad_value_bias,
        grad_out,
        grad_out_bias,
        grad_gain_first,
        grad_shift_first,
        grad_up,
        grad_up_bias,
        grad_down,
        grad_down_bias,
        grad_gain_second,
        grad_shift_second,
        grad_proj,
    )
    owned = spread_grads(terms)
    return (
        losses,
        embeddings.reshape(rows_dev, SEQ, embed_dim),
        grad_input.reshape(rows_dev, SEQ, width),
        owned[0],
        owned[1],
        owned[2],
        owned[3],
        owned[4],
        owned[5],
        owned[6],
        owned[7],
        owned[8],
        owned[9],
        owned[10],
        owned[11],
        owned[12],
        owned[13],
        owned[14],
        owned[15],
    )


MESH = pl.DeviceIdType.MESH
EXP2_SCALE = 1.4426950408889634 / math.sqrt(HEAD)
SHARDS = 32
CHIPS = 16
WIDTH = 768
HIDDEN = 3072
EMBED = 128
SMALL = 40
PAIRS = HEADS // 2
CHUNK = 256


def fits(mesh):
    return dict(mesh.shape) == {"dp": 4, "fsdp": 8}


def dotted(left, right, left_dim, right_dim):
    return lax.dot_general(
        left,
        right,
        (((left_dim,), (right_dim,)), ((), ())),
        preferred_element_type=jnp.float32,
    )


def part_of(start, size):
    return pl.ds(pl.multiple_of(start * size, size), size)


def value_of(number):
    return number() if callable(number) else number


def place():
    outer = lax.axis_index("dp")
    inner = lax.axis_index("fsdp")
    return lax.rem(outer, 2), lax.div(outer, 2), lax.div(inner, 2), lax.rem(inner, 2)


def device(x, y, z, c):
    return (y * 2 + x, z * 2 + c)


class Links:
    def __init__(self):
        x, y, z, c = place()
        self.c = c
        self.z = z
        self.chip_own = (y * 2 + x) * 4
        self.chip_x = (y * 2 + 1 - x) * 4
        self.chip_y = ((1 - y) * 2 + x) * 4
        self.chip_d = ((1 - y) * 2 + 1 - x) * 4
        self.to_core = device(x, y, z, 1 - c)
        self.to_x = device(1 - x, y, z, c)
        self.to_y = device(x, 1 - y, z, c)
        self.to_z = [None] + [device(x, y, lax.rem(z + k, 4), c) for k in (1, 2, 3)]
        self.started = []

    def greet(self):
        barrier = pltpu.get_barrier_semaphore()
        partners = [self.to_core, self.to_x, self.to_y] + self.to_z[1:]
        for partner in partners:
            pl.semaphore_signal(barrier, inc=1, device_id=partner, device_id_type=MESH)
        pl.semaphore_wait(barrier, len(partners))

    def level(self, k):
        return lax.rem(self.z + k, 4)

    def send(self, ends, sems, target):
        def copy():
            src, dst = ends()
            send_sem, recv_sem = sems()
            return pltpu.make_async_remote_copy(
                src_ref=src,
                dst_ref=dst,
                send_sem=send_sem,
                recv_sem=recv_sem,
                device_id=target,
                device_id_type=MESH,
            )

        copy().start()
        self.started.append(copy)

    def arrived(self, ref, sems, source):
        pltpu.make_async_remote_copy(
            src_ref=ref,
            dst_ref=ref,
            send_sem=sems[0],
            recv_sem=sems[1],
            device_id=source,
            device_id_type=MESH,
        ).wait_recv()

    def finish(self, first=0):
        for copy in self.started[first:]:
            copy().wait_send()
        self.started = self.started[:first]


def rows_block(ref, rows, columns, base=0):
    def block(core, chip, count):
        return ref.at[
            pl.ds(pl.multiple_of(chip * rows, rows), count * rows),
            pl.ds(pl.multiple_of(base + core * columns, 128), columns),
        ]

    return block


def lead_block(ref):
    def block(core, chip, count):
        return ref.at[core, pl.ds(chip, count)]

    return block


class Gather:
    Z, X, Y, FX, FY, C = 0, 3, 7, 11, 13, 15
    SEMS = 19

    def __init__(self, links, block, sends, recvs, group):
        self.links = links
        self.block = block
        self.sends = sends
        self.recvs = recvs
        self.group = group

    def sems(self, index, there=None):
        there = index if there is None else there
        return self.sends.at[self.group, index], self.recvs.at[self.group, there]

    def ship(self, chip, count, index, target, there=None):
        def ends():
            ref = self.block(self.links.c, value_of(chip), count)
            return ref, ref

        self.links.send(ends, lambda: self.sems(index, there), target)

    def step_of(self, column, k):
        return lambda: column + self.links.level(k)

    def take(self, chip, count, index, source, core=None):
        core = self.links.c if core is None else core
        self.links.arrived(self.block(core, value_of(chip), count), self.sems(index), source)

    def first(self):
        n = self.links
        own = self.step_of(n.chip_own, 0)
        for j in (1, 2, 3):
            self.ship(own, 1, self.Z + j - 1, n.to_z[j], self.Z + 3 - j)
        self.ship(own, 1, self.X, n.to_x)
        self.ship(own, 1, self.Y, n.to_y)

    def second(self):
        n = self.links
        for k in (1, 2, 3):
            chip = self.step_of(n.chip_own, k)
            self.take(chip, 1, self.Z + k - 1, n.to_z[k])
            self.ship(chip, 1, self.X + k, n.to_x)
            self.ship(chip, 1, self.Y + k, n.to_y)
        self.ship(n.chip_own, 4, self.C, n.to_core)

    def third(self):
        n = self.links
        for k in (0, 1):
            chip = self.step_of(n.chip_x, k)
            self.take(chip, 1, self.X + k, n.to_x)
            self.ship(chip, 1, self.FY + k, n.to_y)
        for k in (2, 3):
            chip = self.step_of(n.chip_y, k)
            self.take(chip, 1, self.Y + k, n.to_y)
            self.ship(chip, 1, self.FX + k - 2, n.to_x)
        for k in (2, 3):
            self.take(self.step_of(n.chip_x, k), 1, self.X + k, n.to_x)
        self.ship(n.chip_x, 4, self.C + 1, n.to_core)
        for k in (0, 1):
            self.take(self.step_of(n.chip_y, k), 1, self.Y + k, n.to_y)
        self.ship(n.chip_y, 4, self.C + 2, n.to_core)

    def fourth(self):
        n = self.links
        for k in (0, 1):
            self.take(self.step_of(n.chip_d, k), 1, self.FY + k, n.to_y)
        for k in (2, 3):
            self.take(self.step_of(n.chip_d, k), 1, self.FX + k - 2, n.to_x)
        self.ship(n.chip_d, 4, self.C + 3, n.to_core)

    def last(self):
        n = self.links
        for index, chip in enumerate((n.chip_own, n.chip_x, n.chip_y, n.chip_d)):
            self.take(chip, 4, self.C + index, n.to_core, 1 - n.c)


class Scatter:
    C, DY, DX, OX, OY, Z, F = 0, 4, 5, 6, 8, 10, 13
    SEMS = 14

    def __init__(self, links, block, mine, rows, held, sends, recvs, group):
        self.links = links
        self.block = block
        self.mine = mine
        self.rows = rows
        self.part, self.d_y, self.d_x, self.o_x, self.o_y, self.z_in = held
        self.sends = sends
        self.recvs = recvs
        self.group = group
        n = links
        self.columns = (n.chip_d, n.chip_x, n.chip_y, n.chip_own)

    def at(self, ref, start, count):
        if isinstance(start, int):
            return ref.at[pl.ds(start * self.rows, count * self.rows)]
        return ref.at[pl.ds(pl.multiple_of(start * self.rows, self.rows), count * self.rows)]

    def sems(self, index, there=None):
        there = index if there is None else there
        return self.sends.at[self.group, index], self.recvs.at[self.group, there]

    def ship(self, ends, index, target, there=None):
        self.links.send(ends, lambda: self.sems(index, there), target)

    def ship_part(self, start, count, ref, there, index, target):
        self.ship(
            lambda: (self.at(self.part, value_of(start), count), self.at(ref, there, count)),
            index,
            target,
        )

    def take(self, ref, start, count, index, source):
        self.links.arrived(self.at(ref, start, count), self.sems(index), source)

    def add(self, count, start, *others):
        def step(i, carry):
            here = self.at(self.part, start + i, 1)
            total = here[...].astype(jnp.float32)
            for other in others:
                total = total + other(i)[...].astype(jnp.float32)
            here[...] = total.astype(self.part.dtype)
            return carry

        lax.fori_loop(0, count, step, 0)

    def first(self):
        n = self.links
        for index, chip in enumerate(self.columns):

            def ends(chip=chip):
                return self.block(1 - n.c, chip, 4), self.at(self.part, chip, 4)

            self.ship(ends, self.C + index, n.to_core)

    def second(self):
        n = self.links
        for index, chip in enumerate(self.columns):
            self.take(self.part, chip, 4, self.C + index, n.to_core)
            self.add(4, chip, lambda i, chip=chip: self.mine(chip + i))
            if index == 0:
                self.ship_part(chip, 2, self.d_y, 0, self.DY, n.to_y)
                self.ship_part(lambda chip=chip: chip + 2, 2, self.d_x, 0, self.DX, n.to_x)
            elif index == 1:
                self.ship_part(lambda chip=chip: chip + 2, 2, self.o_x, 2, self.OX + 1, n.to_x)
            elif index == 2:
                self.ship_part(chip, 2, self.o_y, 0, self.OY, n.to_y)

    def third(self):
        n = self.links
        self.take(self.d_y, 0, 2, self.DY, n.to_y)
        self.add(2, n.chip_x, lambda i: self.at(self.d_y, i, 1))
        self.ship_part(n.chip_x, 2, self.o_x, 0, self.OX, n.to_x)
        self.take(self.d_x, 0, 2, self.DX, n.to_x)
        self.add(2, n.chip_y + 2, lambda i: self.at(self.d_x, i, 1))
        self.ship_part(lambda: n.chip_y + 2, 2, self.o_y, 2, self.OY + 1, n.to_y)

    def fourth(self):
        n = self.links
        self.take(self.o_x, 2, 2, self.OX + 1, n.to_x)
        self.take(self.o_y, 0, 2, self.OY, n.to_y)
        self.take(self.o_x, 0, 2, self.OX, n.to_x)
        self.take(self.o_y, 2, 2, self.OY + 1, n.to_y)
        self.add(
            4,
            n.chip_own,
            lambda i: self.at(self.o_x, i, 1),
            lambda i: self.at(self.o_y, i, 1),
        )
        for j in (1, 2, 3):

            def ends(j=j):
                return (
                    self.at(self.part, n.chip_own + n.level(j), 1),
                    self.at(self.z_in, 3 - j, 1),
                )

            self.ship(ends, self.Z + j - 1, n.to_z[j], self.Z + 3 - j)

    def fifth(self):
        n = self.links
        total = self.at(self.part, n.chip_own + n.z, 1)[...].astype(jnp.float32)
        for k in (1, 2, 3):
            self.take(self.z_in, k - 1, 1, self.Z + k - 1, n.to_z[k])
            total = total + self.at(self.z_in, k - 1, 1)[...].astype(jnp.float32)
        return total

    def trade(self, fin, fin_in):
        n = self.links
        rows = self.rows // 2
        fin[...] = self.fifth()
        self.ship(lambda: (fin.at[part_of(1 - n.c, rows)], fin_in), self.F, n.to_core)

    def whole(self, fin, fin_in):
        n = self.links
        rows = self.rows // 2
        n.arrived(fin_in, self.sems(self.F), n.to_core)
        mine = fin[part_of(n.c, rows), :]
        theirs = fin_in[...]
        return jnp.where(n.c == 0, mine, theirs), jnp.where(n.c == 0, theirs, mine)


def spread_lanes(parts, step):
    lane = lax.broadcasted_iota(jnp.int32, (8, 128), 1)
    tiles = [None] * (len(parts) * step // 128)

    def add(index, value):
        tiles[index] = value if tiles[index] is None else tiles[index] + value

    for i, part in enumerate(parts):
        part = jnp.where(lane < step, part, 0.0)
        index, shift = i * step // 128, i * step % 128
        rolled = pltpu.roll(part, shift, 1) if shift else part
        if shift + step <= 128:
            add(index, rolled)
        else:
            add(index, jnp.where(lane >= shift, rolled, 0.0))
            add(index + 1, jnp.where(lane < shift, rolled, 0.0))
    return tiles


def pick_lanes(tiles, step, count):
    parts = []
    lane = lax.broadcasted_iota(jnp.int32, (8, 128), 1)
    for i in range(count):
        index, shift = i * step // 128, i * step % 128
        part = pltpu.roll(tiles[index], 128 - shift, 1) if shift else tiles[index]
        if shift + step > 128:
            after = pltpu.roll(tiles[index + 1], 128 - shift, 1)
            part = jnp.where(lane < 128 - shift, part, after)
        parts.append(jnp.where(lane < step, part, 0.0))
    return parts


def rounded(value):
    return value.astype(jnp.bfloat16).astype(jnp.float32)


def segment_forms(segment_ids, row_lengths, r):
    segment = segment_ids[r : r + 1, :].astype(jnp.float32)
    position = lax.broadcasted_iota(jnp.int32, (1, SEQ), 1)
    return segment, jnp.where(position < row_lengths[r], segment, -1.0)


def upright(row):
    return jnp.broadcast_to(row, (128, SEQ)).T[:, 0:1]


def mask_of(rows_form, columns_form):
    return jnp.where(upright(rows_form) == columns_form, 0.0, MASK_FILL)


def staged(n, steps):
    for index, step in steps.items():
        pl.when(n == index)(step)


def attend_pair(r, p, qkv, context, logsums, bias):
    rows = part_of(r, SEQ)
    columns = pl.multiple_of(p * 128, 128)
    query = qkv[rows, pl.ds(columns, 128)]
    key = qkv[rows, pl.ds(columns + WIDTH, 128)]
    value = qkv[rows, pl.ds(columns + 2 * WIDTH, 128)]
    low = lax.broadcasted_iota(jnp.int32, (SEQ, 128), 1) < HEAD
    zero = jnp.zeros_like(key)
    outs, sums = [], []
    for j in range(2):
        key_j = jnp.where(low, key, zero) if j == 0 else jnp.where(low, zero, key)
        scores = dotted(query, key_j, 1, 1) * EXP2_SCALE + bias[rows, 0:SEQ]
        peak = jnp.max(scores, -1, keepdims=True)
        shifted = jnp.exp2(scores - peak)
        total = jnp.sum(shifted, -1, keepdims=True)
        out = dotted(shifted.astype(jnp.bfloat16), value, 1, 0)
        outs.append(out * (1.0 / total))
        sums.append(peak + jnp.log2(total))
    context[rows, pl.ds(columns, 128)] = jnp.where(low, outs[0], outs[1]).astype(jnp.bfloat16)
    turned = jnp.where(low, sums[0], sums[1]).T
    logsums[r, p, 0:1] = turned[0:1]
    logsums[r, p, 1:2] = turned[HEAD : HEAD + 1]


def attend_back_pair(r, p, qkv, d_context, logsums, rowdots, bias):
    rows = part_of(r, SEQ)
    columns = pl.multiple_of(p * 128, 128)
    query = qkv[rows, pl.ds(columns, 128)]
    key = qkv[rows, pl.ds(columns + WIDTH, 128)]
    value = qkv[rows, pl.ds(columns + 2 * WIDTH, 128)]
    grad = d_context[rows, pl.ds(columns, 128)]
    low = lax.broadcasted_iota(jnp.int32, (SEQ, 128), 1) < HEAD
    zero = jnp.zeros_like(key)
    d_query, d_key, d_value = None, [], []
    for j in range(2):
        pick = (lambda a: jnp.where(low, a, zero)) if j == 0 else (lambda a: jnp.where(low, zero, a))
        key_j = pick(key)
        scores = dotted(key_j, query, 1, 1) * EXP2_SCALE + bias[r]
        chances = jnp.exp2(scores - logsums[r, p, j : j + 1, :])
        d_chances = dotted(pick(value), grad, 1, 1)
        d_scores = (chances * (d_chances - rowdots[r, p, j : j + 1, :])).astype(jnp.bfloat16)
        d_value.append(dotted(chances.astype(jnp.bfloat16), grad, 1, 0))
        d_key.append(dotted(d_scores, query, 1, 0))
        term = dotted(d_scores, key_j, 0, 0)
        d_query = term if d_query is None else d_query + term
    scale = 1.0 / math.sqrt(HEAD)
    low_type = jnp.bfloat16
    qkv[rows, pl.ds(columns, 128)] = (d_query * scale).astype(low_type)
    qkv[rows, pl.ds(columns + WIDTH, 128)] = (
        jnp.where(low, d_key[0], d_key[1]) * scale
    ).astype(low_type)
    qkv[rows, pl.ds(columns + 2 * WIDTH, 128)] = jnp.where(low, d_value[0], d_value[1]).astype(
        low_type
    )


def row_dots(context, d_context, rowdots):
    shape = (8, 128)
    head = lax.broadcasted_iota(jnp.int32, shape, 1) // HEAD
    pick = (head == lax.broadcasted_iota(jnp.int32, shape, 0)).astype(jnp.float32)
    for r in range(rowdots.shape[0]):
        for p in range(PAIRS):
            part = (slice(r * SEQ, (r + 1) * SEQ), slice(p * 128, (p + 1) * 128))
            both = context[part].astype(jnp.float32) * d_context[part].astype(jnp.float32)
            rowdots[r, p] = lax.dot_general(
                pick,
                both,
                (((1,), (1,)), ((), ())),
                precision=lax.Precision.HIGHEST,
                preferred_element_type=jnp.float32,
            )


def norm_parts(mixed):
    centred = mixed - jnp.mean(mixed, -1, keepdims=True)
    scaled = lax.rsqrt(jnp.mean(centred * centred, -1, keepdims=True) + NORM_EPS)
    return centred * scaled, scaled


def norm_back(grad_out, normed, scaled, gain):
    inner = grad_out * gain
    return scaled * (
        inner
        - jnp.mean(inner, -1, keepdims=True)
        - normed * jnp.mean(inner * normed, -1, keepdims=True)
    )


def halves(links, src, stage, sends, recvs, index):
    rows, width = src.shape
    columns = width // 2

    def ends():
        return src.at[:, part_of(1 - links.c, columns)], stage.at[part_of(links.c, rows), :]

    links.send(ends, lambda: (sends.at[index], recvs.at[index]), links.to_core)
    stage[part_of(links.c, rows), :] = src[:, part_of(links.c, columns)]


def joined(links, stage, sends, recvs, index, block):
    rows = stage.shape[0] // 2
    here = stage.at[part_of(1 - links.c, rows), :]
    links.arrived(here, (sends.at[index], recvs.at[index]), links.to_core)
    block(links.c, links.chip_own + links.z, 1)[...] = stage[...].astype(jnp.bfloat16)


def passage_loss(r, similar, live_row, teacher_index, teacher_table):
    scores = similar * (1.0 / SOFTNESS)
    inside, shares, student, teacher = [], [], [], []
    for p in range(NPASS):
        member = live_row == float(p + 1)
        masked = jnp.where(member, scores, MASK_FILL)
        peak = jnp.max(masked, -1, keepdims=True)
        shifted = jnp.exp(masked - peak)
        total = jnp.sum(shifted, -1, keepdims=True)
        inside.append(jnp.where(member, shifted, 0.0))
        shares.append(1.0 / total)
        student.append(SOFTNESS * jnp.sum(peak + jnp.log(total), axis=0, keepdims=True))
        teacher.append(jnp.full((1, 1), teacher_table[teacher_index[r, p]], jnp.float32))

    def log_softmax(values):
        peak = functools.reduce(jnp.maximum, values)
        total = sum(jnp.exp(value - peak) for value in values)
        return [value - peak - jnp.log(total) for value in values]

    student = log_softmax(student)
    teacher = log_softmax(teacher)
    loss = sum(jnp.exp(t) * (t - s) for t, s in zip(teacher, student))
    d_similar = sum(
        part * (share * (jnp.exp(s) - jnp.exp(t)))
        for part, share, s, t in zip(inside, shares, student, teacher)
    )
    return loss, d_similar


def first_kernel(*refs):
    (
        tokens,
        w_query,
        w_key,
        w_value,
        w_out,
        w_up,
        w_down,
        w_proj,
        *vector_refs,
        b_up,
        segment_ids,
        row_lengths,
        teacher_index,
        teacher_table,
    ) = refs[:21]
    (
        losses,
        embeddings,
        attn_hbm,
        up_hbm,
        down_hbm,
        turned_hbm,
        qkv_hbm,
        context_hbm,
        low_one_hbm,
        normed_one_hbm,
        slope_hbm,
        d_mid_hbm,
        d_branch_hbm,
        grad_down_hbm,
        scaled_one,
        vectors,
        grad_vectors,
        grad_proj,
        logsums,
    ) = refs[21:40]
    (
        attn_mat,
        up_mat,
        down_mat,
        turned,
        qkv,
        context,
        low_one,
        normed_one,
        slope,
        activated,
        d_mid,
        d_branch,
        grad_down,
        small_all,
        cat_attn,
        stage_attn,
        stage_out,
        stage_up,
        stage_down,
        proj,
        up_bias,
        normed_two,
        scaled_two,
        low_two,
        sends,
        recvs,
        half_sends,
        half_recvs,
        local_sems,
        grad_sems,
    ) = refs[40:]
    count = tokens.shape[0]
    rows_dev = count // SEQ
    links = Links()
    attn_block = rows_block(attn_mat, 48, 1152)
    out_block = rows_block(attn_mat, 48, 384, 3 * WIDTH)
    up_block = rows_block(up_mat, 48, 1536)
    down_block = rows_block(down_mat, 192, 384)
    attn = Gather(links, attn_block, sends, recvs, 0)
    out = Gather(links, out_block, sends, recvs, 1)
    up = Gather(links, up_block, sends, recvs, 2)
    down = Gather(links, down_block, sends, recvs, 3)
    tiny = Gather(links, lead_block(small_all), sends, recvs, 4)
    own_chip = links.chip_own + links.z
    kept = []

    def keep(src, dst):
        copy = pltpu.make_async_copy(src, dst, local_sems.at[len(kept)])
        copy.start()
        kept.append(copy)

    for index, ref in enumerate((w_query, w_key, w_value)):
        cat_attn[:, index * WIDTH : (index + 1) * WIDTH] = ref[...]
    own_small = small_all.at[links.c, own_chip]
    own_small[0:24, :] = w_proj[...]
    own_small[24:40, :] = jnp.zeros((16, 128), jnp.float32)
    for index, ref in enumerate(vector_refs):
        own_small[24 + index : 25 + index, 0:24] = ref[...].reshape(1, 24)
    own_small[32:33, 0:96] = b_up[...].reshape(1, 96)

    links.greet()
    halves(links, cat_attn, stage_attn, half_sends, half_recvs, 0)
    tiny.first()
    halves(links, w_out, stage_out, half_sends, half_recvs, 1)
    halves(links, w_up, stage_up, half_sends, half_recvs, 2)
    halves(links, w_down, stage_down, half_sends, half_recvs, 3)
    joined(links, stage_attn, half_sends, half_recvs, 0, attn_block)
    attn.first()
    joined(links, stage_out, half_sends, half_recvs, 1, out_block)
    joined(links, stage_up, half_sends, half_recvs, 2, up_block)
    joined(links, stage_down, half_sends, half_recvs, 3, down_block)
    tiny.second()
    attn.second()
    out.first()
    live_rows = []
    for r in range(rows_dev):
        segment, live = segment_forms(segment_ids, row_lengths, r)
        live_rows.append(live)
        d_mid[r * SEQ : (r + 1) * SEQ, 0:SEQ] = mask_of(segment, live)
    tiny.third()
    attn.third()
    out.second()
    up.first()
    turned[...] = tokens[...].T
    keep(turned, turned_hbm)
    tiny.fourth()
    tiny.last()

    cores = [(i % 2, i // 2) for i in range(SHARDS)]
    for index, tile in enumerate(spread_lanes([small_all[c, n, 24:32, :] for c, n in cores], 24)):
        vectors[:, index * 128 : (index + 1) * 128] = rounded(tile)
    for index, tile in enumerate(spread_lanes([small_all[c, n, 32:40, :] for c, n in cores], 96)):
        up_bias[:, index * 128 : (index + 1) * 128] = rounded(tile)
    for r in range(CHIPS):
        both = jnp.concatenate([small_all[0, r, 0:24, :], small_all[1, r, 0:24, :]], axis=0)
        proj[r * 48 : (r + 1) * 48, :] = both.astype(jnp.bfloat16)
    attn.fourth()
    attn.last()

    def project(step, carry):
        rows = part_of(step, CHUNK)
        part = tokens[rows, :]
        for index in range(3):
            columns = slice(index * WIDTH, (index + 1) * WIDTH)
            value = dotted(part, attn_mat[:, columns], 1, 0)
            if index != 1:
                value = value + vectors[index // 2 : index // 2 + 1, :]
            qkv[rows, columns] = value.astype(jnp.bfloat16)
        staged(step, {1: out.third, 2: up.second, 3: down.first})
        return carry

    lax.fori_loop(0, count // CHUNK, project, 0)
    keep(qkv, qkv_hbm)

    def attend(item, carry):
        attend_pair(lax.div(item, PAIRS), lax.rem(item, PAIRS), qkv, context, logsums, d_mid)
        staged(
            item,
            {
                0: out.fourth,
                2: up.third,
                4: out.last,
                5: down.second,
                6: up.fourth,
                8: up.last,
                9: down.third,
            },
        )
        return carry

    lax.fori_loop(0, rows_dev * PAIRS, attend, 0)
    keep(context, context_hbm)
    keep(attn_mat, attn_hbm)

    def mix(step, carry):
        rows = part_of(step, CHUNK)
        mixed = dotted(context[rows, :], attn_mat[:, 3 * WIDTH :], 1, 0) + vectors[2:3, :]
        normed, scaled = norm_parts(tokens[rows, :].astype(jnp.float32) + mixed)
        normed_one[rows, :] = normed
        scaled_one[rows, :] = jnp.broadcast_to(scaled, (CHUNK, 128))
        low_one[rows, :] = (normed * vectors[3:4, :] + vectors[4:5, :]).astype(jnp.bfloat16)
        return carry

    lax.fori_loop(0, count // CHUNK, mix, 0)
    keep(normed_one, normed_one_hbm)
    keep(low_one, low_one_hbm)
    keep(up_mat, up_hbm)

    def widen(step, carry):
        rows = part_of(step, CHUNK)
        part = low_one[rows, :]
        for index in range(4):
            columns = slice(index * WIDTH, (index + 1) * WIDTH)
            upward = dotted(part, up_mat[:, columns], 1, 0) + up_bias[0:1, columns]
            chance = 0.5 * (1.0 + lax.erf(upward * ROOT_HALF))
            activated[rows, columns] = (upward * chance).astype(jnp.bfloat16)
            density = jnp.exp(-0.5 * upward * upward) * DENSITY_SCALE
            slope[rows, columns] = (chance + upward * density).astype(jnp.bfloat16)
        staged(step, {1: down.fourth})
        return carry

    lax.fori_loop(0, count // CHUNK, widen, 0)
    keep(slope, slope_hbm)
    down.last()
    keep(down_mat, down_hbm)

    grad_vectors[...] = jnp.zeros_like(grad_vectors)
    grad_proj[...] = jnp.zeros_like(grad_proj)
    for r in range(rows_dev):

        def narrow(step, carry):
            here = part_of(step, CHUNK)
            rows = pl.ds(pl.multiple_of(r * SEQ + step * CHUNK, CHUNK), CHUNK)
            mixed = dotted(activated[rows, :], down_mat[...], 1, 0) + vectors[5:6, :]
            mixed = mixed + (normed_one[rows, :] * vectors[3:4, :] + vectors[4:5, :])
            normed, scaled = norm_parts(mixed)
            normed_two[here, :] = normed
            scaled_two[here, :] = jnp.broadcast_to(scaled, (CHUNK, 128))
            low_two[here, :] = (normed * vectors[6:7, :] + vectors[7:8, :]).astype(jnp.bfloat16)
            return carry

        lax.fori_loop(0, SEQ // CHUNK, narrow, 0)
        raw = dotted(low_two[...], proj[...], 1, 0)
        inverse = lax.rsqrt(jnp.sum(raw * raw, -1, keepdims=True) + UNIT_EPS)
        embedded = raw * inverse
        embeddings[r] = embedded
        low_embed = embedded.astype(jnp.bfloat16)
        similar = dotted(low_embed[0:QLEN], low_embed, 1, 1)
        loss, d_similar = passage_loss(r, similar, live_rows[r], teacher_index, teacher_table)
        losses[r] = loss[0, 0]
        d_similar = d_similar.astype(jnp.bfloat16)
        d_embed = dotted(d_similar, low_embed[0:QLEN], 0, 0)
        d_query = dotted(d_similar, low_embed, 1, 0)
        d_embed = jnp.concatenate([d_embed[0:QLEN] + d_query, d_embed[QLEN:]], axis=0)
        along = jnp.sum(d_embed * embedded, -1, keepdims=True)
        d_raw = (inverse * (d_embed - embedded * along)).astype(jnp.bfloat16)
        grad_proj[...] += dotted(low_two[...], d_raw, 0, 0)
        d_hidden = dotted(d_raw, proj[...], 1, 1)
        normed = normed_two[...]
        d_mixed = norm_back(d_hidden, normed, scaled_two[:, 0:1], vectors[6:7, :])
        low_mixed = d_mixed.astype(jnp.bfloat16)
        rows = slice(r * SEQ, (r + 1) * SEQ)
        d_mid[rows, :] = d_mixed
        d_branch[rows, :] = low_mixed
        grad_vectors[5:6, :] += jnp.sum(low_mixed.astype(jnp.float32), 0, keepdims=True)
        grad_vectors[6:7, :] += jnp.sum(d_hidden * normed, 0, keepdims=True)
        grad_vectors[7:8, :] += jnp.sum(d_hidden, 0, keepdims=True)
    keep(d_mid, d_mid_hbm)
    keep(d_branch, d_branch_hbm)

    def grad_copy(step, slot):
        return pltpu.make_async_copy(
            grad_down.at[slot], grad_down_hbm.at[part_of(step, CHUNK), :], grad_sems.at[slot]
        )

    def weigh(step, carry):
        slot = lax.rem(step, 2)

        @pl.when(step >= 2)
        def _():
            grad_copy(step - 2, slot).wait()

        part = activated[:, part_of(step, CHUNK)]
        grad_down[slot] = dotted(part, d_branch[...], 0, 0).astype(jnp.bfloat16)
        grad_copy(step, slot).start()
        return carry

    steps = HIDDEN // CHUNK
    lax.fori_loop(0, steps, weigh, 0)
    for step in (steps - 2, steps - 1):
        grad_copy(step, step % 2).wait()
    links.finish()
    for copy in kept:
        copy.wait()


def run_first(tokens, weights, vectors, segment_ids, row_lengths, teacher_index, teacher_table):
    count = tokens.shape[0]
    rows_dev = count // SEQ
    vmem = pl.BlockSpec(memory_space=pltpu.VMEM)
    smem = pl.BlockSpec(memory_space=pltpu.SMEM)
    anywhere = pl.BlockSpec(memory_space=pl.ANY)
    low = jnp.bfloat16
    wide = jnp.float32

    def array(kind, *shape):
        return jax.ShapeDtypeStruct(shape, kind)

    return pl.pallas_call(
        first_kernel,
        out_shape=[
            array(wide, rows_dev),
            array(wide, rows_dev, SEQ, EMBED),
            array(low, WIDTH, HIDDEN),
            array(low, WIDTH, HIDDEN),
            array(low, HIDDEN, WIDTH),
            array(low, WIDTH, count),
            array(low, count, 3 * WIDTH),
            array(low, count, WIDTH),
            array(low, count, WIDTH),
            array(wide, count, WIDTH),
            array(low, count, HIDDEN),
            array(wide, count, WIDTH),
            array(low, count, WIDTH),
            array(low, HIDDEN, WIDTH),
            array(wide, count, 128),
            array(wide, 8, WIDTH),
            array(wide, 8, WIDTH),
            array(wide, WIDTH, EMBED),
            array(wide, rows_dev, PAIRS, 8, SEQ),
        ],
        in_specs=[vmem] * 18 + [smem] * 3,
        out_specs=[smem, vmem] + [anywhere] * 12 + [vmem] * 5,
        scratch_shapes=[
            pltpu.VMEM((WIDTH, HIDDEN), low),
            pltpu.VMEM((WIDTH, HIDDEN), low),
            pltpu.VMEM((HIDDEN, WIDTH), low),
            pltpu.VMEM((WIDTH, count), low),
            pltpu.VMEM((count, 3 * WIDTH), low),
            pltpu.VMEM((count, WIDTH), low),
            pltpu.VMEM((count, WIDTH), low),
            pltpu.VMEM((count, WIDTH), wide),
            pltpu.VMEM((count, HIDDEN), low),
            pltpu.VMEM((count, HIDDEN), low),
            pltpu.VMEM((count, WIDTH), wide),
            pltpu.VMEM((count, WIDTH), low),
            pltpu.VMEM((2, CHUNK, WIDTH), low),
            pltpu.VMEM((2, CHIPS, SMALL, 128), wide),
            pltpu.VMEM((24, 3 * WIDTH), wide),
            pltpu.VMEM((48, 3 * WIDTH // 2), wide),
            pltpu.VMEM((48, WIDTH // 2), wide),
            pltpu.VMEM((48, HIDDEN // 2), wide),
            pltpu.VMEM((192, WIDTH // 2), wide),
            pltpu.VMEM((WIDTH, EMBED), low),
            pltpu.VMEM((8, HIDDEN), wide),
            pltpu.VMEM((SEQ, WIDTH), wide),
            pltpu.VMEM((SEQ, 128), wide),
            pltpu.VMEM((SEQ, WIDTH), low),
            pltpu.SemaphoreType.DMA((5, Gather.SEMS)),
            pltpu.SemaphoreType.DMA((5, Gather.SEMS)),
            pltpu.SemaphoreType.DMA((4,)),
            pltpu.SemaphoreType.DMA((4,)),
            pltpu.SemaphoreType.DMA((12,)),
            pltpu.SemaphoreType.DMA((2,)),
        ],
        compiler_params=pltpu.CompilerParams(
            collective_id=0, has_side_effects=True, vmem_limit_bytes=62 * 2**20
        ),
        name="forward_gather",
    )(tokens, *weights, *vectors, segment_ids, row_lengths, teacher_index, teacher_table)


def last_kernel(*refs):
    (
        attn_hbm,
        up_hbm,
        down_hbm,
        turned_hbm,
        qkv_hbm,
        context_hbm,
        low_one_hbm,
        normed_one_hbm,
        slope_hbm,
        d_mid_hbm,
        d_branch_hbm,
        grad_down_hbm,
        scaled_one,
        vectors,
        part_vectors,
        grad_proj,
        logsums,
        segment_ids,
        row_lengths,
    ) = refs[:19]
    (
        grad_tokens,
        own_query,
        own_key,
        own_value,
        own_out,
        own_up,
        own_down,
        own_proj,
        *own_vectors,
        own_up_bias,
    ) = refs[19:36]
    (
        attn_mat,
        grads,
        wide,
        low_one,
        turned,
        d_branch,
        d_mid,
        part_down,
        small_all,
        rowdots,
        grad_vectors,
        grad_up_bias,
        sends,
        recvs,
        local_sems,
        *rest,
    ) = refs[36:]
    held = [rest[6 * i : 6 * i + 6] for i in range(6)]
    fins = [rest[36 + 2 * i : 38 + 2 * i] for i in range(5)]
    count = d_mid.shape[0]
    rows_dev = count // SEQ
    links = Links()
    c = links.c

    def scatter(block, rows, group, mine=None):
        def own(chip):
            return block(c, chip, 1)

        return Scatter(
            links, block, own if mine is None else mine, rows, held[group], sends, recvs, group
        )

    down = scatter(
        rows_block(grad_down_hbm, 192, 384), 192, 0, lambda chip: part_down.at[part_of(chip, 192), :]
    )
    up = scatter(rows_block(grads, 48, 1536), 48, 1)
    out = scatter(rows_block(grads, 48, 384), 48, 2)
    most = scatter(rows_block(grads, 48, 768, WIDTH), 48, 3)
    rest_of = scatter(rows_block(grads, 48, 384, 3 * WIDTH), 48, 4)
    tiny = scatter(lead_block(small_all), 1, 5)

    def load(src, dst, index):
        copy = pltpu.make_async_copy(src, dst, local_sems.at[index])
        copy.start()
        return copy

    first_loads = [
        load(d_branch_hbm, d_branch, 0),
    ]
    links.greet()
    down.first()
    grad_vectors[...] = part_vectors[...]

    def feed_forward(up_mat, down_mat, normed_one):
        first = first_loads + [load(down_hbm, down_mat, 1), load(slope_hbm, wide, 2)]
        later = [
            load(low_one_hbm, low_one, 3),
            load(grad_down_hbm.at[:, part_of(c, WIDTH // 2)], part_down, 4),
            load(up_hbm, up_mat, 5),
            load(d_mid_hbm, d_mid, 6),
            load(normed_one_hbm, normed_one, 7),
        ]
        for copy in first:
            copy.wait()

        def widen(step, carry):
            rows = part_of(step, CHUNK)
            part = d_branch[rows, :]
            for index in range(4):
                columns = slice(index * WIDTH, (index + 1) * WIDTH)
                grad = dotted(part, down_mat[columns, :], 1, 1)
                wide[rows, columns] = (grad * wide[rows, columns].astype(jnp.float32)).astype(
                    jnp.bfloat16
                )
            return carry

        lax.fori_loop(0, count // CHUNK, widen, 0)
        for copy in later:
            copy.wait()
        down.second()

        def weigh(step, carry):
            rows = part_of(step, CHUNK)
            part = low_one[:, rows].T
            for index in range(4):
                columns = slice(index * WIDTH, (index + 1) * WIDTH)
                grads[rows, columns] = dotted(part, wide[:, columns], 1, 0).astype(jnp.bfloat16)
            return carry

        lax.fori_loop(0, WIDTH // CHUNK, weigh, 0)
        up.first()
        ones = jnp.ones((8, count), jnp.bfloat16)
        for index in range(4):
            columns = slice(index * WIDTH, (index + 1) * WIDTH)
            grad_up_bias[:, columns] = dotted(ones, wide[:, columns], 1, 0)
        down.third()

        def narrow(step, carry):
            rows = part_of(step, CHUNK)
            d_hidden = d_mid[rows, :] + dotted(wide[rows, :], up_mat[...], 1, 1)
            normed = normed_one[rows, :]
            d_mixed = norm_back(d_hidden, normed, scaled_one[rows, 0:1], vectors[3:4, :])
            d_mid[rows, :] = d_mixed
            d_branch[rows, :] = d_mixed.astype(jnp.bfloat16)
            grad_vectors[3:4, :] += jnp.sum(d_hidden * normed, 0, keepdims=True)
            grad_vectors[4:5, :] += jnp.sum(d_hidden, 0, keepdims=True)
            return carry

        lax.fori_loop(0, count // CHUNK, narrow, 0)

    pl.run_scoped(
        feed_forward,
        pltpu.VMEM((WIDTH, HIDDEN), jnp.bfloat16),
        pltpu.VMEM((HIDDEN, WIDTH), jnp.bfloat16),
        pltpu.VMEM((count, WIDTH), jnp.float32),
    )

    def attention(context, d_context, bias):
        loads = [
            load(context_hbm, context, 8),
            load(attn_hbm, attn_mat, 9),
            load(qkv_hbm, wide.at[:, 0 : 3 * WIDTH], 10),
            load(turned_hbm, turned, 11),
        ]
        up.second()
        links_first = len(links.started)
        down.fourth()
        ones = jnp.ones((8, count), jnp.bfloat16)
        grad_vectors[2:3, :] = dotted(ones, d_branch[...], 1, 0)[0:1]
        for r in range(rows_dev):
            segment, live = segment_forms(segment_ids, row_lengths, r)
            bias[r] = mask_of(live, segment)
        for copy in loads:
            copy.wait()

        def give(step, carry):
            rows = part_of(step, CHUNK)
            d_context[rows, :] = dotted(d_branch[rows, :], attn_mat[:, 3 * WIDTH :], 1, 1).astype(
                jnp.bfloat16
            )
            return carry

        lax.fori_loop(0, count // CHUNK, give, 0)
        row_dots(context, d_context, rowdots)
        links.finish()

        def weigh_out(step, carry):
            rows = part_of(step, CHUNK)
            part = context[:, rows].T
            grads[rows, 0:WIDTH] = dotted(part, d_branch[...], 1, 0).astype(jnp.bfloat16)
            return carry

        lax.fori_loop(0, WIDTH // CHUNK, weigh_out, 0)
        out.first()

        def down_trade():
            down.trade(*fins[0])

        def down_whole():
            low, high = down.whole(*fins[0])
            own_down[:, : WIDTH // 2] = low
            own_down[:, WIDTH // 2 :] = high

        def up_trade():
            up.trade(*fins[1])

        def up_whole():
            low, high = up.whole(*fins[1])
            own_up[:, : HIDDEN // 2] = low
            own_up[:, HIDDEN // 2 :] = high

        def out_trade():
            out.trade(*fins[2])

        def out_whole():
            low, high = out.whole(*fins[2])
            own_out[:, : WIDTH // 2] = low
            own_out[:, WIDTH // 2 :] = high

        def attend(first, steps):
            def step(item, carry):
                r = lax.rem(item, rows_dev)
                p = lax.div(item, rows_dev)
                attend_back_pair(r, p, wide, d_context, logsums, rowdots, bias)
                staged(item, steps)
                return carry

            return step

        lax.fori_loop(
            0,
            4 * rows_dev,
            attend(
                0,
                {0: up.third, 1: out.second, 2: down_trade, 3: up.fourth, 4: out.third, 5: down_whole, 6: out.fourth, 7: up_trade},
            ),
            0,
        )

        def weigh(first, pairs, base):
            def step(step, carry):
                rows = part_of(step, CHUNK)
                part = turned[rows, :]
                for index in range(3):
                    start = index * WIDTH + first * 128
                    there = base + index * pairs * 128
                    grads[rows, there : there + pairs * 128] = dotted(
                        part, wide[:, start : start + pairs * 128], 1, 0
                    ).astype(jnp.bfloat16)
                return carry

            lax.fori_loop(0, WIDTH // CHUNK, step, 0)

        weigh(0, 4, WIDTH)
        most.first()
        lax.fori_loop(
            4 * rows_dev,
            6 * rows_dev,
            attend(4 * rows_dev, {8: up_whole, 9: most.second, 10: out_trade, 11: most.third}),
            0,
        )
        weigh(4, 2, 3 * WIDTH)
        rest_of.first()
        out_whole()
        for index in (0, 2):
            total = dotted(ones, wide[:, index * WIDTH : (index + 1) * WIDTH], 1, 0)
            grad_vectors[index // 2 : index // 2 + 1, :] = total[0:1]

    pl.run_scoped(
        attention,
        pltpu.VMEM((count, WIDTH), jnp.bfloat16),
        pltpu.VMEM((count, WIDTH), jnp.bfloat16),
        pltpu.VMEM((rows_dev, SEQ, SEQ), jnp.float32),
    )

    tiles = [grad_vectors[:, i * 128 : (i + 1) * 128] for i in range(WIDTH // 128)]
    for i, part in enumerate(pick_lanes(tiles, 24, SHARDS)):
        small_all[i % 2, i // 2, 24:32, :] = part
    tiles = [grad_up_bias[:, i * 128 : (i + 1) * 128] for i in range(HIDDEN // 128)]
    for i, part in enumerate(pick_lanes(tiles, 96, SHARDS)):
        small_all[i % 2, i // 2, 32:40, :] = part
        small_all[i % 2, i // 2, 0:24, :] = grad_proj[i * 24 : (i + 1) * 24, :]
    tiny.first()

    def back(step, carry):
        rows = part_of(step, CHUNK)
        value = dotted(wide[rows, 0 : 3 * WIDTH], attn_mat[:, 0 : 3 * WIDTH], 1, 1)
        grad_tokens[rows, :] = value + d_mid[rows, :]
        return carry

    most.fourth()
    rest_of.second()
    tiny.second()
    lax.fori_loop(0, 2, back, 0)
    rest_of.third()
    tiny.third()
    lax.fori_loop(2, 4, back, 0)
    rest_of.fourth()
    tiny.fourth()
    most.trade(*fins[3])
    rest_of.trade(*fins[4])
    total = tiny.fifth()[0]
    own_proj[...] = total[0:24, :]
    for index, ref in enumerate(own_vectors):
        ref[...] = total[24 + index : 25 + index, 0:24].reshape(24)
    own_up_bias[...] = total[32:33, 0:96].reshape(96)
    low, high = most.whole(*fins[3])
    own_query[:, 0:512] = low[:, 0:512]
    own_key[:, 0:256] = low[:, 512:768]
    own_key[:, 256:512] = high[:, 0:256]
    own_value[:, 0:512] = high[:, 256:768]
    low, high = rest_of.whole(*fins[4])
    own_query[:, 512:768] = low[:, 0:256]
    own_key[:, 512:640] = low[:, 256:384]
    own_key[:, 640:768] = high[:, 0:128]
    own_value[:, 512:768] = high[:, 128:384]
    links.finish()


def run_last(kept, segment_ids, row_lengths):
    count = kept[9].shape[0]
    rows_dev = count // SEQ
    vmem = pl.BlockSpec(memory_space=pltpu.VMEM)
    smem = pl.BlockSpec(memory_space=pltpu.SMEM)
    anywhere = pl.BlockSpec(memory_space=pl.ANY)
    low = jnp.bfloat16
    wide = jnp.float32

    def array(*shape):
        return jax.ShapeDtypeStruct(shape, wide)

    def held(unit, kind):
        return [pltpu.VMEM((n * unit[0],) + unit[1:], kind) for n in (16, 2, 2, 4, 4, 3)]

    blocks = ((192, 384), (48, 1536), (48, 384), (48, 768), (48, 384))
    buffers = []
    for block in blocks:
        buffers += held(block, low)
    buffers += held((1, SMALL, 128), wide)
    for rows, columns in blocks:
        buffers += [pltpu.VMEM((rows, columns), wide), pltpu.VMEM((rows // 2, columns), wide)]
    return pl.pallas_call(
        last_kernel,
        out_shape=[
            array(count, WIDTH),
            array(24, WIDTH),
            array(24, WIDTH),
            array(24, WIDTH),
            array(24, WIDTH),
            array(24, HIDDEN),
            array(96, WIDTH),
            array(24, EMBED),
        ]
        + [array(24)] * 8
        + [array(96)],
        in_specs=[anywhere] * 12 + [vmem] * 6 + [smem],
        out_specs=[vmem] * 17,
        scratch_shapes=[
            pltpu.VMEM((WIDTH, HIDDEN), low),
            pltpu.VMEM((WIDTH, HIDDEN), low),
            pltpu.VMEM((count, HIDDEN), low),
            pltpu.VMEM((count, WIDTH), low),
            pltpu.VMEM((WIDTH, count), low),
            pltpu.VMEM((count, WIDTH), low),
            pltpu.VMEM((count, WIDTH), wide),
            pltpu.VMEM((HIDDEN, WIDTH // 2), low),
            pltpu.VMEM((2, CHIPS, SMALL, 128), wide),
            pltpu.VMEM((rows_dev, PAIRS, 8, SEQ), wide),
            pltpu.VMEM((8, WIDTH), wide),
            pltpu.VMEM((8, HIDDEN), wide),
            pltpu.SemaphoreType.DMA((6, Scatter.SEMS)),
            pltpu.SemaphoreType.DMA((6, Scatter.SEMS)),
            pltpu.SemaphoreType.DMA((12,)),
        ]
        + buffers,
        compiler_params=pltpu.CompilerParams(
            collective_id=1, has_side_effects=True, vmem_limit_bytes=63 * 2**20
        ),
        name="backward_scatter",
    )(*kept, segment_ids, row_lengths)


def body_tiles(
    tokens,
    w_query,
    b_query,
    w_key,
    w_value,
    b_value,
    w_out,
    b_out,
    gain_one,
    shift_one,
    w_up,
    b_up,
    w_down,
    b_down,
    gain_two,
    shift_two,
    w_proj,
    segment_ids,
    row_lengths,
    teacher_index,
    teacher_table,
):
    rows_dev, _, width = tokens.shape
    losses, embeddings, *kept = run_first(
        tokens.reshape(rows_dev * SEQ, width),
        (w_query, w_key, w_value, w_out, w_up, w_down, w_proj),
        (b_query, b_value, b_out, gain_one, shift_one, b_down, gain_two, shift_two, b_up),
        segment_ids,
        row_lengths,
        teacher_index,
        teacher_table,
    )
    (
        grad_tokens,
        grad_query,
        grad_key,
        grad_value,
        grad_out,
        grad_up,
        grad_down,
        grad_proj,
        grad_query_bias,
        grad_value_bias,
        grad_out_bias,
        grad_gain_first,
        grad_shift_first,
        grad_down_bias,
        grad_gain_second,
        grad_shift_second,
        grad_up_bias,
    ) = run_last(kept, segment_ids, row_lengths)
    return (
        losses,
        embeddings,
        grad_tokens.reshape(rows_dev, SEQ, width),
        grad_query,
        grad_query_bias,
        grad_key,
        grad_value,
        grad_value_bias,
        grad_out,
        grad_out_bias,
        grad_gain_first,
        grad_shift_first,
        grad_up,
        grad_up_bias,
        grad_down,
        grad_down_bias,
        grad_gain_second,
        grad_shift_second,
        grad_proj,
    )


def solution(mesh):
    in_specs = (
        P(("dp", "fsdp"), None, None),
        P(("dp", "fsdp"), None),
        P(("dp", "fsdp")),
        P(("dp", "fsdp"), None),
        P(("dp", "fsdp"), None),
        P(("dp", "fsdp")),
        P(("dp", "fsdp"), None),
        P(("dp", "fsdp")),
        P(("dp", "fsdp")),
        P(("dp", "fsdp")),
        P(("dp", "fsdp"), None),
        P(("dp", "fsdp")),
        P(("dp", "fsdp"), None),
        P(("dp", "fsdp")),
        P(("dp", "fsdp")),
        P(("dp", "fsdp")),
        P(("dp", "fsdp"), None),
        P(("dp", "fsdp"), None),
        P(("dp", "fsdp")),
        P(("dp", "fsdp"), None),
        P(),
    )
    out_specs = (
        P(("dp", "fsdp")),
        P(("dp", "fsdp"), None, None),
        P(("dp", "fsdp"), None, None),
        P(("dp", "fsdp"), None),
        P(("dp", "fsdp")),
        P(("dp", "fsdp"), None),
        P(("dp", "fsdp"), None),
        P(("dp", "fsdp")),
        P(("dp", "fsdp"), None),
        P(("dp", "fsdp")),
        P(("dp", "fsdp")),
        P(("dp", "fsdp")),
        P(("dp", "fsdp"), None),
        P(("dp", "fsdp")),
        P(("dp", "fsdp"), None),
        P(("dp", "fsdp")),
        P(("dp", "fsdp")),
        P(("dp", "fsdp")),
        P(("dp", "fsdp"), None),
    )
    body = body_tiles if fits(mesh) else body_whole
    return jax.shard_map(body, mesh=mesh, in_specs=in_specs, out_specs=out_specs, check_vma=False)
```

```python
import functools
import math

import jax
import jax.numpy as jnp
from jax import lax
from jax.experimental import pallas as pl
from jax.experimental.pallas import tpu as pltpu
from jax.sharding import PartitionSpec as P

HEADS = 12
HEAD = 64
SEQ = 512
QLEN = 32
NPASS = 8
TABLE = 1024


NORM_EPS = 1e-12
UNIT_EPS = 1e-12
SOFTNESS = 0.1
MASK_FILL = -1000000000.0
ROOT_HALF = 0.7071067811865476
DENSITY_SCALE = 0.3989422804014327


def matmul(left, right):
    return jnp.dot(left, right, preferred_element_type=jnp.float32)


def over_rows(left, right):
    return lax.dot_general(
        left, right, (((0,), (0,)), ((), ())), preferred_element_type=jnp.float32
    )


def against(left, right):
    return lax.dot_general(
        left, right, (((1,), (1,)), ((), ())), preferred_element_type=jnp.float32
    )


def normalise(mixed, gain, shift):
    centred = mixed - jnp.mean(mixed, -1, keepdims=True)
    scaled = lax.rsqrt(jnp.mean(centred * centred, -1, keepdims=True) + NORM_EPS)
    normed = centred * scaled
    return (normed * gain + shift, normed, scaled)


def normalise_back(grad_out, normed, scaled, gain):
    inner = grad_out * gain
    grad_in = scaled * (
        inner
        - jnp.mean(inner, -1, keepdims=True)
        - normed * jnp.mean(inner * normed, -1, keepdims=True)
    )
    return (grad_in, jnp.sum(grad_out * normed, 0), jnp.sum(grad_out, 0))


def gelu_exact(upward):
    return 0.5 * upward * (1.0 + lax.erf(upward * ROOT_HALF))


def gelu_slope(upward):
    return (
        0.5 * (1.0 + lax.erf(upward * ROOT_HALF))
        + upward * jnp.exp(-0.5 * upward * upward) * DENSITY_SCALE
    )


def split_heads(matrix, rows_dev):
    return (
        matrix.reshape(rows_dev, SEQ, HEADS, HEAD)
        .transpose(0, 2, 1, 3)
        .reshape(rows_dev * HEADS, SEQ, HEAD)
    )


def join_heads(stacked, rows_dev):
    return (
        stacked.reshape(rows_dev, HEADS, SEQ, HEAD)
        .transpose(0, 2, 1, 3)
        .reshape(rows_dev * SEQ, HEADS * HEAD)
    )


def collect(sent):
    return (
        lax.all_gather(sent[0], ("dp", "fsdp"), axis=0, tiled=True),
        lax.all_gather(sent[1], ("dp", "fsdp"), axis=0, tiled=True),
        lax.all_gather(sent[2], ("dp", "fsdp"), axis=0, tiled=True),
        lax.all_gather(sent[3], ("dp", "fsdp"), axis=0, tiled=True),
        lax.all_gather(sent[4], ("dp", "fsdp"), axis=0, tiled=True),
        lax.all_gather(sent[5], ("dp", "fsdp"), axis=0, tiled=True),
        lax.all_gather(sent[6], ("dp", "fsdp"), axis=0, tiled=True),
        lax.all_gather(sent[7], ("dp", "fsdp"), axis=0, tiled=True),
        lax.all_gather(sent[8], ("dp", "fsdp"), axis=0, tiled=True),
        lax.all_gather(sent[9], ("dp", "fsdp"), axis=0, tiled=True),
        lax.all_gather(sent[10], ("dp", "fsdp"), axis=0, tiled=True),
        lax.all_gather(sent[11], ("dp", "fsdp"), axis=0, tiled=True),
        lax.all_gather(sent[12], ("dp", "fsdp"), axis=0, tiled=True),
        lax.all_gather(sent[13], ("dp", "fsdp"), axis=0, tiled=True),
        lax.all_gather(sent[14], ("dp", "fsdp"), axis=0, tiled=True),
        lax.all_gather(sent[15], ("dp", "fsdp"), axis=0, tiled=True),
    )


def spread_grads(terms):
    return (
        lax.psum_scatter(terms[0], ("dp", "fsdp"), scatter_dimension=0, tiled=True),
        lax.psum_scatter(terms[1], ("dp", "fsdp"), scatter_dimension=0, tiled=True),
        lax.psum_scatter(terms[2], ("dp", "fsdp"), scatter_dimension=0, tiled=True),
        lax.psum_scatter(terms[3], ("dp", "fsdp"), scatter_dimension=0, tiled=True),
        lax.psum_scatter(terms[4], ("dp", "fsdp"), scatter_dimension=0, tiled=True),
        lax.psum_scatter(terms[5], ("dp", "fsdp"), scatter_dimension=0, tiled=True),
        lax.psum_scatter(terms[6], ("dp", "fsdp"), scatter_dimension=0, tiled=True),
        lax.psum_scatter(terms[7], ("dp", "fsdp"), scatter_dimension=0, tiled=True),
        lax.psum_scatter(terms[8], ("dp", "fsdp"), scatter_dimension=0, tiled=True),
        lax.psum_scatter(terms[9], ("dp", "fsdp"), scatter_dimension=0, tiled=True),
        lax.psum_scatter(terms[10], ("dp", "fsdp"), scatter_dimension=0, tiled=True),
        lax.psum_scatter(terms[11], ("dp", "fsdp"), scatter_dimension=0, tiled=True),
        lax.psum_scatter(terms[12], ("dp", "fsdp"), scatter_dimension=0, tiled=True),
        lax.psum_scatter(terms[13], ("dp", "fsdp"), scatter_dimension=0, tiled=True),
        lax.psum_scatter(terms[14], ("dp", "fsdp"), scatter_dimension=0, tiled=True),
        lax.psum_scatter(terms[15], ("dp", "fsdp"), scatter_dimension=0, tiled=True),
    )


def body_whole(
    tokens,
    w_query,
    b_query,
    w_key,
    w_value,
    b_value,
    w_out,
    b_out,
    gain_one,
    shift_one,
    w_up,
    b_up,
    w_down,
    b_down,
    gain_two,
    shift_two,
    w_proj,
    segment_ids,
    row_lengths,
    teacher_index,
    teacher_table,
):
    rows_dev = tokens.shape[0]
    width = tokens.shape[2]
    scale = 1.0 / math.sqrt(HEAD)
    shards = (
        w_query,
        b_query,
        w_key,
        w_value,
        b_value,
        w_out,
        b_out,
        gain_one,
        shift_one,
        w_up,
        b_up,
        w_down,
        b_down,
        gain_two,
        shift_two,
        w_proj,
    )
    sent = tuple((member.astype(jnp.bfloat16) for member in shards))
    gathered = collect(sent)
    (
        query_mat,
        query_bias,
        key_mat,
        value_mat,
        value_bias,
        out_mat,
        out_bias,
        gain_first,
        shift_first,
        up_mat,
        up_bias,
        down_mat,
        down_bias,
        gain_second,
        shift_second,
        proj_mat,
    ) = gathered

    def visibility(item_index):
        row_index = item_index // HEADS
        segment_row = lax.dynamic_index_in_dim(segment_ids, row_index, 0, keepdims=False)
        length_row = lax.dynamic_index_in_dim(row_lengths, row_index, 0, keepdims=False)
        positions = jnp.arange(SEQ, dtype=jnp.int32)
        return (segment_row[:, None] == segment_row[None, :]) & (positions[None, :] < length_row)

    def attend(inputs):
        query_h, key_h, value_h, item_index = inputs
        scores = jnp.where(visibility(item_index), against(query_h, key_h) * scale, MASK_FILL)
        peak = jnp.max(scores, -1, keepdims=True)
        shifted = jnp.exp(scores - peak)
        totals = jnp.sum(shifted, -1, keepdims=True)
        chances = (shifted / totals).astype(jnp.bfloat16)
        context_h = matmul(chances, value_h).astype(jnp.bfloat16)
        return (context_h, (peak + jnp.log(totals))[:, 0])

    def attend_back(inputs):
        query_h, key_h, value_h, grad_h, logsum, item_index = inputs
        scores = jnp.where(visibility(item_index), against(query_h, key_h) * scale, MASK_FILL)
        chances = jnp.exp(scores - logsum[:, None])
        d_chances = against(grad_h, value_h)
        rowdot = jnp.sum(chances * d_chances, -1, keepdims=True)
        d_scores = (chances * (d_chances - rowdot)).astype(jnp.bfloat16)
        d_query_h = (matmul(d_scores, key_h) * scale).astype(jnp.bfloat16)
        d_key_h = (over_rows(d_scores, query_h) * scale).astype(jnp.bfloat16)
        d_value_h = over_rows(chances.astype(jnp.bfloat16), grad_h).astype(jnp.bfloat16)
        return (d_query_h, d_key_h, d_value_h)

    flat = tokens.reshape(rows_dev * SEQ, width)
    queries = (matmul(flat, query_mat) + query_bias.astype(jnp.float32)).astype(jnp.bfloat16)
    keys_all = matmul(flat, key_mat).astype(jnp.bfloat16)
    values = (matmul(flat, value_mat) + value_bias.astype(jnp.float32)).astype(jnp.bfloat16)
    query_heads = split_heads(queries, rows_dev)
    key_heads = split_heads(keys_all, rows_dev)
    value_heads = split_heads(values, rows_dev)
    items = jnp.arange(rows_dev * HEADS, dtype=jnp.int32)
    context_heads, logsums = lax.map(attend, (query_heads, key_heads, value_heads, items))
    context_low = join_heads(context_heads, rows_dev)
    branch_one = matmul(context_low, out_mat) + out_bias.astype(jnp.float32)
    mid_one = flat.astype(jnp.float32) + branch_one
    hidden_one, normed_one, scaled_one = normalise(
        mid_one, gain_first.astype(jnp.float32), shift_first.astype(jnp.float32)
    )
    hidden_one_low = hidden_one.astype(jnp.bfloat16)
    upward = matmul(hidden_one_low, up_mat) + up_bias.astype(jnp.float32)
    activated = gelu_exact(upward).astype(jnp.bfloat16)
    branch_two = matmul(activated, down_mat) + down_bias.astype(jnp.float32)
    hidden_two, normed_two, scaled_two = normalise(
        hidden_one + branch_two, gain_second.astype(jnp.float32), shift_second.astype(jnp.float32)
    )
    hidden_two_low = hidden_two.astype(jnp.bfloat16)
    raw_embed = matmul(hidden_two_low, proj_mat)
    inverse = lax.rsqrt(jnp.sum(raw_embed * raw_embed, -1, keepdims=True) + UNIT_EPS)
    embeddings = raw_embed * inverse
    embed_dim = embeddings.shape[1]
    embed_low = embeddings.astype(jnp.bfloat16).reshape(rows_dev, SEQ, embed_dim)
    query_low = embed_low[:, :QLEN]
    similar = jnp.einsum("rqc,rsc->rqs", query_low, embed_low, preferred_element_type=jnp.float32)
    positions = jnp.arange(SEQ, dtype=jnp.int32)
    live = positions[None, :] < row_lengths[:, None]
    passages = jnp.arange(1, NPASS + 1, dtype=jnp.int32)
    member = (segment_ids[:, None, :] == passages[None, :, None]) & live[:, None, :]
    masked = jnp.where(member[:, None], similar[:, :, None, :] / SOFTNESS, MASK_FILL)
    peak = jnp.max(masked, -1, keepdims=True)
    shifted = jnp.exp(masked - peak)
    totals = jnp.sum(shifted, -1, keepdims=True)
    student = SOFTNESS * jnp.sum(peak[..., 0] + jnp.log(totals[..., 0]), axis=1)
    choose = teacher_index[..., None] == jnp.arange(TABLE, dtype=jnp.int32)
    teacher = jnp.sum(jnp.where(choose, teacher_table, 0.0), -1)
    teacher_logp = jax.nn.log_softmax(teacher, axis=-1)
    student_logp = jax.nn.log_softmax(student, axis=-1)
    losses = jnp.sum(jnp.exp(teacher_logp) * (teacher_logp - student_logp), -1)
    again = collect(sent)
    (
        query_back,
        query_bias_back,
        key_back,
        value_back,
        value_bias_back,
        out_back,
        out_bias_back,
        gain_first_back,
        shift_first_back,
        up_back,
        up_bias_back,
        down_back,
        down_bias_back,
        gain_second_back,
        shift_second_back,
        proj_back,
    ) = again
    d_student = jnp.exp(student_logp) - jnp.exp(teacher_logp)
    spread_weights = shifted / totals
    d_similar = jnp.einsum("rp,rqps->rqs", d_student, spread_weights).astype(jnp.bfloat16)
    d_embed = jnp.einsum("rqs,rqc->rsc", d_similar, query_low, preferred_element_type=jnp.float32)
    d_query_part = jnp.einsum(
        "rqs,rsc->rqc", d_similar, embed_low, preferred_element_type=jnp.float32
    )
    d_embed = jnp.concatenate([d_embed[:, :QLEN] + d_query_part, d_embed[:, QLEN:]], 1).reshape(
        rows_dev * SEQ, embed_dim
    )
    d_raw = (
        inverse * (d_embed - embeddings * jnp.sum(d_embed * embeddings, -1, keepdims=True))
    ).astype(jnp.bfloat16)
    grad_proj = over_rows(hidden_two_low, d_raw)
    d_hidden_two = against(d_raw, proj_back)
    d_mid_two, grad_gain_second, grad_shift_second = normalise_back(
        d_hidden_two, normed_two, scaled_two, gain_second_back.astype(jnp.float32)
    )
    d_branch_two = d_mid_two.astype(jnp.bfloat16)
    grad_down = over_rows(activated, d_branch_two)
    grad_down_bias = jnp.sum(d_branch_two, 0, dtype=jnp.float32)
    d_upward = (against(d_branch_two, down_back) * gelu_slope(upward)).astype(jnp.bfloat16)
    grad_up = over_rows(hidden_one_low, d_upward)
    grad_up_bias = jnp.sum(d_upward, 0, dtype=jnp.float32)
    d_hidden_one = d_mid_two + against(d_upward, up_back)
    d_mid_one, grad_gain_first, grad_shift_first = normalise_back(
        d_hidden_one, normed_one, scaled_one, gain_first_back.astype(jnp.float32)
    )
    d_branch_one = d_mid_one.astype(jnp.bfloat16)
    grad_out = over_rows(context_low, d_branch_one)
    grad_out_bias = jnp.sum(d_branch_one, 0, dtype=jnp.float32)
    d_context = against(d_branch_one, out_back).astype(jnp.bfloat16)
    d_context_heads = split_heads(d_context, rows_dev)
    d_query_heads, d_key_heads, d_value_heads = lax.map(
        attend_back, (query_heads, key_heads, value_heads, d_context_heads, logsums, items)
    )
    d_queries = join_heads(d_query_heads, rows_dev)
    d_keys = join_heads(d_key_heads, rows_dev)
    d_values = join_heads(d_value_heads, rows_dev)
    grad_query = over_rows(flat, d_queries)
    grad_query_bias = jnp.sum(d_queries, 0, dtype=jnp.float32)
    grad_key = over_rows(flat, d_keys)
    grad_value = over_rows(flat, d_values)
    grad_value_bias = jnp.sum(d_values, 0, dtype=jnp.float32)
    grad_input = (
        d_mid_one
        + against(d_queries, query_back)
        + against(d_keys, key_back)
        + against(d_values, value_back)
    )
    terms = (
        grad_query,
        grad_query_bias,
        grad_key,
        grad_value,
        grad_value_bias,
        grad_out,
        grad_out_bias,
        grad_gain_first,
        grad_shift_first,
        grad_up,
        grad_up_bias,
        grad_down,
        grad_down_bias,
        grad_gain_second,
        grad_shift_second,
        grad_proj,
    )
    owned = spread_grads(terms)
    return (
        losses,
        embeddings.reshape(rows_dev, SEQ, embed_dim),
        grad_input.reshape(rows_dev, SEQ, width),
        owned[0],
        owned[1],
        owned[2],
        owned[3],
        owned[4],
        owned[5],
        owned[6],
        owned[7],
        owned[8],
        owned[9],
        owned[10],
        owned[11],
        owned[12],
        owned[13],
        owned[14],
        owned[15],
    )


MESH = pl.DeviceIdType.MESH
EXP2_SCALE = 1.4426950408889634 / math.sqrt(HEAD)
SHARDS = 32
CHIPS = 16
WIDTH = 768
HIDDEN = 3072
EMBED = 128
SMALL = 40
PAIRS = HEADS // 2
CHUNK = 256


def fits(mesh):
    return dict(mesh.shape) == {"dp": 4, "fsdp": 8}


def dotted(left, right, left_dim, right_dim):
    return lax.dot_general(
        left,
        right,
        (((left_dim,), (right_dim,)), ((), ())),
        preferred_element_type=jnp.float32,
    )


def part_of(start, size):
    return pl.ds(pl.multiple_of(start * size, size), size)


def value_of(number):
    return number() if callable(number) else number


def place():
    outer = lax.axis_index("dp")
    inner = lax.axis_index("fsdp")
    return lax.rem(outer, 2), lax.div(outer, 2), lax.div(inner, 2), lax.rem(inner, 2)


def device(x, y, z, c):
    return (y * 2 + x, z * 2 + c)


class Links:
    def __init__(self):
        x, y, z, c = place()
        self.c = c
        self.z = z
        self.chip_own = (y * 2 + x) * 4
        self.chip_x = (y * 2 + 1 - x) * 4
        self.chip_y = ((1 - y) * 2 + x) * 4
        self.chip_d = ((1 - y) * 2 + 1 - x) * 4
        self.to_core = device(x, y, z, 1 - c)
        self.to_x = device(1 - x, y, z, c)
        self.to_y = device(x, 1 - y, z, c)
        self.to_z = [None] + [device(x, y, lax.rem(z + k, 4), c) for k in (1, 2, 3)]
        self.inner = (z == 1) | (z == 2)
        paired = z + 1 - 2 * lax.rem(z, 2)
        self.to_pair = device(x, y, paired, c)
        self.to_middle = device(x, y, jnp.where(self.inner, 3 - z, paired), c)
        far = jnp.where(z < 2, 1, -1)
        near = jnp.where(self.inner, 3 - z, z + 2 * far)
        last = jnp.where(self.inner, 3 - z + far, z + 3 * far)
        self.levels = [z, paired, near, last]
        self.started = []

    def greet(self):
        barrier = pltpu.get_barrier_semaphore()
        partners = [self.to_core, self.to_x, self.to_y] + self.to_z[1:]
        for partner in partners:
            pl.semaphore_signal(barrier, inc=1, device_id=partner, device_id_type=MESH)
        pl.semaphore_wait(barrier, len(partners))

    def level(self, k):
        return lax.rem(self.z + k, 4)

    def send(self, ends, sems, target, inner=False):
        def copy():
            src, dst = ends()
            send_sem, recv_sem = sems()
            return pltpu.make_async_remote_copy(
                src_ref=src,
                dst_ref=dst,
                send_sem=send_sem,
                recv_sem=recv_sem,
                device_id=target,
                device_id_type=MESH,
            )

        def start():
            copy().start()

        def wait():
            copy().wait_send()

        if inner:
            pl.when(self.inner)(start)
            self.started.append(lambda: pl.when(self.inner)(wait))
        else:
            start()
            self.started.append(wait)

    def arrived(self, ref, sems, source):
        pltpu.make_async_remote_copy(
            src_ref=ref,
            dst_ref=ref,
            send_sem=sems[0],
            recv_sem=sems[1],
            device_id=source,
            device_id_type=MESH,
        ).wait_recv()

    def finish(self, first=0):
        for wait in self.started[first:]:
            wait()
        self.started = self.started[:first]


def rows_block(ref, rows, columns, base=0):
    def block(core, chip, count):
        return ref.at[
            pl.ds(pl.multiple_of(chip * rows, rows), count * rows),
            pl.ds(pl.multiple_of(base + core * columns, 128), columns),
        ]

    return block


def lead_block(ref):
    def block(core, chip, count):
        return ref.at[core, pl.ds(chip, count)]

    return block


class Gather:
    Z, X, Y, FX, FY, C, ZF = 0, 3, 7, 11, 13, 15, 19
    SEMS = 21

    def __init__(self, links, block, sends, recvs, group):
        self.links = links
        self.block = block
        self.sends = sends
        self.recvs = recvs
        self.group = group

    def sems(self, index, there=None):
        there = index if there is None else there
        return self.sends.at[self.group, index], self.recvs.at[self.group, there]

    def ship(self, chip, count, index, target, there=None, inner=False):
        def ends():
            ref = self.block(self.links.c, value_of(chip), count)
            return ref, ref

        self.links.send(ends, lambda: self.sems(index, there), target, inner)

    def step_of(self, column, k):
        return lambda: column + self.links.levels[k]

    def take(self, chip, count, index, source, core=None):
        core = self.links.c if core is None else core
        self.links.arrived(self.block(core, value_of(chip), count), self.sems(index), source)

    def along(self):
        n = self.links
        own = self.step_of(n.chip_own, 0)
        self.ship(own, 1, self.Z, n.to_pair)
        self.ship(own, 1, self.Z + 1, n.to_middle, inner=True)

    def across(self, k):
        n = self.links
        chip = self.step_of(n.chip_own, k)
        if k:
            self.take(chip, 1, self.Z + k - 1, n.to_pair if k == 1 else n.to_middle)
            if k == 1:
                self.ship(chip, 1, self.Z + 2, n.to_middle, inner=True)
            else:
                self.ship(chip, 1, self.ZF + k - 2, n.to_pair, self.Z + k - 1, inner=True)
        self.ship(chip, 1, self.X + k, n.to_x)
        self.ship(chip, 1, self.Y + k, n.to_y)
        if k == 3:
            self.ship(n.chip_own, 4, self.C, n.to_core)

    def onward(self, k):
        n = self.links
        if k < 2:
            chip = self.step_of(n.chip_x, k)
            self.take(chip, 1, self.X + k, n.to_x)
            self.ship(chip, 1, self.FY + k, n.to_y)
        else:
            chip = self.step_of(n.chip_y, k)
            self.take(chip, 1, self.Y + k, n.to_y)
            self.ship(chip, 1, self.FX + k - 2, n.to_x)

    def beside(self):
        n = self.links
        for k in (2, 3):
            self.take(self.step_of(n.chip_x, k), 1, self.X + k, n.to_x)
        self.ship(n.chip_x, 4, self.C + 1, n.to_core)
        for k in (0, 1):
            self.take(self.step_of(n.chip_y, k), 1, self.Y + k, n.to_y)
        self.ship(n.chip_y, 4, self.C + 2, n.to_core)

    def opposite(self):
        n = self.links
        for k in (0, 1):
            self.take(self.step_of(n.chip_d, k), 1, self.FY + k, n.to_y)
        for k in (2, 3):
            self.take(self.step_of(n.chip_d, k), 1, self.FX + k - 2, n.to_x)
        self.ship(n.chip_d, 4, self.C + 3, n.to_core)

    def last(self):
        n = self.links
        for index, chip in enumerate((n.chip_own, n.chip_x, n.chip_y, n.chip_d)):
            self.take(chip, 4, self.C + index, n.to_core, 1 - n.c)


class Scatter:
    C, DY, DX, OX, OY, Z, F = 0, 4, 5, 6, 8, 10, 13
    SEMS = 14

    def __init__(self, links, block, mine, rows, held, fin, deliver, sends, recvs, group):
        self.links = links
        self.block = block
        self.mine = mine
        self.rows = rows
        self.part, self.d_y, self.d_x, self.o_x, self.o_y, self.z_in = held
        self.fin = fin
        self.deliver = deliver
        self.sends = sends
        self.recvs = recvs
        self.group = group
        n = links
        self.sent = []
        self.columns = (n.chip_d, n.chip_x, n.chip_y, n.chip_own)

    def at(self, ref, start, count):
        if isinstance(start, int):
            return ref.at[pl.ds(start * self.rows, count * self.rows)]
        return ref.at[pl.ds(pl.multiple_of(start * self.rows, self.rows), count * self.rows)]

    def sems(self, index, there=None):
        there = index if there is None else there
        return self.sends.at[self.group, index], self.recvs.at[self.group, there]

    def ship(self, ends, index, target, there=None):
        self.links.send(ends, lambda: self.sems(index, there), target)

    def ship_part(self, start, count, ref, there, index, target):
        self.ship(
            lambda: (self.at(self.part, value_of(start), count), self.at(ref, there, count)),
            index,
            target,
        )

    def take(self, ref, start, count, index, source):
        self.links.arrived(self.at(ref, start, count), self.sems(index), source)

    def add(self, count, start, *others):
        def step(i, carry):
            here = self.at(self.part, start + i, 1)
            total = here[...].astype(jnp.float32)
            for other in others:
                total = total + other(i)[...].astype(jnp.float32)
            here[...] = total.astype(self.part.dtype)
            return carry

        lax.fori_loop(0, count, step, 0)

    def first(self):
        n = self.links
        for index, chip in enumerate(self.columns):

            def ends(chip=chip):
                return self.block(1 - n.c, chip, 4), self.at(self.part, chip, 4)

            self.ship(ends, self.C + index, n.to_core)
            self.sent.append(n.started[-1])

    def second(self, index):
        n = self.links
        chip = self.columns[index]
        self.take(self.part, chip, 4, self.C + index, n.to_core)
        self.add(4, chip, lambda i: self.mine(chip + i))
        if index == 0:
            self.ship_part(chip, 2, self.d_y, 0, self.DY, n.to_y)
            self.ship_part(lambda: chip + 2, 2, self.d_x, 0, self.DX, n.to_x)
        elif index == 1:
            self.ship_part(lambda: chip + 2, 2, self.o_x, 2, self.OX + 1, n.to_x)
        elif index == 2:
            self.ship_part(chip, 2, self.o_y, 0, self.OY, n.to_y)

    def third(self, index):
        n = self.links
        if index == 0:
            self.take(self.d_y, 0, 2, self.DY, n.to_y)
            self.add(2, n.chip_x, lambda i: self.at(self.d_y, i, 1))
            self.ship_part(n.chip_x, 2, self.o_x, 0, self.OX, n.to_x)
            return
        self.take(self.d_x, 0, 2, self.DX, n.to_x)
        self.add(2, n.chip_y + 2, lambda i: self.at(self.d_x, i, 1))
        self.ship_part(lambda: n.chip_y + 2, 2, self.o_y, 2, self.OY + 1, n.to_y)

    def fourth(self):
        n = self.links
        self.take(self.o_x, 2, 2, self.OX + 1, n.to_x)
        self.take(self.o_y, 0, 2, self.OY, n.to_y)
        self.take(self.o_x, 0, 2, self.OX, n.to_x)
        self.take(self.o_y, 2, 2, self.OY + 1, n.to_y)
        self.add(
            4,
            n.chip_own,
            lambda i: self.at(self.o_x, i, 1),
            lambda i: self.at(self.o_y, i, 1),
        )
        for j in (1, 2, 3):

            def ends(j=j):
                return (
                    self.at(self.part, n.chip_own + n.level(j), 1),
                    self.at(self.z_in, 3 - j, 1),
                )

            self.ship(ends, self.Z + j - 1, n.to_z[j], self.Z + 3 - j)

    def fifth(self):
        n = self.links
        total = self.at(self.part, n.chip_own + n.z, 1)[...].astype(jnp.float32)
        for k in (1, 2, 3):
            self.take(self.z_in, k - 1, 1, self.Z + k - 1, n.to_z[k])
            total = total + self.at(self.z_in, k - 1, 1)[...].astype(jnp.float32)
        return total

    def trade(self):
        if self.fin is None:
            self.deliver(self.fifth())
            return
        fin, fin_in = self.fin
        n = self.links
        rows = self.rows // 2
        fin[...] = self.fifth()
        self.ship(lambda: (fin.at[part_of(1 - n.c, rows)], fin_in), self.F, n.to_core)

    def whole(self):
        if self.fin is None:
            return
        fin, fin_in = self.fin
        n = self.links
        rows = self.rows // 2
        n.arrived(fin_in, self.sems(self.F), n.to_core)
        mine = fin[part_of(n.c, rows), :]
        theirs = fin_in[...]
        self.deliver(jnp.where(n.c == 0, mine, theirs), jnp.where(n.c == 0, theirs, mine))

    def settle(self):
        for wait in self.sent:
            wait()
            self.links.started.remove(wait)
        self.sent = []


def spread_lanes(parts, step):
    lane = lax.broadcasted_iota(jnp.int32, (8, 128), 1)
    tiles = [None] * (len(parts) * step // 128)

    def add(index, value):
        tiles[index] = value if tiles[index] is None else tiles[index] + value

    for i, part in enumerate(parts):
        part = jnp.where(lane < step, part, 0.0)
        index, shift = i * step // 128, i * step % 128
        rolled = pltpu.roll(part, shift, 1) if shift else part
        if shift + step <= 128:
            add(index, rolled)
        else:
            add(index, jnp.where(lane >= shift, rolled, 0.0))
            add(index + 1, jnp.where(lane < shift, rolled, 0.0))
    return tiles


def pick_lanes(tiles, step, count):
    parts = []
    lane = lax.broadcasted_iota(jnp.int32, (8, 128), 1)
    for i in range(count):
        index, shift = i * step // 128, i * step % 128
        part = pltpu.roll(tiles[index], 128 - shift, 1) if shift else tiles[index]
        if shift + step > 128:
            after = pltpu.roll(tiles[index + 1], 128 - shift, 1)
            part = jnp.where(lane < 128 - shift, part, after)
        parts.append(jnp.where(lane < step, part, 0.0))
    return parts


def rounded(value):
    return value.astype(jnp.bfloat16).astype(jnp.float32)


def segment_forms(segment_ids, row_lengths, r):
    segment = segment_ids[r : r + 1, :].astype(jnp.float32)
    position = lax.broadcasted_iota(jnp.int32, (1, SEQ), 1)
    return segment, jnp.where(position < row_lengths[r], segment, -1.0)


def upright(row):
    return jnp.broadcast_to(row, (128, SEQ)).T[:, 0:1]


def mask_of(rows_form, columns_form):
    return jnp.where(upright(rows_form) == columns_form, 0.0, MASK_FILL)


FIRST_PLAN = (
    "t.across0",
    "u.across0",
    "a.along",
    "o.across0",
    "a.across1",
    "a.across0",
    "t.along",
    "a.across2",
    "o.along",
    "a.across3",
    "t.across1",
    "o.across1",
    "o.across2",
    "t.across2",
    "d.along",
    "bias",
    "t.across3",
    "a.onward0",
    "a.onward1",
    "a.onward2",
    "t.onward0",
    "a.onward3",
    "u.along",
    "t.onward2",
    "t.onward1",
    "t.onward3",
    "a.beside",
    "u.across1",
    "o.across3",
    "u.across2",
    "turn",
    "t.opposite",
    "a.opposite",
    "t.beside",
    "u.across3",
    "a.last",
    "o.onward2",
    "d.across1",
    "t.last",
    "vec",
    "project",
    "p0",
    "p1",
    "d.across2",
    "p2",
    "p3",
    "o.onward0",
    "o.onward1",
    "o.onward3",
    "attend",
    "u.onward2",
    "a0",
    "o.beside",
    "u.onward0",
    "u.onward3",
    "a1",
    "u.onward1",
    "a2",
    "a3",
    "d.across0",
    "u.beside",
    "a4",
    "d.across3",
    "a5",
    "o.opposite",
    "a6",
    "a7",
    "o.last",
    "d.onward2",
    "a8",
    "a9",
    "a10",
    "u.opposite",
    "a11",
    "mix",
    "m0",
    "m1",
    "d.onward0",
    "d.onward1",
    "m2",
    "m3",
    "u.last",
    "widen",
    "w0",
    "d.onward3",
    "d.beside",
    "w1",
    "w2",
    "d.opposite",
    "w3",
    "d.last",
    "narrow",
)

LAST_PLAN = (
    "pre",
    "ld",
    "d.first",
    "w0",
    "w1",
    "d.second0",
    "w2",
    "w3",
    "wu0",
    "d.second1",
    "d.second2",
    "wu1",
    "wu2",
    "d.third0",
    "bc",
    "u.first",
    "n0",
    "d.third1",
    "n1",
    "n2",
    "n3",
    "u.second0",
    "u.second1",
    "misc",
    "g0",
    "u.second2",
    "u.second3",
    "d.second3",
    "g1",
    "g2",
    "g3",
    "d.fourth",
    "rd",
    "wo0",
    "wo1",
    "wo2",
    "a0",
    "o.first",
    "a1",
    "o.second0",
    "a2",
    "u.third0",
    "u.third1",
    "o.second1",
    "a3",
    "a4",
    "a5",
    "a6",
    "a7",
    "u.fourth",
    "o.third0",
    "wm0",
    "o.second2",
    "o.third1",
    "wm1",
    "wm2",
    "m.first",
    "a8",
    "m.second0",
    "a9",
    "m.second1",
    "m.second2",
    "a10",
    "o.second3",
    "m.third1",
    "m.third0",
    "a11",
    "wr0",
    "o.fourth",
    "wr1",
    "wr2",
    "r.first",
    "vec",
    "r.second0",
    "m.second3",
    "r.second1",
    "r.second2",
    "m.fourth",
    "t.first",
    "u.trade",
    "d.trade",
    "b0",
    "t.second0",
    "b1",
    "r.third1",
    "r.third0",
    "d.whole",
    "r.second3",
    "t.second1",
    "t.second2",
    "t.third1",
    "u.whole",
    "t.third0",
    "t.second3",
    "r.fourth",
    "m.trade",
    "t.fourth",
    "o.trade",
    "b2",
    "b3",
    "o.whole",
    "r.trade",
    "m.whole",
    "t.trade",
    "r.whole",
    "t.whole",
    "end",
)


class Plan:
    def __init__(self, names, groups):
        self.groups = groups
        self.inside = {}
        self.queue = list(names)

    def call(self, name):
        group, method = name.split(".")
        if method[-1].isdigit():
            getattr(self.groups[group], method[:-1])(int(method[-1]))
        else:
            getattr(self.groups[group], method)()

    def until(self, name):
        while True:
            step = self.queue.pop(0)
            if step == name:
                return
            self.call(step)

    def loop(self, letter, first, count, body):
        steps = {}
        self.until(f"{letter}{first}")
        for index in range(first, first + count):
            steps[index] = []
            ahead = f"{letter}{index + 1}"
            while self.queue[0] != ahead and "." in self.queue[0]:
                steps[index].append(self.queue.pop(0))
            if index + 1 < first + count:
                self.queue.pop(0)

        def run(step, carry):
            body(step)
            for index, names in steps.items():
                if names:

                    @pl.when(step == index)
                    def _(names=names):
                        for name in names:
                            self.call(name)

            return carry

        lax.fori_loop(first, first + count, run, 0)


def attend_pair(r, p, qkv, context, logsums, bias):
    rows = part_of(r, SEQ)
    columns = pl.multiple_of(p * 128, 128)
    query = qkv[rows, pl.ds(columns, 128)]
    key = qkv[rows, pl.ds(columns + WIDTH, 128)]
    value = qkv[rows, pl.ds(columns + 2 * WIDTH, 128)]
    low = lax.broadcasted_iota(jnp.int32, (SEQ, 128), 1) < HEAD
    zero = jnp.zeros_like(key)
    outs, sums = [], []
    for j in range(2):
        key_j = jnp.where(low, key, zero) if j == 0 else jnp.where(low, zero, key)
        scores = dotted(query, key_j, 1, 1) * EXP2_SCALE + bias[rows, 0:SEQ]
        peak = jnp.max(scores, -1, keepdims=True)
        shifted = jnp.exp2(scores - peak)
        total = jnp.sum(shifted, -1, keepdims=True)
        out = dotted(shifted.astype(jnp.bfloat16), value, 1, 0)
        outs.append(out * (1.0 / total))
        sums.append(peak + jnp.log2(total))
    context[rows, pl.ds(columns, 128)] = jnp.where(low, outs[0], outs[1]).astype(jnp.bfloat16)
    turned = jnp.where(low, sums[0], sums[1]).T
    logsums[r, p, 0:1] = turned[0:1]
    logsums[r, p, 1:2] = turned[HEAD : HEAD + 1]


def attend_back_pair(r, p, qkv, d_context, logsums, rowdots, bias):
    rows = part_of(r, SEQ)
    columns = pl.multiple_of(p * 128, 128)
    query = qkv[rows, pl.ds(columns, 128)]
    key = qkv[rows, pl.ds(columns + WIDTH, 128)]
    value = qkv[rows, pl.ds(columns + 2 * WIDTH, 128)]
    grad = d_context[rows, pl.ds(columns, 128)]
    low = lax.broadcasted_iota(jnp.int32, (SEQ, 128), 1) < HEAD
    zero = jnp.zeros_like(key)
    d_query, d_key, d_value = None, [], []
    for j in range(2):
        pick = (lambda a: jnp.where(low, a, zero)) if j == 0 else (lambda a: jnp.where(low, zero, a))
        key_j = pick(key)
        scores = dotted(key_j, query, 1, 1) * EXP2_SCALE + bias[r]
        chances = jnp.exp2(scores - logsums[r, p, j : j + 1, :])
        d_chances = dotted(pick(value), grad, 1, 1)
        d_scores = (chances * (d_chances - rowdots[r, p, j : j + 1, :])).astype(jnp.bfloat16)
        d_value.append(dotted(chances.astype(jnp.bfloat16), grad, 1, 0))
        d_key.append(dotted(d_scores, query, 1, 0))
        term = dotted(d_scores, key_j, 0, 0)
        d_query = term if d_query is None else d_query + term
    scale = 1.0 / math.sqrt(HEAD)
    low_type = jnp.bfloat16
    qkv[rows, pl.ds(columns, 128)] = (d_query * scale).astype(low_type)
    qkv[rows, pl.ds(columns + WIDTH, 128)] = (
        jnp.where(low, d_key[0], d_key[1]) * scale
    ).astype(low_type)
    qkv[rows, pl.ds(columns + 2 * WIDTH, 128)] = jnp.where(low, d_value[0], d_value[1]).astype(
        low_type
    )


def row_dots(context, d_context, rowdots):
    shape = (8, 128)
    head = lax.broadcasted_iota(jnp.int32, shape, 1) // HEAD
    pick = (head == lax.broadcasted_iota(jnp.int32, shape, 0)).astype(jnp.float32)
    for r in range(rowdots.shape[0]):
        for p in range(PAIRS):
            part = (slice(r * SEQ, (r + 1) * SEQ), slice(p * 128, (p + 1) * 128))
            both = context[part].astype(jnp.float32) * d_context[part].astype(jnp.float32)
            rowdots[r, p] = lax.dot_general(
                pick,
                both,
                (((1,), (1,)), ((), ())),
                precision=lax.Precision.HIGHEST,
                preferred_element_type=jnp.float32,
            )


def norm_parts(mixed):
    centred = mixed - jnp.mean(mixed, -1, keepdims=True)
    scaled = lax.rsqrt(jnp.mean(centred * centred, -1, keepdims=True) + NORM_EPS)
    return centred * scaled, scaled


def norm_back(grad_out, normed, scaled, gain):
    inner = grad_out * gain
    return scaled * (
        inner
        - jnp.mean(inner, -1, keepdims=True)
        - normed * jnp.mean(inner * normed, -1, keepdims=True)
    )


def halves(links, src, stage, sends, recvs, index):
    rows, width = src.shape
    columns = width // 2

    def ends():
        return src.at[:, part_of(1 - links.c, columns)], stage.at[part_of(links.c, rows), :]

    links.send(ends, lambda: (sends.at[index], recvs.at[index]), links.to_core)
    stage[part_of(links.c, rows), :] = src[:, part_of(links.c, columns)]


class Joined(Gather):
    def join_from(self, stage, sends, recvs, index):
        self.parts = (stage, sends, recvs, index)
        return self

    def join(self):
        if self.parts is None:
            return
        n = self.links
        stage, sends, recvs, index = self.parts
        self.parts = None
        rows = stage.shape[0] // 2
        here = stage.at[part_of(1 - n.c, rows), :]
        n.arrived(here, (sends.at[index], recvs.at[index]), n.to_core)
        self.block(n.c, n.chip_own + n.z, 1)[...] = stage[...].astype(jnp.bfloat16)

    def along(self):
        self.join()
        super().along()

    def across(self, k):
        self.join()
        super().across(k)


def passage_loss(r, similar, live_row, teacher_index, teacher_table):
    scores = similar * (1.0 / SOFTNESS)
    inside, shares, student, teacher = [], [], [], []
    for p in range(NPASS):
        member = live_row == float(p + 1)
        masked = jnp.where(member, scores, MASK_FILL)
        peak = jnp.max(masked, -1, keepdims=True)
        shifted = jnp.exp(masked - peak)
        total = jnp.sum(shifted, -1, keepdims=True)
        inside.append(jnp.where(member, shifted, 0.0))
        shares.append(1.0 / total)
        student.append(SOFTNESS * jnp.sum(peak + jnp.log(total), axis=0, keepdims=True))
        teacher.append(jnp.full((1, 1), teacher_table[teacher_index[r, p]], jnp.float32))

    def log_softmax(values):
        peak = functools.reduce(jnp.maximum, values)
        total = sum(jnp.exp(value - peak) for value in values)
        return [value - peak - jnp.log(total) for value in values]

    student = log_softmax(student)
    teacher = log_softmax(teacher)
    loss = sum(jnp.exp(t) * (t - s) for t, s in zip(teacher, student))
    d_similar = sum(
        part * (share * (jnp.exp(s) - jnp.exp(t)))
        for part, share, s, t in zip(inside, shares, student, teacher)
    )
    return loss, d_similar


def first_kernel(*refs):
    (
        tokens,
        w_query,
        w_key,
        w_value,
        w_out,
        w_up,
        w_down,
        w_proj,
        *vector_refs,
        b_up,
        segment_ids,
        row_lengths,
        teacher_index,
        teacher_table,
    ) = refs[:21]
    (
        losses,
        embeddings,
        attn_hbm,
        up_hbm,
        down_hbm,
        turned_hbm,
        qkv_hbm,
        context_hbm,
        low_one_hbm,
        normed_one_hbm,
        slope_hbm,
        d_mid_hbm,
        d_branch_hbm,
        grad_down_hbm,
        scaled_one,
        vectors,
        grad_vectors,
        grad_proj,
        logsums,
    ) = refs[21:40]
    (
        attn_mat,
        up_mat,
        down_mat,
        turned,
        qkv,
        context,
        low_one,
        normed_one,
        slope,
        activated,
        d_mid,
        d_branch,
        grad_down,
        small_all,
        cat_attn,
        stage_attn,
        stage_out,
        stage_up,
        stage_down,
        proj,
        up_bias,
        normed_two,
        scaled_two,
        low_two,
        sends,
        recvs,
        half_sends,
        half_recvs,
        local_sems,
        grad_sems,
    ) = refs[40:]
    count = tokens.shape[0]
    rows_dev = count // SEQ
    links = Links()

    def gather(block, group, stage):
        return Joined(links, block, sends, recvs, group).join_from(
            stage, half_sends, half_recvs, group
        )

    attn = gather(rows_block(attn_mat, 48, 1152), 0, stage_attn)
    out = gather(rows_block(attn_mat, 48, 384, 3 * WIDTH), 1, stage_out)
    up = gather(rows_block(up_mat, 48, 1536), 2, stage_up)
    down = gather(rows_block(down_mat, 192, 384), 3, stage_down)
    tiny = Gather(links, lead_block(small_all), sends, recvs, 4)
    own_chip = links.chip_own + links.z
    kept = []

    def keep(src, dst):
        copy = pltpu.make_async_copy(src, dst, local_sems.at[len(kept)])
        copy.start()
        kept.append(copy)

    for index, ref in enumerate((w_query, w_key, w_value)):
        cat_attn[:, index * WIDTH : (index + 1) * WIDTH] = ref[...]
    own_small = small_all.at[links.c, own_chip]
    own_small[0:24, :] = w_proj[...]
    own_small[24:40, :] = jnp.zeros((16, 128), jnp.float32)
    for index, ref in enumerate(vector_refs):
        own_small[24 + index : 25 + index, 0:24] = ref[...].reshape(1, 24)
    own_small[32:33, 0:96] = b_up[...].reshape(1, 96)

    links.greet()
    halves(links, cat_attn, stage_attn, half_sends, half_recvs, 0)
    halves(links, w_out, stage_out, half_sends, half_recvs, 1)
    halves(links, w_up, stage_up, half_sends, half_recvs, 2)
    halves(links, w_down, stage_down, half_sends, half_recvs, 3)
    plan = Plan(FIRST_PLAN, {"a": attn, "o": out, "u": up, "d": down, "t": tiny})
    plan.until("bias")
    live_rows = []
    for r in range(rows_dev):
        segment, live = segment_forms(segment_ids, row_lengths, r)
        live_rows.append(live)
        d_mid[r * SEQ : (r + 1) * SEQ, 0:SEQ] = mask_of(segment, live)
    plan.until("turn")
    turned[...] = tokens[...].T
    keep(turned, turned_hbm)
    plan.until("vec")
    cores = [(i % 2, i // 2) for i in range(SHARDS)]
    for index, tile in enumerate(spread_lanes([small_all[c, n, 24:32, :] for c, n in cores], 24)):
        vectors[:, index * 128 : (index + 1) * 128] = rounded(tile)
    for index, tile in enumerate(spread_lanes([small_all[c, n, 32:40, :] for c, n in cores], 96)):
        up_bias[:, index * 128 : (index + 1) * 128] = rounded(tile)
    for r in range(CHIPS):
        both = jnp.concatenate([small_all[0, r, 0:24, :], small_all[1, r, 0:24, :]], axis=0)
        proj[r * 48 : (r + 1) * 48, :] = both.astype(jnp.bfloat16)
    plan.until("project")

    def project(step):
        rows = part_of(step, CHUNK)
        part = tokens[rows, :]
        for index in range(3):
            columns = slice(index * WIDTH, (index + 1) * WIDTH)
            value = dotted(part, attn_mat[:, columns], 1, 0)
            if index != 1:
                value = value + vectors[index // 2 : index // 2 + 1, :]
            qkv[rows, columns] = value.astype(jnp.bfloat16)

    plan.loop("p", 0, count // CHUNK, project)
    keep(qkv, qkv_hbm)
    plan.until("attend")

    def attend(item):
        attend_pair(lax.div(item, PAIRS), lax.rem(item, PAIRS), qkv, context, logsums, d_mid)

    plan.loop("a", 0, rows_dev * PAIRS, attend)
    keep(context, context_hbm)
    plan.until("mix")
    keep(attn_mat, attn_hbm)

    def mix(step):
        rows = part_of(step, CHUNK)
        mixed = dotted(context[rows, :], attn_mat[:, 3 * WIDTH :], 1, 0) + vectors[2:3, :]
        normed, scaled = norm_parts(tokens[rows, :].astype(jnp.float32) + mixed)
        normed_one[rows, :] = normed
        scaled_one[rows, :] = jnp.broadcast_to(scaled, (CHUNK, 128))
        low_one[rows, :] = (normed * vectors[3:4, :] + vectors[4:5, :]).astype(jnp.bfloat16)

    plan.loop("m", 0, count // CHUNK, mix)
    keep(normed_one, normed_one_hbm)
    keep(low_one, low_one_hbm)
    plan.until("widen")
    keep(up_mat, up_hbm)

    def widen(step):
        rows = part_of(step, CHUNK)
        part = low_one[rows, :]
        for index in range(4):
            columns = slice(index * WIDTH, (index + 1) * WIDTH)
            upward = dotted(part, up_mat[:, columns], 1, 0) + up_bias[0:1, columns]
            chance = 0.5 * (1.0 + lax.erf(upward * ROOT_HALF))
            activated[rows, columns] = (upward * chance).astype(jnp.bfloat16)
            density = jnp.exp(-0.5 * upward * upward) * DENSITY_SCALE
            slope[rows, columns] = (chance + upward * density).astype(jnp.bfloat16)

    plan.loop("w", 0, count // CHUNK, widen)
    keep(slope, slope_hbm)
    plan.until("narrow")
    keep(down_mat, down_hbm)

    grad_vectors[...] = jnp.zeros_like(grad_vectors)
    grad_proj[...] = jnp.zeros_like(grad_proj)
    for r in range(rows_dev):

        def narrow(step, carry):
            here = part_of(step, CHUNK)
            rows = pl.ds(pl.multiple_of(r * SEQ + step * CHUNK, CHUNK), CHUNK)
            mixed = dotted(activated[rows, :], down_mat[...], 1, 0) + vectors[5:6, :]
            mixed = mixed + (normed_one[rows, :] * vectors[3:4, :] + vectors[4:5, :])
            normed, scaled = norm_parts(mixed)
            normed_two[here, :] = normed
            scaled_two[here, :] = jnp.broadcast_to(scaled, (CHUNK, 128))
            low_two[here, :] = (normed * vectors[6:7, :] + vectors[7:8, :]).astype(jnp.bfloat16)
            return carry

        lax.fori_loop(0, SEQ // CHUNK, narrow, 0)
        raw = dotted(low_two[...], proj[...], 1, 0)
        inverse = lax.rsqrt(jnp.sum(raw * raw, -1, keepdims=True) + UNIT_EPS)
        embedded = raw * inverse
        embeddings[r] = embedded
        low_embed = embedded.astype(jnp.bfloat16)
        similar = dotted(low_embed[0:QLEN], low_embed, 1, 1)
        loss, d_similar = passage_loss(r, similar, live_rows[r], teacher_index, teacher_table)
        losses[r] = loss[0, 0]
        d_similar = d_similar.astype(jnp.bfloat16)
        d_embed = dotted(d_similar, low_embed[0:QLEN], 0, 0)
        d_query = dotted(d_similar, low_embed, 1, 0)
        d_embed = jnp.concatenate([d_embed[0:QLEN] + d_query, d_embed[QLEN:]], axis=0)
        along = jnp.sum(d_embed * embedded, -1, keepdims=True)
        d_raw = (inverse * (d_embed - embedded * along)).astype(jnp.bfloat16)
        grad_proj[...] += dotted(low_two[...], d_raw, 0, 0)
        d_hidden = dotted(d_raw, proj[...], 1, 1)
        normed = normed_two[...]
        d_mixed = norm_back(d_hidden, normed, scaled_two[:, 0:1], vectors[6:7, :])
        low_mixed = d_mixed.astype(jnp.bfloat16)
        rows = slice(r * SEQ, (r + 1) * SEQ)
        d_mid[rows, :] = d_mixed
        d_branch[rows, :] = low_mixed
        grad_vectors[5:6, :] += jnp.sum(low_mixed.astype(jnp.float32), 0, keepdims=True)
        grad_vectors[6:7, :] += jnp.sum(d_hidden * normed, 0, keepdims=True)
        grad_vectors[7:8, :] += jnp.sum(d_hidden, 0, keepdims=True)
    keep(d_mid, d_mid_hbm)
    keep(d_branch, d_branch_hbm)

    def grad_copy(step, slot):
        return pltpu.make_async_copy(
            grad_down.at[slot], grad_down_hbm.at[part_of(step, CHUNK), :], grad_sems.at[slot]
        )

    def weigh(step, carry):
        slot = lax.rem(step, 2)

        @pl.when(step >= 2)
        def _():
            grad_copy(step - 2, slot).wait()

        part = activated[:, part_of(step, CHUNK)]
        grad_down[slot] = dotted(part, d_branch[...], 0, 0).astype(jnp.bfloat16)
        grad_copy(step, slot).start()
        return carry

    steps = HIDDEN // CHUNK
    lax.fori_loop(0, steps, weigh, 0)
    for step in (steps - 2, steps - 1):
        grad_copy(step, step % 2).wait()
    links.finish()
    for copy in kept:
        copy.wait()


def run_first(tokens, weights, vectors, segment_ids, row_lengths, teacher_index, teacher_table):
    count = tokens.shape[0]
    rows_dev = count // SEQ
    vmem = pl.BlockSpec(memory_space=pltpu.VMEM)
    smem = pl.BlockSpec(memory_space=pltpu.SMEM)
    anywhere = pl.BlockSpec(memory_space=pl.ANY)
    low = jnp.bfloat16
    wide = jnp.float32

    def array(kind, *shape):
        return jax.ShapeDtypeStruct(shape, kind)

    return pl.pallas_call(
        first_kernel,
        out_shape=[
            array(wide, rows_dev),
            array(wide, rows_dev, SEQ, EMBED),
            array(low, WIDTH, HIDDEN),
            array(low, WIDTH, HIDDEN),
            array(low, HIDDEN, WIDTH),
            array(low, WIDTH, count),
            array(low, count, 3 * WIDTH),
            array(low, count, WIDTH),
            array(low, count, WIDTH),
            array(wide, count, WIDTH),
            array(low, count, HIDDEN),
            array(wide, count, WIDTH),
            array(low, count, WIDTH),
            array(low, HIDDEN, WIDTH),
            array(wide, count, 128),
            array(wide, 8, WIDTH),
            array(wide, 8, WIDTH),
            array(wide, WIDTH, EMBED),
            array(wide, rows_dev, PAIRS, 8, SEQ),
        ],
        in_specs=[vmem] * 18 + [smem] * 3,
        out_specs=[smem, vmem] + [anywhere] * 12 + [vmem] * 5,
        scratch_shapes=[
            pltpu.VMEM((WIDTH, HIDDEN), low),
            pltpu.VMEM((WIDTH, HIDDEN), low),
            pltpu.VMEM((HIDDEN, WIDTH), low),
            pltpu.VMEM((WIDTH, count), low),
            pltpu.VMEM((count, 3 * WIDTH), low),
            pltpu.VMEM((count, WIDTH), low),
            pltpu.VMEM((count, WIDTH), low),
            pltpu.VMEM((count, WIDTH), wide),
            pltpu.VMEM((count, HIDDEN), low),
            pltpu.VMEM((count, HIDDEN), low),
            pltpu.VMEM((count, WIDTH), wide),
            pltpu.VMEM((count, WIDTH), low),
            pltpu.VMEM((2, CHUNK, WIDTH), low),
            pltpu.VMEM((2, CHIPS, SMALL, 128), wide),
            pltpu.VMEM((24, 3 * WIDTH), wide),
            pltpu.VMEM((48, 3 * WIDTH // 2), wide),
            pltpu.VMEM((48, WIDTH // 2), wide),
            pltpu.VMEM((48, HIDDEN // 2), wide),
            pltpu.VMEM((192, WIDTH // 2), wide),
            pltpu.VMEM((WIDTH, EMBED), low),
            pltpu.VMEM((8, HIDDEN), wide),
            pltpu.VMEM((SEQ, WIDTH), wide),
            pltpu.VMEM((SEQ, 128), wide),
            pltpu.VMEM((SEQ, WIDTH), low),
            pltpu.SemaphoreType.DMA((5, Gather.SEMS)),
            pltpu.SemaphoreType.DMA((5, Gather.SEMS)),
            pltpu.SemaphoreType.DMA((4,)),
            pltpu.SemaphoreType.DMA((4,)),
            pltpu.SemaphoreType.DMA((12,)),
            pltpu.SemaphoreType.DMA((2,)),
        ],
        compiler_params=pltpu.CompilerParams(
            collective_id=0, has_side_effects=True, vmem_limit_bytes=62 * 2**20
        ),
        name="forward_gather",
    )(tokens, *weights, *vectors, segment_ids, row_lengths, teacher_index, teacher_table)


def last_kernel(*refs):
    (
        attn_hbm,
        up_hbm,
        down_hbm,
        turned_hbm,
        qkv_hbm,
        context_hbm,
        low_one_hbm,
        normed_one_hbm,
        slope_hbm,
        d_mid_hbm,
        d_branch_hbm,
        grad_down_hbm,
        scaled_one,
        vectors,
        part_vectors,
        grad_proj,
        logsums,
        segment_ids,
        row_lengths,
    ) = refs[:19]
    (
        grad_tokens_hbm,
        own_rows,
        own_down,
        own_small,
    ) = refs[19:23]
    (
        attn_mat,
        grads,
        wide,
        low_one,
        turned,
        d_branch,
        d_mid,
        part_down,
        small_all,
        rowdots,
        grad_vectors,
        grad_up_bias,
        sends,
        recvs,
        local_sems,
        slope_sems,
        qkv_sems,
        grad_sems,
        context,
        *rest,
    ) = refs[23:]
    held = [rest[6 * i : 6 * i + 6] for i in range(6)]
    fins = [rest[36 + 2 * i : 38 + 2 * i] for i in range(5)]
    count = d_mid.shape[0]
    rows_dev = count // SEQ
    links = Links()
    c = links.c

    def scatter(block, rows, group, deliver, mine=None):
        def own(chip):
            return block(c, chip, 1)

        own = own if mine is None else mine
        fin = fins[group] if group < 5 else None
        return Scatter(links, block, own, rows, held[group], fin, deliver, sends, recvs, group)

    def down_mine(chip):
        return part_down.at[part_of(chip, 192), :]

    def halves_to(ref, start, columns):
        def deliver(low, high):
            ref[:, start : start + columns] = low
            ref[:, start + columns : start + 2 * columns] = high

        return deliver

    def most_out(low, high):
        own_rows[:, 0:512] = low[:, 0:512]
        own_rows[:, 768:1024] = low[:, 512:768]
        own_rows[:, 1024:1280] = high[:, 0:256]
        own_rows[:, 1536:2048] = high[:, 256:768]

    def rest_out(low, high):
        own_rows[:, 512:768] = low[:, 0:256]
        own_rows[:, 1280:1408] = low[:, 256:384]
        own_rows[:, 1408:1536] = high[:, 0:128]
        own_rows[:, 2048:2304] = high[:, 128:384]

    def tiny_out(total):
        own_small[...] = total[0]

    down = scatter(rows_block(grad_down_hbm, 192, 384), 192, 0, halves_to(own_down, 0, WIDTH // 2), down_mine)
    up = scatter(rows_block(grads, 48, 1536), 48, 1, halves_to(own_rows, HIDDEN, HIDDEN // 2))
    out = scatter(rows_block(grads, 48, 384), 48, 2, halves_to(own_rows, 3 * WIDTH, WIDTH // 2))
    most = scatter(rows_block(grads, 48, 768, WIDTH), 48, 3, most_out)
    rest_of = scatter(rows_block(grads, 48, 384, 3 * WIDTH), 48, 4, rest_out)
    tiny = scatter(lead_block(small_all), 1, 5, tiny_out)

    def load(src, dst, index):
        return pltpu.make_async_copy(src, dst, local_sems.at[index])

    def start(copies):
        for copy in copies:
            copy.start()

    def wait(copies):
        for copy in copies:
            copy.wait()

    plan = Plan(
        LAST_PLAN, {"d": down, "u": up, "o": out, "m": most, "r": rest_of, "t": tiny}
    )
    plan.until("pre")
    first_loads = [
        load(d_branch_hbm, d_branch, 0),
        load(grad_down_hbm.at[:, part_of(c, WIDTH // 2)], part_down, 1),
    ]
    late_loads = [
        load(context_hbm, context, 2),
        load(attn_hbm, attn_mat, 3),
        load(turned_hbm, turned, 4),
    ]
    start(first_loads[:1])
    links.greet()
    grad_vectors[...] = part_vectors[...]
    ones = jnp.ones((8, count), jnp.bfloat16)

    def slope_load(step):
        rows = part_of(step, CHUNK)
        return pltpu.make_async_copy(slope_hbm.at[rows, :], wide.at[rows, :], slope_sems.at[step])

    def qkv_load(step):
        rows = part_of(step, CHUNK)
        return pltpu.make_async_copy(
            qkv_hbm.at[rows, :], wide.at[rows, 0 : 3 * WIDTH], qkv_sems.at[step]
        )

    def grad_store(step):
        rows = part_of(step, CHUNK)
        return pltpu.make_async_copy(
            d_mid.at[rows, :], grad_tokens_hbm.at[rows, :], grad_sems.at[step]
        )

    steps = count // CHUNK

    def feed_forward(up_mat, down_mat, normed_one):
        ahead = [load(down_hbm, down_mat, 5)]
        start(ahead)
        for step in range(steps):
            slope_load(step).start()
        start(first_loads[1:])
        middle = [
            load(low_one_hbm, low_one, 6),
            load(up_hbm, up_mat, 7),
            load(d_mid_hbm, d_mid, 8),
            load(normed_one_hbm, normed_one, 9),
        ]
        plan.until("ld")
        wait(first_loads[:1] + ahead)

        def widen(step):
            rows = part_of(step, CHUNK)
            slope_load(step).wait()
            part = d_branch[rows, :]
            for index in range(4):
                columns = slice(index * WIDTH, (index + 1) * WIDTH)
                grad = dotted(part, down_mat[columns, :], 1, 1)
                wide[rows, columns] = (grad * wide[rows, columns].astype(jnp.float32)).astype(
                    jnp.bfloat16
                )

            @pl.when(step == 0)
            def _():
                wait(first_loads[1:])
                start(middle)

        plan.loop("w", 0, steps, widen)
        wait(middle[:1])

        def weigh(step):
            rows = part_of(step, CHUNK)
            part = low_one[:, rows].T
            for index in range(4):
                columns = slice(index * WIDTH, (index + 1) * WIDTH)
                grads[rows, columns] = dotted(part, wide[:, columns], 1, 0).astype(jnp.bfloat16)

        plan.loop("wu", 0, WIDTH // CHUNK, weigh)
        plan.until("bc")
        start(late_loads)
        for index in range(4):
            columns = slice(index * WIDTH, (index + 1) * WIDTH)
            grad_up_bias[:, columns] = dotted(ones, wide[:, columns], 1, 0)
        wait(middle[1:])

        def narrow(step):
            rows = part_of(step, CHUNK)
            d_hidden = d_mid[rows, :] + dotted(wide[rows, :], up_mat[...], 1, 1)
            qkv_load(step).start()
            normed = normed_one[rows, :]
            d_mixed = norm_back(d_hidden, normed, scaled_one[rows, 0:1], vectors[3:4, :])
            d_mid[rows, :] = d_mixed
            d_branch[rows, :] = d_mixed.astype(jnp.bfloat16)
            grad_vectors[3:4, :] += jnp.sum(d_hidden * normed, 0, keepdims=True)
            grad_vectors[4:5, :] += jnp.sum(d_hidden, 0, keepdims=True)

        plan.loop("n", 0, steps, narrow)

    pl.run_scoped(
        feed_forward,
        pltpu.VMEM((WIDTH, HIDDEN), jnp.bfloat16),
        pltpu.VMEM((HIDDEN, WIDTH), jnp.bfloat16),
        pltpu.VMEM((count, WIDTH), jnp.float32),
    )

    def attention(d_context, bias):
        plan.until("misc")
        grad_vectors[2:3, :] = dotted(ones, d_branch[...], 1, 0)[0:1]
        for r in range(rows_dev):
            segment, live = segment_forms(segment_ids, row_lengths, r)
            bias[r] = mask_of(live, segment)
        wait(late_loads)

        def give(step):
            rows = part_of(step, CHUNK)
            d_context[rows, :] = dotted(d_branch[rows, :], attn_mat[:, 3 * WIDTH :], 1, 1).astype(
                jnp.bfloat16
            )

        plan.loop("g", 0, steps, give)
        plan.until("rd")
        row_dots(context, d_context, rowdots)
        up.settle()

        def weigh_out(step):
            rows = part_of(step, CHUNK)
            part = context[:, rows].T
            grads[rows, 0:WIDTH] = dotted(part, d_branch[...], 1, 0).astype(jnp.bfloat16)

        plan.loop("wo", 0, WIDTH // CHUNK, weigh_out)
        for step in range(steps):
            qkv_load(step).wait()

        def attend(item):
            r = lax.rem(item, rows_dev)
            p = lax.div(item, rows_dev)
            attend_back_pair(r, p, wide, d_context, logsums, rowdots, bias)

        def weigh(first, pairs, base):
            def step(step):
                rows = part_of(step, CHUNK)
                part = turned[rows, :]
                for index in range(3):
                    start = index * WIDTH + first * 128
                    there = base + index * pairs * 128
                    grads[rows, there : there + pairs * 128] = dotted(
                        part, wide[:, start : start + pairs * 128], 1, 0
                    ).astype(jnp.bfloat16)

            return step

        plan.loop("a", 0, 4 * rows_dev, attend)
        plan.loop("wm", 0, WIDTH // CHUNK, weigh(0, 4, WIDTH))
        plan.loop("a", 4 * rows_dev, 2 * rows_dev, attend)
        plan.loop("wr", 0, WIDTH // CHUNK, weigh(4, 2, 3 * WIDTH))

    pl.run_scoped(
        attention,
        pltpu.VMEM((count, WIDTH), jnp.bfloat16),
        pltpu.VMEM((rows_dev, SEQ, SEQ), jnp.float32),
    )
    plan.until("vec")
    for index in (0, 2):
        total = dotted(ones, wide[:, index * WIDTH : (index + 1) * WIDTH], 1, 0)
        grad_vectors[index // 2 : index // 2 + 1, :] = total[0:1]
    tiles = [grad_vectors[:, i * 128 : (i + 1) * 128] for i in range(WIDTH // 128)]
    for i, part in enumerate(pick_lanes(tiles, 24, SHARDS)):
        small_all[i % 2, i // 2, 24:32, :] = part
    tiles = [grad_up_bias[:, i * 128 : (i + 1) * 128] for i in range(HIDDEN // 128)]
    for i, part in enumerate(pick_lanes(tiles, 96, SHARDS)):
        small_all[i % 2, i // 2, 32:40, :] = part
        small_all[i % 2, i // 2, 0:24, :] = grad_proj[i * 24 : (i + 1) * 24, :]

    def back(step):
        rows = part_of(step, CHUNK)
        value = dotted(wide[rows, 0 : 3 * WIDTH], attn_mat[:, 0 : 3 * WIDTH], 1, 1)
        d_mid[rows, :] += value
        grad_store(step).start()

    plan.loop("b", 0, steps, back)
    plan.until("end")
    for step in range(steps):
        grad_store(step).wait()
    links.finish()


def run_last(kept, segment_ids, row_lengths):
    count = kept[9].shape[0]
    rows_dev = count // SEQ
    vmem = pl.BlockSpec(memory_space=pltpu.VMEM)
    smem = pl.BlockSpec(memory_space=pltpu.SMEM)
    anywhere = pl.BlockSpec(memory_space=pl.ANY)
    low = jnp.bfloat16
    wide = jnp.float32

    def array(*shape):
        return jax.ShapeDtypeStruct(shape, wide)

    def held(unit, kind):
        return [pltpu.VMEM((n * unit[0],) + unit[1:], kind) for n in (16, 2, 2, 4, 4, 3)]

    blocks = ((192, 384), (48, 1536), (48, 384), (48, 768), (48, 384))
    buffers = []
    for block in blocks:
        buffers += held(block, low)
    buffers += held((1, SMALL, 128), wide)
    for rows, columns in blocks:
        buffers += [pltpu.VMEM((rows, columns), wide), pltpu.VMEM((rows // 2, columns), wide)]
    return pl.pallas_call(
        last_kernel,
        out_shape=[
            array(count, WIDTH),
            array(24, 2 * HIDDEN),
            array(96, WIDTH),
            array(SMALL, 128),
        ],
        in_specs=[anywhere] * 12 + [vmem] * 6 + [smem],
        out_specs=[anywhere] + [vmem] * 3,
        scratch_shapes=[
            pltpu.VMEM((WIDTH, HIDDEN), low),
            pltpu.VMEM((WIDTH, HIDDEN), low),
            pltpu.VMEM((count, HIDDEN), low),
            pltpu.VMEM((count, WIDTH), low),
            pltpu.VMEM((WIDTH, count), low),
            pltpu.VMEM((count, WIDTH), low),
            pltpu.VMEM((count, WIDTH), wide),
            pltpu.VMEM((HIDDEN, WIDTH // 2), low),
            pltpu.VMEM((2, CHIPS, SMALL, 128), wide),
            pltpu.VMEM((rows_dev, PAIRS, 8, SEQ), wide),
            pltpu.VMEM((8, WIDTH), wide),
            pltpu.VMEM((8, HIDDEN), wide),
            pltpu.SemaphoreType.DMA((6, Scatter.SEMS)),
            pltpu.SemaphoreType.DMA((6, Scatter.SEMS)),
            pltpu.SemaphoreType.DMA((10,)),
            pltpu.SemaphoreType.DMA((count // CHUNK,)),
            pltpu.SemaphoreType.DMA((count // CHUNK,)),
            pltpu.SemaphoreType.DMA((count // CHUNK,)),
            pltpu.VMEM((count, WIDTH), low),
        ]
        + buffers,
        compiler_params=pltpu.CompilerParams(
            collective_id=1, has_side_effects=True, vmem_limit_bytes=63 * 2**20
        ),
        name="backward_scatter",
    )(*kept, segment_ids, row_lengths)


def pass_kernel(*refs):
    sources, losses = refs[:5], refs[5]
    grad_tokens, embeddings, query, key, value, out, up, down, proj, *vectors = refs[6:23]
    up_bias, own_losses = refs[23:25]
    held, (in_sems, out_sems) = refs[25:30], refs[30:]
    pieces = 4
    through = []
    for src, mid, dst in zip(sources[:2], held[:2], (grad_tokens, embeddings)):
        rows = src.shape[0] // pieces
        for piece in range(pieces):
            part = pl.ds(piece * rows, rows)
            index = len(through)
            through.append(
                (
                    pltpu.make_async_copy(src.at[part], mid.at[part], in_sems.at[index]),
                    pltpu.make_async_copy(mid.at[part], dst.at[part], out_sems.at[index]),
                )
            )
    small = [
        pltpu.make_async_copy(src, mid, in_sems.at[2 * pieces + index])
        for index, (src, mid) in enumerate(zip(sources[2:], held[2:]))
    ]
    for copy in small:
        copy.start()
    for here, _ in through:
        here.start()
    for copy in small:
        copy.wait()
    rows, down_in, small_in = held[2:]
    for index, ref in enumerate((query, key, value, out)):
        ref[...] = rows[:, index * WIDTH : (index + 1) * WIDTH]
    up[...] = rows[:, HIDDEN:]
    down[...] = down_in[...]
    proj[...] = small_in[0:24, :]
    for index, ref in enumerate(vectors):
        ref[...] = small_in[24 + index : 25 + index, 0:24].reshape(24)
    up_bias[...] = small_in[32:33, 0:96].reshape(96)
    for index in range(losses.shape[0]):
        own_losses[index] = losses[index]
    for here, there in through:
        here.wait()
        there.start()
    for _, there in through:
        there.wait()


def run_pass(*arrays):
    vmem = pl.BlockSpec(memory_space=pltpu.VMEM)
    smem = pl.BlockSpec(memory_space=pltpu.SMEM)
    anywhere = pl.BlockSpec(memory_space=pl.ANY)

    def array(*shape):
        return jax.ShapeDtypeStruct(shape, jnp.float32)

    whole = [array(*a.shape) for a in arrays]
    return pl.pallas_call(
        pass_kernel,
        out_shape=whole[:2]
        + [array(24, WIDTH)] * 4
        + [array(24, HIDDEN), array(96, WIDTH), array(24, EMBED)]
        + [array(24)] * 8
        + [array(96), whole[-1]],
        in_specs=[anywhere] * 5 + [smem],
        out_specs=[anywhere] * 2 + [vmem] * 16 + [smem],
        scratch_shapes=[pltpu.VMEM(a.shape, a.dtype) for a in arrays[:5]]
        + [pltpu.SemaphoreType.DMA((11,)), pltpu.SemaphoreType.DMA((8,))],
        compiler_params=pltpu.CompilerParams(vmem_limit_bytes=62 * 2**20),
        name="hand_over",
    )(*arrays)


def body_tiles(
    tokens,
    w_query,
    b_query,
    w_key,
    w_value,
    b_value,
    w_out,
    b_out,
    gain_one,
    shift_one,
    w_up,
    b_up,
    w_down,
    b_down,
    gain_two,
    shift_two,
    w_proj,
    segment_ids,
    row_lengths,
    teacher_index,
    teacher_table,
):
    rows_dev, _, width = tokens.shape
    losses, embeddings, *kept = run_first(
        tokens.reshape(rows_dev * SEQ, width),
        (w_query, w_key, w_value, w_out, w_up, w_down, w_proj),
        (b_query, b_value, b_out, gain_one, shift_one, b_down, gain_two, shift_two, b_up),
        segment_ids,
        row_lengths,
        teacher_index,
        teacher_table,
    )
    grad_tokens, *small = run_last(kept, segment_ids, row_lengths)
    (
        grad_tokens,
        embeddings,
        grad_query,
        grad_key,
        grad_value,
        grad_out,
        grad_up,
        grad_down,
        grad_proj,
        grad_query_bias,
        grad_value_bias,
        grad_out_bias,
        grad_gain_first,
        grad_shift_first,
        grad_down_bias,
        grad_gain_second,
        grad_shift_second,
        grad_up_bias,
        losses,
    ) = run_pass(grad_tokens, embeddings.reshape(rows_dev * SEQ, EMBED), *small, losses)
    return (
        losses,
        embeddings.reshape(rows_dev, SEQ, EMBED),
        grad_tokens.reshape(rows_dev, SEQ, width),
        grad_query,
        grad_query_bias,
        grad_key,
        grad_value,
        grad_value_bias,
        grad_out,
        grad_out_bias,
        grad_gain_first,
        grad_shift_first,
        grad_up,
        grad_up_bias,
        grad_down,
        grad_down_bias,
        grad_gain_second,
        grad_shift_second,
        grad_proj,
    )


def solution(mesh):
    in_specs = (
        P(("dp", "fsdp"), None, None),
        P(("dp", "fsdp"), None),
        P(("dp", "fsdp")),
        P(("dp", "fsdp"), None),
        P(("dp", "fsdp"), None),
        P(("dp", "fsdp")),
        P(("dp", "fsdp"), None),
        P(("dp", "fsdp")),
        P(("dp", "fsdp")),
        P(("dp", "fsdp")),
        P(("dp", "fsdp"), None),
        P(("dp", "fsdp")),
        P(("dp", "fsdp"), None),
        P(("dp", "fsdp")),
        P(("dp", "fsdp")),
        P(("dp", "fsdp")),
        P(("dp", "fsdp"), None),
        P(("dp", "fsdp"), None),
        P(("dp", "fsdp")),
        P(("dp", "fsdp"), None),
        P(),
    )
    out_specs = (
        P(("dp", "fsdp")),
        P(("dp", "fsdp"), None, None),
        P(("dp", "fsdp"), None, None),
        P(("dp", "fsdp"), None),
        P(("dp", "fsdp")),
        P(("dp", "fsdp"), None),
        P(("dp", "fsdp"), None),
        P(("dp", "fsdp")),
        P(("dp", "fsdp"), None),
        P(("dp", "fsdp")),
        P(("dp", "fsdp")),
        P(("dp", "fsdp")),
        P(("dp", "fsdp"), None),
        P(("dp", "fsdp")),
        P(("dp", "fsdp"), None),
        P(("dp", "fsdp")),
        P(("dp", "fsdp")),
        P(("dp", "fsdp")),
        P(("dp", "fsdp"), None),
    )
    body = body_tiles if fits(mesh) else body_whole
    return jax.shard_map(body, mesh=mesh, in_specs=in_specs, out_specs=out_specs, check_vma=False)
```

```python
import functools
import math

import jax
import jax.numpy as jnp
from jax import lax
from jax.experimental import pallas as pl
from jax.experimental.pallas import tpu as pltpu
from jax.sharding import PartitionSpec as P

HEADS = 12
HEAD = 64
SEQ = 512
QLEN = 32
NPASS = 8
TABLE = 1024


NORM_EPS = 1e-12
UNIT_EPS = 1e-12
SOFTNESS = 0.1
MASK_FILL = -1000000000.0
ROOT_HALF = 0.7071067811865476
DENSITY_SCALE = 0.3989422804014327


def matmul(left, right):
    return jnp.dot(left, right, preferred_element_type=jnp.float32)


def over_rows(left, right):
    return lax.dot_general(
        left, right, (((0,), (0,)), ((), ())), preferred_element_type=jnp.float32
    )


def against(left, right):
    return lax.dot_general(
        left, right, (((1,), (1,)), ((), ())), preferred_element_type=jnp.float32
    )


def normalise(mixed, gain, shift):
    centred = mixed - jnp.mean(mixed, -1, keepdims=True)
    scaled = lax.rsqrt(jnp.mean(centred * centred, -1, keepdims=True) + NORM_EPS)
    normed = centred * scaled
    return (normed * gain + shift, normed, scaled)


def normalise_back(grad_out, normed, scaled, gain):
    inner = grad_out * gain
    grad_in = scaled * (
        inner
        - jnp.mean(inner, -1, keepdims=True)
        - normed * jnp.mean(inner * normed, -1, keepdims=True)
    )
    return (grad_in, jnp.sum(grad_out * normed, 0), jnp.sum(grad_out, 0))


def gelu_exact(upward):
    return 0.5 * upward * (1.0 + lax.erf(upward * ROOT_HALF))


def gelu_slope(upward):
    return (
        0.5 * (1.0 + lax.erf(upward * ROOT_HALF))
        + upward * jnp.exp(-0.5 * upward * upward) * DENSITY_SCALE
    )


def split_heads(matrix, rows_dev):
    return (
        matrix.reshape(rows_dev, SEQ, HEADS, HEAD)
        .transpose(0, 2, 1, 3)
        .reshape(rows_dev * HEADS, SEQ, HEAD)
    )


def join_heads(stacked, rows_dev):
    return (
        stacked.reshape(rows_dev, HEADS, SEQ, HEAD)
        .transpose(0, 2, 1, 3)
        .reshape(rows_dev * SEQ, HEADS * HEAD)
    )


def collect(sent):
    return (
        lax.all_gather(sent[0], ("dp", "fsdp"), axis=0, tiled=True),
        lax.all_gather(sent[1], ("dp", "fsdp"), axis=0, tiled=True),
        lax.all_gather(sent[2], ("dp", "fsdp"), axis=0, tiled=True),
        lax.all_gather(sent[3], ("dp", "fsdp"), axis=0, tiled=True),
        lax.all_gather(sent[4], ("dp", "fsdp"), axis=0, tiled=True),
        lax.all_gather(sent[5], ("dp", "fsdp"), axis=0, tiled=True),
        lax.all_gather(sent[6], ("dp", "fsdp"), axis=0, tiled=True),
        lax.all_gather(sent[7], ("dp", "fsdp"), axis=0, tiled=True),
        lax.all_gather(sent[8], ("dp", "fsdp"), axis=0, tiled=True),
        lax.all_gather(sent[9], ("dp", "fsdp"), axis=0, tiled=True),
        lax.all_gather(sent[10], ("dp", "fsdp"), axis=0, tiled=True),
        lax.all_gather(sent[11], ("dp", "fsdp"), axis=0, tiled=True),
        lax.all_gather(sent[12], ("dp", "fsdp"), axis=0, tiled=True),
        lax.all_gather(sent[13], ("dp", "fsdp"), axis=0, tiled=True),
        lax.all_gather(sent[14], ("dp", "fsdp"), axis=0, tiled=True),
        lax.all_gather(sent[15], ("dp", "fsdp"), axis=0, tiled=True),
    )


def spread_grads(terms):
    return (
        lax.psum_scatter(terms[0], ("dp", "fsdp"), scatter_dimension=0, tiled=True),
        lax.psum_scatter(terms[1], ("dp", "fsdp"), scatter_dimension=0, tiled=True),
        lax.psum_scatter(terms[2], ("dp", "fsdp"), scatter_dimension=0, tiled=True),
        lax.psum_scatter(terms[3], ("dp", "fsdp"), scatter_dimension=0, tiled=True),
        lax.psum_scatter(terms[4], ("dp", "fsdp"), scatter_dimension=0, tiled=True),
        lax.psum_scatter(terms[5], ("dp", "fsdp"), scatter_dimension=0, tiled=True),
        lax.psum_scatter(terms[6], ("dp", "fsdp"), scatter_dimension=0, tiled=True),
        lax.psum_scatter(terms[7], ("dp", "fsdp"), scatter_dimension=0, tiled=True),
        lax.psum_scatter(terms[8], ("dp", "fsdp"), scatter_dimension=0, tiled=True),
        lax.psum_scatter(terms[9], ("dp", "fsdp"), scatter_dimension=0, tiled=True),
        lax.psum_scatter(terms[10], ("dp", "fsdp"), scatter_dimension=0, tiled=True),
        lax.psum_scatter(terms[11], ("dp", "fsdp"), scatter_dimension=0, tiled=True),
        lax.psum_scatter(terms[12], ("dp", "fsdp"), scatter_dimension=0, tiled=True),
        lax.psum_scatter(terms[13], ("dp", "fsdp"), scatter_dimension=0, tiled=True),
        lax.psum_scatter(terms[14], ("dp", "fsdp"), scatter_dimension=0, tiled=True),
        lax.psum_scatter(terms[15], ("dp", "fsdp"), scatter_dimension=0, tiled=True),
    )


def body_whole(
    tokens,
    w_query,
    b_query,
    w_key,
    w_value,
    b_value,
    w_out,
    b_out,
    gain_one,
    shift_one,
    w_up,
    b_up,
    w_down,
    b_down,
    gain_two,
    shift_two,
    w_proj,
    segment_ids,
    row_lengths,
    teacher_index,
    teacher_table,
):
    rows_dev = tokens.shape[0]
    width = tokens.shape[2]
    scale = 1.0 / math.sqrt(HEAD)
    shards = (
        w_query,
        b_query,
        w_key,
        w_value,
        b_value,
        w_out,
        b_out,
        gain_one,
        shift_one,
        w_up,
        b_up,
        w_down,
        b_down,
        gain_two,
        shift_two,
        w_proj,
    )
    sent = tuple((member.astype(jnp.bfloat16) for member in shards))
    gathered = collect(sent)
    (
        query_mat,
        query_bias,
        key_mat,
        value_mat,
        value_bias,
        out_mat,
        out_bias,
        gain_first,
        shift_first,
        up_mat,
        up_bias,
        down_mat,
        down_bias,
        gain_second,
        shift_second,
        proj_mat,
    ) = gathered

    def visibility(item_index):
        row_index = item_index // HEADS
        segment_row = lax.dynamic_index_in_dim(segment_ids, row_index, 0, keepdims=False)
        length_row = lax.dynamic_index_in_dim(row_lengths, row_index, 0, keepdims=False)
        positions = jnp.arange(SEQ, dtype=jnp.int32)
        return (segment_row[:, None] == segment_row[None, :]) & (positions[None, :] < length_row)

    def attend(inputs):
        query_h, key_h, value_h, item_index = inputs
        scores = jnp.where(visibility(item_index), against(query_h, key_h) * scale, MASK_FILL)
        peak = jnp.max(scores, -1, keepdims=True)
        shifted = jnp.exp(scores - peak)
        totals = jnp.sum(shifted, -1, keepdims=True)
        chances = (shifted / totals).astype(jnp.bfloat16)
        context_h = matmul(chances, value_h).astype(jnp.bfloat16)
        return (context_h, (peak + jnp.log(totals))[:, 0])

    def attend_back(inputs):
        query_h, key_h, value_h, grad_h, logsum, item_index = inputs
        scores = jnp.where(visibility(item_index), against(query_h, key_h) * scale, MASK_FILL)
        chances = jnp.exp(scores - logsum[:, None])
        d_chances = against(grad_h, value_h)
        rowdot = jnp.sum(chances * d_chances, -1, keepdims=True)
        d_scores = (chances * (d_chances - rowdot)).astype(jnp.bfloat16)
        d_query_h = (matmul(d_scores, key_h) * scale).astype(jnp.bfloat16)
        d_key_h = (over_rows(d_scores, query_h) * scale).astype(jnp.bfloat16)
        d_value_h = over_rows(chances.astype(jnp.bfloat16), grad_h).astype(jnp.bfloat16)
        return (d_query_h, d_key_h, d_value_h)

    flat = tokens.reshape(rows_dev * SEQ, width)
    queries = (matmul(flat, query_mat) + query_bias.astype(jnp.float32)).astype(jnp.bfloat16)
    keys_all = matmul(flat, key_mat).astype(jnp.bfloat16)
    values = (matmul(flat, value_mat) + value_bias.astype(jnp.float32)).astype(jnp.bfloat16)
    query_heads = split_heads(queries, rows_dev)
    key_heads = split_heads(keys_all, rows_dev)
    value_heads = split_heads(values, rows_dev)
    items = jnp.arange(rows_dev * HEADS, dtype=jnp.int32)
    context_heads, logsums = lax.map(attend, (query_heads, key_heads, value_heads, items))
    context_low = join_heads(context_heads, rows_dev)
    branch_one = matmul(context_low, out_mat) + out_bias.astype(jnp.float32)
    mid_one = flat.astype(jnp.float32) + branch_one
    hidden_one, normed_one, scaled_one = normalise(
        mid_one, gain_first.astype(jnp.float32), shift_first.astype(jnp.float32)
    )
    hidden_one_low = hidden_one.astype(jnp.bfloat16)
    upward = matmul(hidden_one_low, up_mat) + up_bias.astype(jnp.float32)
    activated = gelu_exact(upward).astype(jnp.bfloat16)
    branch_two = matmul(activated, down_mat) + down_bias.astype(jnp.float32)
    hidden_two, normed_two, scaled_two = normalise(
        hidden_one + branch_two, gain_second.astype(jnp.float32), shift_second.astype(jnp.float32)
    )
    hidden_two_low = hidden_two.astype(jnp.bfloat16)
    raw_embed = matmul(hidden_two_low, proj_mat)
    inverse = lax.rsqrt(jnp.sum(raw_embed * raw_embed, -1, keepdims=True) + UNIT_EPS)
    embeddings = raw_embed * inverse
    embed_dim = embeddings.shape[1]
    embed_low = embeddings.astype(jnp.bfloat16).reshape(rows_dev, SEQ, embed_dim)
    query_low = embed_low[:, :QLEN]
    similar = jnp.einsum("rqc,rsc->rqs", query_low, embed_low, preferred_element_type=jnp.float32)
    positions = jnp.arange(SEQ, dtype=jnp.int32)
    live = positions[None, :] < row_lengths[:, None]
    passages = jnp.arange(1, NPASS + 1, dtype=jnp.int32)
    member = (segment_ids[:, None, :] == passages[None, :, None]) & live[:, None, :]
    masked = jnp.where(member[:, None], similar[:, :, None, :] / SOFTNESS, MASK_FILL)
    peak = jnp.max(masked, -1, keepdims=True)
    shifted = jnp.exp(masked - peak)
    totals = jnp.sum(shifted, -1, keepdims=True)
    student = SOFTNESS * jnp.sum(peak[..., 0] + jnp.log(totals[..., 0]), axis=1)
    choose = teacher_index[..., None] == jnp.arange(TABLE, dtype=jnp.int32)
    teacher = jnp.sum(jnp.where(choose, teacher_table, 0.0), -1)
    teacher_logp = jax.nn.log_softmax(teacher, axis=-1)
    student_logp = jax.nn.log_softmax(student, axis=-1)
    losses = jnp.sum(jnp.exp(teacher_logp) * (teacher_logp - student_logp), -1)
    again = collect(sent)
    (
        query_back,
        query_bias_back,
        key_back,
        value_back,
        value_bias_back,
        out_back,
        out_bias_back,
        gain_first_back,
        shift_first_back,
        up_back,
        up_bias_back,
        down_back,
        down_bias_back,
        gain_second_back,
        shift_second_back,
        proj_back,
    ) = again
    d_student = jnp.exp(student_logp) - jnp.exp(teacher_logp)
    spread_weights = shifted / totals
    d_similar = jnp.einsum("rp,rqps->rqs", d_student, spread_weights).astype(jnp.bfloat16)
    d_embed = jnp.einsum("rqs,rqc->rsc", d_similar, query_low, preferred_element_type=jnp.float32)
    d_query_part = jnp.einsum(
        "rqs,rsc->rqc", d_similar, embed_low, preferred_element_type=jnp.float32
    )
    d_embed = jnp.concatenate([d_embed[:, :QLEN] + d_query_part, d_embed[:, QLEN:]], 1).reshape(
        rows_dev * SEQ, embed_dim
    )
    d_raw = (
        inverse * (d_embed - embeddings * jnp.sum(d_embed * embeddings, -1, keepdims=True))
    ).astype(jnp.bfloat16)
    grad_proj = over_rows(hidden_two_low, d_raw)
    d_hidden_two = against(d_raw, proj_back)
    d_mid_two, grad_gain_second, grad_shift_second = normalise_back(
        d_hidden_two, normed_two, scaled_two, gain_second_back.astype(jnp.float32)
    )
    d_branch_two = d_mid_two.astype(jnp.bfloat16)
    grad_down = over_rows(activated, d_branch_two)
    grad_down_bias = jnp.sum(d_branch_two, 0, dtype=jnp.float32)
    d_upward = (against(d_branch_two, down_back) * gelu_slope(upward)).astype(jnp.bfloat16)
    grad_up = over_rows(hidden_one_low, d_upward)
    grad_up_bias = jnp.sum(d_upward, 0, dtype=jnp.float32)
    d_hidden_one = d_mid_two + against(d_upward, up_back)
    d_mid_one, grad_gain_first, grad_shift_first = normalise_back(
        d_hidden_one, normed_one, scaled_one, gain_first_back.astype(jnp.float32)
    )
    d_branch_one = d_mid_one.astype(jnp.bfloat16)
    grad_out = over_rows(context_low, d_branch_one)
    grad_out_bias = jnp.sum(d_branch_one, 0, dtype=jnp.float32)
    d_context = against(d_branch_one, out_back).astype(jnp.bfloat16)
    d_context_heads = split_heads(d_context, rows_dev)
    d_query_heads, d_key_heads, d_value_heads = lax.map(
        attend_back, (query_heads, key_heads, value_heads, d_context_heads, logsums, items)
    )
    d_queries = join_heads(d_query_heads, rows_dev)
    d_keys = join_heads(d_key_heads, rows_dev)
    d_values = join_heads(d_value_heads, rows_dev)
    grad_query = over_rows(flat, d_queries)
    grad_query_bias = jnp.sum(d_queries, 0, dtype=jnp.float32)
    grad_key = over_rows(flat, d_keys)
    grad_value = over_rows(flat, d_values)
    grad_value_bias = jnp.sum(d_values, 0, dtype=jnp.float32)
    grad_input = (
        d_mid_one
        + against(d_queries, query_back)
        + against(d_keys, key_back)
        + against(d_values, value_back)
    )
    terms = (
        grad_query,
        grad_query_bias,
        grad_key,
        grad_value,
        grad_value_bias,
        grad_out,
        grad_out_bias,
        grad_gain_first,
        grad_shift_first,
        grad_up,
        grad_up_bias,
        grad_down,
        grad_down_bias,
        grad_gain_second,
        grad_shift_second,
        grad_proj,
    )
    owned = spread_grads(terms)
    return (
        losses,
        embeddings.reshape(rows_dev, SEQ, embed_dim),
        grad_input.reshape(rows_dev, SEQ, width),
        owned[0],
        owned[1],
        owned[2],
        owned[3],
        owned[4],
        owned[5],
        owned[6],
        owned[7],
        owned[8],
        owned[9],
        owned[10],
        owned[11],
        owned[12],
        owned[13],
        owned[14],
        owned[15],
    )


MESH = pl.DeviceIdType.MESH
LOG2_E = 1.4426950408889634
EXP2_SCALE = LOG2_E / math.sqrt(HEAD)
SHARDS = 32
CHIPS = 16
WIDTH = 768
HIDDEN = 3072
EMBED = 128
SMALL = 40
PAIRS = HEADS // 2
CHUNK = 256
HALF = 512


def fits(mesh):
    return dict(mesh.shape) == {"dp": 4, "fsdp": 8}


def dotted(left, right, left_dim, right_dim):
    return lax.dot_general(
        left,
        right,
        (((left_dim,), (right_dim,)), ((), ())),
        preferred_element_type=jnp.float32,
    )


def part_of(start, size):
    return pl.ds(pl.multiple_of(start * size, size), size)


def value_of(number):
    return number() if callable(number) else number


def place():
    outer = lax.axis_index("dp")
    inner = lax.axis_index("fsdp")
    return lax.rem(outer, 2), lax.div(outer, 2), lax.div(inner, 2), lax.rem(inner, 2)


def device(x, y, z, c):
    return (y * 2 + x, z * 2 + c)


class Links:
    def __init__(self):
        x, y, z, c = place()
        self.c = c
        self.z = z
        self.chip_own = (y * 2 + x) * 4
        self.chip_x = (y * 2 + 1 - x) * 4
        self.chip_y = ((1 - y) * 2 + x) * 4
        self.chip_d = ((1 - y) * 2 + 1 - x) * 4
        self.to_core = device(x, y, z, 1 - c)
        self.to_x = device(1 - x, y, z, c)
        self.to_y = device(x, 1 - y, z, c)
        self.to_z = [None] + [device(x, y, lax.rem(z + k, 4), c) for k in (1, 2, 3)]
        self.inner = (z == 1) | (z == 2)
        paired = z + 1 - 2 * lax.rem(z, 2)
        self.to_pair = device(x, y, paired, c)
        self.to_middle = device(x, y, jnp.where(self.inner, 3 - z, paired), c)
        far = jnp.where(z < 2, 1, -1)
        near = jnp.where(self.inner, 3 - z, z + 2 * far)
        last = jnp.where(self.inner, 3 - z + far, z + 3 * far)
        self.levels = [z, paired, near, last]
        self.started = []

    def greet(self):
        barrier = pltpu.get_barrier_semaphore()
        partners = [self.to_core, self.to_x, self.to_y] + self.to_z[1:]
        for partner in partners:
            pl.semaphore_signal(barrier, inc=1, device_id=partner, device_id_type=MESH)
        pl.semaphore_wait(barrier, len(partners))

    def level(self, k):
        return lax.rem(self.z + k, 4)

    def send(self, ends, sems, target, inner=False):
        def copy():
            src, dst = ends()
            send_sem, recv_sem = sems()
            return pltpu.make_async_remote_copy(
                src_ref=src,
                dst_ref=dst,
                send_sem=send_sem,
                recv_sem=recv_sem,
                device_id=target,
                device_id_type=MESH,
            )

        def start():
            copy().start()

        def wait():
            copy().wait_send()

        if inner:
            pl.when(self.inner)(start)
            self.started.append(lambda: pl.when(self.inner)(wait))
        else:
            start()
            self.started.append(wait)

    def arrived(self, ref, sems, source):
        pltpu.make_async_remote_copy(
            src_ref=ref,
            dst_ref=ref,
            send_sem=sems[0],
            recv_sem=sems[1],
            device_id=source,
            device_id_type=MESH,
        ).wait_recv()

    def finish(self, first=0):
        for wait in self.started[first:]:
            wait()
        self.started = self.started[:first]


def rows_block(ref, rows, columns, base=0):
    def block(core, chip, count):
        return ref.at[
            pl.ds(pl.multiple_of(chip * rows, rows), count * rows),
            pl.ds(pl.multiple_of(base + core * columns, 128), columns),
        ]

    return block


def lead_block(ref):
    def block(core, chip, count):
        return ref.at[core, pl.ds(chip, count)]

    return block


def column_of(chip):
    return lax.div(chip, 4)


def level_of(chip):
    return lax.rem(chip, 4)


def grid_block(ref, columns, base=0):
    def block(core, chip, count):
        lanes = pl.ds(pl.multiple_of(base + core * columns, 128), columns)
        if count == 4:
            return ref.at[column_of(chip), :, :, lanes]
        if count == 0:
            return ref.at[:, level_of(chip), :, lanes]
        return ref.at[column_of(chip), level_of(chip), :, lanes]

    return block


def lead_grid_block(ref):
    def block(core, chip, count):
        if count == 0:
            return ref.at[core, :, level_of(chip)]
        return ref.at[core, column_of(chip), level_of(chip)]

    return block


class Gather:
    Z, X, Y, FX, FY, C, ZF = 0, 3, 7, 11, 13, 15, 19
    SEMS = 21

    def __init__(self, links, block, sends, recvs, group):
        self.links = links
        self.block = block
        self.sends = sends
        self.recvs = recvs
        self.group = group

    def sems(self, index, there=None):
        there = index if there is None else there
        return self.sends.at[self.group, index], self.recvs.at[self.group, there]

    def ship(self, chip, count, index, target, there=None, inner=False):
        def ends():
            ref = self.block(self.links.c, value_of(chip), count)
            return ref, ref

        self.links.send(ends, lambda: self.sems(index, there), target, inner)

    def step_of(self, column, k):
        return lambda: column + self.links.levels[k]

    def take(self, chip, count, index, source, core=None):
        core = self.links.c if core is None else core
        self.links.arrived(self.block(core, value_of(chip), count), self.sems(index), source)

    def along(self):
        n = self.links
        own = self.step_of(n.chip_own, 0)
        self.ship(own, 1, self.Z, n.to_pair)
        self.ship(own, 1, self.Z + 1, n.to_middle, inner=True)

    def across(self, k):
        n = self.links
        chip = self.step_of(n.chip_own, k)
        if k:
            self.take(chip, 1, self.Z + k - 1, n.to_pair if k == 1 else n.to_middle)
            if k == 1:
                self.ship(chip, 1, self.Z + 2, n.to_middle, inner=True)
            else:
                self.ship(chip, 1, self.ZF + k - 2, n.to_pair, self.Z + k - 1, inner=True)
        self.ship(chip, 1, self.X + k, n.to_x)
        self.ship(chip, 1, self.Y + k, n.to_y)
        if k == 3:
            self.ship(n.chip_own, 4, self.C, n.to_core)

    def onward(self, k):
        n = self.links
        if k < 2:
            chip = self.step_of(n.chip_x, k)
            self.take(chip, 1, self.X + k, n.to_x)
            self.ship(chip, 1, self.FY + k, n.to_y)
        else:
            chip = self.step_of(n.chip_y, k)
            self.take(chip, 1, self.Y + k, n.to_y)
            self.ship(chip, 1, self.FX + k - 2, n.to_x)

    def beside(self):
        n = self.links
        for k in (2, 3):
            self.take(self.step_of(n.chip_x, k), 1, self.X + k, n.to_x)
        self.ship(n.chip_x, 4, self.C + 1, n.to_core)
        for k in (0, 1):
            self.take(self.step_of(n.chip_y, k), 1, self.Y + k, n.to_y)
        self.ship(n.chip_y, 4, self.C + 2, n.to_core)

    def opposite(self):
        n = self.links
        for k in (0, 1):
            self.take(self.step_of(n.chip_d, k), 1, self.FY + k, n.to_y)
        for k in (2, 3):
            self.take(self.step_of(n.chip_d, k), 1, self.FX + k - 2, n.to_x)
        self.ship(n.chip_d, 4, self.C + 3, n.to_core)

    def last(self):
        n = self.links
        for index, chip in enumerate((n.chip_own, n.chip_x, n.chip_y, n.chip_d)):
            self.take(chip, 4, self.C + index, n.to_core, 1 - n.c)


class LevelGather(Gather):
    X, Y, F, Z, ZF, C = 0, 1, 2, 3, 6, 8

    def own(self):
        n = self.links
        chip = self.step_of(n.chip_own, 0)
        self.ship(chip, 1, self.X, n.to_x)
        self.ship(chip, 1, self.Y, n.to_y)

    def diag(self):
        n = self.links
        chip = self.step_of(n.chip_x, 0)
        self.take(chip, 1, self.X, n.to_x)
        self.ship(chip, 1, self.F, n.to_y)

    def set(self, k):
        n = self.links
        level = self.step_of(n.chip_own, k)
        if k == 0:
            self.take(self.step_of(n.chip_y, 0), 1, self.Y, n.to_y)
            self.take(self.step_of(n.chip_d, 0), 1, self.F, n.to_y)
            self.ship(level, 0, self.Z, n.to_pair)
            self.ship(level, 0, self.Z + 1, n.to_middle, inner=True)
        else:
            self.take(level, 0, self.Z + k - 1, n.to_pair if k == 1 else n.to_middle)
            if k == 1:
                self.ship(level, 0, self.Z + 2, n.to_middle, inner=True)
            else:
                self.ship(level, 0, self.ZF + k - 2, n.to_pair, self.Z + k - 1, inner=True)
        self.ship(level, 0, self.C + k, n.to_core)

    def last(self):
        n = self.links
        for k in range(4):
            self.take(self.step_of(n.chip_own, k), 0, self.C + k, n.to_core, 1 - n.c)


class Joined:
    def join_from(self, stage, sends, recvs, index):
        self.parts = (stage, sends, recvs, index)
        return self

    def join(self):
        if self.parts is None:
            return
        n = self.links
        stage, sends, recvs, index = self.parts
        self.parts = None
        rows = stage.shape[0] // 2
        here = stage.at[part_of(1 - n.c, rows), :]
        n.arrived(here, (sends.at[index], recvs.at[index]), n.to_core)
        self.block(n.c, n.chip_own + n.z, 1)[...] = stage[...].astype(jnp.bfloat16)


class JoinedGather(Joined, Gather):
    def along(self):
        self.join()
        super().along()

    def across(self, k):
        self.join()
        super().across(k)


class JoinedLevelGather(Joined, LevelGather):
    def own(self):
        self.join()
        super().own()


class Scatter:
    C, DY, DX, OX, OY, Z, F = 0, 4, 5, 6, 8, 10, 13
    SEMS = 14

    def __init__(self, links, block, mine, rows, held, fin, deliver, sends, recvs, group, whole=False):
        self.links = links
        self.block = block
        self.mine = mine
        self.rows = rows
        self.part, self.d_y, self.d_x, self.o_x, self.o_y, self.z_in = held
        self.fin = fin
        self.deliver = deliver
        self.sends = sends
        self.recvs = recvs
        self.group = group
        n = links
        self.sent = []
        self.once = whole
        self.columns = (n.chip_d, n.chip_x, n.chip_y, n.chip_own)

    def at(self, ref, start, count):
        if isinstance(start, int):
            return ref.at[pl.ds(start * self.rows, count * self.rows)]
        return ref.at[pl.ds(pl.multiple_of(start * self.rows, self.rows), count * self.rows)]

    def sems(self, index, there=None):
        there = index if there is None else there
        return self.sends.at[self.group, index], self.recvs.at[self.group, there]

    def ship(self, ends, index, target, there=None):
        self.links.send(ends, lambda: self.sems(index, there), target)

    def ship_part(self, start, count, ref, there, index, target):
        self.ship(
            lambda: (self.at(self.part, value_of(start), count), self.at(ref, there, count)),
            index,
            target,
        )

    def take(self, ref, start, count, index, source):
        self.links.arrived(self.at(ref, start, count), self.sems(index), source)

    def add(self, count, start, *others):
        def step(i, carry):
            here = self.at(self.part, start + i, 1)
            total = here[...].astype(jnp.float32)
            for other in others:
                total = total + other(i)[...].astype(jnp.float32)
            here[...] = total.astype(self.part.dtype)
            return carry

        lax.fori_loop(0, count, step, 0)

    def first(self):
        n = self.links
        if self.once:
            self.ship(lambda: (self.block(1 - n.c, 0, 16), self.at(self.part, 0, 16)), self.C, n.to_core)
            return
        for index, chip in enumerate(self.columns):

            def ends(chip=chip):
                return self.block(1 - n.c, chip, 4), self.at(self.part, chip, 4)

            self.ship(ends, self.C + index, n.to_core)
            self.sent.append(n.started[-1])

    def second(self, index):
        n = self.links
        if self.once:
            self.take(self.part, 0, 16, self.C, n.to_core)
            self.add(16, 0, self.mine)
            for index in range(3):
                self.pass_on(index)
            return
        chip = self.columns[index]
        self.take(self.part, chip, 4, self.C + index, n.to_core)
        self.add(4, chip, lambda i: self.mine(chip + i))
        self.pass_on(index)

    def pass_on(self, index):
        n = self.links
        chip = self.columns[index]
        if index == 0:
            self.ship_part(chip, 2, self.d_y, 0, self.DY, n.to_y)
            self.ship_part(lambda: chip + 2, 2, self.d_x, 0, self.DX, n.to_x)
        elif index == 1:
            self.ship_part(lambda: chip + 2, 2, self.o_x, 2, self.OX + 1, n.to_x)
        elif index == 2:
            self.ship_part(chip, 2, self.o_y, 0, self.OY, n.to_y)

    def third(self, index):
        n = self.links
        if index == 0:
            self.take(self.d_y, 0, 2, self.DY, n.to_y)
            self.add(2, n.chip_x, lambda i: self.at(self.d_y, i, 1))
            self.ship_part(n.chip_x, 2, self.o_x, 0, self.OX, n.to_x)
            return
        self.take(self.d_x, 0, 2, self.DX, n.to_x)
        self.add(2, n.chip_y + 2, lambda i: self.at(self.d_x, i, 1))
        self.ship_part(lambda: n.chip_y + 2, 2, self.o_y, 2, self.OY + 1, n.to_y)

    def fourth(self):
        n = self.links
        self.take(self.o_x, 2, 2, self.OX + 1, n.to_x)
        self.take(self.o_y, 0, 2, self.OY, n.to_y)
        self.take(self.o_x, 0, 2, self.OX, n.to_x)
        self.take(self.o_y, 2, 2, self.OY + 1, n.to_y)
        self.add(
            4,
            n.chip_own,
            lambda i: self.at(self.o_x, i, 1),
            lambda i: self.at(self.o_y, i, 1),
        )
        for j in (1, 2, 3):

            def ends(j=j):
                return (
                    self.at(self.part, n.chip_own + n.level(j), 1),
                    self.at(self.z_in, 3 - j, 1),
                )

            self.ship(ends, self.Z + j - 1, n.to_z[j], self.Z + 3 - j)

    def fifth(self):
        n = self.links
        total = self.at(self.part, n.chip_own + n.z, 1)[...].astype(jnp.float32)
        for k in (1, 2, 3):
            self.take(self.z_in, k - 1, 1, self.Z + k - 1, n.to_z[k])
            total = total + self.at(self.z_in, k - 1, 1)[...].astype(jnp.float32)
        return total

    def trade(self):
        if self.fin is None:
            self.deliver(self.fifth())
            return
        fin, fin_in = self.fin
        n = self.links
        rows = self.rows // 2
        fin[...] = self.fifth()
        self.ship(lambda: (fin.at[part_of(1 - n.c, rows)], fin_in), self.F, n.to_core)

    def whole(self):
        if self.fin is None:
            return
        fin, fin_in = self.fin
        n = self.links
        rows = self.rows // 2
        n.arrived(fin_in, self.sems(self.F), n.to_core)
        mine = fin[part_of(n.c, rows), :]
        theirs = fin_in[...]
        self.deliver(jnp.where(n.c == 0, mine, theirs), jnp.where(n.c == 0, theirs, mine))

    def settle(self):
        for wait in self.sent:
            wait()
            self.links.started.remove(wait)
        self.sent = []


def spread_lanes(parts, step):
    lane = lax.broadcasted_iota(jnp.int32, (8, 128), 1)
    tiles = [None] * (len(parts) * step // 128)

    def add(index, value):
        tiles[index] = value if tiles[index] is None else tiles[index] + value

    for i, part in enumerate(parts):
        part = jnp.where(lane < step, part, 0.0)
        index, shift = i * step // 128, i * step % 128
        rolled = pltpu.roll(part, shift, 1) if shift else part
        if shift + step <= 128:
            add(index, rolled)
        else:
            add(index, jnp.where(lane >= shift, rolled, 0.0))
            add(index + 1, jnp.where(lane < shift, rolled, 0.0))
    return tiles


def pick_lanes(tiles, step, count):
    parts = []
    lane = lax.broadcasted_iota(jnp.int32, (8, 128), 1)
    for i in range(count):
        index, shift = i * step // 128, i * step % 128
        part = pltpu.roll(tiles[index], 128 - shift, 1) if shift else tiles[index]
        if shift + step > 128:
            after = pltpu.roll(tiles[index + 1], 128 - shift, 1)
            part = jnp.where(lane < 128 - shift, part, after)
        parts.append(jnp.where(lane < step, part, 0.0))
    return parts


def rounded(value):
    return value.astype(jnp.bfloat16).astype(jnp.float32)


def segment_forms(segment_ids, row_lengths, r):
    segment = segment_ids[r : r + 1, :].astype(jnp.float32)
    position = lax.broadcasted_iota(jnp.int32, (1, SEQ), 1)
    return segment, jnp.where(position < row_lengths[r], segment, -1.0)


def upright(row):
    return jnp.broadcast_to(row, (128, SEQ)).T[:, 0:1]


def mask_of(rows_form, columns_form):
    return jnp.where(upright(rows_form) == columns_form, 0.0, MASK_FILL)


FIRST_PLAN = (
    "o.own",
    "t.own",
    "a.along",
    "u.along",
    "a.across0",
    "t.diag",
    "u.across0",
    "a.across1",
    "a.across2",
    "t.set0",
    "a.across3",
    "bias",
    "d.along",
    "a.onward0",
    "a.onward1",
    "a.onward2",
    "t.set1",
    "o.diag",
    "a.onward3",
    "a.beside",
    "t.set2",
    "u.across1",
    "u.across2",
    "turn",
    "t.set3",
    "a.opposite",
    "t.last",
    "vec",
    "a.last",
    "project",
    "u.across3",
    "o.set0",
    "p0",
    "p1",
    "p2",
    "d.across1",
    "p3",
    "attend",
    "u.onward0",
    "a0",
    "a1",
    "a2",
    "u.onward2",
    "a3",
    "d.across2",
    "u.onward1",
    "u.onward3",
    "a4",
    "o.set1",
    "a5",
    "a6",
    "o.set2",
    "a7",
    "a8",
    "a9",
    "o.set3",
    "u.beside",
    "d.across0",
    "a10",
    "a11",
    "o.last",
    "mix",
    "d.across3",
    "d.onward2",
    "m0",
    "u.opposite",
    "m1",
    "m2",
    "m3",
    "d.onward0",
    "d.onward1",
    "u.last",
    "widen",
    "w0",
    "w1",
    "w2",
    "d.onward3",
    "w3",
    "w4",
    "d.beside",
    "w5",
    "w6",
    "w7",
    "w8",
    "d.opposite",
    "w9",
    "w10",
    "w11",
    "d.last",
    "narrow",
)

LAST_PLAN = (
    "pre",
    "d.first",
    "d.second0",
    "ld",
    "w0",
    "d.second1",
    "w1",
    "w2",
    "d.second2",
    "w3",
    "wu0",
    "wu1",
    "d.third0",
    "wu2",
    "bc",
    "u.first",
    "d.third1",
    "n0",
    "n1",
    "u.second0",
    "u.second1",
    "misc",
    "d.second3",
    "g0",
    "d.fourth",
    "u.second2",
    "rd",
    "u.second3",
    "wo0",
    "a0",
    "a1",
    "o.first",
    "u.third0",
    "a2",
    "u.third1",
    "a3",
    "a4",
    "a5",
    "a6",
    "o.second0",
    "a7",
    "u.fourth",
    "wm0",
    "wm1",
    "wm2",
    "o.third0",
    "o.third1",
    "m.first",
    "a8",
    "m.second0",
    "a9",
    "m.second1",
    "m.second2",
    "a10",
    "a11",
    "m.third1",
    "m.third0",
    "m.second3",
    "wr0",
    "wr1",
    "wr2",
    "r.first",
    "o.fourth",
    "vec",
    "r.second0",
    "t.first",
    "u.trade",
    "m.fourth",
    "b0",
    "r.third1",
    "r.third0",
    "t.second0",
    "b1",
    "r.fourth",
    "t.third0",
    "d.trade",
    "t.third1",
    "t.fourth",
    "u.whole",
    "o.trade",
    "r.trade",
    "d.whole",
    "m.trade",
    "t.trade",
    "m.whole",
    "r.whole",
    "o.whole",
    "t.whole",
    "end",
)


class Plan:
    def __init__(self, names, groups):
        self.groups = groups
        self.inside = {}
        self.queue = list(names)

    def call(self, name):
        group, method = name.split(".")
        if method[-1].isdigit():
            getattr(self.groups[group], method[:-1])(int(method[-1]))
        else:
            getattr(self.groups[group], method)()

    def until(self, name):
        while True:
            step = self.queue.pop(0)
            if step == name:
                return
            self.call(step)

    def loop(self, letter, first, count, body):
        steps = {}
        self.until(f"{letter}{first}")
        for index in range(first, first + count):
            steps[index] = []
            ahead = f"{letter}{index + 1}"
            while self.queue[0] != ahead and "." in self.queue[0]:
                steps[index].append(self.queue.pop(0))
            if index + 1 < first + count:
                self.queue.pop(0)

        def run(step, carry):
            body(step)
            for index, names in steps.items():
                if names:

                    @pl.when(step == index)
                    def _(names=names):
                        for name in names:
                            self.call(name)

            return carry

        lax.fori_loop(first, first + count, run, 0)


def lanes_in_head(shape):
    return lax.broadcasted_iota(jnp.int32, shape, 1) & (HEAD - 1)


def low_head(shape):
    return lax.broadcasted_iota(jnp.int32, shape, 1) < HEAD


def two_parts(value):
    first = rounded(value)
    return first, value - first


def three_parts(value):
    first, rest = two_parts(value)
    second, third = two_parts(rest)
    return first, second, third


PARTS = 16


def query_codes(segment):
    lane = lanes_in_head((SEQ, 128)).astype(jnp.float32)
    return jnp.where(lane == upright(segment), 1.0, 0.0).astype(jnp.bfloat16)


def key_codes(live):
    lane = lanes_in_head((SEQ, 128))
    hidden = jnp.where(lane.astype(jnp.float32) == upright(live), 0.0, MASK_FILL)
    parts = jnp.where((lane >= PARTS) & (lane < PARTS + 3), 1.0, 0.0)
    return jnp.where(lane <= NPASS, hidden, parts).astype(jnp.bfloat16)


def attend_pair(r, p, qkv, context, codes, bias, segments):
    rows = part_of(r, SEQ)
    columns = pl.multiple_of(p * 128, 128)
    query = qkv[rows, pl.ds(columns, 128)]
    key = qkv[rows, pl.ds(columns + WIDTH, 128)]
    value = qkv[rows, pl.ds(columns + 2 * WIDTH, 128)]
    low = low_head((SEQ, 128))
    zero = jnp.zeros_like(key)
    outs, sums = [], []
    for j in range(2):
        key_j = jnp.where(low, key, zero) if j == 0 else jnp.where(low, zero, key)
        scores = dotted(query, key_j, 1, 1) * EXP2_SCALE + bias[rows, 0:SEQ]
        peak = jnp.max(scores, -1, keepdims=True)
        shifted = jnp.exp2(scores - peak)
        total = jnp.sum(shifted, -1, keepdims=True)
        out = dotted(shifted.astype(jnp.bfloat16), value, 1, 0)
        outs.append(out * (1.0 / total))
        sums.append(peak + jnp.log2(total))
    context[rows, pl.ds(columns, 128)] = jnp.where(low, outs[0], outs[1]).astype(jnp.bfloat16)
    first, second, third = three_parts(jnp.where(low, sums[1], sums[0]) * (-1.0 / EXP2_SCALE))
    lane = lanes_in_head((SEQ, 128))
    code = jnp.where(lane == PARTS + 2, third, segments[rows, :].astype(jnp.float32))
    code = jnp.where(lane == PARTS + 1, second, code)
    code = jnp.where(lane == PARTS, first, code)
    codes[rows, pl.ds(columns, 128)] = code.astype(jnp.bfloat16)


def dot_codes(r, p, context, d_context, codes):
    rows = part_of(r, SEQ)
    columns = part_of(p, 128)
    both = context[rows, columns].astype(jnp.float32) * d_context[rows, columns].astype(jnp.float32)
    first, second = two_parts(both)
    shape = (128, 128)
    other = low_head(shape) != (lax.broadcasted_iota(jnp.int32, shape, 0) < HEAD)
    other = jnp.where(other, -1.0, 0.0).astype(jnp.bfloat16)
    total = dotted(first.astype(jnp.bfloat16), other, 1, 0)
    total = total + dotted(second.astype(jnp.bfloat16), other, 1, 0)
    first, second = two_parts(total)
    lane = lanes_in_head((SEQ, 128))
    code = jnp.where(lane == PARTS, first, jnp.where(lane == PARTS + 1, second, 0.0))
    codes[rows, columns] = code.astype(jnp.bfloat16)


def pick_head(masks, j, value, code):
    return value * masks[j] + code * masks[1 - j]


def attend_back_pair(r, p, qkv, d_context, query_code, grad_code, key_code, value_code, lows):
    rows = part_of(r, SEQ)
    columns = pl.multiple_of(p * 128, 128)
    query = qkv[rows, pl.ds(columns, 128)]
    key = qkv[rows, pl.ds(columns + WIDTH, 128)]
    value = qkv[rows, pl.ds(columns + 2 * WIDTH, 128)]
    grad = d_context[rows, pl.ds(columns, 128)]
    query_c = query_code[rows, pl.ds(columns, 128)]
    grad_c = grad_code[rows, pl.ds(columns, 128)]
    key_c = key_code[rows, :]
    value_c = value_code[...]
    masks = (lows[0], lows[1])
    d_query, d_key, d_value = [], [], []
    for j in range(2):
        scores = dotted(pick_head(masks, j, key, key_c), pick_head(masks, j, query, query_c), 1, 1)
        chances = jnp.exp2(scores * EXP2_SCALE)
        d_chances = dotted(
            pick_head(masks, j, value, value_c), pick_head(masks, j, grad, grad_c), 1, 1
        )
        d_scores = (chances * d_chances).astype(jnp.bfloat16)
        d_value.append(dotted(chances.astype(jnp.bfloat16), grad, 1, 0))
        d_key.append(dotted(d_scores, query, 1, 0))
        d_query.append(dotted(d_scores, key, 0, 0))
    low = low_head((SEQ, 128))
    scale = 1.0 / math.sqrt(HEAD)
    low_type = jnp.bfloat16
    qkv[rows, pl.ds(columns, 128)] = (jnp.where(low, d_query[0], d_query[1]) * scale).astype(
        low_type
    )
    qkv[rows, pl.ds(columns + WIDTH, 128)] = (
        jnp.where(low, d_key[0], d_key[1]) * scale
    ).astype(low_type)
    qkv[rows, pl.ds(columns + 2 * WIDTH, 128)] = jnp.where(low, d_value[0], d_value[1]).astype(
        low_type
    )


def norm_parts(mixed):
    centred = mixed - jnp.mean(mixed, -1, keepdims=True)
    scaled = lax.rsqrt(jnp.mean(centred * centred, -1, keepdims=True) + NORM_EPS)
    return centred * scaled, scaled


def norm_back(grad_out, normed, scaled, gain):
    inner = grad_out * gain
    return scaled * (
        inner
        - jnp.mean(inner, -1, keepdims=True)
        - normed * jnp.mean(inner * normed, -1, keepdims=True)
    )


def halves(links, src, stage, sends, recvs, index):
    rows, width = src.shape
    columns = width // 2

    def ends():
        return src.at[:, part_of(1 - links.c, columns)], stage.at[part_of(links.c, rows), :]

    links.send(ends, lambda: (sends.at[index], recvs.at[index]), links.to_core)
    stage[part_of(links.c, rows), :] = src[:, part_of(links.c, columns)]


def passage_loss(r, similar, live_row, teacher_index, teacher_table):
    scores = similar * (1.0 / SOFTNESS)
    inside, shares, student, teacher = [], [], [], []
    for p in range(NPASS):
        member = live_row == float(p + 1)
        masked = jnp.where(member, scores, MASK_FILL)
        peak = jnp.max(masked, -1, keepdims=True)
        shifted = jnp.exp(masked - peak)
        total = jnp.sum(shifted, -1, keepdims=True)
        inside.append(jnp.where(member, shifted, 0.0))
        shares.append(1.0 / total)
        student.append(SOFTNESS * jnp.sum(peak + jnp.log(total), axis=0, keepdims=True))
        teacher.append(jnp.full((1, 1), teacher_table[teacher_index[r, p]], jnp.float32))

    def log_softmax(values):
        peak = functools.reduce(jnp.maximum, values)
        total = sum(jnp.exp(value - peak) for value in values)
        return [value - peak - jnp.log(total) for value in values]

    student = log_softmax(student)
    teacher = log_softmax(teacher)
    loss = sum(jnp.exp(t) * (t - s) for t, s in zip(teacher, student))
    d_similar = sum(
        part * (share * (jnp.exp(s) - jnp.exp(t)))
        for part, share, s, t in zip(inside, shares, student, teacher)
    )
    return loss, d_similar


def first_kernel(*refs):
    (
        tokens,
        w_query,
        w_key,
        w_value,
        w_out,
        w_up,
        w_down,
        w_proj,
        *vector_refs,
        b_up,
        segment_ids,
        row_lengths,
        teacher_index,
        teacher_table,
    ) = refs[:21]
    (
        losses,
        embeddings,
        attn_hbm,
        up_hbm,
        down_hbm,
        turned_hbm,
        qkv_hbm,
        context_hbm,
        low_one_hbm,
        normed_one_hbm,
        slope_hbm,
        d_mid_hbm,
        d_branch_hbm,
        grad_down_hbm,
        codes_hbm,
        scaled_one,
        vectors,
        grad_vectors,
        grad_proj,
    ) = refs[21:40]
    (
        attn_mat,
        up_mat,
        down_mat,
        turned,
        qkv,
        context,
        low_one,
        normed_one,
        slope,
        activated,
        d_mid,
        d_branch,
        grad_down,
        small_all,
        cat_attn,
        stage_attn,
        stage_out,
        stage_up,
        stage_down,
        proj,
        up_bias,
        normed_two,
        scaled_two,
        low_two,
        codes,
        segments,
        sends,
        recvs,
        half_sends,
        half_recvs,
        local_sems,
        grad_sems,
    ) = refs[40:]
    count = tokens.shape[0]
    rows_dev = count // SEQ
    links = Links()

    def gather(kind, block, group, stage):
        return kind(links, block, sends, recvs, group).join_from(
            stage, half_sends, half_recvs, group
        )

    attn = gather(JoinedGather, grid_block(attn_mat, 1152), 0, stage_attn)
    out = gather(JoinedLevelGather, grid_block(attn_mat, 384, 3 * WIDTH), 1, stage_out)
    up = gather(JoinedGather, rows_block(up_mat, 48, 1536), 2, stage_up)
    down = gather(JoinedGather, rows_block(down_mat, 192, 384), 3, stage_down)
    tiny = LevelGather(links, lead_grid_block(small_all), sends, recvs, 4)
    own_chip = links.chip_own + links.z
    kept = []

    def keep(src, dst):
        copy = pltpu.make_async_copy(src, dst, local_sems.at[len(kept)])
        copy.start()
        kept.append(copy)

    for index, ref in enumerate((w_query, w_key, w_value)):
        cat_attn[:, index * WIDTH : (index + 1) * WIDTH] = ref[...]
    own_small = tiny.block(links.c, own_chip, 1)
    own_small[0:24, :] = w_proj[...]
    own_small[24:40, :] = jnp.zeros((16, 128), jnp.float32)
    for index, ref in enumerate(vector_refs):
        own_small[24 + index : 25 + index, 0:24] = ref[...].reshape(1, 24)
    own_small[32:33, 0:96] = b_up[...].reshape(1, 96)

    links.greet()
    halves(links, cat_attn, stage_attn, half_sends, half_recvs, 0)
    halves(links, w_out, stage_out, half_sends, half_recvs, 1)
    halves(links, w_up, stage_up, half_sends, half_recvs, 2)
    halves(links, w_down, stage_down, half_sends, half_recvs, 3)
    plan = Plan(FIRST_PLAN, {"a": attn, "o": out, "u": up, "d": down, "t": tiny})
    plan.until("bias")
    live_rows = []
    for r in range(rows_dev):
        segment, live = segment_forms(segment_ids, row_lengths, r)
        live_rows.append(live)
        d_mid[r * SEQ : (r + 1) * SEQ, 0:SEQ] = mask_of(segment, live)
        segments[r * SEQ : (r + 1) * SEQ, :] = query_codes(segment)
    plan.until("turn")
    turned[...] = tokens[...].T
    keep(turned, turned_hbm)
    plan.until("vec")
    cores = [(i % 2, i // 8, i // 2 % 4) for i in range(SHARDS)]
    for index, tile in enumerate(spread_lanes([small_all[c, n, m, 24:32, :] for c, n, m in cores], 24)):
        vectors[:, index * 128 : (index + 1) * 128] = rounded(tile)
    for index, tile in enumerate(spread_lanes([small_all[c, n, m, 32:40, :] for c, n, m in cores], 96)):
        up_bias[:, index * 128 : (index + 1) * 128] = rounded(tile)
    for r in range(CHIPS):
        both = [small_all[c, r // 4, r % 4, 0:24, :] for c in range(2)]
        both = jnp.concatenate(both, axis=0)
        proj[r * 48 : (r + 1) * 48, :] = both.astype(jnp.bfloat16)
    plan.until("project")

    def project(step):
        rows = part_of(step, CHUNK)
        weights = attn_mat[:, :, :, 0 : 3 * WIDTH].reshape(WIDTH, 3 * WIDTH)
        value = dotted(tokens[rows, :], weights, 1, 0)
        qkv[rows, 0:WIDTH] = (value[:, 0:WIDTH] + vectors[0:1, :]).astype(jnp.bfloat16)
        qkv[rows, WIDTH : 2 * WIDTH] = value[:, WIDTH : 2 * WIDTH].astype(jnp.bfloat16)
        qkv[rows, 2 * WIDTH :] = (value[:, 2 * WIDTH :] + vectors[1:2, :]).astype(jnp.bfloat16)

    plan.loop("p", 0, count // CHUNK, project)
    keep(qkv, qkv_hbm)
    plan.until("attend")

    def attend(item):
        r, p = lax.div(item, PAIRS), lax.rem(item, PAIRS)
        attend_pair(r, p, qkv, context, codes, d_mid, segments)

    plan.loop("a", 0, rows_dev * PAIRS, attend)
    keep(context, context_hbm)
    keep(codes, codes_hbm)
    plan.until("mix")
    keep(attn_mat, attn_hbm)

    def mix(step):
        rows = part_of(step, CHUNK)
        weights = attn_mat[:, :, :, 3 * WIDTH :].reshape(WIDTH, WIDTH)
        mixed = dotted(context[rows, :], weights, 1, 0) + vectors[2:3, :]
        normed, scaled = norm_parts(tokens[rows, :].astype(jnp.float32) + mixed)
        normed_one[rows, :] = normed
        scaled_one[rows, :] = jnp.broadcast_to(scaled, (CHUNK, 128))
        low_one[rows, :] = (normed * vectors[3:4, :] + vectors[4:5, :]).astype(jnp.bfloat16)

    plan.loop("m", 0, count // CHUNK, mix)
    keep(normed_one, normed_one_hbm)
    keep(low_one, low_one_hbm)
    plan.until("widen")
    keep(up_mat, up_hbm)

    def widen(step):
        columns = part_of(step, CHUNK)
        upward = dotted(low_one[...], up_mat[:, columns], 1, 0) + up_bias[0:1, columns]
        chance = 0.5 * (1.0 + lax.erf(upward * ROOT_HALF))
        density = jnp.exp2(upward * upward * (-0.5 * LOG2_E)) * DENSITY_SCALE
        activated[:, columns] = (upward * chance).astype(jnp.bfloat16)
        slope[:, columns] = (chance + upward * density).astype(jnp.bfloat16)

    plan.loop("w", 0, HIDDEN // CHUNK, widen)
    keep(slope, slope_hbm)
    plan.until("narrow")
    keep(down_mat, down_hbm)

    grad_vectors[...] = jnp.zeros_like(grad_vectors)
    grad_proj[...] = jnp.zeros_like(grad_proj)
    for r in range(rows_dev):

        rows = slice(r * SEQ, (r + 1) * SEQ)
        mixed = dotted(activated[rows, :], down_mat[...], 1, 0) + vectors[5:6, :]
        mixed = mixed + (normed_one[rows, :] * vectors[3:4, :] + vectors[4:5, :])
        normed, scaled = norm_parts(mixed)
        normed_two[...] = normed
        scaled_two[...] = jnp.broadcast_to(scaled, (SEQ, 128))
        low_two[...] = (normed * vectors[6:7, :] + vectors[7:8, :]).astype(jnp.bfloat16)
        raw = dotted(low_two[...], proj[...], 1, 0)
        inverse = lax.rsqrt(jnp.sum(raw * raw, -1, keepdims=True) + UNIT_EPS)
        embedded = raw * inverse
        embeddings[r] = embedded
        low_embed = embedded.astype(jnp.bfloat16)
        similar = dotted(low_embed[0:QLEN], low_embed, 1, 1)
        loss, d_similar = passage_loss(r, similar, live_rows[r], teacher_index, teacher_table)
        losses[r] = loss[0, 0]
        d_similar = d_similar.astype(jnp.bfloat16)
        d_embed = dotted(d_similar, low_embed[0:QLEN], 0, 0)
        d_query = dotted(d_similar, low_embed, 1, 0)
        d_embed = jnp.concatenate([d_embed[0:QLEN] + d_query, d_embed[QLEN:]], axis=0)
        along = jnp.sum(d_embed * embedded, -1, keepdims=True)
        d_raw = (inverse * (d_embed - embedded * along)).astype(jnp.bfloat16)
        grad_proj[...] += dotted(low_two[...], d_raw, 0, 0)
        d_hidden = dotted(d_raw, proj[...], 1, 1)
        normed = normed_two[...]
        d_mixed = norm_back(d_hidden, normed, scaled_two[:, 0:1], vectors[6:7, :])
        low_mixed = d_mixed.astype(jnp.bfloat16)
        rows = slice(r * SEQ, (r + 1) * SEQ)
        d_mid[rows, :] = d_mixed
        d_branch[rows, :] = low_mixed
        grad_vectors[5:6, :] += jnp.sum(low_mixed.astype(jnp.float32), 0, keepdims=True)
        grad_vectors[6:7, :] += jnp.sum(d_hidden * normed, 0, keepdims=True)
        grad_vectors[7:8, :] += jnp.sum(d_hidden, 0, keepdims=True)
    keep(d_mid, d_mid_hbm)
    keep(d_branch, d_branch_hbm)

    def grad_copy(step, slot):
        return pltpu.make_async_copy(
            grad_down.at[slot], grad_down_hbm.at[part_of(step, WIDTH), :], grad_sems.at[slot]
        )

    def weigh(step, carry):
        slot = lax.rem(step, 2)

        @pl.when(step >= 2)
        def _():
            grad_copy(step - 2, slot).wait()

        part = activated[:, part_of(step, WIDTH)]
        grad_down[slot] = dotted(part, d_branch[...], 0, 0).astype(jnp.bfloat16)
        grad_copy(step, slot).start()
        return carry

    steps = HIDDEN // WIDTH
    lax.fori_loop(0, steps, weigh, 0)
    for step in (steps - 2, steps - 1):
        grad_copy(step, step % 2).wait()
    links.finish()
    for copy in kept:
        copy.wait()


def run_first(tokens, weights, vectors, segment_ids, row_lengths, teacher_index, teacher_table):
    count = tokens.shape[0]
    rows_dev = count // SEQ
    vmem = pl.BlockSpec(memory_space=pltpu.VMEM)
    smem = pl.BlockSpec(memory_space=pltpu.SMEM)
    anywhere = pl.BlockSpec(memory_space=pl.ANY)
    low = jnp.bfloat16
    wide = jnp.float32

    def array(kind, *shape):
        return jax.ShapeDtypeStruct(shape, kind)

    return pl.pallas_call(
        first_kernel,
        out_shape=[
            array(wide, rows_dev),
            array(wide, rows_dev, SEQ, EMBED),
            array(low, 4, 4, 48, HIDDEN),
            array(low, WIDTH, HIDDEN),
            array(low, HIDDEN, WIDTH),
            array(low, WIDTH, count),
            array(low, count, 3 * WIDTH),
            array(low, count, WIDTH),
            array(low, count, WIDTH),
            array(wide, count, WIDTH),
            array(low, count, HIDDEN),
            array(wide, count, WIDTH),
            array(low, count, WIDTH),
            array(low, HIDDEN, WIDTH),
            array(low, count, WIDTH),
            array(wide, count, 128),
            array(wide, 8, WIDTH),
            array(wide, 8, WIDTH),
            array(wide, WIDTH, EMBED),
        ],
        in_specs=[vmem] * 18 + [smem] * 3,
        out_specs=[smem, vmem] + [anywhere] * 13 + [vmem] * 4,
        scratch_shapes=[
            pltpu.VMEM((4, 4, 48, HIDDEN), low),
            pltpu.VMEM((WIDTH, HIDDEN), low),
            pltpu.VMEM((HIDDEN, WIDTH), low),
            pltpu.VMEM((WIDTH, count), low),
            pltpu.VMEM((count, 3 * WIDTH), low),
            pltpu.VMEM((count, WIDTH), low),
            pltpu.VMEM((count, WIDTH), low),
            pltpu.VMEM((count, WIDTH), wide),
            pltpu.VMEM((count, HIDDEN), low),
            pltpu.VMEM((count, HIDDEN), low),
            pltpu.VMEM((count, WIDTH), wide),
            pltpu.VMEM((count, WIDTH), low),
            pltpu.VMEM((2, WIDTH, WIDTH), low),
            pltpu.VMEM((2, 4, 4, SMALL, 128), wide),
            pltpu.VMEM((24, 3 * WIDTH), wide),
            pltpu.VMEM((48, 3 * WIDTH // 2), wide),
            pltpu.VMEM((48, WIDTH // 2), wide),
            pltpu.VMEM((48, HIDDEN // 2), wide),
            pltpu.VMEM((192, WIDTH // 2), wide),
            pltpu.VMEM((WIDTH, EMBED), low),
            pltpu.VMEM((8, HIDDEN), wide),
            pltpu.VMEM((SEQ, WIDTH), wide),
            pltpu.VMEM((SEQ, 128), wide),
            pltpu.VMEM((SEQ, WIDTH), low),
            pltpu.VMEM((count, WIDTH), low),
            pltpu.VMEM((count, 128), low),
            pltpu.SemaphoreType.DMA((5, Gather.SEMS)),
            pltpu.SemaphoreType.DMA((5, Gather.SEMS)),
            pltpu.SemaphoreType.DMA((4,)),
            pltpu.SemaphoreType.DMA((4,)),
            pltpu.SemaphoreType.DMA((13,)),
            pltpu.SemaphoreType.DMA((2,)),
        ],
        compiler_params=pltpu.CompilerParams(
            collective_id=0, has_side_effects=True, vmem_limit_bytes=62 * 2**20
        ),
        name="forward_gather",
    )(tokens, *weights, *vectors, segment_ids, row_lengths, teacher_index, teacher_table)


def last_kernel(*refs):
    (
        attn_hbm,
        up_hbm,
        down_hbm,
        turned_hbm,
        qkv_hbm,
        context_hbm,
        low_one_hbm,
        normed_one_hbm,
        slope_hbm,
        d_mid_hbm,
        d_branch_hbm,
        grad_down_hbm,
        codes_hbm,
        scaled_one,
        vectors,
        part_vectors,
        grad_proj,
        segment_ids,
        row_lengths,
    ) = refs[:19]
    (
        grad_tokens_hbm,
        own_rows,
        own_down,
        own_small,
    ) = refs[19:23]
    (
        attn_mat,
        grads,
        wide,
        low_one,
        d_branch,
        d_mid,
        part_down,
        small_all,
        grad_vectors,
        grad_up_bias,
        sends,
        recvs,
        local_sems,
        slope_sems,
        qkv_sems,
        grad_sems,
        key_code,
        value_code,
        lows,
        *rest,
    ) = refs[23:]
    held = [rest[6 * i : 6 * i + 6] for i in range(6)]
    fins = [rest[36 + 2 * i : 38 + 2 * i] for i in range(5)]
    count = d_mid.shape[0]
    rows_dev = count // SEQ
    links = Links()
    c = links.c

    def scatter(block, rows, group, deliver, mine=None):
        def own(chip):
            return block(c, chip, 1)

        own = own if mine is None else mine
        fin = fins[group] if group < 5 else None
        return Scatter(
            links, block, own, rows, held[group], fin, deliver, sends, recvs, group, group in (2, 4, 5)
        )

    def down_mine(chip):
        return part_down.at[part_of(chip, 192), :]

    def halves_to(ref, start, columns):
        def deliver(low, high):
            ref[:, start : start + columns] = low
            ref[:, start + columns : start + 2 * columns] = high

        return deliver

    def most_out(low, high):
        own_rows[:, 0:512] = low[:, 0:512]
        own_rows[:, 768:1024] = low[:, 512:768]
        own_rows[:, 1024:1280] = high[:, 0:256]
        own_rows[:, 1536:2048] = high[:, 256:768]

    def rest_out(low, high):
        own_rows[:, 512:768] = low[:, 0:256]
        own_rows[:, 1280:1408] = low[:, 256:384]
        own_rows[:, 1408:1536] = high[:, 0:128]
        own_rows[:, 2048:2304] = high[:, 128:384]

    def tiny_out(total):
        own_small[...] = total[0]

    down = scatter(rows_block(grad_down_hbm, 192, 384), 192, 0, halves_to(own_down, 0, WIDTH // 2), down_mine)
    up = scatter(rows_block(grads, 48, 1536), 48, 1, halves_to(own_rows, HIDDEN, HIDDEN // 2))
    out = scatter(rows_block(grads, 48, 384), 48, 2, halves_to(own_rows, 3 * WIDTH, WIDTH // 2))
    most = scatter(rows_block(grads, 48, 768, WIDTH), 48, 3, most_out)
    rest_of = scatter(rows_block(grads, 48, 384, 3 * WIDTH), 48, 4, rest_out)
    tiny = scatter(lead_block(small_all), 1, 5, tiny_out)

    def load(src, dst, index):
        return pltpu.make_async_copy(src, dst, local_sems.at[index])

    def start(copies):
        for copy in copies:
            copy.start()

    def wait(copies):
        for copy in copies:
            copy.wait()

    plan = Plan(
        LAST_PLAN, {"d": down, "u": up, "o": out, "m": most, "r": rest_of, "t": tiny}
    )
    plan.until("pre")
    first_loads = [
        load(d_branch_hbm, d_branch, 0),
        load(grad_down_hbm.at[:, part_of(c, WIDTH // 2)], part_down, 1),
    ]
    attn_load = load(attn_hbm, attn_mat, 3)
    start(first_loads)
    links.greet()
    wait(first_loads[1:])
    grad_vectors[...] = part_vectors[...]
    ones = jnp.ones((8, count), jnp.bfloat16)

    def slope_load(step):
        columns = part_of(step, WIDTH)
        return pltpu.make_async_copy(
            slope_hbm.at[:, columns], wide.at[:, columns], slope_sems.at[step]
        )

    def qkv_load(step):
        rows = part_of(step, HALF)
        return pltpu.make_async_copy(
            qkv_hbm.at[rows, :], wide.at[rows, 0 : 3 * WIDTH], qkv_sems.at[step]
        )

    def grad_store(step):
        rows = part_of(step, HALF)
        return pltpu.make_async_copy(
            d_mid.at[rows, :], grad_tokens_hbm.at[rows, :], grad_sems.at[step]
        )

    steps = count // HALF
    quarters = HIDDEN // WIDTH

    def weights(start, columns):
        return attn_mat[:, :, :, start : start + columns].reshape(WIDTH, columns)

    def feed_forward(up_mat, down_mat, normed_one):
        ahead = [load(down_hbm, down_mat, 5)]
        start(ahead)
        for step in range(quarters):
            slope_load(step).start()
        middle = [
            load(low_one_hbm, low_one, 6),
            load(up_hbm, up_mat, 7),
            load(d_mid_hbm, d_mid, 8),
            load(normed_one_hbm, normed_one, 9),
        ]
        plan.until("ld")
        wait(first_loads[:1] + ahead)

        def widen(step):
            columns = part_of(step, WIDTH)
            slope_load(step).wait()
            grad = dotted(d_branch[...], down_mat[columns, :], 1, 1)
            wide[:, columns] = (grad * wide[:, columns].astype(jnp.float32)).astype(jnp.bfloat16)

            @pl.when(step == 0)
            def _():
                start(middle)

        plan.loop("w", 0, quarters, widen)
        wait(middle[:1])

        def weigh(step):
            rows = part_of(step, CHUNK)
            grads[rows, :] = dotted(low_one[:, rows], wide[...], 0, 0).astype(jnp.bfloat16)

        plan.loop("wu", 0, WIDTH // CHUNK, weigh)
        plan.until("bc")
        attn_load.start()
        for index in range(4):
            columns = slice(index * WIDTH, (index + 1) * WIDTH)
            grad_up_bias[:, columns] = dotted(ones, wide[:, columns], 1, 0)
        wait(middle[1:])

        def narrow(step):
            rows = part_of(step, HALF)
            d_hidden = d_mid[rows, :] + dotted(wide[rows, :], up_mat[...], 1, 1)
            qkv_load(step).start()
            normed = normed_one[rows, :]
            d_mixed = norm_back(d_hidden, normed, scaled_one[rows, 0:1], vectors[3:4, :])
            d_mid[rows, :] = d_mixed
            d_branch[rows, :] = d_mixed.astype(jnp.bfloat16)
            grad_vectors[3:4, :] += jnp.sum(d_hidden * normed, 0, keepdims=True)
            grad_vectors[4:5, :] += jnp.sum(d_hidden, 0, keepdims=True)

        plan.loop("n", 0, steps, narrow)

    pl.run_scoped(
        feed_forward,
        pltpu.VMEM((WIDTH, HIDDEN), jnp.bfloat16),
        pltpu.VMEM((HIDDEN, WIDTH), jnp.bfloat16),
        pltpu.VMEM((count, WIDTH), jnp.float32),
    )

    def attention(d_context, context, codes, turned):
        loads = [
            load(context_hbm, context, 2),
            load(codes_hbm, codes, 4),
            load(turned_hbm, turned, 10),
        ]
        start(loads)
        plan.until("misc")
        grad_vectors[2:3, :] = dotted(ones, d_branch[...], 1, 0)[0:1]
        for r in range(rows_dev):
            _, live = segment_forms(segment_ids, row_lengths, r)
            key_code[r * SEQ : (r + 1) * SEQ, :] = key_codes(live)
        low = low_head((SEQ, 128))
        lows[0] = jnp.where(low, 1.0, 0.0).astype(jnp.bfloat16)
        lows[1] = jnp.where(low, 0.0, 1.0).astype(jnp.bfloat16)
        lane = lanes_in_head((SEQ, 128))
        parts = (lane == PARTS) | (lane == PARTS + 1)
        value_code[...] = jnp.where(parts, 1.0, 0.0).astype(jnp.bfloat16)
        attn_load.wait()

        plan.until("g0")
        d_context[...] = dotted(d_branch[...], weights(3 * WIDTH, WIDTH), 1, 1).astype(jnp.bfloat16)
        plan.until("rd")

        wait(loads[:1])

        def gather_dots(item, carry):
            dot_codes(lax.rem(item, rows_dev), lax.div(item, rows_dev), context, d_context, low_one)
            return carry

        lax.fori_loop(0, rows_dev * PAIRS, gather_dots, 0)
        up.settle()

        plan.until("wo0")
        grads[:, 0:WIDTH] = dotted(context[...], d_branch[...], 0, 0).astype(jnp.bfloat16)
        for step in range(steps):
            qkv_load(step).wait()

        wait(loads[1:])

        def attend(item):
            r = lax.rem(item, rows_dev)
            p = lax.div(item, rows_dev)
            attend_back_pair(
                r, p, wide, d_context, codes, low_one, key_code, value_code, lows
            )

        def weigh(first, pairs, base):
            def step(index):
                size = pairs * 128
                here = pl.ds(pl.multiple_of(index * WIDTH + first * 128, 128), size)
                there = pl.ds(pl.multiple_of(base + index * size, 128), size)
                grads[:, there] = dotted(turned[...], wide[:, here], 1, 0).astype(jnp.bfloat16)

            return step

        plan.loop("a", 0, 4 * rows_dev, attend)
        plan.loop("wm", 0, 3, weigh(0, 4, WIDTH))
        plan.loop("a", 4 * rows_dev, 2 * rows_dev, attend)
        plan.loop("wr", 0, 3, weigh(4, 2, 3 * WIDTH))

    pl.run_scoped(
        attention,
        pltpu.VMEM((count, WIDTH), jnp.bfloat16),
        pltpu.VMEM((count, WIDTH), jnp.bfloat16),
        pltpu.VMEM((count, WIDTH), jnp.bfloat16),
        pltpu.VMEM((WIDTH, count), jnp.bfloat16),
    )
    plan.until("vec")
    for index in (0, 2):
        total = dotted(ones, wide[:, index * WIDTH : (index + 1) * WIDTH], 1, 0)
        grad_vectors[index // 2 : index // 2 + 1, :] = total[0:1]
    tiles = [grad_vectors[:, i * 128 : (i + 1) * 128] for i in range(WIDTH // 128)]
    for i, part in enumerate(pick_lanes(tiles, 24, SHARDS)):
        small_all[i % 2, i // 2, 24:32, :] = part
    tiles = [grad_up_bias[:, i * 128 : (i + 1) * 128] for i in range(HIDDEN // 128)]
    for i, part in enumerate(pick_lanes(tiles, 96, SHARDS)):
        small_all[i % 2, i // 2, 32:40, :] = part
        small_all[i % 2, i // 2, 0:24, :] = grad_proj[i * 24 : (i + 1) * 24, :]

    def back(step):
        rows = part_of(step, HALF)
        value = dotted(wide[rows, 0 : 3 * WIDTH], weights(0, 3 * WIDTH), 1, 1)
        d_mid[rows, :] += value
        grad_store(step).start()

    plan.loop("b", 0, steps, back)
    plan.until("end")
    for step in range(steps):
        grad_store(step).wait()
    links.finish()


def run_last(kept, segment_ids, row_lengths):
    count = kept[9].shape[0]
    rows_dev = count // SEQ
    vmem = pl.BlockSpec(memory_space=pltpu.VMEM)
    smem = pl.BlockSpec(memory_space=pltpu.SMEM)
    anywhere = pl.BlockSpec(memory_space=pl.ANY)
    low = jnp.bfloat16
    wide = jnp.float32

    def array(*shape):
        return jax.ShapeDtypeStruct(shape, wide)

    def held(unit, kind):
        return [pltpu.VMEM((n * unit[0],) + unit[1:], kind) for n in (16, 2, 2, 4, 4, 3)]

    blocks = ((192, 384), (48, 1536), (48, 384), (48, 768), (48, 384))
    buffers = []
    for block in blocks:
        buffers += held(block, low)
    buffers += held((1, SMALL, 128), wide)
    for rows, columns in blocks:
        buffers += [pltpu.VMEM((rows, columns), wide), pltpu.VMEM((rows // 2, columns), wide)]
    return pl.pallas_call(
        last_kernel,
        out_shape=[
            array(count, WIDTH),
            array(24, 2 * HIDDEN),
            array(96, WIDTH),
            array(SMALL, 128),
        ],
        in_specs=[anywhere] * 13 + [vmem] * 5 + [smem],
        out_specs=[anywhere] + [vmem] * 3,
        scratch_shapes=[
            pltpu.VMEM((4, 4, 48, HIDDEN), low),
            pltpu.VMEM((WIDTH, HIDDEN), low),
            pltpu.VMEM((count, HIDDEN), low),
            pltpu.VMEM((count, WIDTH), low),
            pltpu.VMEM((count, WIDTH), low),
            pltpu.VMEM((count, WIDTH), wide),
            pltpu.VMEM((HIDDEN, WIDTH // 2), low),
            pltpu.VMEM((2, CHIPS, SMALL, 128), wide),
            pltpu.VMEM((8, WIDTH), wide),
            pltpu.VMEM((8, HIDDEN), wide),
            pltpu.SemaphoreType.DMA((6, Scatter.SEMS)),
            pltpu.SemaphoreType.DMA((6, Scatter.SEMS)),
            pltpu.SemaphoreType.DMA((11,)),
            pltpu.SemaphoreType.DMA((HIDDEN // WIDTH,)),
            pltpu.SemaphoreType.DMA((count // HALF,)),
            pltpu.SemaphoreType.DMA((count // HALF,)),
            pltpu.VMEM((count, 128), low),
            pltpu.VMEM((SEQ, 128), low),
            pltpu.VMEM((2, SEQ, 128), low),
        ]
        + buffers,
        compiler_params=pltpu.CompilerParams(
            collective_id=1, has_side_effects=True, vmem_limit_bytes=63 * 2**20
        ),
        name="backward_scatter",
    )(*kept, segment_ids, row_lengths)


def pass_kernel(*refs):
    sources, losses = refs[:5], refs[5]
    grad_tokens, embeddings, query, key, value, out, up, down, proj, *vectors = refs[6:23]
    up_bias, own_losses = refs[23:25]
    held, (in_sems, out_sems) = refs[25:30], refs[30:]
    pieces = 4
    through = []
    for src, mid, dst in zip(sources[:2], held[:2], (grad_tokens, embeddings)):
        rows = src.shape[0] // pieces
        for piece in range(pieces):
            part = pl.ds(piece * rows, rows)
            index = len(through)
            through.append(
                (
                    pltpu.make_async_copy(src.at[part], mid.at[part], in_sems.at[index]),
                    pltpu.make_async_copy(mid.at[part], dst.at[part], out_sems.at[index]),
                )
            )
    small = [
        pltpu.make_async_copy(src, mid, in_sems.at[2 * pieces + index])
        for index, (src, mid) in enumerate(zip(sources[2:], held[2:]))
    ]
    for copy in small:
        copy.start()
    for here, _ in through:
        here.start()
    for copy in small:
        copy.wait()
    rows, down_in, small_in = held[2:]
    for index, ref in enumerate((query, key, value, out)):
        ref[...] = rows[:, index * WIDTH : (index + 1) * WIDTH]
    up[...] = rows[:, HIDDEN:]
    down[...] = down_in[...]
    proj[...] = small_in[0:24, :]
    for index, ref in enumerate(vectors):
        ref[...] = small_in[24 + index : 25 + index, 0:24].reshape(24)
    up_bias[...] = small_in[32:33, 0:96].reshape(96)
    for index in range(losses.shape[0]):
        own_losses[index] = losses[index]
    for here, there in through:
        here.wait()
        there.start()
    for _, there in through:
        there.wait()


def run_pass(*arrays):
    vmem = pl.BlockSpec(memory_space=pltpu.VMEM)
    smem = pl.BlockSpec(memory_space=pltpu.SMEM)
    anywhere = pl.BlockSpec(memory_space=pl.ANY)

    def array(*shape):
        return jax.ShapeDtypeStruct(shape, jnp.float32)

    whole = [array(*a.shape) for a in arrays]
    return pl.pallas_call(
        pass_kernel,
        out_shape=whole[:2]
        + [array(24, WIDTH)] * 4
        + [array(24, HIDDEN), array(96, WIDTH), array(24, EMBED)]
        + [array(24)] * 8
        + [array(96), whole[-1]],
        in_specs=[anywhere] * 5 + [smem],
        out_specs=[anywhere] * 2 + [vmem] * 16 + [smem],
        scratch_shapes=[pltpu.VMEM(a.shape, a.dtype) for a in arrays[:5]]
        + [pltpu.SemaphoreType.DMA((11,)), pltpu.SemaphoreType.DMA((8,))],
        compiler_params=pltpu.CompilerParams(vmem_limit_bytes=62 * 2**20),
        name="hand_over",
    )(*arrays)


def body_tiles(
    tokens,
    w_query,
    b_query,
    w_key,
    w_value,
    b_value,
    w_out,
    b_out,
    gain_one,
    shift_one,
    w_up,
    b_up,
    w_down,
    b_down,
    gain_two,
    shift_two,
    w_proj,
    segment_ids,
    row_lengths,
    teacher_index,
    teacher_table,
):
    rows_dev, _, width = tokens.shape
    losses, embeddings, *kept = run_first(
        tokens.reshape(rows_dev * SEQ, width),
        (w_query, w_key, w_value, w_out, w_up, w_down, w_proj),
        (b_query, b_value, b_out, gain_one, shift_one, b_down, gain_two, shift_two, b_up),
        segment_ids,
        row_lengths,
        teacher_index,
        teacher_table,
    )
    grad_tokens, *small = run_last(kept, segment_ids, row_lengths)
    (
        grad_tokens,
        embeddings,
        grad_query,
        grad_key,
        grad_value,
        grad_out,
        grad_up,
        grad_down,
        grad_proj,
        grad_query_bias,
        grad_value_bias,
        grad_out_bias,
        grad_gain_first,
        grad_shift_first,
        grad_down_bias,
        grad_gain_second,
        grad_shift_second,
        grad_up_bias,
        losses,
    ) = run_pass(grad_tokens, embeddings.reshape(rows_dev * SEQ, EMBED), *small, losses)
    return (
        losses,
        embeddings.reshape(rows_dev, SEQ, EMBED),
        grad_tokens.reshape(rows_dev, SEQ, width),
        grad_query,
        grad_query_bias,
        grad_key,
        grad_value,
        grad_value_bias,
        grad_out,
        grad_out_bias,
        grad_gain_first,
        grad_shift_first,
        grad_up,
        grad_up_bias,
        grad_down,
        grad_down_bias,
        grad_gain_second,
        grad_shift_second,
        grad_proj,
    )


def solution(mesh):
    in_specs = (
        P(("dp", "fsdp"), None, None),
        P(("dp", "fsdp"), None),
        P(("dp", "fsdp")),
        P(("dp", "fsdp"), None),
        P(("dp", "fsdp"), None),
        P(("dp", "fsdp")),
        P(("dp", "fsdp"), None),
        P(("dp", "fsdp")),
        P(("dp", "fsdp")),
        P(("dp", "fsdp")),
        P(("dp", "fsdp"), None),
        P(("dp", "fsdp")),
        P(("dp", "fsdp"), None),
        P(("dp", "fsdp")),
        P(("dp", "fsdp")),
        P(("dp", "fsdp")),
        P(("dp", "fsdp"), None),
        P(("dp", "fsdp"), None),
        P(("dp", "fsdp")),
        P(("dp", "fsdp"), None),
        P(),
    )
    out_specs = (
        P(("dp", "fsdp")),
        P(("dp", "fsdp"), None, None),
        P(("dp", "fsdp"), None, None),
        P(("dp", "fsdp"), None),
        P(("dp", "fsdp")),
        P(("dp", "fsdp"), None),
        P(("dp", "fsdp"), None),
        P(("dp", "fsdp")),
        P(("dp", "fsdp"), None),
        P(("dp", "fsdp")),
        P(("dp", "fsdp")),
        P(("dp", "fsdp")),
        P(("dp", "fsdp"), None),
        P(("dp", "fsdp")),
        P(("dp", "fsdp"), None),
        P(("dp", "fsdp")),
        P(("dp", "fsdp")),
        P(("dp", "fsdp")),
        P(("dp", "fsdp"), None),
    )
    body = body_tiles if fits(mesh) else body_whole
    return jax.shard_map(body, mesh=mesh, in_specs=in_specs, out_specs=out_specs, check_vma=False)
```

```python
import functools
import math

import jax
import jax.numpy as jnp
from jax import lax
from jax.experimental import pallas as pl
from jax.experimental.pallas import tpu as pltpu
from jax.sharding import PartitionSpec as P

HEADS = 12
HEAD = 64
SEQ = 512
QLEN = 32
NPASS = 8
TABLE = 1024


NORM_EPS = 1e-12
UNIT_EPS = 1e-12
SOFTNESS = 0.1
MASK_FILL = -1000000000.0
ROOT_HALF = 0.7071067811865476
DENSITY_SCALE = 0.3989422804014327


def matmul(left, right):
    return jnp.dot(left, right, preferred_element_type=jnp.float32)


def over_rows(left, right):
    return lax.dot_general(
        left, right, (((0,), (0,)), ((), ())), preferred_element_type=jnp.float32
    )


def against(left, right):
    return lax.dot_general(
        left, right, (((1,), (1,)), ((), ())), preferred_element_type=jnp.float32
    )


def normalise(mixed, gain, shift):
    centred = mixed - jnp.mean(mixed, -1, keepdims=True)
    scaled = lax.rsqrt(jnp.mean(centred * centred, -1, keepdims=True) + NORM_EPS)
    normed = centred * scaled
    return (normed * gain + shift, normed, scaled)


def normalise_back(grad_out, normed, scaled, gain):
    inner = grad_out * gain
    grad_in = scaled * (
        inner
        - jnp.mean(inner, -1, keepdims=True)
        - normed * jnp.mean(inner * normed, -1, keepdims=True)
    )
    return (grad_in, jnp.sum(grad_out * normed, 0), jnp.sum(grad_out, 0))


def gelu_exact(upward):
    return 0.5 * upward * (1.0 + lax.erf(upward * ROOT_HALF))


def gelu_slope(upward):
    return (
        0.5 * (1.0 + lax.erf(upward * ROOT_HALF))
        + upward * jnp.exp(-0.5 * upward * upward) * DENSITY_SCALE
    )


def split_heads(matrix, rows_dev):
    return (
        matrix.reshape(rows_dev, SEQ, HEADS, HEAD)
        .transpose(0, 2, 1, 3)
        .reshape(rows_dev * HEADS, SEQ, HEAD)
    )


def join_heads(stacked, rows_dev):
    return (
        stacked.reshape(rows_dev, HEADS, SEQ, HEAD)
        .transpose(0, 2, 1, 3)
        .reshape(rows_dev * SEQ, HEADS * HEAD)
    )


def collect(sent):
    return (
        lax.all_gather(sent[0], ("dp", "fsdp"), axis=0, tiled=True),
        lax.all_gather(sent[1], ("dp", "fsdp"), axis=0, tiled=True),
        lax.all_gather(sent[2], ("dp", "fsdp"), axis=0, tiled=True),
        lax.all_gather(sent[3], ("dp", "fsdp"), axis=0, tiled=True),
        lax.all_gather(sent[4], ("dp", "fsdp"), axis=0, tiled=True),
        lax.all_gather(sent[5], ("dp", "fsdp"), axis=0, tiled=True),
        lax.all_gather(sent[6], ("dp", "fsdp"), axis=0, tiled=True),
        lax.all_gather(sent[7], ("dp", "fsdp"), axis=0, tiled=True),
        lax.all_gather(sent[8], ("dp", "fsdp"), axis=0, tiled=True),
        lax.all_gather(sent[9], ("dp", "fsdp"), axis=0, tiled=True),
        lax.all_gather(sent[10], ("dp", "fsdp"), axis=0, tiled=True),
        lax.all_gather(sent[11], ("dp", "fsdp"), axis=0, tiled=True),
        lax.all_gather(sent[12], ("dp", "fsdp"), axis=0, tiled=True),
        lax.all_gather(sent[13], ("dp", "fsdp"), axis=0, tiled=True),
        lax.all_gather(sent[14], ("dp", "fsdp"), axis=0, tiled=True),
        lax.all_gather(sent[15], ("dp", "fsdp"), axis=0, tiled=True),
    )


def spread_grads(terms):
    return (
        lax.psum_scatter(terms[0], ("dp", "fsdp"), scatter_dimension=0, tiled=True),
        lax.psum_scatter(terms[1], ("dp", "fsdp"), scatter_dimension=0, tiled=True),
        lax.psum_scatter(terms[2], ("dp", "fsdp"), scatter_dimension=0, tiled=True),
        lax.psum_scatter(terms[3], ("dp", "fsdp"), scatter_dimension=0, tiled=True),
        lax.psum_scatter(terms[4], ("dp", "fsdp"), scatter_dimension=0, tiled=True),
        lax.psum_scatter(terms[5], ("dp", "fsdp"), scatter_dimension=0, tiled=True),
        lax.psum_scatter(terms[6], ("dp", "fsdp"), scatter_dimension=0, tiled=True),
        lax.psum_scatter(terms[7], ("dp", "fsdp"), scatter_dimension=0, tiled=True),
        lax.psum_scatter(terms[8], ("dp", "fsdp"), scatter_dimension=0, tiled=True),
        lax.psum_scatter(terms[9], ("dp", "fsdp"), scatter_dimension=0, tiled=True),
        lax.psum_scatter(terms[10], ("dp", "fsdp"), scatter_dimension=0, tiled=True),
        lax.psum_scatter(terms[11], ("dp", "fsdp"), scatter_dimension=0, tiled=True),
        lax.psum_scatter(terms[12], ("dp", "fsdp"), scatter_dimension=0, tiled=True),
        lax.psum_scatter(terms[13], ("dp", "fsdp"), scatter_dimension=0, tiled=True),
        lax.psum_scatter(terms[14], ("dp", "fsdp"), scatter_dimension=0, tiled=True),
        lax.psum_scatter(terms[15], ("dp", "fsdp"), scatter_dimension=0, tiled=True),
    )


def body_whole(
    tokens,
    w_query,
    b_query,
    w_key,
    w_value,
    b_value,
    w_out,
    b_out,
    gain_one,
    shift_one,
    w_up,
    b_up,
    w_down,
    b_down,
    gain_two,
    shift_two,
    w_proj,
    segment_ids,
    row_lengths,
    teacher_index,
    teacher_table,
):
    rows_dev = tokens.shape[0]
    width = tokens.shape[2]
    scale = 1.0 / math.sqrt(HEAD)
    shards = (
        w_query,
        b_query,
        w_key,
        w_value,
        b_value,
        w_out,
        b_out,
        gain_one,
        shift_one,
        w_up,
        b_up,
        w_down,
        b_down,
        gain_two,
        shift_two,
        w_proj,
    )
    sent = tuple((member.astype(jnp.bfloat16) for member in shards))
    gathered = collect(sent)
    (
        query_mat,
        query_bias,
        key_mat,
        value_mat,
        value_bias,
        out_mat,
        out_bias,
        gain_first,
        shift_first,
        up_mat,
        up_bias,
        down_mat,
        down_bias,
        gain_second,
        shift_second,
        proj_mat,
    ) = gathered

    def visibility(item_index):
        row_index = item_index // HEADS
        segment_row = lax.dynamic_index_in_dim(segment_ids, row_index, 0, keepdims=False)
        length_row = lax.dynamic_index_in_dim(row_lengths, row_index, 0, keepdims=False)
        positions = jnp.arange(SEQ, dtype=jnp.int32)
        return (segment_row[:, None] == segment_row[None, :]) & (positions[None, :] < length_row)

    def attend(inputs):
        query_h, key_h, value_h, item_index = inputs
        scores = jnp.where(visibility(item_index), against(query_h, key_h) * scale, MASK_FILL)
        peak = jnp.max(scores, -1, keepdims=True)
        shifted = jnp.exp(scores - peak)
        totals = jnp.sum(shifted, -1, keepdims=True)
        chances = (shifted / totals).astype(jnp.bfloat16)
        context_h = matmul(chances, value_h).astype(jnp.bfloat16)
        return (context_h, (peak + jnp.log(totals))[:, 0])

    def attend_back(inputs):
        query_h, key_h, value_h, grad_h, logsum, item_index = inputs
        scores = jnp.where(visibility(item_index), against(query_h, key_h) * scale, MASK_FILL)
        chances = jnp.exp(scores - logsum[:, None])
        d_chances = against(grad_h, value_h)
        rowdot = jnp.sum(chances * d_chances, -1, keepdims=True)
        d_scores = (chances * (d_chances - rowdot)).astype(jnp.bfloat16)
        d_query_h = (matmul(d_scores, key_h) * scale).astype(jnp.bfloat16)
        d_key_h = (over_rows(d_scores, query_h) * scale).astype(jnp.bfloat16)
        d_value_h = over_rows(chances.astype(jnp.bfloat16), grad_h).astype(jnp.bfloat16)
        return (d_query_h, d_key_h, d_value_h)

    flat = tokens.reshape(rows_dev * SEQ, width)
    queries = (matmul(flat, query_mat) + query_bias.astype(jnp.float32)).astype(jnp.bfloat16)
    keys_all = matmul(flat, key_mat).astype(jnp.bfloat16)
    values = (matmul(flat, value_mat) + value_bias.astype(jnp.float32)).astype(jnp.bfloat16)
    query_heads = split_heads(queries, rows_dev)
    key_heads = split_heads(keys_all, rows_dev)
    value_heads = split_heads(values, rows_dev)
    items = jnp.arange(rows_dev * HEADS, dtype=jnp.int32)
    context_heads, logsums = lax.map(attend, (query_heads, key_heads, value_heads, items))
    context_low = join_heads(context_heads, rows_dev)
    branch_one = matmul(context_low, out_mat) + out_bias.astype(jnp.float32)
    mid_one = flat.astype(jnp.float32) + branch_one
    hidden_one, normed_one, scaled_one = normalise(
        mid_one, gain_first.astype(jnp.float32), shift_first.astype(jnp.float32)
    )
    hidden_one_low = hidden_one.astype(jnp.bfloat16)
    upward = matmul(hidden_one_low, up_mat) + up_bias.astype(jnp.float32)
    activated = gelu_exact(upward).astype(jnp.bfloat16)
    branch_two = matmul(activated, down_mat) + down_bias.astype(jnp.float32)
    hidden_two, normed_two, scaled_two = normalise(
        hidden_one + branch_two, gain_second.astype(jnp.float32), shift_second.astype(jnp.float32)
    )
    hidden_two_low = hidden_two.astype(jnp.bfloat16)
    raw_embed = matmul(hidden_two_low, proj_mat)
    inverse = lax.rsqrt(jnp.sum(raw_embed * raw_embed, -1, keepdims=True) + UNIT_EPS)
    embeddings = raw_embed * inverse
    embed_dim = embeddings.shape[1]
    embed_low = embeddings.astype(jnp.bfloat16).reshape(rows_dev, SEQ, embed_dim)
    query_low = embed_low[:, :QLEN]
    similar = jnp.einsum("rqc,rsc->rqs", query_low, embed_low, preferred_element_type=jnp.float32)
    positions = jnp.arange(SEQ, dtype=jnp.int32)
    live = positions[None, :] < row_lengths[:, None]
    passages = jnp.arange(1, NPASS + 1, dtype=jnp.int32)
    member = (segment_ids[:, None, :] == passages[None, :, None]) & live[:, None, :]
    masked = jnp.where(member[:, None], similar[:, :, None, :] / SOFTNESS, MASK_FILL)
    peak = jnp.max(masked, -1, keepdims=True)
    shifted = jnp.exp(masked - peak)
    totals = jnp.sum(shifted, -1, keepdims=True)
    student = SOFTNESS * jnp.sum(peak[..., 0] + jnp.log(totals[..., 0]), axis=1)
    choose = teacher_index[..., None] == jnp.arange(TABLE, dtype=jnp.int32)
    teacher = jnp.sum(jnp.where(choose, teacher_table, 0.0), -1)
    teacher_logp = jax.nn.log_softmax(teacher, axis=-1)
    student_logp = jax.nn.log_softmax(student, axis=-1)
    losses = jnp.sum(jnp.exp(teacher_logp) * (teacher_logp - student_logp), -1)
    again = collect(sent)
    (
        query_back,
        query_bias_back,
        key_back,
        value_back,
        value_bias_back,
        out_back,
        out_bias_back,
        gain_first_back,
        shift_first_back,
        up_back,
        up_bias_back,
        down_back,
        down_bias_back,
        gain_second_back,
        shift_second_back,
        proj_back,
    ) = again
    d_student = jnp.exp(student_logp) - jnp.exp(teacher_logp)
    spread_weights = shifted / totals
    d_similar = jnp.einsum("rp,rqps->rqs", d_student, spread_weights).astype(jnp.bfloat16)
    d_embed = jnp.einsum("rqs,rqc->rsc", d_similar, query_low, preferred_element_type=jnp.float32)
    d_query_part = jnp.einsum(
        "rqs,rsc->rqc", d_similar, embed_low, preferred_element_type=jnp.float32
    )
    d_embed = jnp.concatenate([d_embed[:, :QLEN] + d_query_part, d_embed[:, QLEN:]], 1).reshape(
        rows_dev * SEQ, embed_dim
    )
    d_raw = (
        inverse * (d_embed - embeddings * jnp.sum(d_embed * embeddings, -1, keepdims=True))
    ).astype(jnp.bfloat16)
    grad_proj = over_rows(hidden_two_low, d_raw)
    d_hidden_two = against(d_raw, proj_back)
    d_mid_two, grad_gain_second, grad_shift_second = normalise_back(
        d_hidden_two, normed_two, scaled_two, gain_second_back.astype(jnp.float32)
    )
    d_branch_two = d_mid_two.astype(jnp.bfloat16)
    grad_down = over_rows(activated, d_branch_two)
    grad_down_bias = jnp.sum(d_branch_two, 0, dtype=jnp.float32)
    d_upward = (against(d_branch_two, down_back) * gelu_slope(upward)).astype(jnp.bfloat16)
    grad_up = over_rows(hidden_one_low, d_upward)
    grad_up_bias = jnp.sum(d_upward, 0, dtype=jnp.float32)
    d_hidden_one = d_mid_two + against(d_upward, up_back)
    d_mid_one, grad_gain_first, grad_shift_first = normalise_back(
        d_hidden_one, normed_one, scaled_one, gain_first_back.astype(jnp.float32)
    )
    d_branch_one = d_mid_one.astype(jnp.bfloat16)
    grad_out = over_rows(context_low, d_branch_one)
    grad_out_bias = jnp.sum(d_branch_one, 0, dtype=jnp.float32)
    d_context = against(d_branch_one, out_back).astype(jnp.bfloat16)
    d_context_heads = split_heads(d_context, rows_dev)
    d_query_heads, d_key_heads, d_value_heads = lax.map(
        attend_back, (query_heads, key_heads, value_heads, d_context_heads, logsums, items)
    )
    d_queries = join_heads(d_query_heads, rows_dev)
    d_keys = join_heads(d_key_heads, rows_dev)
    d_values = join_heads(d_value_heads, rows_dev)
    grad_query = over_rows(flat, d_queries)
    grad_query_bias = jnp.sum(d_queries, 0, dtype=jnp.float32)
    grad_key = over_rows(flat, d_keys)
    grad_value = over_rows(flat, d_values)
    grad_value_bias = jnp.sum(d_values, 0, dtype=jnp.float32)
    grad_input = (
        d_mid_one
        + against(d_queries, query_back)
        + against(d_keys, key_back)
        + against(d_values, value_back)
    )
    terms = (
        grad_query,
        grad_query_bias,
        grad_key,
        grad_value,
        grad_value_bias,
        grad_out,
        grad_out_bias,
        grad_gain_first,
        grad_shift_first,
        grad_up,
        grad_up_bias,
        grad_down,
        grad_down_bias,
        grad_gain_second,
        grad_shift_second,
        grad_proj,
    )
    owned = spread_grads(terms)
    return (
        losses,
        embeddings.reshape(rows_dev, SEQ, embed_dim),
        grad_input.reshape(rows_dev, SEQ, width),
        owned[0],
        owned[1],
        owned[2],
        owned[3],
        owned[4],
        owned[5],
        owned[6],
        owned[7],
        owned[8],
        owned[9],
        owned[10],
        owned[11],
        owned[12],
        owned[13],
        owned[14],
        owned[15],
    )


MESH = pl.DeviceIdType.MESH
LOG2_E = 1.4426950408889634
EXP2_SCALE = LOG2_E / math.sqrt(HEAD)
SHARDS = 32
CHIPS = 16
WIDTH = 768
HIDDEN = 3072
EMBED = 128
SMALL = 40
PAIRS = HEADS // 2
CHUNK = 256
HALF = 512


def fits(mesh):
    return dict(mesh.shape) == {"dp": 4, "fsdp": 8}


def dotted(left, right, left_dim, right_dim):
    return lax.dot_general(
        left,
        right,
        (((left_dim,), (right_dim,)), ((), ())),
        preferred_element_type=jnp.float32,
    )


def part_of(start, size):
    return pl.ds(pl.multiple_of(start * size, size), size)


def value_of(number):
    return number() if callable(number) else number


def place():
    outer = lax.axis_index("dp")
    inner = lax.axis_index("fsdp")
    return lax.rem(outer, 2), lax.div(outer, 2), lax.div(inner, 2), lax.rem(inner, 2)


def device(x, y, z, c):
    return (y * 2 + x, z * 2 + c)


class Links:
    def __init__(self):
        x, y, z, c = place()
        self.c = c
        self.z = z
        self.chip_own = (y * 2 + x) * 4
        self.chip_x = (y * 2 + 1 - x) * 4
        self.chip_y = ((1 - y) * 2 + x) * 4
        self.chip_d = ((1 - y) * 2 + 1 - x) * 4
        self.to_core = device(x, y, z, 1 - c)
        self.to_x = device(1 - x, y, z, c)
        self.to_y = device(x, 1 - y, z, c)
        self.to_z = [None] + [device(x, y, lax.rem(z + k, 4), c) for k in (1, 2, 3)]
        self.inner = (z == 1) | (z == 2)
        paired = z + 1 - 2 * lax.rem(z, 2)
        self.to_pair = device(x, y, paired, c)
        self.to_middle = device(x, y, jnp.where(self.inner, 3 - z, paired), c)
        far = jnp.where(z < 2, 1, -1)
        near = jnp.where(self.inner, 3 - z, z + 2 * far)
        last = jnp.where(self.inner, 3 - z + far, z + 3 * far)
        self.levels = [z, paired, near, last]
        self.started = []

    def hail(self):
        barrier = pltpu.get_barrier_semaphore()
        self.partners = [self.to_core, self.to_x, self.to_y] + self.to_z[1:]
        for partner in self.partners:
            pl.semaphore_signal(barrier, inc=1, device_id=partner, device_id_type=MESH)

    def greet(self):
        pl.semaphore_wait(pltpu.get_barrier_semaphore(), len(self.partners))

    def level(self, k):
        return lax.rem(self.z + k, 4)

    def send(self, ends, sems, target, inner=False):
        def copy():
            src, dst = ends()
            send_sem, recv_sem = sems()
            return pltpu.make_async_remote_copy(
                src_ref=src,
                dst_ref=dst,
                send_sem=send_sem,
                recv_sem=recv_sem,
                device_id=target,
                device_id_type=MESH,
            )

        def start():
            copy().start()

        def wait():
            copy().wait_send()

        if inner:
            pl.when(self.inner)(start)
            self.started.append(lambda: pl.when(self.inner)(wait))
        else:
            start()
            self.started.append(wait)

    def arrived(self, ref, sems, source):
        pltpu.make_async_remote_copy(
            src_ref=ref,
            dst_ref=ref,
            send_sem=sems[0],
            recv_sem=sems[1],
            device_id=source,
            device_id_type=MESH,
        ).wait_recv()

    def finish(self, first=0):
        for wait in self.started[first:]:
            wait()
        self.started = self.started[:first]


def rows_block(ref, rows, columns, base=0):
    def block(core, chip, count):
        return ref.at[
            pl.ds(pl.multiple_of(chip * rows, rows), count * rows),
            pl.ds(pl.multiple_of(base + core * columns, 128), columns),
        ]

    return block


def lead_block(ref):
    def block(core, chip, count):
        return ref.at[core, pl.ds(chip, count)]

    return block


def column_of(chip):
    return lax.div(chip, 4)


def level_of(chip):
    return lax.rem(chip, 4)


def grid_block(ref, columns, base=0):
    def block(core, chip, count):
        lanes = pl.ds(pl.multiple_of(base + core * columns, 128), columns)
        if count == 4:
            return ref.at[column_of(chip), :, :, lanes]
        if count == 0:
            return ref.at[:, level_of(chip), :, lanes]
        return ref.at[column_of(chip), level_of(chip), :, lanes]

    return block


def lead_grid_block(ref):
    def block(core, chip, count):
        if count == 0:
            return ref.at[core, :, level_of(chip)]
        return ref.at[core, column_of(chip), level_of(chip)]

    return block


class Gather:
    Z, X, Y, FX, FY, C, ZF = 0, 3, 7, 11, 13, 15, 19
    SEMS = 21

    def __init__(self, links, block, sends, recvs, group):
        self.links = links
        self.block = block
        self.sends = sends
        self.recvs = recvs
        self.group = group

    def sems(self, index, there=None):
        there = index if there is None else there
        return self.sends.at[self.group, index], self.recvs.at[self.group, there]

    def ship(self, chip, count, index, target, there=None, inner=False):
        def ends():
            ref = self.block(self.links.c, value_of(chip), count)
            return ref, ref

        self.links.send(ends, lambda: self.sems(index, there), target, inner)

    def step_of(self, column, k):
        return lambda: column + self.links.levels[k]

    def take(self, chip, count, index, source, core=None):
        core = self.links.c if core is None else core
        self.links.arrived(self.block(core, value_of(chip), count), self.sems(index), source)

    def along(self):
        n = self.links
        own = self.step_of(n.chip_own, 0)
        self.ship(own, 1, self.Z, n.to_pair)
        self.ship(own, 1, self.Z + 1, n.to_middle, inner=True)

    def across(self, k):
        n = self.links
        chip = self.step_of(n.chip_own, k)
        if k:
            self.take(chip, 1, self.Z + k - 1, n.to_pair if k == 1 else n.to_middle)
            if k == 1:
                self.ship(chip, 1, self.Z + 2, n.to_middle, inner=True)
            else:
                self.ship(chip, 1, self.ZF + k - 2, n.to_pair, self.Z + k - 1, inner=True)
        self.ship(chip, 1, self.X + k, n.to_x)
        self.ship(chip, 1, self.Y + k, n.to_y)
        if k == 3:
            self.ship(n.chip_own, 4, self.C, n.to_core)

    def onward(self, k):
        n = self.links
        if k < 2:
            chip = self.step_of(n.chip_x, k)
            self.take(chip, 1, self.X + k, n.to_x)
            self.ship(chip, 1, self.FY + k, n.to_y)
        else:
            chip = self.step_of(n.chip_y, k)
            self.take(chip, 1, self.Y + k, n.to_y)
            self.ship(chip, 1, self.FX + k - 2, n.to_x)

    def beside(self):
        n = self.links
        for k in (2, 3):
            self.take(self.step_of(n.chip_x, k), 1, self.X + k, n.to_x)
        self.ship(n.chip_x, 4, self.C + 1, n.to_core)
        for k in (0, 1):
            self.take(self.step_of(n.chip_y, k), 1, self.Y + k, n.to_y)
        self.ship(n.chip_y, 4, self.C + 2, n.to_core)

    def opposite(self):
        n = self.links
        for k in (0, 1):
            self.take(self.step_of(n.chip_d, k), 1, self.FY + k, n.to_y)
        for k in (2, 3):
            self.take(self.step_of(n.chip_d, k), 1, self.FX + k - 2, n.to_x)
        self.ship(n.chip_d, 4, self.C + 3, n.to_core)

    def last(self):
        n = self.links
        for index, chip in enumerate((n.chip_own, n.chip_x, n.chip_y, n.chip_d)):
            self.take(chip, 4, self.C + index, n.to_core, 1 - n.c)


class LevelGather(Gather):
    X, Y, F, Z, ZF, C = 0, 1, 2, 3, 6, 8

    def own(self):
        n = self.links
        chip = self.step_of(n.chip_own, 0)
        self.ship(chip, 1, self.X, n.to_x)
        self.ship(chip, 1, self.Y, n.to_y)

    def diag(self):
        n = self.links
        chip = self.step_of(n.chip_x, 0)
        self.take(chip, 1, self.X, n.to_x)
        self.ship(chip, 1, self.F, n.to_y)

    def set(self, k):
        n = self.links
        level = self.step_of(n.chip_own, k)
        if k == 0:
            self.take(self.step_of(n.chip_y, 0), 1, self.Y, n.to_y)
            self.take(self.step_of(n.chip_d, 0), 1, self.F, n.to_y)
            self.ship(level, 0, self.Z, n.to_pair)
            self.ship(level, 0, self.Z + 1, n.to_middle, inner=True)
        else:
            self.take(level, 0, self.Z + k - 1, n.to_pair if k == 1 else n.to_middle)
            if k == 1:
                self.ship(level, 0, self.Z + 2, n.to_middle, inner=True)
            else:
                self.ship(level, 0, self.ZF + k - 2, n.to_pair, self.Z + k - 1, inner=True)
        self.ship(level, 0, self.C + k, n.to_core)

    def last(self):
        n = self.links
        for k in range(4):
            self.take(self.step_of(n.chip_own, k), 0, self.C + k, n.to_core, 1 - n.c)


class Joined:
    def join_from(self, stage, sends, recvs, index):
        self.parts = (stage, sends, recvs, index)
        return self

    def join(self):
        if self.parts is None:
            return
        n = self.links
        stage, sends, recvs, index = self.parts
        self.parts = None
        rows = stage.shape[0] // 2
        here = stage.at[part_of(1 - n.c, rows), :]
        n.arrived(here, (sends.at[index], recvs.at[index]), n.to_core)
        self.block(n.c, n.chip_own + n.z, 1)[...] = stage[...].astype(jnp.bfloat16)


class JoinedGather(Joined, Gather):
    def along(self):
        self.join()
        super().along()

    def across(self, k):
        self.join()
        super().across(k)


class JoinedLevelGather(Joined, LevelGather):
    def own(self):
        self.join()
        super().own()


class Scatter:
    C, DY, DX, OX, OY, Z, F = 0, 4, 5, 6, 8, 10, 13
    SEMS = 14

    def __init__(self, links, block, mine, rows, held, fin, deliver, sends, recvs, group, whole=False):
        self.links = links
        self.block = block
        self.mine = mine
        self.rows = rows
        self.part, self.d_y, self.d_x, self.o_x, self.o_y, self.z_in = held
        self.fin = fin
        self.deliver = deliver
        self.sends = sends
        self.recvs = recvs
        self.group = group
        n = links
        self.sent = []
        self.once = whole
        self.span = 4 if whole else 2
        self.columns = (n.chip_d, n.chip_x, n.chip_y, n.chip_own)

    def at(self, ref, start, count):
        if isinstance(start, int):
            return ref.at[pl.ds(start * self.rows, count * self.rows)]
        return ref.at[pl.ds(pl.multiple_of(start * self.rows, self.rows), count * self.rows)]

    def sems(self, index, there=None):
        there = index if there is None else there
        return self.sends.at[self.group, index], self.recvs.at[self.group, there]

    def ship(self, ends, index, target, there=None):
        self.links.send(ends, lambda: self.sems(index, there), target)

    def ship_part(self, start, count, ref, there, index, target):
        self.ship(
            lambda: (self.at(self.part, value_of(start), count), self.at(ref, there, count)),
            index,
            target,
        )

    def take(self, ref, start, count, index, source):
        self.links.arrived(self.at(ref, start, count), self.sems(index), source)

    def add(self, count, start, *others):
        size = min(count, self.span)

        def step(i, carry):
            here = self.at(self.part, start + i * size, size)
            total = here[...]
            for other in others:
                total = total + other(i * size, size)[...]
            here[...] = total
            return carry

        lax.fori_loop(0, count // size, step, 0)

    def first(self):
        n = self.links
        if self.once:
            self.ship(lambda: (self.block(1 - n.c, 0, 16), self.at(self.part, 0, 16)), self.C, n.to_core)
            return
        for index, chip in enumerate(self.columns):

            def ends(chip=chip):
                return self.block(1 - n.c, chip, 4), self.at(self.part, chip, 4)

            self.ship(ends, self.C + index, n.to_core)
            self.sent.append(n.started[-1])

    def second(self, index):
        n = self.links
        if self.once:
            self.take(self.part, 0, 16, self.C, n.to_core)
            self.add(16, 0, self.mine)
            for index in range(3):
                self.pass_on(index)
            return
        chip = self.columns[index]
        self.take(self.part, chip, 4, self.C + index, n.to_core)
        self.add(4, chip, lambda i, size: self.mine(chip + i, size))
        self.pass_on(index)

    def pass_on(self, index):
        n = self.links
        chip = self.columns[index]
        if index == 0:
            self.ship_part(chip, 2, self.d_y, 0, self.DY, n.to_y)
            self.ship_part(lambda: chip + 2, 2, self.d_x, 0, self.DX, n.to_x)
        elif index == 1:
            self.ship_part(lambda: chip + 2, 2, self.o_x, 2, self.OX + 1, n.to_x)
        elif index == 2:
            self.ship_part(chip, 2, self.o_y, 0, self.OY, n.to_y)

    def third(self, index):
        n = self.links
        if index == 0:
            self.take(self.d_y, 0, 2, self.DY, n.to_y)
            self.add(2, n.chip_x, lambda i, size: self.at(self.d_y, i, size))
            self.ship_part(n.chip_x, 2, self.o_x, 0, self.OX, n.to_x)
            return
        self.take(self.d_x, 0, 2, self.DX, n.to_x)
        self.add(2, n.chip_y + 2, lambda i, size: self.at(self.d_x, i, size))
        self.ship_part(lambda: n.chip_y + 2, 2, self.o_y, 2, self.OY + 1, n.to_y)

    def fourth(self):
        n = self.links
        self.take(self.o_x, 2, 2, self.OX + 1, n.to_x)
        self.take(self.o_y, 0, 2, self.OY, n.to_y)
        self.take(self.o_x, 0, 2, self.OX, n.to_x)
        self.take(self.o_y, 2, 2, self.OY + 1, n.to_y)
        self.add(
            4,
            n.chip_own,
            lambda i, size: self.at(self.o_x, i, size),
            lambda i, size: self.at(self.o_y, i, size),
        )
        for j in (1, 2, 3):

            def ends(j=j):
                return (
                    self.at(self.part, n.chip_own + n.level(j), 1),
                    self.at(self.z_in, 3 - j, 1),
                )

            self.ship(ends, self.Z + j - 1, n.to_z[j], self.Z + 3 - j)

    def fifth(self):
        n = self.links
        total = self.at(self.part, n.chip_own + n.z, 1)[...].astype(jnp.float32)
        for k in (1, 2, 3):
            self.take(self.z_in, k - 1, 1, self.Z + k - 1, n.to_z[k])
            total = total + self.at(self.z_in, k - 1, 1)[...].astype(jnp.float32)
        return total

    def trade(self):
        if self.fin is None:
            self.deliver(self.fifth())
            return
        fin, fin_in = self.fin
        n = self.links
        rows = self.rows // 2
        fin[...] = self.fifth()
        self.ship(lambda: (fin.at[part_of(1 - n.c, rows)], fin_in), self.F, n.to_core)

    def whole(self):
        if self.fin is None:
            return
        fin, fin_in = self.fin
        n = self.links
        rows = self.rows // 2
        n.arrived(fin_in, self.sems(self.F), n.to_core)
        mine = fin[part_of(n.c, rows), :]
        theirs = fin_in[...]
        self.deliver(jnp.where(n.c == 0, mine, theirs), jnp.where(n.c == 0, theirs, mine))

    def settle(self):
        for wait in self.sent:
            if wait in self.links.started:
                wait()
                self.links.started.remove(wait)
        self.sent = []


def spread_lanes(parts, step):
    lane = lax.broadcasted_iota(jnp.int32, (8, 128), 1)
    tiles = [None] * (len(parts) * step // 128)

    def add(index, value):
        tiles[index] = value if tiles[index] is None else tiles[index] + value

    for i, part in enumerate(parts):
        part = jnp.where(lane < step, part, 0.0)
        index, shift = i * step // 128, i * step % 128
        rolled = pltpu.roll(part, shift, 1) if shift else part
        if shift + step <= 128:
            add(index, rolled)
        else:
            add(index, jnp.where(lane >= shift, rolled, 0.0))
            add(index + 1, jnp.where(lane < shift, rolled, 0.0))
    return tiles


def pick_lanes(tiles, step, count):
    parts = []
    lane = lax.broadcasted_iota(jnp.int32, (8, 128), 1)
    for i in range(count):
        index, shift = i * step // 128, i * step % 128
        part = pltpu.roll(tiles[index], 128 - shift, 1) if shift else tiles[index]
        if shift + step > 128:
            after = pltpu.roll(tiles[index + 1], 128 - shift, 1)
            part = jnp.where(lane < 128 - shift, part, after)
        parts.append(jnp.where(lane < step, part, 0.0))
    return parts


def rounded(value):
    return value.astype(jnp.bfloat16).astype(jnp.float32)


def segment_forms(segment_ids, row_lengths, r):
    segment = segment_ids[r : r + 1, :].astype(jnp.float32)
    position = lax.broadcasted_iota(jnp.int32, (1, SEQ), 1)
    return segment, jnp.where(position < row_lengths[r], segment, -1.0)


def upright(row):
    return jnp.broadcast_to(row, (128, SEQ)).T[:, 0:1]


def mask_of(rows_form, columns_form):
    return jnp.where(upright(rows_form) == columns_form, 0.0, MASK_FILL)


FIRST_PLAN = (
    "a.along",
    "t.own",
    "a.across0",
    "t.diag",
    "u.along",
    "o.own",
    "u.across0",
    "a.across1",
    "t.set0",
    "a.across2",
    "bias",
    "t.set1",
    "a.across3",
    "a.onward0",
    "a.onward1",
    "d.along",
    "turn",
    "a.onward2",
    "t.set2",
    "a.onward3",
    "t.set3",
    "o.diag",
    "a.beside",
    "u.across1",
    "u.across2",
    "a.opposite",
    "u.across3",
    "t.last",
    "u.onward0",
    "o.set0",
    "vec",
    "u.onward1",
    "a.last",
    "project",
    "d.across1",
    "p0",
    "p1",
    "p2",
    "p3",
    "u.onward2",
    "attend",
    "d.across2",
    "d.across0",
    "a0",
    "a1",
    "a2",
    "u.onward3",
    "a3",
    "o.set1",
    "o.set2",
    "a4",
    "a5",
    "a6",
    "a7",
    "o.set3",
    "a8",
    "u.beside",
    "a9",
    "a10",
    "d.across3",
    "d.onward0",
    "o.last",
    "a11",
    "mix",
    "d.onward2",
    "u.opposite",
    "m0",
    "d.onward1",
    "m1",
    "m2",
    "m3",
    "u.last",
    "widen",
    "w0",
    "w1",
    "d.onward3",
    "w2",
    "w3",
    "d.beside",
    "w4",
    "w5",
    "w6",
    "w7",
    "w8",
    "d.opposite",
    "w9",
    "w10",
    "w11",
    "d.last",
    "narrow",
)

LAST_PLAN = (
    "pre",
    "d.first",
    "d.second0",
    "ld",
    "w0",
    "w1",
    "d.second1",
    "w2",
    "w3",
    "wu0",
    "d.second2",
    "wu1",
    "wu2",
    "d.third0",
    "u.first",
    "bc",
    "d.third1",
    "n0",
    "n1",
    "misc",
    "g0",
    "u.second0",
    "u.second1",
    "rd",
    "u.second2",
    "u.second3",
    "wo0",
    "d.second3",
    "o.first",
    "a0",
    "d.fourth",
    "a1",
    "a2",
    "a3",
    "u.third1",
    "u.third0",
    "a4",
    "o.second0",
    "a5",
    "a6",
    "a7",
    "wm0",
    "wm1",
    "u.fourth",
    "wm2",
    "m.first",
    "o.third1",
    "o.third0",
    "a8",
    "m.second0",
    "a9",
    "a10",
    "m.second1",
    "m.second2",
    "a11",
    "wr0",
    "o.fourth",
    "m.third1",
    "m.second3",
    "m.third0",
    "wr1",
    "wr2",
    "r.first",
    "vec",
    "d.trade",
    "r.second0",
    "m.fourth",
    "b0",
    "t.first",
    "r.third0",
    "r.third1",
    "t.second0",
    "u.trade",
    "r.fourth",
    "d.whole",
    "t.third1",
    "o.trade",
    "t.third0",
    "u.whole",
    "b1",
    "m.trade",
    "t.fourth",
    "r.trade",
    "t.trade",
    "r.whole",
    "m.whole",
    "o.whole",
    "t.whole",
    "end",
)


class Plan:
    def __init__(self, names, groups):
        self.groups = groups
        self.inside = {}
        self.queue = list(names)

    def call(self, name):
        group, method = name.split(".")
        if method[-1].isdigit():
            getattr(self.groups[group], method[:-1])(int(method[-1]))
        else:
            getattr(self.groups[group], method)()

    def until(self, name):
        while True:
            step = self.queue.pop(0)
            if step == name:
                return
            self.call(step)

    def loop(self, letter, first, count, body):
        steps = {}
        self.until(f"{letter}{first}")
        for index in range(first, first + count):
            steps[index] = []
            ahead = f"{letter}{index + 1}"
            while self.queue[0] != ahead and "." in self.queue[0]:
                steps[index].append(self.queue.pop(0))
            if index + 1 < first + count:
                self.queue.pop(0)

        def run(step, carry):
            body(step)
            for index, names in steps.items():
                if names:

                    @pl.when(step == index)
                    def _(names=names):
                        for name in names:
                            self.call(name)

            return carry

        lax.fori_loop(first, first + count, run, 0)


def lanes_in_head(shape):
    return lax.broadcasted_iota(jnp.int32, shape, 1) & (HEAD - 1)


def low_head(shape):
    return lax.broadcasted_iota(jnp.int32, shape, 1) < HEAD


def two_parts(value):
    first = rounded(value)
    return first, value - first


def three_parts(value):
    first, rest = two_parts(value)
    second, third = two_parts(rest)
    return first, second, third


PARTS = 16


def query_codes(segment):
    lane = lanes_in_head((SEQ, 128)).astype(jnp.float32)
    return jnp.where(lane == upright(segment), 1.0, 0.0).astype(jnp.bfloat16)


def key_codes(live):
    lane = lanes_in_head((SEQ, 128))
    hidden = jnp.where(lane.astype(jnp.float32) == upright(live), 0.0, MASK_FILL)
    parts = jnp.where((lane >= PARTS) & (lane < PARTS + 3), 1.0, 0.0)
    return jnp.where(lane <= NPASS, hidden, parts).astype(jnp.bfloat16)


def attend_pair(r, p, qkv, context, codes, bias, segments):
    rows = part_of(r, SEQ)
    columns = pl.multiple_of(p * 128, 128)
    query = qkv[rows, pl.ds(columns, 128)]
    key = qkv[rows, pl.ds(columns + WIDTH, 128)]
    value = qkv[rows, pl.ds(columns + 2 * WIDTH, 128)]
    low = low_head((SEQ, 128))
    zero = jnp.zeros_like(key)
    outs, sums = [], []
    for j in range(2):
        key_j = jnp.where(low, key, zero) if j == 0 else jnp.where(low, zero, key)
        scores = dotted(query, key_j, 1, 1) * EXP2_SCALE + bias[rows, 0:SEQ]
        peak = jnp.max(scores, -1, keepdims=True)
        shifted = jnp.exp2(scores - peak)
        total = jnp.sum(shifted, -1, keepdims=True)
        out = dotted(shifted.astype(jnp.bfloat16), value, 1, 0)
        outs.append(out * (1.0 / total))
        sums.append(peak + jnp.log2(total))
    context[rows, pl.ds(columns, 128)] = jnp.where(low, outs[0], outs[1]).astype(jnp.bfloat16)
    first, second, third = three_parts(jnp.where(low, sums[1], sums[0]) * (-1.0 / EXP2_SCALE))
    lane = lanes_in_head((SEQ, 128))
    code = jnp.where(lane == PARTS + 2, third, segments[rows, :].astype(jnp.float32))
    code = jnp.where(lane == PARTS + 1, second, code)
    code = jnp.where(lane == PARTS, first, code)
    codes[rows, pl.ds(columns, 128)] = code.astype(jnp.bfloat16)


def dot_codes(p, context, d_context, codes):
    columns = part_of(p, 128)
    both = context[:, columns].astype(jnp.float32) * d_context[:, columns].astype(jnp.float32)
    first, second = two_parts(both)
    shape = (128, 128)
    other = low_head(shape) != (lax.broadcasted_iota(jnp.int32, shape, 0) < HEAD)
    other = jnp.where(other, -1.0, 0.0).astype(jnp.bfloat16)
    total = dotted(first.astype(jnp.bfloat16), other, 1, 0)
    total = total + dotted(second.astype(jnp.bfloat16), other, 1, 0)
    first, second = two_parts(total)
    lane = lanes_in_head(total.shape)
    code = jnp.where(lane == PARTS, first, jnp.where(lane == PARTS + 1, second, 0.0))
    codes[:, columns] = code.astype(jnp.bfloat16)


def pick_head(masks, j, value, code):
    return value * masks[j] + code * masks[1 - j]


def attend_back_pair(r, p, qkv, d_context, query_code, grad_code, key_code, value_code, lows):
    rows = part_of(r, SEQ)
    columns = pl.multiple_of(p * 128, 128)
    query = qkv[rows, pl.ds(columns, 128)]
    key = qkv[rows, pl.ds(columns + WIDTH, 128)]
    value = qkv[rows, pl.ds(columns + 2 * WIDTH, 128)]
    grad = d_context[rows, pl.ds(columns, 128)]
    query_c = query_code[rows, pl.ds(columns, 128)]
    grad_c = grad_code[rows, pl.ds(columns, 128)]
    key_c = key_code[rows, :]
    value_c = value_code[...]
    masks = (lows[0], lows[1])
    d_query, d_key, d_value = [], [], []
    for j in range(2):
        scores = dotted(pick_head(masks, j, key, key_c), pick_head(masks, j, query, query_c), 1, 1)
        chances = jnp.exp2(scores * EXP2_SCALE)
        d_chances = dotted(
            pick_head(masks, j, value, value_c), pick_head(masks, j, grad, grad_c), 1, 1
        )
        d_scores = (chances * d_chances).astype(jnp.bfloat16)
        d_value.append(dotted(chances.astype(jnp.bfloat16), grad, 1, 0))
        d_key.append(dotted(d_scores, query, 1, 0))
        d_query.append(dotted(d_scores, key, 0, 0))
    low = low_head((SEQ, 128))
    scale = 1.0 / math.sqrt(HEAD)
    low_type = jnp.bfloat16
    qkv[rows, pl.ds(columns, 128)] = (jnp.where(low, d_query[0], d_query[1]) * scale).astype(
        low_type
    )
    qkv[rows, pl.ds(columns + WIDTH, 128)] = (
        jnp.where(low, d_key[0], d_key[1]) * scale
    ).astype(low_type)
    qkv[rows, pl.ds(columns + 2 * WIDTH, 128)] = jnp.where(low, d_value[0], d_value[1]).astype(
        low_type
    )


def norm_parts(mixed):
    centred = mixed - jnp.mean(mixed, -1, keepdims=True)
    scaled = lax.rsqrt(jnp.mean(centred * centred, -1, keepdims=True) + NORM_EPS)
    return centred * scaled, scaled


def norm_back(grad_out, normed, scaled, gain):
    inner = grad_out * gain
    return scaled * (
        inner
        - jnp.mean(inner, -1, keepdims=True)
        - normed * jnp.mean(inner * normed, -1, keepdims=True)
    )


def halves(links, src, stage, sends, recvs, index):
    rows, width = src.shape
    columns = width // 2

    def ends():
        return src.at[:, part_of(1 - links.c, columns)], stage.at[part_of(links.c, rows), :]

    links.send(ends, lambda: (sends.at[index], recvs.at[index]), links.to_core)
    stage[part_of(links.c, rows), :] = src[:, part_of(links.c, columns)]


def passage_loss(similar, live, teacher_index, teacher_table):
    rows_dev = similar.shape[0] // QLEN
    scores = similar * (1.0 / SOFTNESS)
    inside, shares, student, teacher = [], [], [], []
    for p in range(NPASS):
        member = live == float(p + 1)
        masked = jnp.where(member, scores, MASK_FILL)
        peak = jnp.max(masked, -1, keepdims=True)
        shifted = jnp.exp(masked - peak)
        total = jnp.sum(shifted, -1, keepdims=True)
        inside.append(jnp.where(member, shifted, 0.0))
        shares.append(1.0 / total)
        sums = peak + jnp.log(total)
        student.append(
            [
                SOFTNESS * jnp.sum(sums[r * QLEN : (r + 1) * QLEN], axis=0, keepdims=True)
                for r in range(rows_dev)
            ]
        )
        teacher.append(
            [
                jnp.full((1, 1), teacher_table[teacher_index[r, p]], jnp.float32)
                for r in range(rows_dev)
            ]
        )

    def log_softmax(values):
        peak = functools.reduce(jnp.maximum, values)
        total = sum(jnp.exp(value - peak) for value in values)
        return [value - peak - jnp.log(total) for value in values]

    losses, slopes = [], []
    for r in range(rows_dev):
        ours = log_softmax([row[r] for row in student])
        theirs = log_softmax([row[r] for row in teacher])
        losses.append(sum(jnp.exp(t) * (t - s) for t, s in zip(theirs, ours)))
        slopes.append([jnp.broadcast_to(jnp.exp(s) - jnp.exp(t), (QLEN, 1)) for t, s in zip(theirs, ours)])
    d_similar = sum(
        part * (share * jnp.concatenate([row[p] for row in slopes], axis=0))
        for p, (part, share) in enumerate(zip(inside, shares))
    )
    return losses, d_similar


def first_kernel(*refs):
    given = refs[:18]
    row_lengths, teacher_index, teacher_table = refs[18:21]
    (
        losses,
        embeddings_hbm,
        attn_hbm,
        up_hbm,
        down_hbm,
        turned_hbm,
        qkv_hbm,
        context_hbm,
        low_one_hbm,
        normed_one_hbm,
        slope_hbm,
        d_mid_hbm,
        d_branch_hbm,
        grad_down_hbm,
        codes_hbm,
        scaled_one_hbm,
        vectors_hbm,
        grad_vectors_hbm,
        grad_proj_hbm,
    ) = refs[21:40]
    (
        attn_mat,
        up_mat,
        down_mat,
        turned,
        qkv,
        context,
        low_one,
        normed_one,
        slope,
        activated,
        d_mid,
        d_branch,
        grad_down,
        small_all,
        cat_attn,
        stage_attn,
        stage_out,
        stage_up,
        stage_down,
        proj,
        up_bias,
        scaled_two,
        d_raw,
        codes,
        segments,
        sends,
        recvs,
        half_sends,
        half_recvs,
        local_sems,
        grad_sems,
        embeddings,
        scaled_one,
        vectors,
        grad_vectors,
        grad_proj,
        given_sems,
        *taken,
    ) = refs[40:]
    (
        tokens,
        w_query,
        w_key,
        w_value,
        w_out,
        w_up,
        w_down,
        w_proj,
        *vector_refs,
        b_up,
        segment_ids,
    ) = taken
    count = tokens.shape[0]
    rows_dev = count // SEQ
    links = Links()
    links.hail()
    loads = [
        pltpu.make_async_copy(src, dst, given_sems.at[index])
        for index, (src, dst) in enumerate(zip(given, taken))
    ]
    later = (0, len(loads) - 1)
    for index, load in enumerate(loads):
        if index not in later:
            load.start()
    for index in later:
        loads[index].start()

    def gather(kind, block, group, stage):
        return kind(links, block, sends, recvs, group).join_from(
            stage, half_sends, half_recvs, group
        )

    attn = gather(JoinedGather, grid_block(attn_mat, 1152), 0, stage_attn)
    out = gather(JoinedLevelGather, grid_block(attn_mat, 384, 3 * WIDTH), 1, stage_out)
    up = gather(JoinedGather, rows_block(up_mat, 48, 1536), 2, stage_up)
    down = gather(JoinedGather, rows_block(down_mat, 192, 384), 3, stage_down)
    tiny = LevelGather(links, lead_grid_block(small_all), sends, recvs, 4)
    own_chip = links.chip_own + links.z
    kept = []

    def keep(src, dst):
        copy = pltpu.make_async_copy(src, dst, local_sems.at[len(kept)])
        copy.start()
        kept.append(copy)

    for index, load in enumerate(loads):
        if index not in later:
            load.wait()
    for index, ref in enumerate((w_query, w_key, w_value)):
        cat_attn[:, index * WIDTH : (index + 1) * WIDTH] = ref[...]
    own_small = tiny.block(links.c, own_chip, 1)
    own_small[0:24, :] = w_proj[...]
    own_small[24:40, :] = jnp.zeros((16, 128), jnp.float32)
    for index, ref in enumerate(vector_refs):
        own_small[24 + index : 25 + index, 0:24] = ref[...].reshape(1, 24)
    own_small[32:33, 0:96] = b_up[...].reshape(1, 96)

    links.greet()
    halves(links, cat_attn, stage_attn, half_sends, half_recvs, 0)
    halves(links, w_out, stage_out, half_sends, half_recvs, 1)
    halves(links, w_up, stage_up, half_sends, half_recvs, 2)
    halves(links, w_down, stage_down, half_sends, half_recvs, 3)
    plan = Plan(FIRST_PLAN, {"a": attn, "o": out, "u": up, "d": down, "t": tiny, "l": links})
    plan.until("bias")
    for index in later:
        loads[index].wait()
    live_rows = []
    for r in range(rows_dev):
        segment, live = segment_forms(segment_ids, row_lengths, r)
        live_rows.append(live)
        d_mid[r * SEQ : (r + 1) * SEQ, 0:SEQ] = mask_of(segment, live)
        segments[r * SEQ : (r + 1) * SEQ, :] = query_codes(segment)
    plan.until("turn")
    turned[...] = tokens[...].T
    keep(turned, turned_hbm)
    plan.until("vec")
    cores = [(i % 2, i // 8, i // 2 % 4) for i in range(SHARDS)]
    for index, tile in enumerate(spread_lanes([small_all[c, n, m, 24:32, :] for c, n, m in cores], 24)):
        vectors[:, index * 128 : (index + 1) * 128] = rounded(tile)
    for index, tile in enumerate(spread_lanes([small_all[c, n, m, 32:40, :] for c, n, m in cores], 96)):
        up_bias[:, index * 128 : (index + 1) * 128] = rounded(tile)
    for r in range(CHIPS):
        both = [small_all[c, r // 4, r % 4, 0:24, :] for c in range(2)]
        both = jnp.concatenate(both, axis=0)
        proj[r * 48 : (r + 1) * 48, :] = both.astype(jnp.bfloat16)
    keep(vectors, vectors_hbm)
    plan.until("project")

    def project(step):
        rows = part_of(step, CHUNK)
        weights = attn_mat[:, :, :, 0 : 3 * WIDTH].reshape(WIDTH, 3 * WIDTH)
        value = dotted(tokens[rows, :], weights, 1, 0)
        qkv[rows, 0:WIDTH] = (value[:, 0:WIDTH] + vectors[0:1, :]).astype(jnp.bfloat16)
        qkv[rows, WIDTH : 2 * WIDTH] = value[:, WIDTH : 2 * WIDTH].astype(jnp.bfloat16)
        qkv[rows, 2 * WIDTH :] = (value[:, 2 * WIDTH :] + vectors[1:2, :]).astype(jnp.bfloat16)

    plan.loop("p", 0, count // CHUNK, project)
    keep(qkv, qkv_hbm)
    plan.until("attend")

    def attend(item):
        r, p = lax.div(item, PAIRS), lax.rem(item, PAIRS)
        attend_pair(r, p, qkv, context, codes, d_mid, segments)

    plan.loop("a", 0, rows_dev * PAIRS, attend)
    keep(context, context_hbm)
    keep(codes, codes_hbm)
    plan.until("mix")
    keep(attn_mat, attn_hbm)

    def mix(step):
        rows = part_of(step, CHUNK)
        weights = attn_mat[:, :, :, 3 * WIDTH :].reshape(WIDTH, WIDTH)
        mixed = dotted(context[rows, :], weights, 1, 0) + vectors[2:3, :]
        normed, scaled = norm_parts(tokens[rows, :].astype(jnp.float32) + mixed)
        normed_one[rows, :] = normed
        scaled_one[rows, :] = jnp.broadcast_to(scaled, (CHUNK, 128))
        low_one[rows, :] = (normed * vectors[3:4, :] + vectors[4:5, :]).astype(jnp.bfloat16)

    plan.loop("m", 0, count // CHUNK, mix)
    keep(normed_one, normed_one_hbm)
    keep(scaled_one, scaled_one_hbm)
    keep(low_one, low_one_hbm)
    plan.until("widen")
    keep(up_mat, up_hbm)

    def widen(step):
        columns = part_of(step, CHUNK)
        upward = dotted(low_one[...], up_mat[:, columns], 1, 0) + up_bias[0:1, columns]
        chance = 0.5 * (1.0 + lax.erf(upward * ROOT_HALF))
        density = jnp.exp2(upward * upward * (-0.5 * LOG2_E)) * DENSITY_SCALE
        activated[:, columns] = (upward * chance).astype(jnp.bfloat16)
        slope[:, columns] = (chance + upward * density).astype(jnp.bfloat16)

    plan.loop("w", 0, HIDDEN // CHUNK, widen)
    keep(slope, slope_hbm)
    plan.until("narrow")
    keep(down_mat, down_hbm)

    grad_vectors[...] = jnp.zeros_like(grad_vectors)
    for r in range(rows_dev):
        rows = slice(r * SEQ, (r + 1) * SEQ)
        mixed = dotted(activated[rows, :], down_mat[...], 1, 0) + vectors[5:6, :]
        mixed = mixed + (normed_one[rows, :] * vectors[3:4, :] + vectors[4:5, :])
        normed, scaled = norm_parts(mixed)
        d_mid[rows, :] = normed
        scaled_two[rows, :] = jnp.broadcast_to(scaled, (SEQ, 128))
        d_branch[rows, :] = (normed * vectors[6:7, :] + vectors[7:8, :]).astype(jnp.bfloat16)
    raw = dotted(d_branch[...], proj[...], 1, 0)
    inverse = lax.rsqrt(jnp.sum(raw * raw, -1, keepdims=True) + UNIT_EPS)
    embedded = raw * inverse
    embeddings[...] = embedded.reshape(rows_dev, SEQ, EMBED)
    keep(embeddings, embeddings_hbm)
    low_embed = embedded.astype(jnp.bfloat16)
    starts = [r * SEQ for r in range(rows_dev)]
    heads = [low_embed[start : start + QLEN] for start in starts]
    wholes = [low_embed[start : start + SEQ] for start in starts]
    similar = jnp.concatenate([dotted(h, w, 1, 1) for h, w in zip(heads, wholes)], axis=0)
    live = jnp.concatenate([jnp.broadcast_to(row, (QLEN, SEQ)) for row in live_rows], axis=0)
    row_losses, d_similar = passage_loss(similar, live, teacher_index, teacher_table)
    for r in range(rows_dev):
        losses[r] = row_losses[r][0, 0]
    d_similar = d_similar.astype(jnp.bfloat16)
    d_parts = []
    for r in range(rows_dev):
        d_row = d_similar[r * QLEN : (r + 1) * QLEN]
        d_whole = dotted(d_row, heads[r], 0, 0)
        d_parts += [d_whole[0:QLEN] + dotted(d_row, wholes[r], 1, 0), d_whole[QLEN:]]
    d_embed = jnp.concatenate(d_parts, axis=0)
    along = jnp.sum(d_embed * embedded, -1, keepdims=True)
    d_raw[...] = (inverse * (d_embed - embedded * along)).astype(jnp.bfloat16)
    grad_proj[...] = dotted(d_branch[...], d_raw[...], 0, 0)
    keep(grad_proj, grad_proj_hbm)

    def unmix(step, carry):
        rows = part_of(step, CHUNK)
        d_hidden = dotted(d_raw[rows, :], proj[...], 1, 1)
        normed = d_mid[rows, :]
        d_mixed = norm_back(d_hidden, normed, scaled_two[rows, 0:1], vectors[6:7, :])
        low_mixed = d_mixed.astype(jnp.bfloat16)
        d_mid[rows, :] = d_mixed
        d_branch[rows, :] = low_mixed
        grad_vectors[5:6, :] += jnp.sum(low_mixed.astype(jnp.float32), 0, keepdims=True)
        grad_vectors[6:7, :] += jnp.sum(d_hidden * normed, 0, keepdims=True)
        grad_vectors[7:8, :] += jnp.sum(d_hidden, 0, keepdims=True)
        return carry

    lax.fori_loop(0, count // CHUNK, unmix, 0)
    keep(grad_vectors, grad_vectors_hbm)
    keep(d_mid, d_mid_hbm)
    keep(d_branch, d_branch_hbm)

    def grad_copy(step, slot):
        return pltpu.make_async_copy(
            grad_down.at[slot], grad_down_hbm.at[part_of(step, WIDTH), :], grad_sems.at[slot]
        )

    def weigh(step, carry):
        slot = lax.rem(step, 2)

        @pl.when(step >= 2)
        def _():
            grad_copy(step - 2, slot).wait()

        part = activated[:, part_of(step, WIDTH)]
        grad_down[slot] = dotted(part, d_branch[...], 0, 0).astype(jnp.bfloat16)
        grad_copy(step, slot).start()
        return carry

    steps = HIDDEN // WIDTH
    lax.fori_loop(0, steps, weigh, 0)
    for step in (steps - 2, steps - 1):
        grad_copy(step, step % 2).wait()
    links.finish()
    for copy in kept:
        copy.wait()


def run_first(tokens, weights, vectors, segment_ids, row_lengths, teacher_index, teacher_table):
    count = tokens.shape[0]
    rows_dev = count // SEQ
    smem = pl.BlockSpec(memory_space=pltpu.SMEM)
    anywhere = pl.BlockSpec(memory_space=pl.ANY)
    low = jnp.bfloat16
    wide = jnp.float32

    def array(kind, *shape):
        return jax.ShapeDtypeStruct(shape, kind)

    return pl.pallas_call(
        first_kernel,
        out_shape=[
            array(wide, rows_dev),
            array(wide, rows_dev, SEQ, EMBED),
            array(low, 4, 4, 48, HIDDEN),
            array(low, WIDTH, HIDDEN),
            array(low, HIDDEN, WIDTH),
            array(low, WIDTH, count),
            array(low, count, 3 * WIDTH),
            array(low, count, WIDTH),
            array(low, count, WIDTH),
            array(wide, count, WIDTH),
            array(low, count, HIDDEN),
            array(wide, count, WIDTH),
            array(low, count, WIDTH),
            array(low, HIDDEN, WIDTH),
            array(low, count, WIDTH),
            array(wide, count, 128),
            array(wide, 8, WIDTH),
            array(wide, 8, WIDTH),
            array(wide, WIDTH, EMBED),
        ],
        in_specs=[anywhere] * 18 + [smem] * 3,
        out_specs=[smem] + [anywhere] * 18,
        scratch_shapes=[
            pltpu.VMEM((4, 4, 48, HIDDEN), low),
            pltpu.VMEM((WIDTH, HIDDEN), low),
            pltpu.VMEM((HIDDEN, WIDTH), low),
            pltpu.VMEM((WIDTH, count), low),
            pltpu.VMEM((count, 3 * WIDTH), low),
            pltpu.VMEM((count, WIDTH), low),
            pltpu.VMEM((count, WIDTH), low),
            pltpu.VMEM((count, WIDTH), wide),
            pltpu.VMEM((count, HIDDEN), low),
            pltpu.VMEM((count, HIDDEN), low),
            pltpu.VMEM((count, WIDTH), wide),
            pltpu.VMEM((count, WIDTH), low),
            pltpu.VMEM((2, WIDTH, WIDTH), low),
            pltpu.VMEM((2, 4, 4, SMALL, 128), wide),
            pltpu.VMEM((24, 3 * WIDTH), wide),
            pltpu.VMEM((48, 3 * WIDTH // 2), wide),
            pltpu.VMEM((48, WIDTH // 2), wide),
            pltpu.VMEM((48, HIDDEN // 2), wide),
            pltpu.VMEM((192, WIDTH // 2), wide),
            pltpu.VMEM((WIDTH, EMBED), low),
            pltpu.VMEM((8, HIDDEN), wide),
            pltpu.VMEM((count, 128), wide),
            pltpu.VMEM((count, EMBED), low),
            pltpu.VMEM((count, WIDTH), low),
            pltpu.VMEM((count, 128), low),
            pltpu.SemaphoreType.DMA((5, Gather.SEMS)),
            pltpu.SemaphoreType.DMA((5, Gather.SEMS)),
            pltpu.SemaphoreType.DMA((4,)),
            pltpu.SemaphoreType.DMA((4,)),
            pltpu.SemaphoreType.DMA((18,)),
            pltpu.SemaphoreType.DMA((2,)),
            pltpu.VMEM((rows_dev, SEQ, EMBED), wide),
            pltpu.VMEM((count, 128), wide),
            pltpu.VMEM((8, WIDTH), wide),
            pltpu.VMEM((8, WIDTH), wide),
            pltpu.VMEM((WIDTH, EMBED), wide),
            pltpu.SemaphoreType.DMA((18,)),
        ]
        + [pltpu.VMEM(a.shape, a.dtype) for a in (tokens, *weights, *vectors, segment_ids)],
        compiler_params=pltpu.CompilerParams(
            collective_id=0, has_side_effects=True, vmem_limit_bytes=62 * 2**20
        ),
        name="forward_gather",
    )(tokens, *weights, *vectors, segment_ids, row_lengths, teacher_index, teacher_table)


def last_kernel(*refs):
    (
        attn_hbm,
        up_hbm,
        down_hbm,
        turned_hbm,
        qkv_hbm,
        context_hbm,
        low_one_hbm,
        normed_one_hbm,
        slope_hbm,
        d_mid_hbm,
        d_branch_hbm,
        grad_down_hbm,
        codes_hbm,
        scaled_one_hbm,
        vectors_hbm,
        part_vectors_hbm,
        grad_proj_hbm,
        segment_ids_hbm,
        row_lengths,
    ) = refs[:19]
    (
        grad_tokens_hbm,
        own_rows,
        own_down,
        own_small,
    ) = refs[19:23]
    (
        attn_mat,
        grads,
        wide,
        low_one,
        d_branch,
        d_mid,
        part_down,
        small_all,
        grad_vectors,
        grad_up_bias,
        sends,
        recvs,
        local_sems,
        slope_sems,
        down_sems,
        qkv_sems,
        grad_sems,
        key_code,
        value_code,
        lows,
        scaled_one,
        vectors,
        grad_proj,
        segment_ids,
        *rest,
    ) = refs[23:]
    held = [rest[6 * i : 6 * i + 6] for i in range(6)]
    fins = [rest[36 + 2 * i : 38 + 2 * i] for i in range(5)]
    count = d_mid.shape[0]
    rows_dev = count // SEQ
    links = Links()
    c = links.c

    def scatter(block, rows, group, deliver, mine=None):
        def own(chip, units):
            return block(c, chip, units)

        own = own if mine is None else mine
        fin = fins[group] if group < 5 else None
        return Scatter(
            links, block, own, rows, held[group], fin, deliver, sends, recvs, group, group in (2, 4, 5)
        )

    def down_mine(chip, units):
        return part_down.at[pl.ds(pl.multiple_of(chip * 192, 192), units * 192), :]

    def halves_to(ref, start, columns):
        def deliver(low, high):
            ref[:, start : start + columns] = low
            ref[:, start + columns : start + 2 * columns] = high

        return deliver

    def most_out(low, high):
        own_rows[:, 0:512] = low[:, 0:512]
        own_rows[:, 768:1024] = low[:, 512:768]
        own_rows[:, 1024:1280] = high[:, 0:256]
        own_rows[:, 1536:2048] = high[:, 256:768]

    def rest_out(low, high):
        own_rows[:, 512:768] = low[:, 0:256]
        own_rows[:, 1280:1408] = low[:, 256:384]
        own_rows[:, 1408:1536] = high[:, 0:128]
        own_rows[:, 2048:2304] = high[:, 128:384]

    def tiny_out(total):
        own_small[...] = total[0]

    down = scatter(rows_block(grad_down_hbm, 192, 384), 192, 0, halves_to(own_down, 0, WIDTH // 2), down_mine)
    up = scatter(rows_block(grads, 48, 1536), 48, 1, halves_to(own_rows, HIDDEN, HIDDEN // 2))
    out = scatter(rows_block(grads, 48, 384), 48, 2, halves_to(own_rows, 3 * WIDTH, WIDTH // 2))
    most = scatter(rows_block(grads, 48, 768, WIDTH), 48, 3, most_out)
    rest_of = scatter(rows_block(grads, 48, 384, 3 * WIDTH), 48, 4, rest_out)
    tiny = scatter(lead_block(small_all), 1, 5, tiny_out)

    def load(src, dst, index):
        return pltpu.make_async_copy(src, dst, local_sems.at[index])

    def start(copies):
        for copy in copies:
            copy.start()

    def wait(copies):
        for copy in copies:
            copy.wait()

    plan = Plan(
        LAST_PLAN,
        {"d": down, "u": up, "o": out, "m": most, "r": rest_of, "t": tiny, "l": links},
    )
    plan.until("pre")
    links.hail()
    first_loads = [
        load(d_branch_hbm, d_branch, 0),
        load(grad_down_hbm.at[:, part_of(c, WIDTH // 2)], part_down, 1),
    ]
    side_loads = [
        load(segment_ids_hbm, segment_ids, 11),
        load(grad_proj_hbm, grad_proj, 12),
        load(part_vectors_hbm, grad_vectors, 13),
        load(vectors_hbm, vectors, 14),
        load(scaled_one_hbm, scaled_one, 15),
    ]
    attn_load = load(attn_hbm, attn_mat, 3)
    start(first_loads + side_loads[:2])
    links.greet()
    wait(first_loads[1:])
    ones = jnp.ones((8, count), jnp.bfloat16)

    def slope_load(step):
        columns = part_of(step, WIDTH)
        return pltpu.make_async_copy(
            slope_hbm.at[:, columns], wide.at[:, columns], slope_sems.at[step]
        )

    def qkv_load(step):
        rows = part_of(step, HALF)
        return pltpu.make_async_copy(
            qkv_hbm.at[rows, :], wide.at[rows, 0 : 3 * WIDTH], qkv_sems.at[step]
        )

    def grad_store(step):
        rows = part_of(step, HALF)
        return pltpu.make_async_copy(
            d_mid.at[rows, :], grad_tokens_hbm.at[rows, :], grad_sems.at[step]
        )

    steps = count // HALF
    quarters = HIDDEN // WIDTH

    def weights(start, columns):
        return attn_mat[:, :, :, start : start + columns].reshape(WIDTH, columns)

    def feed_forward(up_mat, down_mat, normed_one):
        def down_load(step):
            rows = part_of(step, WIDTH)
            return pltpu.make_async_copy(
                down_hbm.at[rows, :], down_mat.at[rows, :], down_sems.at[step]
            )

        for step in range(quarters):
            down_load(step).start()
            slope_load(step).start()
        start(side_loads[2:])
        middle = [
            load(low_one_hbm, low_one, 6),
            load(up_hbm, up_mat, 7),
            load(d_mid_hbm, d_mid, 8),
            load(normed_one_hbm, normed_one, 9),
        ]
        plan.until("ld")
        wait(side_loads[:2])
        for r in range(rows_dev):
            _, live = segment_forms(segment_ids, row_lengths, r)
            key_code[r * SEQ : (r + 1) * SEQ, :] = key_codes(live)
        low = low_head((SEQ, 128))
        lows[0] = jnp.where(low, 1.0, 0.0).astype(jnp.bfloat16)
        lows[1] = jnp.where(low, 0.0, 1.0).astype(jnp.bfloat16)
        lane = lanes_in_head((SEQ, 128))
        parts = (lane == PARTS) | (lane == PARTS + 1)
        value_code[...] = jnp.where(parts, 1.0, 0.0).astype(jnp.bfloat16)
        for i in range(SHARDS):
            small_all[i % 2, i // 2, 0:24, :] = grad_proj[i * 24 : (i + 1) * 24, :]
        wait(first_loads[:1])

        def widen(step):
            columns = part_of(step, WIDTH)
            down_load(step).wait()
            slope_load(step).wait()
            grad = dotted(d_branch[...], down_mat[columns, :], 1, 1)
            wide[:, columns] = (grad * wide[:, columns].astype(jnp.float32)).astype(jnp.bfloat16)

            @pl.when(step == 0)
            def _():
                start(middle)

        plan.loop("w", 0, quarters, widen)
        wait(middle[:1])

        def weigh(step):
            rows = part_of(step, CHUNK)
            grads[rows, :] = dotted(low_one[:, rows], wide[...], 0, 0).astype(jnp.bfloat16)

        plan.loop("wu", 0, WIDTH // CHUNK, weigh)
        plan.until("bc")
        attn_load.start()
        for index in range(4):
            columns = slice(index * WIDTH, (index + 1) * WIDTH)
            grad_up_bias[:, columns] = dotted(ones, wide[:, columns], 1, 0)
        wait(middle[1:] + side_loads[2:])

        def narrow(step):
            rows = part_of(step, HALF)
            d_hidden = d_mid[rows, :] + dotted(wide[rows, :], up_mat[...], 1, 1)
            qkv_load(step).start()
            normed = normed_one[rows, :]
            d_mixed = norm_back(d_hidden, normed, scaled_one[rows, 0:1], vectors[3:4, :])
            d_mid[rows, :] = d_mixed
            d_branch[rows, :] = d_mixed.astype(jnp.bfloat16)
            grad_vectors[3:4, :] += jnp.sum(d_hidden * normed, 0, keepdims=True)
            grad_vectors[4:5, :] += jnp.sum(d_hidden, 0, keepdims=True)

        plan.loop("n", 0, steps, narrow)

    pl.run_scoped(
        feed_forward,
        pltpu.VMEM((WIDTH, HIDDEN), jnp.bfloat16),
        pltpu.VMEM((HIDDEN, WIDTH), jnp.bfloat16),
        pltpu.VMEM((count, WIDTH), jnp.float32),
    )

    def attention(d_context, context, codes, turned):
        loads = [
            load(context_hbm, context, 2),
            load(codes_hbm, codes, 4),
            load(turned_hbm, turned, 10),
        ]
        start(loads)
        plan.until("misc")
        grad_vectors[2:3, :] = dotted(ones, d_branch[...], 1, 0)[0:1]
        attn_load.wait()

        plan.until("g0")
        d_context[...] = dotted(d_branch[...], weights(3 * WIDTH, WIDTH), 1, 1).astype(jnp.bfloat16)
        plan.until("rd")

        wait(loads[:1])

        def gather_dots(p, carry):
            dot_codes(p, context, d_context, low_one)
            return carry

        lax.fori_loop(0, PAIRS, gather_dots, 0)
        up.settle()

        plan.until("wo0")
        grads[:, 0:WIDTH] = dotted(context[...], d_branch[...], 0, 0).astype(jnp.bfloat16)
        for step in range(steps):
            qkv_load(step).wait()

        wait(loads[1:])

        def attend(item):
            r = lax.rem(item, rows_dev)
            p = lax.div(item, rows_dev)
            attend_back_pair(
                r, p, wide, d_context, codes, low_one, key_code, value_code, lows
            )

        def weigh(first, pairs, base):
            def step(index):
                size = pairs * 128
                here = pl.ds(pl.multiple_of(index * WIDTH + first * 128, 128), size)
                there = pl.ds(pl.multiple_of(base + index * size, 128), size)
                grads[:, there] = dotted(turned[...], wide[:, here], 1, 0).astype(jnp.bfloat16)

            return step

        plan.loop("a", 0, 4 * rows_dev, attend)
        plan.loop("wm", 0, 3, weigh(0, 4, WIDTH))
        plan.loop("a", 4 * rows_dev, 2 * rows_dev, attend)
        plan.loop("wr", 0, 3, weigh(4, 2, 3 * WIDTH))

    pl.run_scoped(
        attention,
        pltpu.VMEM((count, WIDTH), jnp.bfloat16),
        pltpu.VMEM((count, WIDTH), jnp.bfloat16),
        pltpu.VMEM((count, WIDTH), jnp.bfloat16),
        pltpu.VMEM((WIDTH, count), jnp.bfloat16),
    )
    plan.until("vec")
    for index in (0, 2):
        total = dotted(ones, wide[:, index * WIDTH : (index + 1) * WIDTH], 1, 0)
        grad_vectors[index // 2 : index // 2 + 1, :] = total[0:1]
    tiles = [grad_vectors[:, i * 128 : (i + 1) * 128] for i in range(WIDTH // 128)]
    for i, part in enumerate(pick_lanes(tiles, 24, SHARDS)):
        small_all[i % 2, i // 2, 24:32, :] = part
    tiles = [grad_up_bias[:, i * 128 : (i + 1) * 128] for i in range(HIDDEN // 128)]
    for i, part in enumerate(pick_lanes(tiles, 96, SHARDS)):
        small_all[i % 2, i // 2, 32:40, :] = part

    def back(step):
        rows = part_of(step, HALF)
        value = dotted(wide[rows, 0 : 3 * WIDTH], weights(0, 3 * WIDTH), 1, 1)
        d_mid[rows, :] += value
        grad_store(step).start()

    plan.loop("b", 0, steps, back)
    plan.until("end")
    for step in range(steps):
        grad_store(step).wait()
    links.finish()


def run_last(kept, segment_ids, row_lengths):
    count = kept[9].shape[0]
    rows_dev = count // SEQ
    vmem = pl.BlockSpec(memory_space=pltpu.VMEM)
    smem = pl.BlockSpec(memory_space=pltpu.SMEM)
    anywhere = pl.BlockSpec(memory_space=pl.ANY)
    low = jnp.bfloat16
    wide = jnp.float32

    def array(*shape):
        return jax.ShapeDtypeStruct(shape, wide)

    def held(unit, kind):
        return [pltpu.VMEM((n * unit[0],) + unit[1:], kind) for n in (16, 2, 2, 4, 4, 3)]

    blocks = ((192, 384), (48, 1536), (48, 384), (48, 768), (48, 384))
    buffers = []
    for block in blocks:
        buffers += held(block, low)
    buffers += held((1, SMALL, 128), wide)
    for rows, columns in blocks:
        buffers += [pltpu.VMEM((rows, columns), wide), pltpu.VMEM((rows // 2, columns), wide)]
    return pl.pallas_call(
        last_kernel,
        out_shape=[
            array(count, WIDTH),
            array(24, 2 * HIDDEN),
            array(96, WIDTH),
            array(SMALL, 128),
        ],
        in_specs=[anywhere] * 18 + [smem],
        out_specs=[anywhere] + [vmem] * 3,
        scratch_shapes=[
            pltpu.VMEM((4, 4, 48, HIDDEN), low),
            pltpu.VMEM((WIDTH, HIDDEN), low),
            pltpu.VMEM((count, HIDDEN), low),
            pltpu.VMEM((count, WIDTH), low),
            pltpu.VMEM((count, WIDTH), low),
            pltpu.VMEM((count, WIDTH), wide),
            pltpu.VMEM((HIDDEN, WIDTH // 2), low),
            pltpu.VMEM((2, CHIPS, SMALL, 128), wide),
            pltpu.VMEM((8, WIDTH), wide),
            pltpu.VMEM((8, HIDDEN), wide),
            pltpu.SemaphoreType.DMA((6, Scatter.SEMS)),
            pltpu.SemaphoreType.DMA((6, Scatter.SEMS)),
            pltpu.SemaphoreType.DMA((16,)),
            pltpu.SemaphoreType.DMA((HIDDEN // WIDTH,)),
            pltpu.SemaphoreType.DMA((HIDDEN // WIDTH,)),
            pltpu.SemaphoreType.DMA((count // HALF,)),
            pltpu.SemaphoreType.DMA((count // HALF,)),
            pltpu.VMEM((count, 128), low),
            pltpu.VMEM((SEQ, 128), low),
            pltpu.VMEM((2, SEQ, 128), low),
            pltpu.VMEM((count, 128), wide),
            pltpu.VMEM((8, WIDTH), wide),
            pltpu.VMEM((WIDTH, EMBED), wide),
            pltpu.VMEM((rows_dev, SEQ), jnp.int32),
        ]
        + buffers,
        compiler_params=pltpu.CompilerParams(
            collective_id=1, has_side_effects=True, vmem_limit_bytes=63 * 2**20
        ),
        name="backward_scatter",
    )(*kept, segment_ids, row_lengths)


def pass_kernel(*refs):
    sources, targets = refs[:6], refs[6:25]
    held, ready = refs[25:31], refs[31:40]
    in_sems, out_sems = refs[40:]
    grad_tokens, embeddings, query, key, value, out, up, down, proj = targets[:9]
    rows, down_in, small_in, losses_in = held[2:]
    pieces = 8
    through = []
    for src, mid, dst in zip(sources[:2], held[:2], (grad_tokens, embeddings)):
        size = src.shape[0] // pieces
        for piece in range(pieces):
            part = pl.ds(piece * size, size)
            index = len(through)
            through.append(
                (
                    pltpu.make_async_copy(src.at[part], mid.at[part], in_sems.at[index]),
                    pltpu.make_async_copy(mid.at[part], dst.at[part], out_sems.at[index]),
                )
            )
    small = [
        pltpu.make_async_copy(src, mid, in_sems.at[2 * pieces + index])
        for index, (src, mid) in enumerate(zip(sources[2:], held[2:]))
    ]
    for copy in small:
        copy.start()
    for here, _ in through:
        here.start()
    for copy in small:
        copy.wait()
    for index, ref in enumerate(ready[:8]):
        ref[...] = small_in[24 + index : 25 + index, 0:24].reshape(24)
    ready[8][...] = small_in[32:33, 0:96].reshape(96)
    made = [
        (rows.at[:, index * WIDTH : (index + 1) * WIDTH], ref)
        for index, ref in enumerate((query, key, value, out))
    ]
    made += [(rows.at[:, HIDDEN:], up), (down_in, down), (small_in.at[0:24, :], proj)]
    made += list(zip(ready, targets[9:18])) + [(losses_in, targets[18])]
    outs = [
        pltpu.make_async_copy(mid, dst, out_sems.at[2 * pieces + index])
        for index, (mid, dst) in enumerate(made)
    ]
    for copy in outs:
        copy.start()
    for here, there in through:
        here.wait()
        there.start()
    for copy in outs:
        copy.wait()
    for _, there in through:
        there.wait()


def run_pass(*arrays):
    anywhere = pl.BlockSpec(memory_space=pl.ANY)

    def array(*shape):
        return jax.ShapeDtypeStruct(shape, jnp.float32)

    whole = [array(*a.shape) for a in arrays]
    vectors = [array(24)] * 8 + [array(96)]
    return pl.pallas_call(
        pass_kernel,
        out_shape=whole[:2]
        + [array(24, WIDTH)] * 4
        + [array(24, HIDDEN), array(96, WIDTH), array(24, EMBED)]
        + vectors
        + [whole[-1]],
        in_specs=[anywhere] * 6,
        out_specs=[anywhere] * 19,
        scratch_shapes=[pltpu.VMEM(a.shape, a.dtype) for a in (*arrays, *vectors)]
        + [pltpu.SemaphoreType.DMA((20,)), pltpu.SemaphoreType.DMA((33,))],
        compiler_params=pltpu.CompilerParams(vmem_limit_bytes=62 * 2**20),
        name="hand_over",
    )(*arrays)


def body_tiles(
    tokens,
    w_query,
    b_query,
    w_key,
    w_value,
    b_value,
    w_out,
    b_out,
    gain_one,
    shift_one,
    w_up,
    b_up,
    w_down,
    b_down,
    gain_two,
    shift_two,
    w_proj,
    segment_ids,
    row_lengths,
    teacher_index,
    teacher_table,
):
    rows_dev, _, width = tokens.shape
    losses, embeddings, *kept = run_first(
        tokens.reshape(rows_dev * SEQ, width),
        (w_query, w_key, w_value, w_out, w_up, w_down, w_proj),
        (b_query, b_value, b_out, gain_one, shift_one, b_down, gain_two, shift_two, b_up),
        segment_ids,
        row_lengths,
        teacher_index,
        teacher_table,
    )
    grad_tokens, *small = run_last(kept, segment_ids, row_lengths)
    (
        grad_tokens,
        embeddings,
        grad_query,
        grad_key,
        grad_value,
        grad_out,
        grad_up,
        grad_down,
        grad_proj,
        grad_query_bias,
        grad_value_bias,
        grad_out_bias,
        grad_gain_first,
        grad_shift_first,
        grad_down_bias,
        grad_gain_second,
        grad_shift_second,
        grad_up_bias,
        losses,
    ) = run_pass(grad_tokens, embeddings.reshape(rows_dev * SEQ, EMBED), *small, losses)
    return (
        losses,
        embeddings.reshape(rows_dev, SEQ, EMBED),
        grad_tokens.reshape(rows_dev, SEQ, width),
        grad_query,
        grad_query_bias,
        grad_key,
        grad_value,
        grad_value_bias,
        grad_out,
        grad_out_bias,
        grad_gain_first,
        grad_shift_first,
        grad_up,
        grad_up_bias,
        grad_down,
        grad_down_bias,
        grad_gain_second,
        grad_shift_second,
        grad_proj,
    )


def solution(mesh):
    in_specs = (
        P(("dp", "fsdp"), None, None),
        P(("dp", "fsdp"), None),
        P(("dp", "fsdp")),
        P(("dp", "fsdp"), None),
        P(("dp", "fsdp"), None),
        P(("dp", "fsdp")),
        P(("dp", "fsdp"), None),
        P(("dp", "fsdp")),
        P(("dp", "fsdp")),
        P(("dp", "fsdp")),
        P(("dp", "fsdp"), None),
        P(("dp", "fsdp")),
        P(("dp", "fsdp"), None),
        P(("dp", "fsdp")),
        P(("dp", "fsdp")),
        P(("dp", "fsdp")),
        P(("dp", "fsdp"), None),
        P(("dp", "fsdp"), None),
        P(("dp", "fsdp")),
        P(("dp", "fsdp"), None),
        P(),
    )
    out_specs = (
        P(("dp", "fsdp")),
        P(("dp", "fsdp"), None, None),
        P(("dp", "fsdp"), None, None),
        P(("dp", "fsdp"), None),
        P(("dp", "fsdp")),
        P(("dp", "fsdp"), None),
        P(("dp", "fsdp"), None),
        P(("dp", "fsdp")),
        P(("dp", "fsdp"), None),
        P(("dp", "fsdp")),
        P(("dp", "fsdp")),
        P(("dp", "fsdp")),
        P(("dp", "fsdp"), None),
        P(("dp", "fsdp")),
        P(("dp", "fsdp"), None),
        P(("dp", "fsdp")),
        P(("dp", "fsdp")),
        P(("dp", "fsdp")),
        P(("dp", "fsdp"), None),
    )
    body = body_tiles if fits(mesh) else body_whole
    return jax.shard_map(body, mesh=mesh, in_specs=in_specs, out_specs=out_specs, check_vma=False)
```

```python
import functools
import math

import jax
import jax.numpy as jnp
from jax import lax
from jax.experimental import pallas as pl
from jax.experimental.pallas import tpu as pltpu
from jax.sharding import PartitionSpec as P

HEADS = 12
HEAD = 64
SEQ = 512
QLEN = 32
NPASS = 8
TABLE = 1024


NORM_EPS = 1e-12
UNIT_EPS = 1e-12
SOFTNESS = 0.1
MASK_FILL = -1000000000.0
ROOT_HALF = 0.7071067811865476
DENSITY_SCALE = 0.3989422804014327


def matmul(left, right):
    return jnp.dot(left, right, preferred_element_type=jnp.float32)


def over_rows(left, right):
    return lax.dot_general(
        left, right, (((0,), (0,)), ((), ())), preferred_element_type=jnp.float32
    )


def against(left, right):
    return lax.dot_general(
        left, right, (((1,), (1,)), ((), ())), preferred_element_type=jnp.float32
    )


def normalise(mixed, gain, shift):
    centred = mixed - jnp.mean(mixed, -1, keepdims=True)
    scaled = lax.rsqrt(jnp.mean(centred * centred, -1, keepdims=True) + NORM_EPS)
    normed = centred * scaled
    return (normed * gain + shift, normed, scaled)


def normalise_back(grad_out, normed, scaled, gain):
    inner = grad_out * gain
    grad_in = scaled * (
        inner
        - jnp.mean(inner, -1, keepdims=True)
        - normed * jnp.mean(inner * normed, -1, keepdims=True)
    )
    return (grad_in, jnp.sum(grad_out * normed, 0), jnp.sum(grad_out, 0))


def gelu_exact(upward):
    return 0.5 * upward * (1.0 + lax.erf(upward * ROOT_HALF))


def gelu_slope(upward):
    return (
        0.5 * (1.0 + lax.erf(upward * ROOT_HALF))
        + upward * jnp.exp(-0.5 * upward * upward) * DENSITY_SCALE
    )


def split_heads(matrix, rows_dev):
    return (
        matrix.reshape(rows_dev, SEQ, HEADS, HEAD)
        .transpose(0, 2, 1, 3)
        .reshape(rows_dev * HEADS, SEQ, HEAD)
    )


def join_heads(stacked, rows_dev):
    return (
        stacked.reshape(rows_dev, HEADS, SEQ, HEAD)
        .transpose(0, 2, 1, 3)
        .reshape(rows_dev * SEQ, HEADS * HEAD)
    )


def collect(sent):
    return (
        lax.all_gather(sent[0], ("dp", "fsdp"), axis=0, tiled=True),
        lax.all_gather(sent[1], ("dp", "fsdp"), axis=0, tiled=True),
        lax.all_gather(sent[2], ("dp", "fsdp"), axis=0, tiled=True),
        lax.all_gather(sent[3], ("dp", "fsdp"), axis=0, tiled=True),
        lax.all_gather(sent[4], ("dp", "fsdp"), axis=0, tiled=True),
        lax.all_gather(sent[5], ("dp", "fsdp"), axis=0, tiled=True),
        lax.all_gather(sent[6], ("dp", "fsdp"), axis=0, tiled=True),
        lax.all_gather(sent[7], ("dp", "fsdp"), axis=0, tiled=True),
        lax.all_gather(sent[8], ("dp", "fsdp"), axis=0, tiled=True),
        lax.all_gather(sent[9], ("dp", "fsdp"), axis=0, tiled=True),
        lax.all_gather(sent[10], ("dp", "fsdp"), axis=0, tiled=True),
        lax.all_gather(sent[11], ("dp", "fsdp"), axis=0, tiled=True),
        lax.all_gather(sent[12], ("dp", "fsdp"), axis=0, tiled=True),
        lax.all_gather(sent[13], ("dp", "fsdp"), axis=0, tiled=True),
        lax.all_gather(sent[14], ("dp", "fsdp"), axis=0, tiled=True),
        lax.all_gather(sent[15], ("dp", "fsdp"), axis=0, tiled=True),
    )


def spread_grads(terms):
    return (
        lax.psum_scatter(terms[0], ("dp", "fsdp"), scatter_dimension=0, tiled=True),
        lax.psum_scatter(terms[1], ("dp", "fsdp"), scatter_dimension=0, tiled=True),
        lax.psum_scatter(terms[2], ("dp", "fsdp"), scatter_dimension=0, tiled=True),
        lax.psum_scatter(terms[3], ("dp", "fsdp"), scatter_dimension=0, tiled=True),
        lax.psum_scatter(terms[4], ("dp", "fsdp"), scatter_dimension=0, tiled=True),
        lax.psum_scatter(terms[5], ("dp", "fsdp"), scatter_dimension=0, tiled=True),
        lax.psum_scatter(terms[6], ("dp", "fsdp"), scatter_dimension=0, tiled=True),
        lax.psum_scatter(terms[7], ("dp", "fsdp"), scatter_dimension=0, tiled=True),
        lax.psum_scatter(terms[8], ("dp", "fsdp"), scatter_dimension=0, tiled=True),
        lax.psum_scatter(terms[9], ("dp", "fsdp"), scatter_dimension=0, tiled=True),
        lax.psum_scatter(terms[10], ("dp", "fsdp"), scatter_dimension=0, tiled=True),
        lax.psum_scatter(terms[11], ("dp", "fsdp"), scatter_dimension=0, tiled=True),
        lax.psum_scatter(terms[12], ("dp", "fsdp"), scatter_dimension=0, tiled=True),
        lax.psum_scatter(terms[13], ("dp", "fsdp"), scatter_dimension=0, tiled=True),
        lax.psum_scatter(terms[14], ("dp", "fsdp"), scatter_dimension=0, tiled=True),
        lax.psum_scatter(terms[15], ("dp", "fsdp"), scatter_dimension=0, tiled=True),
    )


def body_whole(
    tokens,
    w_query,
    b_query,
    w_key,
    w_value,
    b_value,
    w_out,
    b_out,
    gain_one,
    shift_one,
    w_up,
    b_up,
    w_down,
    b_down,
    gain_two,
    shift_two,
    w_proj,
    segment_ids,
    row_lengths,
    teacher_index,
    teacher_table,
):
    rows_dev = tokens.shape[0]
    width = tokens.shape[2]
    scale = 1.0 / math.sqrt(HEAD)
    shards = (
        w_query,
        b_query,
        w_key,
        w_value,
        b_value,
        w_out,
        b_out,
        gain_one,
        shift_one,
        w_up,
        b_up,
        w_down,
        b_down,
        gain_two,
        shift_two,
        w_proj,
    )
    sent = tuple((member.astype(jnp.bfloat16) for member in shards))
    gathered = collect(sent)
    (
        query_mat,
        query_bias,
        key_mat,
        value_mat,
        value_bias,
        out_mat,
        out_bias,
        gain_first,
        shift_first,
        up_mat,
        up_bias,
        down_mat,
        down_bias,
        gain_second,
        shift_second,
        proj_mat,
    ) = gathered

    def visibility(item_index):
        row_index = item_index // HEADS
        segment_row = lax.dynamic_index_in_dim(segment_ids, row_index, 0, keepdims=False)
        length_row = lax.dynamic_index_in_dim(row_lengths, row_index, 0, keepdims=False)
        positions = jnp.arange(SEQ, dtype=jnp.int32)
        return (segment_row[:, None] == segment_row[None, :]) & (positions[None, :] < length_row)

    def attend(inputs):
        query_h, key_h, value_h, item_index = inputs
        scores = jnp.where(visibility(item_index), against(query_h, key_h) * scale, MASK_FILL)
        peak = jnp.max(scores, -1, keepdims=True)
        shifted = jnp.exp(scores - peak)
        totals = jnp.sum(shifted, -1, keepdims=True)
        chances = (shifted / totals).astype(jnp.bfloat16)
        context_h = matmul(chances, value_h).astype(jnp.bfloat16)
        return (context_h, (peak + jnp.log(totals))[:, 0])

    def attend_back(inputs):
        query_h, key_h, value_h, grad_h, logsum, item_index = inputs
        scores = jnp.where(visibility(item_index), against(query_h, key_h) * scale, MASK_FILL)
        chances = jnp.exp(scores - logsum[:, None])
        d_chances = against(grad_h, value_h)
        rowdot = jnp.sum(chances * d_chances, -1, keepdims=True)
        d_scores = (chances * (d_chances - rowdot)).astype(jnp.bfloat16)
        d_query_h = (matmul(d_scores, key_h) * scale).astype(jnp.bfloat16)
        d_key_h = (over_rows(d_scores, query_h) * scale).astype(jnp.bfloat16)
        d_value_h = over_rows(chances.astype(jnp.bfloat16), grad_h).astype(jnp.bfloat16)
        return (d_query_h, d_key_h, d_value_h)

    flat = tokens.reshape(rows_dev * SEQ, width)
    queries = (matmul(flat, query_mat) + query_bias.astype(jnp.float32)).astype(jnp.bfloat16)
    keys_all = matmul(flat, key_mat).astype(jnp.bfloat16)
    values = (matmul(flat, value_mat) + value_bias.astype(jnp.float32)).astype(jnp.bfloat16)
    query_heads = split_heads(queries, rows_dev)
    key_heads = split_heads(keys_all, rows_dev)
    value_heads = split_heads(values, rows_dev)
    items = jnp.arange(rows_dev * HEADS, dtype=jnp.int32)
    context_heads, logsums = lax.map(attend, (query_heads, key_heads, value_heads, items))
    context_low = join_heads(context_heads, rows_dev)
    branch_one = matmul(context_low, out_mat) + out_bias.astype(jnp.float32)
    mid_one = flat.astype(jnp.float32) + branch_one
    hidden_one, normed_one, scaled_one = normalise(
        mid_one, gain_first.astype(jnp.float32), shift_first.astype(jnp.float32)
    )
    hidden_one_low = hidden_one.astype(jnp.bfloat16)
    upward = matmul(hidden_one_low, up_mat) + up_bias.astype(jnp.float32)
    activated = gelu_exact(upward).astype(jnp.bfloat16)
    branch_two = matmul(activated, down_mat) + down_bias.astype(jnp.float32)
    hidden_two, normed_two, scaled_two = normalise(
        hidden_one + branch_two, gain_second.astype(jnp.float32), shift_second.astype(jnp.float32)
    )
    hidden_two_low = hidden_two.astype(jnp.bfloat16)
    raw_embed = matmul(hidden_two_low, proj_mat)
    inverse = lax.rsqrt(jnp.sum(raw_embed * raw_embed, -1, keepdims=True) + UNIT_EPS)
    embeddings = raw_embed * inverse
    embed_dim = embeddings.shape[1]
    embed_low = embeddings.astype(jnp.bfloat16).reshape(rows_dev, SEQ, embed_dim)
    query_low = embed_low[:, :QLEN]
    similar = jnp.einsum("rqc,rsc->rqs", query_low, embed_low, preferred_element_type=jnp.float32)
    positions = jnp.arange(SEQ, dtype=jnp.int32)
    live = positions[None, :] < row_lengths[:, None]
    passages = jnp.arange(1, NPASS + 1, dtype=jnp.int32)
    member = (segment_ids[:, None, :] == passages[None, :, None]) & live[:, None, :]
    masked = jnp.where(member[:, None], similar[:, :, None, :] / SOFTNESS, MASK_FILL)
    peak = jnp.max(masked, -1, keepdims=True)
    shifted = jnp.exp(masked - peak)
    totals = jnp.sum(shifted, -1, keepdims=True)
    student = SOFTNESS * jnp.sum(peak[..., 0] + jnp.log(totals[..., 0]), axis=1)
    choose = teacher_index[..., None] == jnp.arange(TABLE, dtype=jnp.int32)
    teacher = jnp.sum(jnp.where(choose, teacher_table, 0.0), -1)
    teacher_logp = jax.nn.log_softmax(teacher, axis=-1)
    student_logp = jax.nn.log_softmax(student, axis=-1)
    losses = jnp.sum(jnp.exp(teacher_logp) * (teacher_logp - student_logp), -1)
    again = collect(sent)
    (
        query_back,
        query_bias_back,
        key_back,
        value_back,
        value_bias_back,
        out_back,
        out_bias_back,
        gain_first_back,
        shift_first_back,
        up_back,
        up_bias_back,
        down_back,
        down_bias_back,
        gain_second_back,
        shift_second_back,
        proj_back,
    ) = again
    d_student = jnp.exp(student_logp) - jnp.exp(teacher_logp)
    spread_weights = shifted / totals
    d_similar = jnp.einsum("rp,rqps->rqs", d_student, spread_weights).astype(jnp.bfloat16)
    d_embed = jnp.einsum("rqs,rqc->rsc", d_similar, query_low, preferred_element_type=jnp.float32)
    d_query_part = jnp.einsum(
        "rqs,rsc->rqc", d_similar, embed_low, preferred_element_type=jnp.float32
    )
    d_embed = jnp.concatenate([d_embed[:, :QLEN] + d_query_part, d_embed[:, QLEN:]], 1).reshape(
        rows_dev * SEQ, embed_dim
    )
    d_raw = (
        inverse * (d_embed - embeddings * jnp.sum(d_embed * embeddings, -1, keepdims=True))
    ).astype(jnp.bfloat16)
    grad_proj = over_rows(hidden_two_low, d_raw)
    d_hidden_two = against(d_raw, proj_back)
    d_mid_two, grad_gain_second, grad_shift_second = normalise_back(
        d_hidden_two, normed_two, scaled_two, gain_second_back.astype(jnp.float32)
    )
    d_branch_two = d_mid_two.astype(jnp.bfloat16)
    grad_down = over_rows(activated, d_branch_two)
    grad_down_bias = jnp.sum(d_branch_two, 0, dtype=jnp.float32)
    d_upward = (against(d_branch_two, down_back) * gelu_slope(upward)).astype(jnp.bfloat16)
    grad_up = over_rows(hidden_one_low, d_upward)
    grad_up_bias = jnp.sum(d_upward, 0, dtype=jnp.float32)
    d_hidden_one = d_mid_two + against(d_upward, up_back)
    d_mid_one, grad_gain_first, grad_shift_first = normalise_back(
        d_hidden_one, normed_one, scaled_one, gain_first_back.astype(jnp.float32)
    )
    d_branch_one = d_mid_one.astype(jnp.bfloat16)
    grad_out = over_rows(context_low, d_branch_one)
    grad_out_bias = jnp.sum(d_branch_one, 0, dtype=jnp.float32)
    d_context = against(d_branch_one, out_back).astype(jnp.bfloat16)
    d_context_heads = split_heads(d_context, rows_dev)
    d_query_heads, d_key_heads, d_value_heads = lax.map(
        attend_back, (query_heads, key_heads, value_heads, d_context_heads, logsums, items)
    )
    d_queries = join_heads(d_query_heads, rows_dev)
    d_keys = join_heads(d_key_heads, rows_dev)
    d_values = join_heads(d_value_heads, rows_dev)
    grad_query = over_rows(flat, d_queries)
    grad_query_bias = jnp.sum(d_queries, 0, dtype=jnp.float32)
    grad_key = over_rows(flat, d_keys)
    grad_value = over_rows(flat, d_values)
    grad_value_bias = jnp.sum(d_values, 0, dtype=jnp.float32)
    grad_input = (
        d_mid_one
        + against(d_queries, query_back)
        + against(d_keys, key_back)
        + against(d_values, value_back)
    )
    terms = (
        grad_query,
        grad_query_bias,
        grad_key,
        grad_value,
        grad_value_bias,
        grad_out,
        grad_out_bias,
        grad_gain_first,
        grad_shift_first,
        grad_up,
        grad_up_bias,
        grad_down,
        grad_down_bias,
        grad_gain_second,
        grad_shift_second,
        grad_proj,
    )
    owned = spread_grads(terms)
    return (
        losses,
        embeddings.reshape(rows_dev, SEQ, embed_dim),
        grad_input.reshape(rows_dev, SEQ, width),
        owned[0],
        owned[1],
        owned[2],
        owned[3],
        owned[4],
        owned[5],
        owned[6],
        owned[7],
        owned[8],
        owned[9],
        owned[10],
        owned[11],
        owned[12],
        owned[13],
        owned[14],
        owned[15],
    )


MESH = pl.DeviceIdType.MESH
LOG2_E = 1.4426950408889634
EXP2_SCALE = LOG2_E / math.sqrt(HEAD)
SHARDS = 32
CHIPS = 16
WIDTH = 768
HIDDEN = 3072
EMBED = 128
SMALL = 40
PAIRS = HEADS // 2
CHUNK = 256
HALF = 512


def fits(mesh):
    return dict(mesh.shape) == {"dp": 4, "fsdp": 8}


def dotted(left, right, left_dim, right_dim):
    return lax.dot_general(
        left,
        right,
        (((left_dim,), (right_dim,)), ((), ())),
        preferred_element_type=jnp.float32,
    )


def part_of(start, size):
    return pl.ds(pl.multiple_of(start * size, size), size)


def value_of(number):
    return number() if callable(number) else number


def place():
    outer = lax.axis_index("dp")
    inner = lax.axis_index("fsdp")
    return lax.rem(outer, 2), lax.div(outer, 2), lax.div(inner, 2), lax.rem(inner, 2)


def device(x, y, z, c):
    return (y * 2 + x, z * 2 + c)


class Links:
    def __init__(self):
        x, y, z, c = place()
        self.c = c
        self.z = z
        self.chip_own = (y * 2 + x) * 4
        self.chip_x = (y * 2 + 1 - x) * 4
        self.chip_y = ((1 - y) * 2 + x) * 4
        self.chip_d = ((1 - y) * 2 + 1 - x) * 4
        self.to_core = device(x, y, z, 1 - c)
        self.to_x = device(1 - x, y, z, c)
        self.to_y = device(x, 1 - y, z, c)
        self.to_z = [None] + [device(x, y, lax.rem(z + k, 4), c) for k in (1, 2, 3)]
        self.inner = (z == 1) | (z == 2)
        paired = z + 1 - 2 * lax.rem(z, 2)
        self.to_pair = device(x, y, paired, c)
        self.to_middle = device(x, y, jnp.where(self.inner, 3 - z, paired), c)
        far = jnp.where(z < 2, 1, -1)
        near = jnp.where(self.inner, 3 - z, z + 2 * far)
        last = jnp.where(self.inner, 3 - z + far, z + 3 * far)
        self.levels = [z, paired, near, last]
        self.started = []

    def hail(self):
        barrier = pltpu.get_barrier_semaphore()
        self.partners = [self.to_core, self.to_x, self.to_y] + self.to_z[1:]
        for partner in self.partners:
            pl.semaphore_signal(barrier, inc=1, device_id=partner, device_id_type=MESH)

    def greet(self):
        pl.semaphore_wait(pltpu.get_barrier_semaphore(), len(self.partners))

    def level(self, k):
        return lax.rem(self.z + k, 4)

    def send(self, ends, sems, target, inner=False):
        def copy():
            src, dst = ends()
            send_sem, recv_sem = sems()
            return pltpu.make_async_remote_copy(
                src_ref=src,
                dst_ref=dst,
                send_sem=send_sem,
                recv_sem=recv_sem,
                device_id=target,
                device_id_type=MESH,
            )

        def start():
            copy().start()

        def wait():
            copy().wait_send()

        if inner:
            pl.when(self.inner)(start)
            self.started.append(lambda: pl.when(self.inner)(wait))
        else:
            start()
            self.started.append(wait)

    def arrived(self, ref, sems, source):
        pltpu.make_async_remote_copy(
            src_ref=ref,
            dst_ref=ref,
            send_sem=sems[0],
            recv_sem=sems[1],
            device_id=source,
            device_id_type=MESH,
        ).wait_recv()

    def finish(self, first=0):
        for wait in self.started[first:]:
            wait()
        self.started = self.started[:first]


def rows_block(ref, rows, columns, base=0):
    def block(core, chip, count):
        return ref.at[
            pl.ds(pl.multiple_of(chip * rows, rows), count * rows),
            pl.ds(pl.multiple_of(base + core * columns, 128), columns),
        ]

    return block


def lead_block(ref):
    def block(core, chip, count):
        return ref.at[core, pl.ds(chip, count)]

    return block


def column_of(chip):
    return lax.div(chip, 4)


def level_of(chip):
    return lax.rem(chip, 4)


def grid_block(ref, columns, base=0):
    def block(core, chip, count):
        lanes = pl.ds(pl.multiple_of(base + core * columns, 128), columns)
        if count == 4:
            return ref.at[column_of(chip), :, :, lanes]
        if count == 0:
            return ref.at[:, level_of(chip), :, lanes]
        return ref.at[column_of(chip), level_of(chip), :, lanes]

    return block


def lead_grid_block(ref):
    def block(core, chip, count):
        if count == 0:
            return ref.at[core, :, level_of(chip)]
        return ref.at[core, column_of(chip), level_of(chip)]

    return block


class Gather:
    Z, X, Y, FX, FY, C, ZF = 0, 3, 7, 11, 13, 15, 19
    SEMS = 21

    def __init__(self, links, block, sends, recvs, group):
        self.links = links
        self.block = block
        self.sends = sends
        self.recvs = recvs
        self.group = group

    def sems(self, index, there=None):
        there = index if there is None else there
        return self.sends.at[self.group, index], self.recvs.at[self.group, there]

    def ship(self, chip, count, index, target, there=None, inner=False):
        def ends():
            ref = self.block(self.links.c, value_of(chip), count)
            return ref, ref

        self.links.send(ends, lambda: self.sems(index, there), target, inner)

    def step_of(self, column, k):
        return lambda: column + self.links.levels[k]

    def take(self, chip, count, index, source, core=None):
        core = self.links.c if core is None else core
        self.links.arrived(self.block(core, value_of(chip), count), self.sems(index), source)

    def along(self):
        n = self.links
        own = self.step_of(n.chip_own, 0)
        self.ship(own, 1, self.Z, n.to_pair)
        self.ship(own, 1, self.Z + 1, n.to_middle, inner=True)

    def across(self, k):
        n = self.links
        chip = self.step_of(n.chip_own, k)
        if k:
            self.take(chip, 1, self.Z + k - 1, n.to_pair if k == 1 else n.to_middle)
            if k == 1:
                self.ship(chip, 1, self.Z + 2, n.to_middle, inner=True)
            else:
                self.ship(chip, 1, self.ZF + k - 2, n.to_pair, self.Z + k - 1, inner=True)
        self.ship(chip, 1, self.X + k, n.to_x)
        self.ship(chip, 1, self.Y + k, n.to_y)
        if k == 3:
            self.ship(n.chip_own, 4, self.C, n.to_core)

    def onward(self, k):
        n = self.links
        if k < 2:
            chip = self.step_of(n.chip_x, k)
            self.take(chip, 1, self.X + k, n.to_x)
            self.ship(chip, 1, self.FY + k, n.to_y)
        else:
            chip = self.step_of(n.chip_y, k)
            self.take(chip, 1, self.Y + k, n.to_y)
            self.ship(chip, 1, self.FX + k - 2, n.to_x)

    def beside(self):
        n = self.links
        for k in (2, 3):
            self.take(self.step_of(n.chip_x, k), 1, self.X + k, n.to_x)
        self.ship(n.chip_x, 4, self.C + 1, n.to_core)
        for k in (0, 1):
            self.take(self.step_of(n.chip_y, k), 1, self.Y + k, n.to_y)
        self.ship(n.chip_y, 4, self.C + 2, n.to_core)

    def opposite(self):
        n = self.links
        for k in (0, 1):
            self.take(self.step_of(n.chip_d, k), 1, self.FY + k, n.to_y)
        for k in (2, 3):
            self.take(self.step_of(n.chip_d, k), 1, self.FX + k - 2, n.to_x)
        self.ship(n.chip_d, 4, self.C + 3, n.to_core)

    def last(self):
        n = self.links
        for index, chip in enumerate((n.chip_own, n.chip_x, n.chip_y, n.chip_d)):
            self.take(chip, 4, self.C + index, n.to_core, 1 - n.c)


class LevelGather(Gather):
    X, Y, F, Z, ZF, C = 0, 1, 2, 3, 6, 8

    def own(self):
        n = self.links
        chip = self.step_of(n.chip_own, 0)
        self.ship(chip, 1, self.X, n.to_x)
        self.ship(chip, 1, self.Y, n.to_y)

    def diag(self):
        n = self.links
        chip = self.step_of(n.chip_x, 0)
        self.take(chip, 1, self.X, n.to_x)
        self.ship(chip, 1, self.F, n.to_y)

    def set(self, k):
        n = self.links
        level = self.step_of(n.chip_own, k)
        if k == 0:
            self.take(self.step_of(n.chip_y, 0), 1, self.Y, n.to_y)
            self.take(self.step_of(n.chip_d, 0), 1, self.F, n.to_y)
            self.ship(level, 0, self.Z, n.to_pair)
            self.ship(level, 0, self.Z + 1, n.to_middle, inner=True)
        else:
            self.take(level, 0, self.Z + k - 1, n.to_pair if k == 1 else n.to_middle)
            if k == 1:
                self.ship(level, 0, self.Z + 2, n.to_middle, inner=True)
            else:
                self.ship(level, 0, self.ZF + k - 2, n.to_pair, self.Z + k - 1, inner=True)
        self.ship(level, 0, self.C + k, n.to_core)

    def last(self):
        n = self.links
        for k in range(4):
            self.take(self.step_of(n.chip_own, k), 0, self.C + k, n.to_core, 1 - n.c)


class Joined:
    def join_from(self, stage, sends, recvs, index):
        self.parts = (stage, sends, recvs, index)
        return self

    def join(self):
        if self.parts is None:
            return
        n = self.links
        stage, sends, recvs, index = self.parts
        self.parts = None
        rows = stage.shape[0] // 2
        here = stage.at[part_of(1 - n.c, rows), :]
        n.arrived(here, (sends.at[index], recvs.at[index]), n.to_core)
        self.block(n.c, n.chip_own + n.z, 1)[...] = stage[...].astype(jnp.bfloat16)


class JoinedGather(Joined, Gather):
    def along(self):
        self.join()
        super().along()

    def across(self, k):
        self.join()
        super().across(k)


class JoinedLevelGather(Joined, LevelGather):
    def own(self):
        self.join()
        super().own()


class Scatter:
    C, DY, DX, OX, OY, Z, F = 0, 4, 5, 6, 8, 10, 13
    SEMS = 14

    def __init__(self, links, block, mine, rows, held, fin, deliver, sends, recvs, group, whole=False):
        self.links = links
        self.block = block
        self.mine = mine
        self.rows = rows
        self.part, self.d_y, self.d_x, self.o_x, self.o_y, self.z_in = held
        self.fin = fin
        self.deliver = deliver
        self.sends = sends
        self.recvs = recvs
        self.group = group
        n = links
        self.sent = []
        self.gone = []
        self.once = whole
        self.span = 4 if whole else 2
        self.columns = (n.chip_d, n.chip_x, n.chip_y, n.chip_own)

    def at(self, ref, start, count):
        if isinstance(start, int):
            return ref.at[pl.ds(start * self.rows, count * self.rows)]
        return ref.at[pl.ds(pl.multiple_of(start * self.rows, self.rows), count * self.rows)]

    def sems(self, index, there=None):
        there = index if there is None else there
        return self.sends.at[self.group, index], self.recvs.at[self.group, there]

    def ship(self, ends, index, target, there=None):
        self.links.send(ends, lambda: self.sems(index, there), target)
        self.gone.append(self.links.started[-1])

    def done(self):
        for wait in self.gone:
            if wait in self.links.started:
                wait()
                self.links.started.remove(wait)
        self.gone = []

    def ship_part(self, start, count, ref, there, index, target):
        self.ship(
            lambda: (self.at(self.part, value_of(start), count), self.at(ref, there, count)),
            index,
            target,
        )

    def take(self, ref, start, count, index, source):
        self.links.arrived(self.at(ref, start, count), self.sems(index), source)

    def add(self, count, start, *others):
        size = min(count, self.span)

        def step(i, carry):
            here = self.at(self.part, start + i * size, size)
            total = here[...]
            for other in others:
                total = total + other(i * size, size)[...]
            here[...] = total
            return carry

        lax.fori_loop(0, count // size, step, 0)

    def first(self):
        n = self.links
        if self.once:
            self.ship(lambda: (self.block(1 - n.c, 0, 16), self.at(self.part, 0, 16)), self.C, n.to_core)
            return
        for index, chip in enumerate(self.columns):

            def ends(chip=chip):
                return self.block(1 - n.c, chip, 4), self.at(self.part, chip, 4)

            self.ship(ends, self.C + index, n.to_core)
            self.sent.append(n.started[-1])

    def second(self, index):
        n = self.links
        if self.once:
            self.take(self.part, 0, 16, self.C, n.to_core)
            self.add(16, 0, self.mine)
            for index in range(3):
                self.pass_on(index)
            return
        chip = self.columns[index]
        self.take(self.part, chip, 4, self.C + index, n.to_core)
        self.add(4, chip, lambda i, size: self.mine(chip + i, size))
        self.pass_on(index)

    def pass_on(self, index):
        n = self.links
        chip = self.columns[index]
        if index == 0:
            self.ship_part(chip, 2, self.d_y, 0, self.DY, n.to_y)
            self.ship_part(lambda: chip + 2, 2, self.d_x, 0, self.DX, n.to_x)
        elif index == 1:
            self.ship_part(lambda: chip + 2, 2, self.o_x, 2, self.OX + 1, n.to_x)
        elif index == 2:
            self.ship_part(chip, 2, self.o_y, 0, self.OY, n.to_y)

    def third(self, index):
        n = self.links
        if index == 0:
            self.take(self.d_y, 0, 2, self.DY, n.to_y)
            self.add(2, n.chip_x, lambda i, size: self.at(self.d_y, i, size))
            self.ship_part(n.chip_x, 2, self.o_x, 0, self.OX, n.to_x)
            return
        self.take(self.d_x, 0, 2, self.DX, n.to_x)
        self.add(2, n.chip_y + 2, lambda i, size: self.at(self.d_x, i, size))
        self.ship_part(lambda: n.chip_y + 2, 2, self.o_y, 2, self.OY + 1, n.to_y)

    def fourth(self):
        n = self.links
        self.take(self.o_x, 2, 2, self.OX + 1, n.to_x)
        self.take(self.o_y, 0, 2, self.OY, n.to_y)
        self.take(self.o_x, 0, 2, self.OX, n.to_x)
        self.take(self.o_y, 2, 2, self.OY + 1, n.to_y)
        self.add(
            4,
            n.chip_own,
            lambda i, size: self.at(self.o_x, i, size),
            lambda i, size: self.at(self.o_y, i, size),
        )
        for j in (1, 2, 3):

            def ends(j=j):
                return (
                    self.at(self.part, n.chip_own + n.level(j), 1),
                    self.at(self.z_in, 3 - j, 1),
                )

            self.ship(ends, self.Z + j - 1, n.to_z[j], self.Z + 3 - j)

    def fifth(self):
        n = self.links
        total = self.at(self.part, n.chip_own + n.z, 1)[...].astype(jnp.float32)
        for k in (1, 2, 3):
            self.take(self.z_in, k - 1, 1, self.Z + k - 1, n.to_z[k])
            total = total + self.at(self.z_in, k - 1, 1)[...].astype(jnp.float32)
        return total

    def trade(self):
        if self.fin is None:
            self.deliver(self.fifth())
            return
        fin, fin_in = self.fin
        n = self.links
        rows = self.rows // 2
        fin[...] = self.fifth()
        self.ship(lambda: (fin.at[part_of(1 - n.c, rows)], fin_in), self.F, n.to_core)

    def whole(self):
        if self.fin is None:
            return
        fin, fin_in = self.fin
        n = self.links
        rows = self.rows // 2
        n.arrived(fin_in, self.sems(self.F), n.to_core)
        mine = fin[part_of(n.c, rows), :]
        theirs = fin_in[...]
        self.deliver(jnp.where(n.c == 0, mine, theirs), jnp.where(n.c == 0, theirs, mine))

    def settle(self):
        for wait in self.sent:
            if wait in self.links.started:
                wait()
                self.links.started.remove(wait)
        self.sent = []


def spread_lanes(parts, step):
    lane = lax.broadcasted_iota(jnp.int32, (8, 128), 1)
    tiles = [None] * (len(parts) * step // 128)

    def add(index, value):
        tiles[index] = value if tiles[index] is None else tiles[index] + value

    for i, part in enumerate(parts):
        part = jnp.where(lane < step, part, 0.0)
        index, shift = i * step // 128, i * step % 128
        rolled = pltpu.roll(part, shift, 1) if shift else part
        if shift + step <= 128:
            add(index, rolled)
        else:
            add(index, jnp.where(lane >= shift, rolled, 0.0))
            add(index + 1, jnp.where(lane < shift, rolled, 0.0))
    return tiles


def pick_lanes(tiles, step, count):
    parts = []
    lane = lax.broadcasted_iota(jnp.int32, (8, 128), 1)
    for i in range(count):
        index, shift = i * step // 128, i * step % 128
        part = pltpu.roll(tiles[index], 128 - shift, 1) if shift else tiles[index]
        if shift + step > 128:
            after = pltpu.roll(tiles[index + 1], 128 - shift, 1)
            part = jnp.where(lane < 128 - shift, part, after)
        parts.append(jnp.where(lane < step, part, 0.0))
    return parts


def rounded(value):
    return value.astype(jnp.bfloat16).astype(jnp.float32)


def segment_forms(segment_ids, row_lengths, r):
    segment = segment_ids[r : r + 1, :].astype(jnp.float32)
    position = lax.broadcasted_iota(jnp.int32, (1, SEQ), 1)
    return segment, jnp.where(position < row_lengths[r], segment, -1.0)


def upright(row):
    return jnp.broadcast_to(row, (128, SEQ)).T[:, 0:1]


def mask_of(rows_form, columns_form):
    return jnp.where(upright(rows_form) == columns_form, 0.0, MASK_FILL)


FIRST_PLAN = (
    "a.along",
    "t.own",
    "a.across0",
    "t.diag",
    "u.along",
    "o.own",
    "u.across0",
    "a.across1",
    "t.set0",
    "a.across2",
    "bias",
    "t.set1",
    "a.across3",
    "a.onward0",
    "a.onward1",
    "d.along",
    "turn",
    "a.onward2",
    "t.set2",
    "a.onward3",
    "t.set3",
    "o.diag",
    "a.beside",
    "u.across1",
    "u.across2",
    "a.opposite",
    "u.across3",
    "t.last",
    "u.onward0",
    "o.set0",
    "vec",
    "u.onward1",
    "a.last",
    "project",
    "d.across1",
    "p0",
    "p1",
    "p2",
    "p3",
    "u.onward2",
    "attend",
    "d.across2",
    "d.across0",
    "a0",
    "a1",
    "a2",
    "u.onward3",
    "a3",
    "o.set1",
    "o.set2",
    "a4",
    "a5",
    "a6",
    "a7",
    "o.set3",
    "a8",
    "u.beside",
    "a9",
    "a10",
    "d.across3",
    "d.onward0",
    "o.last",
    "a11",
    "mix",
    "d.onward2",
    "u.opposite",
    "m0",
    "d.onward1",
    "m1",
    "u.last",
    "widen",
    "w0",
    "w1",
    "d.onward3",
    "w2",
    "w3",
    "d.beside",
    "w4",
    "w5",
    "w6",
    "w7",
    "w8",
    "d.opposite",
    "w9",
    "w10",
    "w11",
    "d.last",
    "narrow",
)

LAST_PLAN = (
    "pre",
    "d.first",
    "ld",
    "w0",
    "d.second0",
    "w1",
    "d.second1",
    "w2",
    "w3",
    "wu0",
    "wu1",
    "d.second2",
    "wu2",
    "d.third0",
    "u.first",
    "bc",
    "d.third1",
    "d.second3",
    "n0",
    "u.second0",
    "n1",
    "misc",
    "u.second1",
    "g0",
    "u.second2",
    "rd",
    "u.second3",
    "wo0",
    "a0",
    "a1",
    "d.fourth",
    "a2",
    "o.first",
    "u.third0",
    "a3",
    "u.third1",
    "a4",
    "a5",
    "a6",
    "a7",
    "wm0",
    "wm1",
    "o.second0",
    "u.fourth",
    "wm2",
    "m.first",
    "a8",
    "o.third0",
    "o.third1",
    "a9",
    "m.second0",
    "a10",
    "m.second1",
    "m.second2",
    "a11",
    "wr0",
    "m.third0",
    "m.third1",
    "m.second3",
    "wr1",
    "o.fourth",
    "wr2",
    "r.first",
    "vec",
    "t.first",
    "r.second0",
    "d.trade",
    "m.fourth",
    "r.third1",
    "r.third0",
    "t.second0",
    "o.trade",
    "r.fourth",
    "u.trade",
    "t.third0",
    "t.third1",
    "b0",
    "t.fourth",
    "b1",
    "d.done",
    "o.done",
    "u.done",
    "r.trade",
    "m.trade",
    "t.trade",
    "u.whole",
    "r.whole",
    "d.whole",
    "m.whole",
    "o.whole",
    "t.whole",
    "end",
)


class Plan:
    def __init__(self, names, groups):
        self.groups = groups
        self.inside = {}
        self.queue = list(names)

    def call(self, name):
        group, method = name.split(".")
        if method[-1].isdigit():
            getattr(self.groups[group], method[:-1])(int(method[-1]))
        else:
            getattr(self.groups[group], method)()

    def until(self, name):
        while True:
            step = self.queue.pop(0)
            if step == name:
                return
            self.call(step)

    def loop(self, letter, first, count, body):
        steps = {}
        self.until(f"{letter}{first}")
        for index in range(first, first + count):
            steps[index] = []
            ahead = f"{letter}{index + 1}"
            while self.queue[0] != ahead and "." in self.queue[0]:
                steps[index].append(self.queue.pop(0))
            if index + 1 < first + count:
                self.queue.pop(0)

        def run(step, carry):
            body(step)
            for index, names in steps.items():
                if names:

                    @pl.when(step == index)
                    def _(names=names):
                        for name in names:
                            self.call(name)

            return carry

        lax.fori_loop(first, first + count, run, 0)


def lanes_in_head(shape):
    return lax.broadcasted_iota(jnp.int32, shape, 1) & (HEAD - 1)


def low_head(shape):
    return lax.broadcasted_iota(jnp.int32, shape, 1) < HEAD


def two_parts(value):
    first = rounded(value)
    return first, value - first


def three_parts(value):
    first, rest = two_parts(value)
    second, third = two_parts(rest)
    return first, second, third


PARTS = 16


def query_codes(segment):
    lane = lanes_in_head((SEQ, 128)).astype(jnp.float32)
    return jnp.where(lane == upright(segment), 1.0, 0.0).astype(jnp.bfloat16)


def key_codes(live):
    lane = lanes_in_head((SEQ, 128))
    hidden = jnp.where(lane.astype(jnp.float32) == upright(live), 0.0, MASK_FILL)
    parts = jnp.where((lane >= PARTS) & (lane < PARTS + 3), 1.0, 0.0)
    return jnp.where(lane <= NPASS, hidden, parts).astype(jnp.bfloat16)


def attend_pair(r, p, qkv, context, codes, bias, segments):
    rows = part_of(r, SEQ)
    columns = pl.multiple_of(p * 128, 128)
    query = qkv[rows, pl.ds(columns, 128)]
    key = qkv[rows, pl.ds(columns + WIDTH, 128)]
    value = qkv[rows, pl.ds(columns + 2 * WIDTH, 128)]
    low = low_head((SEQ, 128))
    zero = jnp.zeros_like(key)
    outs, sums = [], []
    for j in range(2):
        key_j = jnp.where(low, key, zero) if j == 0 else jnp.where(low, zero, key)
        scores = dotted(query, key_j, 1, 1) * EXP2_SCALE + bias[rows, 0:SEQ]
        peak = jnp.max(scores, -1, keepdims=True)
        shifted = jnp.exp2(scores - peak)
        total = jnp.sum(shifted, -1, keepdims=True)
        out = dotted(shifted.astype(jnp.bfloat16), value, 1, 0)
        outs.append(out * (1.0 / total))
        sums.append(peak + jnp.log2(total))
    context[rows, pl.ds(columns, 128)] = jnp.where(low, outs[0], outs[1]).astype(jnp.bfloat16)
    first, second, third = three_parts(jnp.where(low, sums[1], sums[0]) * (-1.0 / EXP2_SCALE))
    lane = lanes_in_head((SEQ, 128))
    code = jnp.where(lane == PARTS + 2, third, segments[rows, :].astype(jnp.float32))
    code = jnp.where(lane == PARTS + 1, second, code)
    code = jnp.where(lane == PARTS, first, code)
    codes[rows, pl.ds(columns, 128)] = code.astype(jnp.bfloat16)


def dot_codes(p, context, d_context, codes):
    columns = part_of(p, 128)
    both = context[:, columns].astype(jnp.float32) * d_context[:, columns].astype(jnp.float32)
    first, second = two_parts(both)
    shape = (128, 128)
    other = low_head(shape) != (lax.broadcasted_iota(jnp.int32, shape, 0) < HEAD)
    other = jnp.where(other, -1.0, 0.0).astype(jnp.bfloat16)
    total = dotted(first.astype(jnp.bfloat16), other, 1, 0)
    total = total + dotted(second.astype(jnp.bfloat16), other, 1, 0)
    first, second = two_parts(total)
    lane = lanes_in_head(total.shape)
    code = jnp.where(lane == PARTS, first, jnp.where(lane == PARTS + 1, second, 0.0))
    codes[:, columns] = code.astype(jnp.bfloat16)


def pick_head(masks, j, value, code):
    return value * masks[j] + code * masks[1 - j]


def attend_back_pair(r, p, qkv, d_context, query_code, grad_code, key_code, value_code, lows):
    rows = part_of(r, SEQ)
    columns = pl.multiple_of(p * 128, 128)
    query = qkv[rows, pl.ds(columns, 128)]
    key = qkv[rows, pl.ds(columns + WIDTH, 128)]
    value = qkv[rows, pl.ds(columns + 2 * WIDTH, 128)]
    grad = d_context[rows, pl.ds(columns, 128)]
    query_c = query_code[rows, pl.ds(columns, 128)]
    grad_c = grad_code[rows, pl.ds(columns, 128)]
    key_c = key_code[rows, :]
    value_c = value_code[...]
    masks = (lows[0], lows[1])
    d_query, d_key, d_value = [], [], []
    for j in range(2):
        scores = dotted(pick_head(masks, j, key, key_c), pick_head(masks, j, query, query_c), 1, 1)
        chances = jnp.exp2(scores * EXP2_SCALE)
        d_chances = dotted(
            pick_head(masks, j, value, value_c), pick_head(masks, j, grad, grad_c), 1, 1
        )
        d_scores = (chances * d_chances).astype(jnp.bfloat16)
        d_value.append(dotted(chances.astype(jnp.bfloat16), grad, 1, 0))
        d_key.append(dotted(d_scores, query, 1, 0))
        d_query.append(dotted(d_scores, key, 0, 0))
    low = low_head((SEQ, 128))
    scale = 1.0 / math.sqrt(HEAD)
    low_type = jnp.bfloat16
    qkv[rows, pl.ds(columns, 128)] = (jnp.where(low, d_query[0], d_query[1]) * scale).astype(
        low_type
    )
    qkv[rows, pl.ds(columns + WIDTH, 128)] = (
        jnp.where(low, d_key[0], d_key[1]) * scale
    ).astype(low_type)
    qkv[rows, pl.ds(columns + 2 * WIDTH, 128)] = jnp.where(low, d_value[0], d_value[1]).astype(
        low_type
    )


def norm_parts(mixed):
    centred = mixed - jnp.mean(mixed, -1, keepdims=True)
    scaled = lax.rsqrt(jnp.mean(centred * centred, -1, keepdims=True) + NORM_EPS)
    return centred * scaled, scaled


def norm_back(grad_out, normed, scaled, gain):
    inner = grad_out * gain
    return scaled * (
        inner
        - jnp.mean(inner, -1, keepdims=True)
        - normed * jnp.mean(inner * normed, -1, keepdims=True)
    )


def halves(links, src, stage, sends, recvs, index):
    rows, width = src.shape
    columns = width // 2

    def ends():
        return src.at[:, part_of(1 - links.c, columns)], stage.at[part_of(links.c, rows), :]

    links.send(ends, lambda: (sends.at[index], recvs.at[index]), links.to_core)
    stage[part_of(links.c, rows), :] = src[:, part_of(links.c, columns)]


def passage_loss(similar, live, teacher_index, teacher_table):
    rows_dev = similar.shape[0] // QLEN
    scores = similar * (1.0 / SOFTNESS)
    inside, shares, student, teacher = [], [], [], []
    for p in range(NPASS):
        member = live == float(p + 1)
        masked = jnp.where(member, scores, MASK_FILL)
        peak = jnp.max(masked, -1, keepdims=True)
        shifted = jnp.exp(masked - peak)
        total = jnp.sum(shifted, -1, keepdims=True)
        inside.append(jnp.where(member, shifted, 0.0))
        shares.append(1.0 / total)
        sums = peak + jnp.log(total)
        student.append(
            [
                SOFTNESS * jnp.sum(sums[r * QLEN : (r + 1) * QLEN], axis=0, keepdims=True)
                for r in range(rows_dev)
            ]
        )
        teacher.append(
            [
                jnp.full((1, 1), teacher_table[teacher_index[r, p]], jnp.float32)
                for r in range(rows_dev)
            ]
        )

    def log_softmax(values):
        peak = functools.reduce(jnp.maximum, values)
        total = sum(jnp.exp(value - peak) for value in values)
        return [value - peak - jnp.log(total) for value in values]

    losses, slopes = [], []
    for r in range(rows_dev):
        ours = log_softmax([row[r] for row in student])
        theirs = log_softmax([row[r] for row in teacher])
        losses.append(sum(jnp.exp(t) * (t - s) for t, s in zip(theirs, ours)))
        slopes.append([jnp.broadcast_to(jnp.exp(s) - jnp.exp(t), (QLEN, 1)) for t, s in zip(theirs, ours)])
    d_similar = sum(
        part * (share * jnp.concatenate([row[p] for row in slopes], axis=0))
        for p, (part, share) in enumerate(zip(inside, shares))
    )
    return losses, d_similar


def first_kernel(*refs):
    given = refs[:18]
    row_lengths, teacher_index, teacher_table = refs[18:21]
    (
        losses,
        embeddings_hbm,
        attn_hbm,
        up_hbm,
        down_hbm,
        turned_hbm,
        qkv_hbm,
        context_hbm,
        low_one_hbm,
        normed_one_hbm,
        slope_hbm,
        d_mid_hbm,
        d_branch_hbm,
        grad_down_hbm,
        codes_hbm,
        scaled_one_hbm,
        vectors_hbm,
        grad_vectors_hbm,
        grad_proj_hbm,
    ) = refs[21:40]
    (
        attn_mat,
        up_mat,
        down_mat,
        turned,
        qkv,
        context,
        low_one,
        normed_one,
        slope,
        activated,
        d_mid,
        d_branch,
        grad_down,
        small_all,
        cat_attn,
        stage_attn,
        stage_out,
        stage_up,
        stage_down,
        proj,
        up_bias,
        scaled_two,
        d_raw,
        codes,
        segments,
        sends,
        recvs,
        half_sends,
        half_recvs,
        local_sems,
        grad_sems,
        embeddings,
        scaled_one,
        vectors,
        grad_vectors,
        grad_proj,
        given_sems,
        *taken,
    ) = refs[40:]
    (
        tokens,
        w_query,
        w_key,
        w_value,
        w_out,
        w_up,
        w_down,
        w_proj,
        *vector_refs,
        b_up,
        segment_ids,
    ) = taken
    count = tokens.shape[0]
    rows_dev = count // SEQ
    links = Links()
    links.hail()
    loads = [
        pltpu.make_async_copy(src, dst, given_sems.at[index])
        for index, (src, dst) in enumerate(zip(given, taken))
    ]
    later = (0, len(loads) - 1)
    for index, load in enumerate(loads):
        if index not in later:
            load.start()
    for index in later:
        loads[index].start()

    def gather(kind, block, group, stage):
        return kind(links, block, sends, recvs, group).join_from(
            stage, half_sends, half_recvs, group
        )

    attn = gather(JoinedGather, grid_block(attn_mat, 1152), 0, stage_attn)
    out = gather(JoinedLevelGather, grid_block(attn_mat, 384, 3 * WIDTH), 1, stage_out)
    up = gather(JoinedGather, rows_block(up_mat, 48, 1536), 2, stage_up)
    down = gather(JoinedGather, rows_block(down_mat, 192, 384), 3, stage_down)
    tiny = LevelGather(links, lead_grid_block(small_all), sends, recvs, 4)
    own_chip = links.chip_own + links.z
    kept = []

    def keep(src, dst):
        copy = pltpu.make_async_copy(src, dst, local_sems.at[len(kept)])
        copy.start()
        kept.append(copy)

    for index, load in enumerate(loads):
        if index not in later:
            load.wait()
    for index, ref in enumerate((w_query, w_key, w_value)):
        cat_attn[:, index * WIDTH : (index + 1) * WIDTH] = ref[...]
    own_small = tiny.block(links.c, own_chip, 1)
    own_small[0:24, :] = w_proj[...]
    own_small[24:40, :] = jnp.zeros((16, 128), jnp.float32)
    for index, ref in enumerate(vector_refs):
        own_small[24 + index : 25 + index, 0:24] = ref[...].reshape(1, 24)
    own_small[32:33, 0:96] = b_up[...].reshape(1, 96)

    links.greet()
    halves(links, cat_attn, stage_attn, half_sends, half_recvs, 0)
    halves(links, w_out, stage_out, half_sends, half_recvs, 1)
    halves(links, w_up, stage_up, half_sends, half_recvs, 2)
    halves(links, w_down, stage_down, half_sends, half_recvs, 3)
    plan = Plan(FIRST_PLAN, {"a": attn, "o": out, "u": up, "d": down, "t": tiny, "l": links})
    plan.until("bias")
    for index in later:
        loads[index].wait()
    live_rows = []
    for r in range(rows_dev):
        segment, live = segment_forms(segment_ids, row_lengths, r)
        live_rows.append(live)
        d_mid[r * SEQ : (r + 1) * SEQ, 0:SEQ] = mask_of(segment, live)
        segments[r * SEQ : (r + 1) * SEQ, :] = query_codes(segment)
    plan.until("turn")
    turned[...] = tokens[...].T
    keep(turned, turned_hbm)
    plan.until("vec")
    cores = [(i % 2, i // 8, i // 2 % 4) for i in range(SHARDS)]
    for index, tile in enumerate(spread_lanes([small_all[c, n, m, 24:32, :] for c, n, m in cores], 24)):
        vectors[:, index * 128 : (index + 1) * 128] = rounded(tile)
    for index, tile in enumerate(spread_lanes([small_all[c, n, m, 32:40, :] for c, n, m in cores], 96)):
        up_bias[:, index * 128 : (index + 1) * 128] = rounded(tile)
    for r in range(CHIPS):
        both = [small_all[c, r // 4, r % 4, 0:24, :] for c in range(2)]
        both = jnp.concatenate(both, axis=0)
        proj[r * 48 : (r + 1) * 48, :] = both.astype(jnp.bfloat16)
    keep(vectors, vectors_hbm)
    plan.until("project")

    def project(step):
        rows = part_of(step, CHUNK)
        weights = attn_mat[:, :, :, 0 : 3 * WIDTH].reshape(WIDTH, 3 * WIDTH)
        value = dotted(tokens[rows, :], weights, 1, 0)
        qkv[rows, 0:WIDTH] = (value[:, 0:WIDTH] + vectors[0:1, :]).astype(jnp.bfloat16)
        qkv[rows, WIDTH : 2 * WIDTH] = value[:, WIDTH : 2 * WIDTH].astype(jnp.bfloat16)
        qkv[rows, 2 * WIDTH :] = (value[:, 2 * WIDTH :] + vectors[1:2, :]).astype(jnp.bfloat16)

    plan.loop("p", 0, count // CHUNK, project)
    keep(qkv, qkv_hbm)
    plan.until("attend")

    def attend(item):
        r, p = lax.div(item, PAIRS), lax.rem(item, PAIRS)
        attend_pair(r, p, qkv, context, codes, d_mid, segments)

    plan.loop("a", 0, rows_dev * PAIRS, attend)
    keep(context, context_hbm)
    keep(codes, codes_hbm)
    plan.until("mix")
    keep(attn_mat, attn_hbm)

    def mix(step):
        rows = part_of(step, HALF)
        weights = attn_mat[:, :, :, 3 * WIDTH :].reshape(WIDTH, WIDTH)
        mixed = dotted(context[rows, :], weights, 1, 0) + vectors[2:3, :]
        normed, scaled = norm_parts(tokens[rows, :].astype(jnp.float32) + mixed)
        normed_one[rows, :] = normed
        scaled_one[rows, :] = jnp.broadcast_to(scaled, (HALF, 128))
        low_one[rows, :] = (normed * vectors[3:4, :] + vectors[4:5, :]).astype(jnp.bfloat16)

    plan.loop("m", 0, count // HALF, mix)
    keep(normed_one, normed_one_hbm)
    keep(scaled_one, scaled_one_hbm)
    keep(low_one, low_one_hbm)
    plan.until("widen")
    keep(up_mat, up_hbm)

    def widen(step):
        columns = part_of(step, CHUNK)
        upward = dotted(low_one[...], up_mat[:, columns], 1, 0) + up_bias[0:1, columns]
        chance = 0.5 * (1.0 + lax.erf(upward * ROOT_HALF))
        density = jnp.exp2(upward * upward * (-0.5 * LOG2_E)) * DENSITY_SCALE
        activated[:, columns] = (upward * chance).astype(jnp.bfloat16)
        slope[:, columns] = (chance + upward * density).astype(jnp.bfloat16)

    plan.loop("w", 0, HIDDEN // CHUNK, widen)
    keep(slope, slope_hbm)
    plan.until("narrow")
    keep(down_mat, down_hbm)

    grad_vectors[...] = jnp.zeros_like(grad_vectors)
    for r in range(rows_dev):
        rows = slice(r * SEQ, (r + 1) * SEQ)
        mixed = dotted(activated[rows, :], down_mat[...], 1, 0) + vectors[5:6, :]
        mixed = mixed + (normed_one[rows, :] * vectors[3:4, :] + vectors[4:5, :])
        normed, scaled = norm_parts(mixed)
        d_mid[rows, :] = normed
        scaled_two[rows, :] = jnp.broadcast_to(scaled, (SEQ, 128))
        d_branch[rows, :] = (normed * vectors[6:7, :] + vectors[7:8, :]).astype(jnp.bfloat16)
    raw = dotted(d_branch[...], proj[...], 1, 0)
    inverse = lax.rsqrt(jnp.sum(raw * raw, -1, keepdims=True) + UNIT_EPS)
    embedded = raw * inverse
    embeddings[...] = embedded.reshape(rows_dev, SEQ, EMBED)
    keep(embeddings, embeddings_hbm)
    low_embed = embedded.astype(jnp.bfloat16)
    starts = [r * SEQ for r in range(rows_dev)]
    heads = [low_embed[start : start + QLEN] for start in starts]
    wholes = [low_embed[start : start + SEQ] for start in starts]
    similar = jnp.concatenate([dotted(h, w, 1, 1) for h, w in zip(heads, wholes)], axis=0)
    live = jnp.concatenate([jnp.broadcast_to(row, (QLEN, SEQ)) for row in live_rows], axis=0)
    row_losses, d_similar = passage_loss(similar, live, teacher_index, teacher_table)
    for r in range(rows_dev):
        losses[r] = row_losses[r][0, 0]
    d_similar = d_similar.astype(jnp.bfloat16)
    d_parts = []
    for r in range(rows_dev):
        d_row = d_similar[r * QLEN : (r + 1) * QLEN]
        d_whole = dotted(d_row, heads[r], 0, 0)
        d_parts += [d_whole[0:QLEN] + dotted(d_row, wholes[r], 1, 0), d_whole[QLEN:]]
    d_embed = jnp.concatenate(d_parts, axis=0)
    along = jnp.sum(d_embed * embedded, -1, keepdims=True)
    d_raw[...] = (inverse * (d_embed - embedded * along)).astype(jnp.bfloat16)
    grad_proj[...] = dotted(d_branch[...], d_raw[...], 0, 0)
    keep(grad_proj, grad_proj_hbm)

    def unmix(step, carry):
        rows = part_of(step, CHUNK)
        d_hidden = dotted(d_raw[rows, :], proj[...], 1, 1)
        normed = d_mid[rows, :]
        d_mixed = norm_back(d_hidden, normed, scaled_two[rows, 0:1], vectors[6:7, :])
        low_mixed = d_mixed.astype(jnp.bfloat16)
        d_mid[rows, :] = d_mixed
        d_branch[rows, :] = low_mixed
        grad_vectors[5:6, :] += jnp.sum(low_mixed.astype(jnp.float32), 0, keepdims=True)
        grad_vectors[6:7, :] += jnp.sum(d_hidden * normed, 0, keepdims=True)
        grad_vectors[7:8, :] += jnp.sum(d_hidden, 0, keepdims=True)
        return carry

    lax.fori_loop(0, count // CHUNK, unmix, 0)
    keep(grad_vectors, grad_vectors_hbm)
    keep(d_mid, d_mid_hbm)
    keep(d_branch, d_branch_hbm)

    def grad_copy(step, slot):
        return pltpu.make_async_copy(
            grad_down.at[slot], grad_down_hbm.at[part_of(step, WIDTH), :], grad_sems.at[slot]
        )

    def weigh(step, carry):
        slot = lax.rem(step, 2)

        @pl.when(step >= 2)
        def _():
            grad_copy(step - 2, slot).wait()

        part = activated[:, part_of(step, WIDTH)]
        grad_down[slot] = dotted(part, d_branch[...], 0, 0).astype(jnp.bfloat16)
        grad_copy(step, slot).start()
        return carry

    steps = HIDDEN // WIDTH
    lax.fori_loop(0, steps, weigh, 0)
    links.finish()
    for step in (steps - 2, steps - 1):
        grad_copy(step, step % 2).wait()
    for copy in kept:
        copy.wait()


def run_first(tokens, weights, vectors, segment_ids, row_lengths, teacher_index, teacher_table):
    count = tokens.shape[0]
    rows_dev = count // SEQ
    smem = pl.BlockSpec(memory_space=pltpu.SMEM)
    anywhere = pl.BlockSpec(memory_space=pl.ANY)
    low = jnp.bfloat16
    wide = jnp.float32

    def array(kind, *shape):
        return jax.ShapeDtypeStruct(shape, kind)

    return pl.pallas_call(
        first_kernel,
        out_shape=[
            array(wide, rows_dev),
            array(wide, rows_dev, SEQ, EMBED),
            array(low, 4, 4, 48, HIDDEN),
            array(low, WIDTH, HIDDEN),
            array(low, HIDDEN, WIDTH),
            array(low, WIDTH, count),
            array(low, count, 3 * WIDTH),
            array(low, count, WIDTH),
            array(low, count, WIDTH),
            array(wide, count, WIDTH),
            array(low, count, HIDDEN),
            array(wide, count, WIDTH),
            array(low, count, WIDTH),
            array(low, HIDDEN, WIDTH),
            array(low, count, WIDTH),
            array(wide, count, 128),
            array(wide, 8, WIDTH),
            array(wide, 8, WIDTH),
            array(wide, WIDTH, EMBED),
        ],
        in_specs=[anywhere] * 18 + [smem] * 3,
        out_specs=[smem] + [anywhere] * 18,
        scratch_shapes=[
            pltpu.VMEM((4, 4, 48, HIDDEN), low),
            pltpu.VMEM((WIDTH, HIDDEN), low),
            pltpu.VMEM((HIDDEN, WIDTH), low),
            pltpu.VMEM((WIDTH, count), low),
            pltpu.VMEM((count, 3 * WIDTH), low),
            pltpu.VMEM((count, WIDTH), low),
            pltpu.VMEM((count, WIDTH), low),
            pltpu.VMEM((count, WIDTH), wide),
            pltpu.VMEM((count, HIDDEN), low),
            pltpu.VMEM((count, HIDDEN), low),
            pltpu.VMEM((count, WIDTH), wide),
            pltpu.VMEM((count, WIDTH), low),
            pltpu.VMEM((2, WIDTH, WIDTH), low),
            pltpu.VMEM((2, 4, 4, SMALL, 128), wide),
            pltpu.VMEM((24, 3 * WIDTH), wide),
            pltpu.VMEM((48, 3 * WIDTH // 2), wide),
            pltpu.VMEM((48, WIDTH // 2), wide),
            pltpu.VMEM((48, HIDDEN // 2), wide),
            pltpu.VMEM((192, WIDTH // 2), wide),
            pltpu.VMEM((WIDTH, EMBED), low),
            pltpu.VMEM((8, HIDDEN), wide),
            pltpu.VMEM((count, 128), wide),
            pltpu.VMEM((count, EMBED), low),
            pltpu.VMEM((count, WIDTH), low),
            pltpu.VMEM((count, 128), low),
            pltpu.SemaphoreType.DMA((5, Gather.SEMS)),
            pltpu.SemaphoreType.DMA((5, Gather.SEMS)),
            pltpu.SemaphoreType.DMA((4,)),
            pltpu.SemaphoreType.DMA((4,)),
            pltpu.SemaphoreType.DMA((18,)),
            pltpu.SemaphoreType.DMA((2,)),
            pltpu.VMEM((rows_dev, SEQ, EMBED), wide),
            pltpu.VMEM((count, 128), wide),
            pltpu.VMEM((8, WIDTH), wide),
            pltpu.VMEM((8, WIDTH), wide),
            pltpu.VMEM((WIDTH, EMBED), wide),
            pltpu.SemaphoreType.DMA((18,)),
        ]
        + [pltpu.VMEM(a.shape, a.dtype) for a in (tokens, *weights, *vectors, segment_ids)],
        compiler_params=pltpu.CompilerParams(
            collective_id=0, has_side_effects=True, vmem_limit_bytes=62 * 2**20
        ),
        name="forward_gather",
    )(tokens, *weights, *vectors, segment_ids, row_lengths, teacher_index, teacher_table)


def last_kernel(*refs):
    (
        attn_hbm,
        up_hbm,
        down_hbm,
        turned_hbm,
        qkv_hbm,
        context_hbm,
        low_one_hbm,
        normed_one_hbm,
        slope_hbm,
        d_mid_hbm,
        d_branch_hbm,
        grad_down_hbm,
        codes_hbm,
        scaled_one_hbm,
        vectors_hbm,
        part_vectors_hbm,
        grad_proj_hbm,
        segment_ids_hbm,
        row_lengths,
    ) = refs[:19]
    (
        grad_tokens_hbm,
        own_rows_hbm,
        own_down_hbm,
        own_small_hbm,
    ) = refs[19:23]
    (
        attn_mat,
        grads,
        wide,
        low_one,
        d_branch,
        d_mid,
        part_down,
        small_all,
        grad_vectors,
        grad_up_bias,
        sends,
        recvs,
        local_sems,
        slope_sems,
        down_sems,
        qkv_sems,
        grad_sems,
        key_code,
        value_code,
        lows,
        scaled_one,
        vectors,
        grad_proj,
        segment_ids,
        own_rows,
        own_down,
        own_small,
        *rest,
    ) = refs[23:]
    held = [rest[6 * i : 6 * i + 6] for i in range(6)]
    fins = [rest[36 + 2 * i : 38 + 2 * i] for i in range(5)]
    count = d_mid.shape[0]
    rows_dev = count // SEQ
    links = Links()
    c = links.c

    def scatter(block, rows, group, deliver, mine=None):
        def own(chip, units):
            return block(c, chip, units)

        own = own if mine is None else mine
        fin = fins[group] if group < 5 else None
        return Scatter(
            links, block, own, rows, held[group], fin, deliver, sends, recvs, group, group in (2, 4, 5)
        )

    def down_mine(chip, units):
        return part_down.at[pl.ds(pl.multiple_of(chip * 192, 192), units * 192), :]

    def halves_to(ref, start, columns):
        def deliver(low, high):
            ref[:, start : start + columns] = low
            ref[:, start + columns : start + 2 * columns] = high

        return deliver

    def most_out(low, high):
        own_rows[:, 0:512] = low[:, 0:512]
        own_rows[:, 768:1024] = low[:, 512:768]
        own_rows[:, 1024:1280] = high[:, 0:256]
        own_rows[:, 1536:2048] = high[:, 256:768]

    def rest_out(low, high):
        own_rows[:, 512:768] = low[:, 0:256]
        own_rows[:, 1280:1408] = low[:, 256:384]
        own_rows[:, 1408:1536] = high[:, 0:128]
        own_rows[:, 2048:2304] = high[:, 128:384]

    def tiny_out(total):
        own_small[...] = total[0]

    down = scatter(rows_block(grad_down_hbm, 192, 384), 192, 0, halves_to(own_down, 0, WIDTH // 2), down_mine)
    up = scatter(rows_block(grads, 48, 1536), 48, 1, halves_to(own_rows, HIDDEN, HIDDEN // 2))
    out = scatter(rows_block(grads, 48, 384), 48, 2, halves_to(own_rows, 3 * WIDTH, WIDTH // 2))
    most = scatter(rows_block(grads, 48, 768, WIDTH), 48, 3, most_out)
    rest_of = scatter(rows_block(grads, 48, 384, 3 * WIDTH), 48, 4, rest_out)
    tiny = scatter(lead_block(small_all), 1, 5, tiny_out)

    def load(src, dst, index):
        return pltpu.make_async_copy(src, dst, local_sems.at[index])

    def start(copies):
        for copy in copies:
            copy.start()

    def wait(copies):
        for copy in copies:
            copy.wait()

    plan = Plan(
        LAST_PLAN,
        {"d": down, "u": up, "o": out, "m": most, "r": rest_of, "t": tiny, "l": links},
    )
    plan.until("pre")
    links.hail()
    first_loads = [
        load(d_branch_hbm, d_branch, 0),
        load(grad_down_hbm.at[:, part_of(c, WIDTH // 2)], part_down, 1),
    ]
    side_loads = [
        load(segment_ids_hbm, segment_ids, 11),
        load(grad_proj_hbm, grad_proj, 12),
        load(part_vectors_hbm, grad_vectors, 13),
        load(vectors_hbm, vectors, 14),
        load(scaled_one_hbm, scaled_one, 15),
    ]
    attn_load = load(attn_hbm, attn_mat, 3)
    start(first_loads + side_loads[:2])
    links.greet()
    wait(first_loads[1:])
    ones = jnp.ones((8, count), jnp.bfloat16)

    def slope_load(step):
        columns = part_of(step, WIDTH)
        return pltpu.make_async_copy(
            slope_hbm.at[:, columns], wide.at[:, columns], slope_sems.at[step]
        )

    def qkv_load(step):
        rows = part_of(step, HALF)
        return pltpu.make_async_copy(
            qkv_hbm.at[rows, :], wide.at[rows, 0 : 3 * WIDTH], qkv_sems.at[step]
        )

    def grad_store(step):
        rows = part_of(step, HALF)
        return pltpu.make_async_copy(
            d_mid.at[rows, :], grad_tokens_hbm.at[rows, :], grad_sems.at[step]
        )

    steps = count // HALF
    quarters = HIDDEN // WIDTH

    def weights(start, columns):
        return attn_mat[:, :, :, start : start + columns].reshape(WIDTH, columns)

    def feed_forward(up_mat, down_mat, normed_one):
        def down_load(step):
            rows = part_of(step, WIDTH)
            return pltpu.make_async_copy(
                down_hbm.at[rows, :], down_mat.at[rows, :], down_sems.at[step]
            )

        for step in range(quarters):
            down_load(step).start()
            slope_load(step).start()
        start(side_loads[2:])
        middle = [
            load(low_one_hbm, low_one, 6),
            load(up_hbm, up_mat, 7),
            load(d_mid_hbm, d_mid, 8),
            load(normed_one_hbm, normed_one, 9),
        ]
        plan.until("ld")
        wait(side_loads[:2])
        for r in range(rows_dev):
            _, live = segment_forms(segment_ids, row_lengths, r)
            key_code[r * SEQ : (r + 1) * SEQ, :] = key_codes(live)
        low = low_head((SEQ, 128))
        lows[0] = jnp.where(low, 1.0, 0.0).astype(jnp.bfloat16)
        lows[1] = jnp.where(low, 0.0, 1.0).astype(jnp.bfloat16)
        lane = lanes_in_head((SEQ, 128))
        parts = (lane == PARTS) | (lane == PARTS + 1)
        value_code[...] = jnp.where(parts, 1.0, 0.0).astype(jnp.bfloat16)
        for i in range(SHARDS):
            small_all[i % 2, i // 2, 0:24, :] = grad_proj[i * 24 : (i + 1) * 24, :]
        wait(first_loads[:1])

        def widen(step):
            columns = part_of(step, WIDTH)
            down_load(step).wait()
            slope_load(step).wait()
            grad = dotted(d_branch[...], down_mat[columns, :], 1, 1)
            wide[:, columns] = (grad * wide[:, columns].astype(jnp.float32)).astype(jnp.bfloat16)

            @pl.when(step == 0)
            def _():
                start(middle)

        plan.loop("w", 0, quarters, widen)
        wait(middle[:1])

        def weigh(step):
            rows = part_of(step, CHUNK)
            grads[rows, :] = dotted(low_one[:, rows], wide[...], 0, 0).astype(jnp.bfloat16)

        plan.loop("wu", 0, WIDTH // CHUNK, weigh)
        plan.until("bc")
        attn_load.start()
        for index in range(4):
            columns = slice(index * WIDTH, (index + 1) * WIDTH)
            grad_up_bias[:, columns] = dotted(ones, wide[:, columns], 1, 0)
        wait(middle[1:] + side_loads[2:])

        def narrow(step):
            rows = part_of(step, HALF)
            d_hidden = d_mid[rows, :] + dotted(wide[rows, :], up_mat[...], 1, 1)
            qkv_load(step).start()
            normed = normed_one[rows, :]
            d_mixed = norm_back(d_hidden, normed, scaled_one[rows, 0:1], vectors[3:4, :])
            d_mid[rows, :] = d_mixed
            d_branch[rows, :] = d_mixed.astype(jnp.bfloat16)
            grad_vectors[3:4, :] += jnp.sum(d_hidden * normed, 0, keepdims=True)
            grad_vectors[4:5, :] += jnp.sum(d_hidden, 0, keepdims=True)

        plan.loop("n", 0, steps, narrow)

    pl.run_scoped(
        feed_forward,
        pltpu.VMEM((WIDTH, HIDDEN), jnp.bfloat16),
        pltpu.VMEM((HIDDEN, WIDTH), jnp.bfloat16),
        pltpu.VMEM((count, WIDTH), jnp.float32),
    )

    def attention(d_context, context, codes, turned):
        loads = [
            load(context_hbm, context, 2),
            load(codes_hbm, codes, 4),
            load(turned_hbm, turned, 10),
        ]
        start(loads)
        plan.until("misc")
        grad_vectors[2:3, :] = dotted(ones, d_branch[...], 1, 0)[0:1]
        attn_load.wait()

        plan.until("g0")
        d_context[...] = dotted(d_branch[...], weights(3 * WIDTH, WIDTH), 1, 1).astype(jnp.bfloat16)
        plan.until("rd")

        wait(loads[:1])

        def gather_dots(p, carry):
            dot_codes(p, context, d_context, low_one)
            return carry

        lax.fori_loop(0, PAIRS, gather_dots, 0)
        up.settle()

        plan.until("wo0")
        grads[:, 0:WIDTH] = dotted(context[...], d_branch[...], 0, 0).astype(jnp.bfloat16)
        for step in range(steps):
            qkv_load(step).wait()

        wait(loads[1:])

        def attend(item):
            r = lax.rem(item, rows_dev)
            p = lax.div(item, rows_dev)
            attend_back_pair(
                r, p, wide, d_context, codes, low_one, key_code, value_code, lows
            )

        def weigh(first, pairs, base):
            def step(index):
                size = pairs * 128
                here = pl.ds(pl.multiple_of(index * WIDTH + first * 128, 128), size)
                there = pl.ds(pl.multiple_of(base + index * size, 128), size)
                grads[:, there] = dotted(turned[...], wide[:, here], 1, 0).astype(jnp.bfloat16)

            return step

        plan.loop("a", 0, 4 * rows_dev, attend)
        plan.loop("wm", 0, 3, weigh(0, 4, WIDTH))
        plan.loop("a", 4 * rows_dev, 2 * rows_dev, attend)
        plan.loop("wr", 0, 3, weigh(4, 2, 3 * WIDTH))

    pl.run_scoped(
        attention,
        pltpu.VMEM((count, WIDTH), jnp.bfloat16),
        pltpu.VMEM((count, WIDTH), jnp.bfloat16),
        pltpu.VMEM((count, WIDTH), jnp.bfloat16),
        pltpu.VMEM((WIDTH, count), jnp.bfloat16),
    )
    plan.until("vec")
    for index in (0, 2):
        total = dotted(ones, wide[:, index * WIDTH : (index + 1) * WIDTH], 1, 0)
        grad_vectors[index // 2 : index // 2 + 1, :] = total[0:1]
    tiles = [grad_vectors[:, i * 128 : (i + 1) * 128] for i in range(WIDTH // 128)]
    for i, part in enumerate(pick_lanes(tiles, 24, SHARDS)):
        small_all[i % 2, i // 2, 24:32, :] = part
    tiles = [grad_up_bias[:, i * 128 : (i + 1) * 128] for i in range(HIDDEN // 128)]
    for i, part in enumerate(pick_lanes(tiles, 96, SHARDS)):
        small_all[i % 2, i // 2, 32:40, :] = part

    def back(step):
        rows = part_of(step, HALF)
        value = dotted(wide[rows, 0 : 3 * WIDTH], weights(0, 3 * WIDTH), 1, 1)
        d_mid[rows, :] += value
        grad_store(step).start()

    plan.loop("b", 0, steps, back)
    plan.until("end")
    stores = [
        load(own_rows, own_rows_hbm, 16),
        load(own_down, own_down_hbm, 17),
        load(own_small, own_small_hbm, 18),
    ]
    start(stores)
    links.finish()
    for step in range(steps):
        grad_store(step).wait()
    wait(stores)


def run_last(kept, segment_ids, row_lengths):
    count = kept[9].shape[0]
    rows_dev = count // SEQ
    smem = pl.BlockSpec(memory_space=pltpu.SMEM)
    anywhere = pl.BlockSpec(memory_space=pl.ANY)
    low = jnp.bfloat16
    wide = jnp.float32

    def array(*shape):
        return jax.ShapeDtypeStruct(shape, wide)

    def held(unit, kind):
        return [pltpu.VMEM((n * unit[0],) + unit[1:], kind) for n in (16, 2, 2, 4, 4, 3)]

    blocks = ((192, 384), (48, 1536), (48, 384), (48, 768), (48, 384))
    buffers = []
    for block in blocks:
        buffers += held(block, low)
    buffers += held((1, SMALL, 128), wide)
    for rows, columns in blocks:
        buffers += [pltpu.VMEM((rows, columns), wide), pltpu.VMEM((rows // 2, columns), wide)]
    return pl.pallas_call(
        last_kernel,
        out_shape=[
            array(count, WIDTH),
            array(24, 2 * HIDDEN),
            array(96, WIDTH),
            array(SMALL, 128),
        ],
        in_specs=[anywhere] * 18 + [smem],
        out_specs=[anywhere] * 4,
        scratch_shapes=[
            pltpu.VMEM((4, 4, 48, HIDDEN), low),
            pltpu.VMEM((WIDTH, HIDDEN), low),
            pltpu.VMEM((count, HIDDEN), low),
            pltpu.VMEM((count, WIDTH), low),
            pltpu.VMEM((count, WIDTH), low),
            pltpu.VMEM((count, WIDTH), wide),
            pltpu.VMEM((HIDDEN, WIDTH // 2), low),
            pltpu.VMEM((2, CHIPS, SMALL, 128), wide),
            pltpu.VMEM((8, WIDTH), wide),
            pltpu.VMEM((8, HIDDEN), wide),
            pltpu.SemaphoreType.DMA((6, Scatter.SEMS)),
            pltpu.SemaphoreType.DMA((6, Scatter.SEMS)),
            pltpu.SemaphoreType.DMA((19,)),
            pltpu.SemaphoreType.DMA((HIDDEN // WIDTH,)),
            pltpu.SemaphoreType.DMA((HIDDEN // WIDTH,)),
            pltpu.SemaphoreType.DMA((count // HALF,)),
            pltpu.SemaphoreType.DMA((count // HALF,)),
            pltpu.VMEM((count, 128), low),
            pltpu.VMEM((SEQ, 128), low),
            pltpu.VMEM((2, SEQ, 128), low),
            pltpu.VMEM((count, 128), wide),
            pltpu.VMEM((8, WIDTH), wide),
            pltpu.VMEM((WIDTH, EMBED), wide),
            pltpu.VMEM((rows_dev, SEQ), jnp.int32),
            pltpu.VMEM((24, 2 * HIDDEN), wide),
            pltpu.VMEM((96, WIDTH), wide),
            pltpu.VMEM((SMALL, 128), wide),
        ]
        + buffers,
        compiler_params=pltpu.CompilerParams(
            collective_id=1, has_side_effects=True, vmem_limit_bytes=63 * 2**20
        ),
        name="backward_scatter",
    )(*kept, segment_ids, row_lengths)


def pass_kernel(*refs):
    sources, targets = refs[:6], refs[6:25]
    held, ready = refs[25:31], refs[31:40]
    in_sems, out_sems = refs[40:]
    grad_tokens, embeddings, query, key, value, out, up, down, proj = targets[:9]
    rows, down_in, small_in, losses_in = held[2:]
    pieces = 8
    through = []
    for src, mid, dst in zip(sources[:2], held[:2], (grad_tokens, embeddings)):
        size = src.shape[0] // pieces
        for piece in range(pieces):
            part = pl.ds(piece * size, size)
            index = len(through)
            through.append(
                (
                    pltpu.make_async_copy(src.at[part], mid.at[part], in_sems.at[index]),
                    pltpu.make_async_copy(mid.at[part], dst.at[part], out_sems.at[index]),
                )
            )
    small = [
        pltpu.make_async_copy(src, mid, in_sems.at[2 * pieces + index])
        for index, (src, mid) in enumerate(zip(sources[2:], held[2:]))
    ]
    for copy in small:
        copy.start()
    for here, _ in through:
        here.start()
    for copy in small:
        copy.wait()
    for index, ref in enumerate(ready[:8]):
        ref[...] = small_in[24 + index : 25 + index, 0:24].reshape(24)
    ready[8][...] = small_in[32:33, 0:96].reshape(96)
    made = [
        (rows.at[:, index * WIDTH : (index + 1) * WIDTH], ref)
        for index, ref in enumerate((query, key, value, out))
    ]
    made += [(rows.at[:, HIDDEN:], up), (down_in, down), (small_in.at[0:24, :], proj)]
    made += list(zip(ready, targets[9:18])) + [(losses_in, targets[18])]
    outs = [
        pltpu.make_async_copy(mid, dst, out_sems.at[2 * pieces + index])
        for index, (mid, dst) in enumerate(made)
    ]
    for copy in outs:
        copy.start()
    for here, there in through:
        here.wait()
        there.start()
    for copy in outs:
        copy.wait()
    for _, there in through:
        there.wait()


def run_pass(*arrays):
    anywhere = pl.BlockSpec(memory_space=pl.ANY)

    def array(*shape):
        return jax.ShapeDtypeStruct(shape, jnp.float32)

    whole = [array(*a.shape) for a in arrays]
    vectors = [array(24)] * 8 + [array(96)]
    return pl.pallas_call(
        pass_kernel,
        out_shape=whole[:2]
        + [array(24, WIDTH)] * 4
        + [array(24, HIDDEN), array(96, WIDTH), array(24, EMBED)]
        + vectors
        + [whole[-1]],
        in_specs=[anywhere] * 6,
        out_specs=[anywhere] * 19,
        scratch_shapes=[pltpu.VMEM(a.shape, a.dtype) for a in (*arrays, *vectors)]
        + [pltpu.SemaphoreType.DMA((20,)), pltpu.SemaphoreType.DMA((33,))],
        compiler_params=pltpu.CompilerParams(vmem_limit_bytes=62 * 2**20),
        name="hand_over",
    )(*arrays)


def body_tiles(
    tokens,
    w_query,
    b_query,
    w_key,
    w_value,
    b_value,
    w_out,
    b_out,
    gain_one,
    shift_one,
    w_up,
    b_up,
    w_down,
    b_down,
    gain_two,
    shift_two,
    w_proj,
    segment_ids,
    row_lengths,
    teacher_index,
    teacher_table,
):
    rows_dev, _, width = tokens.shape
    losses, embeddings, *kept = run_first(
        tokens.reshape(rows_dev * SEQ, width),
        (w_query, w_key, w_value, w_out, w_up, w_down, w_proj),
        (b_query, b_value, b_out, gain_one, shift_one, b_down, gain_two, shift_two, b_up),
        segment_ids,
        row_lengths,
        teacher_index,
        teacher_table,
    )
    grad_tokens, *small = run_last(kept, segment_ids, row_lengths)
    (
        grad_tokens,
        embeddings,
        grad_query,
        grad_key,
        grad_value,
        grad_out,
        grad_up,
        grad_down,
        grad_proj,
        grad_query_bias,
        grad_value_bias,
        grad_out_bias,
        grad_gain_first,
        grad_shift_first,
        grad_down_bias,
        grad_gain_second,
        grad_shift_second,
        grad_up_bias,
        losses,
    ) = run_pass(grad_tokens, embeddings.reshape(rows_dev * SEQ, EMBED), *small, losses)
    return (
        losses,
        embeddings.reshape(rows_dev, SEQ, EMBED),
        grad_tokens.reshape(rows_dev, SEQ, width),
        grad_query,
        grad_query_bias,
        grad_key,
        grad_value,
        grad_value_bias,
        grad_out,
        grad_out_bias,
        grad_gain_first,
        grad_shift_first,
        grad_up,
        grad_up_bias,
        grad_down,
        grad_down_bias,
        grad_gain_second,
        grad_shift_second,
        grad_proj,
    )


def solution(mesh):
    in_specs = (
        P(("dp", "fsdp"), None, None),
        P(("dp", "fsdp"), None),
        P(("dp", "fsdp")),
        P(("dp", "fsdp"), None),
        P(("dp", "fsdp"), None),
        P(("dp", "fsdp")),
        P(("dp", "fsdp"), None),
        P(("dp", "fsdp")),
        P(("dp", "fsdp")),
        P(("dp", "fsdp")),
        P(("dp", "fsdp"), None),
        P(("dp", "fsdp")),
        P(("dp", "fsdp"), None),
        P(("dp", "fsdp")),
        P(("dp", "fsdp")),
        P(("dp", "fsdp")),
        P(("dp", "fsdp"), None),
        P(("dp", "fsdp"), None),
        P(("dp", "fsdp")),
        P(("dp", "fsdp"), None),
        P(),
    )
    out_specs = (
        P(("dp", "fsdp")),
        P(("dp", "fsdp"), None, None),
        P(("dp", "fsdp"), None, None),
        P(("dp", "fsdp"), None),
        P(("dp", "fsdp")),
        P(("dp", "fsdp"), None),
        P(("dp", "fsdp"), None),
        P(("dp", "fsdp")),
        P(("dp", "fsdp"), None),
        P(("dp", "fsdp")),
        P(("dp", "fsdp")),
        P(("dp", "fsdp")),
        P(("dp", "fsdp"), None),
        P(("dp", "fsdp")),
        P(("dp", "fsdp"), None),
        P(("dp", "fsdp")),
        P(("dp", "fsdp")),
        P(("dp", "fsdp")),
        P(("dp", "fsdp"), None),
    )
    body = body_tiles if fits(mesh) else body_whole
    return jax.shard_map(body, mesh=mesh, in_specs=in_specs, out_specs=out_specs, check_vma=False)
```

```python
import functools
import math

import jax
import jax.numpy as jnp
from jax import lax
from jax.experimental import pallas as pl
from jax.experimental.pallas import tpu as pltpu
from jax.sharding import PartitionSpec as P

HEADS = 12
HEAD = 64
SEQ = 512
QLEN = 32
NPASS = 8
TABLE = 1024


NORM_EPS = 1e-12
UNIT_EPS = 1e-12
SOFTNESS = 0.1
MASK_FILL = -1000000000.0
ROOT_HALF = 0.7071067811865476
DENSITY_SCALE = 0.3989422804014327


def matmul(left, right):
    return jnp.dot(left, right, preferred_element_type=jnp.float32)


def over_rows(left, right):
    return lax.dot_general(
        left, right, (((0,), (0,)), ((), ())), preferred_element_type=jnp.float32
    )


def against(left, right):
    return lax.dot_general(
        left, right, (((1,), (1,)), ((), ())), preferred_element_type=jnp.float32
    )


def normalise(mixed, gain, shift):
    centred = mixed - jnp.mean(mixed, -1, keepdims=True)
    scaled = lax.rsqrt(jnp.mean(centred * centred, -1, keepdims=True) + NORM_EPS)
    normed = centred * scaled
    return (normed * gain + shift, normed, scaled)


def normalise_back(grad_out, normed, scaled, gain):
    inner = grad_out * gain
    grad_in = scaled * (
        inner
        - jnp.mean(inner, -1, keepdims=True)
        - normed * jnp.mean(inner * normed, -1, keepdims=True)
    )
    return (grad_in, jnp.sum(grad_out * normed, 0), jnp.sum(grad_out, 0))


def gelu_exact(upward):
    return 0.5 * upward * (1.0 + lax.erf(upward * ROOT_HALF))


def gelu_slope(upward):
    return (
        0.5 * (1.0 + lax.erf(upward * ROOT_HALF))
        + upward * jnp.exp(-0.5 * upward * upward) * DENSITY_SCALE
    )


def split_heads(matrix, rows_dev):
    return (
        matrix.reshape(rows_dev, SEQ, HEADS, HEAD)
        .transpose(0, 2, 1, 3)
        .reshape(rows_dev * HEADS, SEQ, HEAD)
    )


def join_heads(stacked, rows_dev):
    return (
        stacked.reshape(rows_dev, HEADS, SEQ, HEAD)
        .transpose(0, 2, 1, 3)
        .reshape(rows_dev * SEQ, HEADS * HEAD)
    )


def collect(sent):
    return (
        lax.all_gather(sent[0], ("dp", "fsdp"), axis=0, tiled=True),
        lax.all_gather(sent[1], ("dp", "fsdp"), axis=0, tiled=True),
        lax.all_gather(sent[2], ("dp", "fsdp"), axis=0, tiled=True),
        lax.all_gather(sent[3], ("dp", "fsdp"), axis=0, tiled=True),
        lax.all_gather(sent[4], ("dp", "fsdp"), axis=0, tiled=True),
        lax.all_gather(sent[5], ("dp", "fsdp"), axis=0, tiled=True),
        lax.all_gather(sent[6], ("dp", "fsdp"), axis=0, tiled=True),
        lax.all_gather(sent[7], ("dp", "fsdp"), axis=0, tiled=True),
        lax.all_gather(sent[8], ("dp", "fsdp"), axis=0, tiled=True),
        lax.all_gather(sent[9], ("dp", "fsdp"), axis=0, tiled=True),
        lax.all_gather(sent[10], ("dp", "fsdp"), axis=0, tiled=True),
        lax.all_gather(sent[11], ("dp", "fsdp"), axis=0, tiled=True),
        lax.all_gather(sent[12], ("dp", "fsdp"), axis=0, tiled=True),
        lax.all_gather(sent[13], ("dp", "fsdp"), axis=0, tiled=True),
        lax.all_gather(sent[14], ("dp", "fsdp"), axis=0, tiled=True),
        lax.all_gather(sent[15], ("dp", "fsdp"), axis=0, tiled=True),
    )


def spread_grads(terms):
    return (
        lax.psum_scatter(terms[0], ("dp", "fsdp"), scatter_dimension=0, tiled=True),
        lax.psum_scatter(terms[1], ("dp", "fsdp"), scatter_dimension=0, tiled=True),
        lax.psum_scatter(terms[2], ("dp", "fsdp"), scatter_dimension=0, tiled=True),
        lax.psum_scatter(terms[3], ("dp", "fsdp"), scatter_dimension=0, tiled=True),
        lax.psum_scatter(terms[4], ("dp", "fsdp"), scatter_dimension=0, tiled=True),
        lax.psum_scatter(terms[5], ("dp", "fsdp"), scatter_dimension=0, tiled=True),
        lax.psum_scatter(terms[6], ("dp", "fsdp"), scatter_dimension=0, tiled=True),
        lax.psum_scatter(terms[7], ("dp", "fsdp"), scatter_dimension=0, tiled=True),
        lax.psum_scatter(terms[8], ("dp", "fsdp"), scatter_dimension=0, tiled=True),
        lax.psum_scatter(terms[9], ("dp", "fsdp"), scatter_dimension=0, tiled=True),
        lax.psum_scatter(terms[10], ("dp", "fsdp"), scatter_dimension=0, tiled=True),
        lax.psum_scatter(terms[11], ("dp", "fsdp"), scatter_dimension=0, tiled=True),
        lax.psum_scatter(terms[12], ("dp", "fsdp"), scatter_dimension=0, tiled=True),
        lax.psum_scatter(terms[13], ("dp", "fsdp"), scatter_dimension=0, tiled=True),
        lax.psum_scatter(terms[14], ("dp", "fsdp"), scatter_dimension=0, tiled=True),
        lax.psum_scatter(terms[15], ("dp", "fsdp"), scatter_dimension=0, tiled=True),
    )


def body_whole(
    tokens,
    w_query,
    b_query,
    w_key,
    w_value,
    b_value,
    w_out,
    b_out,
    gain_one,
    shift_one,
    w_up,
    b_up,
    w_down,
    b_down,
    gain_two,
    shift_two,
    w_proj,
    segment_ids,
    row_lengths,
    teacher_index,
    teacher_table,
):
    rows_dev = tokens.shape[0]
    width = tokens.shape[2]
    scale = 1.0 / math.sqrt(HEAD)
    shards = (
        w_query,
        b_query,
        w_key,
        w_value,
        b_value,
        w_out,
        b_out,
        gain_one,
        shift_one,
        w_up,
        b_up,
        w_down,
        b_down,
        gain_two,
        shift_two,
        w_proj,
    )
    sent = tuple((member.astype(jnp.bfloat16) for member in shards))
    gathered = collect(sent)
    (
        query_mat,
        query_bias,
        key_mat,
        value_mat,
        value_bias,
        out_mat,
        out_bias,
        gain_first,
        shift_first,
        up_mat,
        up_bias,
        down_mat,
        down_bias,
        gain_second,
        shift_second,
        proj_mat,
    ) = gathered

    def visibility(item_index):
        row_index = item_index // HEADS
        segment_row = lax.dynamic_index_in_dim(segment_ids, row_index, 0, keepdims=False)
        length_row = lax.dynamic_index_in_dim(row_lengths, row_index, 0, keepdims=False)
        positions = jnp.arange(SEQ, dtype=jnp.int32)
        return (segment_row[:, None] == segment_row[None, :]) & (positions[None, :] < length_row)

    def attend(inputs):
        query_h, key_h, value_h, item_index = inputs
        scores = jnp.where(visibility(item_index), against(query_h, key_h) * scale, MASK_FILL)
        peak = jnp.max(scores, -1, keepdims=True)
        shifted = jnp.exp(scores - peak)
        totals = jnp.sum(shifted, -1, keepdims=True)
        chances = (shifted / totals).astype(jnp.bfloat16)
        context_h = matmul(chances, value_h).astype(jnp.bfloat16)
        return (context_h, (peak + jnp.log(totals))[:, 0])

    def attend_back(inputs):
        query_h, key_h, value_h, grad_h, logsum, item_index = inputs
        scores = jnp.where(visibility(item_index), against(query_h, key_h) * scale, MASK_FILL)
        chances = jnp.exp(scores - logsum[:, None])
        d_chances = against(grad_h, value_h)
        rowdot = jnp.sum(chances * d_chances, -1, keepdims=True)
        d_scores = (chances * (d_chances - rowdot)).astype(jnp.bfloat16)
        d_query_h = (matmul(d_scores, key_h) * scale).astype(jnp.bfloat16)
        d_key_h = (over_rows(d_scores, query_h) * scale).astype(jnp.bfloat16)
        d_value_h = over_rows(chances.astype(jnp.bfloat16), grad_h).astype(jnp.bfloat16)
        return (d_query_h, d_key_h, d_value_h)

    flat = tokens.reshape(rows_dev * SEQ, width)
    queries = (matmul(flat, query_mat) + query_bias.astype(jnp.float32)).astype(jnp.bfloat16)
    keys_all = matmul(flat, key_mat).astype(jnp.bfloat16)
    values = (matmul(flat, value_mat) + value_bias.astype(jnp.float32)).astype(jnp.bfloat16)
    query_heads = split_heads(queries, rows_dev)
    key_heads = split_heads(keys_all, rows_dev)
    value_heads = split_heads(values, rows_dev)
    items = jnp.arange(rows_dev * HEADS, dtype=jnp.int32)
    context_heads, logsums = lax.map(attend, (query_heads, key_heads, value_heads, items))
    context_low = join_heads(context_heads, rows_dev)
    branch_one = matmul(context_low, out_mat) + out_bias.astype(jnp.float32)
    mid_one = flat.astype(jnp.float32) + branch_one
    hidden_one, normed_one, scaled_one = normalise(
        mid_one, gain_first.astype(jnp.float32), shift_first.astype(jnp.float32)
    )
    hidden_one_low = hidden_one.astype(jnp.bfloat16)
    upward = matmul(hidden_one_low, up_mat) + up_bias.astype(jnp.float32)
    activated = gelu_exact(upward).astype(jnp.bfloat16)
    branch_two = matmul(activated, down_mat) + down_bias.astype(jnp.float32)
    hidden_two, normed_two, scaled_two = normalise(
        hidden_one + branch_two, gain_second.astype(jnp.float32), shift_second.astype(jnp.float32)
    )
    hidden_two_low = hidden_two.astype(jnp.bfloat16)
    raw_embed = matmul(hidden_two_low, proj_mat)
    inverse = lax.rsqrt(jnp.sum(raw_embed * raw_embed, -1, keepdims=True) + UNIT_EPS)
    embeddings = raw_embed * inverse
    embed_dim = embeddings.shape[1]
    embed_low = embeddings.astype(jnp.bfloat16).reshape(rows_dev, SEQ, embed_dim)
    query_low = embed_low[:, :QLEN]
    similar = jnp.einsum("rqc,rsc->rqs", query_low, embed_low, preferred_element_type=jnp.float32)
    positions = jnp.arange(SEQ, dtype=jnp.int32)
    live = positions[None, :] < row_lengths[:, None]
    passages = jnp.arange(1, NPASS + 1, dtype=jnp.int32)
    member = (segment_ids[:, None, :] == passages[None, :, None]) & live[:, None, :]
    masked = jnp.where(member[:, None], similar[:, :, None, :] / SOFTNESS, MASK_FILL)
    peak = jnp.max(masked, -1, keepdims=True)
    shifted = jnp.exp(masked - peak)
    totals = jnp.sum(shifted, -1, keepdims=True)
    student = SOFTNESS * jnp.sum(peak[..., 0] + jnp.log(totals[..., 0]), axis=1)
    choose = teacher_index[..., None] == jnp.arange(TABLE, dtype=jnp.int32)
    teacher = jnp.sum(jnp.where(choose, teacher_table, 0.0), -1)
    teacher_logp = jax.nn.log_softmax(teacher, axis=-1)
    student_logp = jax.nn.log_softmax(student, axis=-1)
    losses = jnp.sum(jnp.exp(teacher_logp) * (teacher_logp - student_logp), -1)
    again = collect(sent)
    (
        query_back,
        query_bias_back,
        key_back,
        value_back,
        value_bias_back,
        out_back,
        out_bias_back,
        gain_first_back,
        shift_first_back,
        up_back,
        up_bias_back,
        down_back,
        down_bias_back,
        gain_second_back,
        shift_second_back,
        proj_back,
    ) = again
    d_student = jnp.exp(student_logp) - jnp.exp(teacher_logp)
    spread_weights = shifted / totals
    d_similar = jnp.einsum("rp,rqps->rqs", d_student, spread_weights).astype(jnp.bfloat16)
    d_embed = jnp.einsum("rqs,rqc->rsc", d_similar, query_low, preferred_element_type=jnp.float32)
    d_query_part = jnp.einsum(
        "rqs,rsc->rqc", d_similar, embed_low, preferred_element_type=jnp.float32
    )
    d_embed = jnp.concatenate([d_embed[:, :QLEN] + d_query_part, d_embed[:, QLEN:]], 1).reshape(
        rows_dev * SEQ, embed_dim
    )
    d_raw = (
        inverse * (d_embed - embeddings * jnp.sum(d_embed * embeddings, -1, keepdims=True))
    ).astype(jnp.bfloat16)
    grad_proj = over_rows(hidden_two_low, d_raw)
    d_hidden_two = against(d_raw, proj_back)
    d_mid_two, grad_gain_second, grad_shift_second = normalise_back(
        d_hidden_two, normed_two, scaled_two, gain_second_back.astype(jnp.float32)
    )
    d_branch_two = d_mid_two.astype(jnp.bfloat16)
    grad_down = over_rows(activated, d_branch_two)
    grad_down_bias = jnp.sum(d_branch_two, 0, dtype=jnp.float32)
    d_upward = (against(d_branch_two, down_back) * gelu_slope(upward)).astype(jnp.bfloat16)
    grad_up = over_rows(hidden_one_low, d_upward)
    grad_up_bias = jnp.sum(d_upward, 0, dtype=jnp.float32)
    d_hidden_one = d_mid_two + against(d_upward, up_back)
    d_mid_one, grad_gain_first, grad_shift_first = normalise_back(
        d_hidden_one, normed_one, scaled_one, gain_first_back.astype(jnp.float32)
    )
    d_branch_one = d_mid_one.astype(jnp.bfloat16)
    grad_out = over_rows(context_low, d_branch_one)
    grad_out_bias = jnp.sum(d_branch_one, 0, dtype=jnp.float32)
    d_context = against(d_branch_one, out_back).astype(jnp.bfloat16)
    d_context_heads = split_heads(d_context, rows_dev)
    d_query_heads, d_key_heads, d_value_heads = lax.map(
        attend_back, (query_heads, key_heads, value_heads, d_context_heads, logsums, items)
    )
    d_queries = join_heads(d_query_heads, rows_dev)
    d_keys = join_heads(d_key_heads, rows_dev)
    d_values = join_heads(d_value_heads, rows_dev)
    grad_query = over_rows(flat, d_queries)
    grad_query_bias = jnp.sum(d_queries, 0, dtype=jnp.float32)
    grad_key = over_rows(flat, d_keys)
    grad_value = over_rows(flat, d_values)
    grad_value_bias = jnp.sum(d_values, 0, dtype=jnp.float32)
    grad_input = (
        d_mid_one
        + against(d_queries, query_back)
        + against(d_keys, key_back)
        + against(d_values, value_back)
    )
    terms = (
        grad_query,
        grad_query_bias,
        grad_key,
        grad_value,
        grad_value_bias,
        grad_out,
        grad_out_bias,
        grad_gain_first,
        grad_shift_first,
        grad_up,
        grad_up_bias,
        grad_down,
        grad_down_bias,
        grad_gain_second,
        grad_shift_second,
        grad_proj,
    )
    owned = spread_grads(terms)
    return (
        losses,
        embeddings.reshape(rows_dev, SEQ, embed_dim),
        grad_input.reshape(rows_dev, SEQ, width),
        owned[0],
        owned[1],
        owned[2],
        owned[3],
        owned[4],
        owned[5],
        owned[6],
        owned[7],
        owned[8],
        owned[9],
        owned[10],
        owned[11],
        owned[12],
        owned[13],
        owned[14],
        owned[15],
    )


MESH = pl.DeviceIdType.MESH
LOG2_E = 1.4426950408889634
EXP2_SCALE = LOG2_E / math.sqrt(HEAD)
SHARDS = 32
CHIPS = 16
WIDTH = 768
HIDDEN = 3072
EMBED = 128
SMALL = 40
PAIRS = HEADS // 2
CHUNK = 256
HALF = 512


def fits(mesh):
    return dict(mesh.shape) == {"dp": 4, "fsdp": 8}


def dotted(left, right, left_dim, right_dim):
    return lax.dot_general(
        left,
        right,
        (((left_dim,), (right_dim,)), ((), ())),
        preferred_element_type=jnp.float32,
    )


def part_of(start, size):
    return pl.ds(pl.multiple_of(start * size, size), size)


def value_of(number):
    return number() if callable(number) else number


def place():
    outer = lax.axis_index("dp")
    inner = lax.axis_index("fsdp")
    return lax.rem(outer, 2), lax.div(outer, 2), lax.div(inner, 2), lax.rem(inner, 2)


def device(x, y, z, c):
    return (y * 2 + x, z * 2 + c)


class Links:
    def __init__(self):
        x, y, z, c = place()
        self.c = c
        self.z = z
        self.chip_own = (y * 2 + x) * 4
        self.chip_x = (y * 2 + 1 - x) * 4
        self.chip_y = ((1 - y) * 2 + x) * 4
        self.chip_d = ((1 - y) * 2 + 1 - x) * 4
        self.to_core = device(x, y, z, 1 - c)
        self.to_x = device(1 - x, y, z, c)
        self.to_y = device(x, 1 - y, z, c)
        self.to_z = [None] + [device(x, y, lax.rem(z + k, 4), c) for k in (1, 2, 3)]
        self.inner = (z == 1) | (z == 2)
        paired = z + 1 - 2 * lax.rem(z, 2)
        self.to_pair = device(x, y, paired, c)
        self.to_middle = device(x, y, jnp.where(self.inner, 3 - z, paired), c)
        far = jnp.where(z < 2, 1, -1)
        near = jnp.where(self.inner, 3 - z, z + 2 * far)
        last = jnp.where(self.inner, 3 - z + far, z + 3 * far)
        self.levels = [z, paired, near, last]
        self.started = []

    def hail(self):
        barrier = pltpu.get_barrier_semaphore()
        self.partners = [self.to_core, self.to_x, self.to_y] + self.to_z[1:]
        for partner in self.partners:
            pl.semaphore_signal(barrier, inc=1, device_id=partner, device_id_type=MESH)

    def greet(self):
        pl.semaphore_wait(pltpu.get_barrier_semaphore(), len(self.partners))

    def level(self, k):
        return lax.rem(self.z + k, 4)

    def send(self, ends, sems, target, inner=False):
        def copy():
            src, dst = ends()
            send_sem, recv_sem = sems()
            return pltpu.make_async_remote_copy(
                src_ref=src,
                dst_ref=dst,
                send_sem=send_sem,
                recv_sem=recv_sem,
                device_id=target,
                device_id_type=MESH,
            )

        def start():
            copy().start()

        def wait():
            copy().wait_send()

        if inner:
            pl.when(self.inner)(start)
            self.started.append(lambda: pl.when(self.inner)(wait))
        else:
            start()
            self.started.append(wait)

    def arrived(self, ref, sems, source):
        pltpu.make_async_remote_copy(
            src_ref=ref,
            dst_ref=ref,
            send_sem=sems[0],
            recv_sem=sems[1],
            device_id=source,
            device_id_type=MESH,
        ).wait_recv()

    def finish(self, first=0):
        for wait in self.started[first:]:
            wait()
        self.started = self.started[:first]


def rows_block(ref, rows, columns, base=0):
    def block(core, chip, count):
        return ref.at[
            pl.ds(pl.multiple_of(chip * rows, rows), count * rows),
            pl.ds(pl.multiple_of(base + core * columns, 128), columns),
        ]

    return block


def lead_block(ref):
    def block(core, chip, count):
        return ref.at[core, pl.ds(chip, count)]

    return block


def column_of(chip):
    return lax.div(chip, 4)


def level_of(chip):
    return lax.rem(chip, 4)


def grid_block(ref, columns, base=0):
    def block(core, chip, count):
        lanes = pl.ds(pl.multiple_of(base + core * columns, 128), columns)
        if count == 4:
            return ref.at[column_of(chip), :, :, lanes]
        if count == 0:
            return ref.at[:, level_of(chip), :, lanes]
        return ref.at[column_of(chip), level_of(chip), :, lanes]

    return block


def lead_grid_block(ref):
    def block(core, chip, count):
        if count == 0:
            return ref.at[core, :, level_of(chip)]
        return ref.at[core, column_of(chip), level_of(chip)]

    return block


class Gather:
    Z, X, Y, FX, FY, C, ZF = 0, 3, 7, 11, 13, 15, 19
    SEMS = 21

    def __init__(self, links, block, sends, recvs, group):
        self.links = links
        self.block = block
        self.sends = sends
        self.recvs = recvs
        self.group = group

    def sems(self, index, there=None):
        there = index if there is None else there
        return self.sends.at[self.group, index], self.recvs.at[self.group, there]

    def ship(self, chip, count, index, target, there=None, inner=False):
        def ends():
            ref = self.block(self.links.c, value_of(chip), count)
            return ref, ref

        self.links.send(ends, lambda: self.sems(index, there), target, inner)

    def step_of(self, column, k):
        return lambda: column + self.links.levels[k]

    def take(self, chip, count, index, source, core=None):
        core = self.links.c if core is None else core
        self.links.arrived(self.block(core, value_of(chip), count), self.sems(index), source)

    def along(self):
        n = self.links
        own = self.step_of(n.chip_own, 0)
        self.ship(own, 1, self.Z, n.to_pair)
        self.ship(own, 1, self.Z + 1, n.to_middle, inner=True)

    def across(self, k):
        n = self.links
        chip = self.step_of(n.chip_own, k)
        if k:
            self.take(chip, 1, self.Z + k - 1, n.to_pair if k == 1 else n.to_middle)
            if k == 1:
                self.ship(chip, 1, self.Z + 2, n.to_middle, inner=True)
            else:
                self.ship(chip, 1, self.ZF + k - 2, n.to_pair, self.Z + k - 1, inner=True)
        self.ship(chip, 1, self.X + k, n.to_x)
        self.ship(chip, 1, self.Y + k, n.to_y)
        if k == 3:
            self.ship(n.chip_own, 4, self.C, n.to_core)

    def onward(self, k):
        n = self.links
        if k < 2:
            chip = self.step_of(n.chip_x, k)
            self.take(chip, 1, self.X + k, n.to_x)
            self.ship(chip, 1, self.FY + k, n.to_y)
        else:
            chip = self.step_of(n.chip_y, k)
            self.take(chip, 1, self.Y + k, n.to_y)
            self.ship(chip, 1, self.FX + k - 2, n.to_x)

    def beside(self):
        n = self.links
        for k in (2, 3):
            self.take(self.step_of(n.chip_x, k), 1, self.X + k, n.to_x)
        self.ship(n.chip_x, 4, self.C + 1, n.to_core)
        for k in (0, 1):
            self.take(self.step_of(n.chip_y, k), 1, self.Y + k, n.to_y)
        self.ship(n.chip_y, 4, self.C + 2, n.to_core)

    def opposite(self):
        n = self.links
        for k in (0, 1):
            self.take(self.step_of(n.chip_d, k), 1, self.FY + k, n.to_y)
        for k in (2, 3):
            self.take(self.step_of(n.chip_d, k), 1, self.FX + k - 2, n.to_x)
        self.ship(n.chip_d, 4, self.C + 3, n.to_core)

    def last(self):
        n = self.links
        for index, chip in enumerate((n.chip_own, n.chip_x, n.chip_y, n.chip_d)):
            self.take(chip, 4, self.C + index, n.to_core, 1 - n.c)


class LevelGather(Gather):
    X, Y, F, Z, ZF, C = 0, 1, 2, 3, 6, 8

    def own(self):
        n = self.links
        chip = self.step_of(n.chip_own, 0)
        self.ship(chip, 1, self.X, n.to_x)
        self.ship(chip, 1, self.Y, n.to_y)

    def diag(self):
        n = self.links
        chip = self.step_of(n.chip_x, 0)
        self.take(chip, 1, self.X, n.to_x)
        self.ship(chip, 1, self.F, n.to_y)

    def set(self, k):
        n = self.links
        level = self.step_of(n.chip_own, k)
        if k == 0:
            self.take(self.step_of(n.chip_y, 0), 1, self.Y, n.to_y)
            self.take(self.step_of(n.chip_d, 0), 1, self.F, n.to_y)
            self.ship(level, 0, self.Z, n.to_pair)
            self.ship(level, 0, self.Z + 1, n.to_middle, inner=True)
        else:
            self.take(level, 0, self.Z + k - 1, n.to_pair if k == 1 else n.to_middle)
            if k == 1:
                self.ship(level, 0, self.Z + 2, n.to_middle, inner=True)
            else:
                self.ship(level, 0, self.ZF + k - 2, n.to_pair, self.Z + k - 1, inner=True)
        self.ship(level, 0, self.C + k, n.to_core)

    def last(self):
        n = self.links
        for k in range(4):
            self.take(self.step_of(n.chip_own, k), 0, self.C + k, n.to_core, 1 - n.c)


class Joined:
    def join_from(self, stage, sends, recvs, index):
        self.parts = (stage, sends, recvs, index)
        return self

    def join(self):
        if self.parts is None:
            return
        n = self.links
        stage, sends, recvs, index = self.parts
        self.parts = None
        rows = stage.shape[0] // 2
        here = stage.at[part_of(1 - n.c, rows), :]
        n.arrived(here, (sends.at[index], recvs.at[index]), n.to_core)
        self.block(n.c, n.chip_own + n.z, 1)[...] = stage[...].astype(jnp.bfloat16)


class JoinedGather(Joined, Gather):
    def along(self):
        self.join()
        super().along()

    def across(self, k):
        self.join()
        super().across(k)


class JoinedLevelGather(Joined, LevelGather):
    def own(self):
        self.join()
        super().own()


class Scatter:
    C, DY, DX, OX, OY, Z, F = 0, 4, 5, 6, 8, 10, 13
    SEMS = 14

    def __init__(self, links, block, mine, rows, held, fin, deliver, sends, recvs, group, whole=False):
        self.links = links
        self.block = block
        self.mine = mine
        self.rows = rows
        self.part, self.d_y, self.d_x, self.o_x, self.o_y, self.z_in = held
        self.fin = fin
        self.deliver = deliver
        self.sends = sends
        self.recvs = recvs
        self.group = group
        n = links
        self.sent = []
        self.gone = []
        self.once = whole
        self.span = 4 if whole else 2
        self.columns = (n.chip_d, n.chip_x, n.chip_y, n.chip_own)

    def at(self, ref, start, count):
        if isinstance(start, int):
            return ref.at[pl.ds(start * self.rows, count * self.rows)]
        return ref.at[pl.ds(pl.multiple_of(start * self.rows, self.rows), count * self.rows)]

    def sems(self, index, there=None):
        there = index if there is None else there
        return self.sends.at[self.group, index], self.recvs.at[self.group, there]

    def ship(self, ends, index, target, there=None):
        self.links.send(ends, lambda: self.sems(index, there), target)
        self.gone.append(self.links.started[-1])

    def done(self):
        for wait in self.gone:
            if wait in self.links.started:
                wait()
                self.links.started.remove(wait)
        self.gone = []

    def ship_part(self, start, count, ref, there, index, target):
        self.ship(
            lambda: (self.at(self.part, value_of(start), count), self.at(ref, there, count)),
            index,
            target,
        )

    def take(self, ref, start, count, index, source):
        self.links.arrived(self.at(ref, start, count), self.sems(index), source)

    def add(self, count, start, *others):
        size = min(count, self.span)

        def step(i, carry):
            here = self.at(self.part, start + i * size, size)
            total = here[...]
            for other in others:
                total = total + other(i * size, size)[...]
            here[...] = total
            return carry

        lax.fori_loop(0, count // size, step, 0)

    def first(self):
        n = self.links
        if self.once:
            self.ship(lambda: (self.block(1 - n.c, 0, 16), self.at(self.part, 0, 16)), self.C, n.to_core)
            return
        for index, chip in enumerate(self.columns):

            def ends(chip=chip):
                return self.block(1 - n.c, chip, 4), self.at(self.part, chip, 4)

            self.ship(ends, self.C + index, n.to_core)
            self.sent.append(n.started[-1])

    def second(self, index):
        n = self.links
        if self.once:
            self.take(self.part, 0, 16, self.C, n.to_core)
            self.add(16, 0, self.mine)
            for index in range(3):
                self.pass_on(index)
            return
        chip = self.columns[index]
        self.take(self.part, chip, 4, self.C + index, n.to_core)
        self.add(4, chip, lambda i, size: self.mine(chip + i, size))
        self.pass_on(index)

    def pass_on(self, index):
        n = self.links
        chip = self.columns[index]
        if index == 0:
            self.ship_part(chip, 2, self.d_y, 0, self.DY, n.to_y)
            self.ship_part(lambda: chip + 2, 2, self.d_x, 0, self.DX, n.to_x)
        elif index == 1:
            self.ship_part(lambda: chip + 2, 2, self.o_x, 2, self.OX + 1, n.to_x)
        elif index == 2:
            self.ship_part(chip, 2, self.o_y, 0, self.OY, n.to_y)

    def third(self, index):
        n = self.links
        if index == 0:
            self.take(self.d_y, 0, 2, self.DY, n.to_y)
            self.add(2, n.chip_x, lambda i, size: self.at(self.d_y, i, size))
            self.ship_part(n.chip_x, 2, self.o_x, 0, self.OX, n.to_x)
            return
        self.take(self.d_x, 0, 2, self.DX, n.to_x)
        self.add(2, n.chip_y + 2, lambda i, size: self.at(self.d_x, i, size))
        self.ship_part(lambda: n.chip_y + 2, 2, self.o_y, 2, self.OY + 1, n.to_y)

    def fourth(self):
        n = self.links
        self.take(self.o_x, 2, 2, self.OX + 1, n.to_x)
        self.take(self.o_y, 0, 2, self.OY, n.to_y)
        self.take(self.o_x, 0, 2, self.OX, n.to_x)
        self.take(self.o_y, 2, 2, self.OY + 1, n.to_y)
        self.add(
            4,
            n.chip_own,
            lambda i, size: self.at(self.o_x, i, size),
            lambda i, size: self.at(self.o_y, i, size),
        )
        for j in (1, 2, 3):

            def ends(j=j):
                return (
                    self.at(self.part, n.chip_own + n.level(j), 1),
                    self.at(self.z_in, 3 - j, 1),
                )

            self.ship(ends, self.Z + j - 1, n.to_z[j], self.Z + 3 - j)

    def fifth(self):
        n = self.links
        total = self.at(self.part, n.chip_own + n.z, 1)[...].astype(jnp.float32)
        for k in (1, 2, 3):
            self.take(self.z_in, k - 1, 1, self.Z + k - 1, n.to_z[k])
            total = total + self.at(self.z_in, k - 1, 1)[...].astype(jnp.float32)
        return total

    def trade(self):
        if self.fin is None:
            self.deliver(self.fifth())
            return
        fin, fin_in = self.fin
        n = self.links
        rows = self.rows // 2
        fin[...] = self.fifth()
        self.ship(lambda: (fin.at[part_of(1 - n.c, rows)], fin_in), self.F, n.to_core)

    def whole(self):
        if self.fin is None:
            return
        fin, fin_in = self.fin
        n = self.links
        rows = self.rows // 2
        n.arrived(fin_in, self.sems(self.F), n.to_core)
        mine = fin[part_of(n.c, rows), :]
        theirs = fin_in[...]
        self.deliver(jnp.where(n.c == 0, mine, theirs), jnp.where(n.c == 0, theirs, mine))

    def settle(self):
        for wait in self.sent:
            if wait in self.links.started:
                wait()
                self.links.started.remove(wait)
        self.sent = []


def spread_lanes(parts, step):
    lane = lax.broadcasted_iota(jnp.int32, (8, 128), 1)
    tiles = [None] * (len(parts) * step // 128)

    def add(index, value):
        tiles[index] = value if tiles[index] is None else tiles[index] + value

    for i, part in enumerate(parts):
        part = jnp.where(lane < step, part, 0.0)
        index, shift = i * step // 128, i * step % 128
        rolled = pltpu.roll(part, shift, 1) if shift else part
        if shift + step <= 128:
            add(index, rolled)
        else:
            add(index, jnp.where(lane >= shift, rolled, 0.0))
            add(index + 1, jnp.where(lane < shift, rolled, 0.0))
    return tiles


def pick_lanes(tiles, step, count):
    parts = []
    lane = lax.broadcasted_iota(jnp.int32, (8, 128), 1)
    for i in range(count):
        index, shift = i * step // 128, i * step % 128
        part = pltpu.roll(tiles[index], 128 - shift, 1) if shift else tiles[index]
        if shift + step > 128:
            after = pltpu.roll(tiles[index + 1], 128 - shift, 1)
            part = jnp.where(lane < 128 - shift, part, after)
        parts.append(jnp.where(lane < step, part, 0.0))
    return parts


def rounded(value):
    return value.astype(jnp.bfloat16).astype(jnp.float32)


def segment_forms(segment_ids, row_lengths, r):
    segment = segment_ids[r : r + 1, :].astype(jnp.float32)
    position = lax.broadcasted_iota(jnp.int32, (1, SEQ), 1)
    return segment, jnp.where(position < row_lengths[r], segment, -1.0)


def upright(row):
    return jnp.broadcast_to(row, (128, SEQ)).T[:, 0:1]


FIRST_PLAN = (
    "a.along",
    "t.own",
    "a.across0",
    "t.diag",
    "u.along",
    "o.own",
    "u.across0",
    "a.across1",
    "t.set0",
    "a.across2",
    "bias",
    "t.set1",
    "a.across3",
    "a.onward0",
    "a.onward1",
    "d.along",
    "turn",
    "a.onward2",
    "t.set2",
    "a.onward3",
    "t.set3",
    "o.diag",
    "a.beside",
    "u.across1",
    "u.across2",
    "a.opposite",
    "u.across3",
    "t.last",
    "u.onward0",
    "o.set0",
    "vec",
    "u.onward1",
    "a.last",
    "project",
    "d.across1",
    "p0",
    "p1",
    "p2",
    "p3",
    "u.onward2",
    "attend",
    "d.across2",
    "d.across0",
    "a0",
    "a1",
    "a2",
    "u.onward3",
    "a3",
    "o.set1",
    "o.set2",
    "a4",
    "a5",
    "a6",
    "a7",
    "o.set3",
    "a8",
    "u.beside",
    "a9",
    "a10",
    "d.across3",
    "d.onward0",
    "o.last",
    "a11",
    "mix",
    "d.onward2",
    "u.opposite",
    "m0",
    "d.onward1",
    "m1",
    "u.last",
    "widen",
    "w0",
    "w1",
    "d.onward3",
    "w2",
    "w3",
    "d.beside",
    "w4",
    "w5",
    "w6",
    "w7",
    "w8",
    "d.opposite",
    "w9",
    "w10",
    "w11",
    "d.last",
    "narrow",
)

LAST_PLAN = (
    "pre",
    "d.first",
    "ld",
    "w0",
    "d.second0",
    "w1",
    "d.second1",
    "w2",
    "w3",
    "wu0",
    "wu1",
    "d.second2",
    "wu2",
    "d.third0",
    "u.first",
    "bc",
    "d.third1",
    "d.second3",
    "n0",
    "u.second0",
    "n1",
    "misc",
    "u.second1",
    "g0",
    "u.second2",
    "rd",
    "u.second3",
    "wo0",
    "a0",
    "a1",
    "d.fourth",
    "a2",
    "o.first",
    "u.third0",
    "a3",
    "u.third1",
    "a4",
    "a5",
    "a6",
    "a7",
    "wm0",
    "wm1",
    "o.second0",
    "u.fourth",
    "wm2",
    "m.first",
    "a8",
    "o.third0",
    "o.third1",
    "a9",
    "m.second0",
    "a10",
    "m.second1",
    "m.second2",
    "a11",
    "wr0",
    "m.third0",
    "m.third1",
    "m.second3",
    "wr1",
    "o.fourth",
    "wr2",
    "r.first",
    "vec",
    "t.first",
    "r.second0",
    "d.trade",
    "m.fourth",
    "r.third1",
    "r.third0",
    "t.second0",
    "o.trade",
    "r.fourth",
    "u.trade",
    "t.third0",
    "t.third1",
    "b0",
    "t.fourth",
    "b1",
    "d.done",
    "o.done",
    "u.done",
    "r.trade",
    "m.trade",
    "t.trade",
    "u.whole",
    "r.whole",
    "d.whole",
    "m.whole",
    "o.whole",
    "t.whole",
    "end",
)


class Plan:
    def __init__(self, names, groups):
        self.groups = groups
        self.inside = {}
        self.queue = list(names)

    def call(self, name):
        group, method = name.split(".")
        if method[-1].isdigit():
            getattr(self.groups[group], method[:-1])(int(method[-1]))
        else:
            getattr(self.groups[group], method)()

    def until(self, name):
        while True:
            step = self.queue.pop(0)
            if step == name:
                return
            self.call(step)

    def loop(self, letter, first, count, body):
        steps = {}
        self.until(f"{letter}{first}")
        for index in range(first, first + count):
            steps[index] = []
            ahead = f"{letter}{index + 1}"
            while self.queue[0] != ahead and "." in self.queue[0]:
                steps[index].append(self.queue.pop(0))
            if index + 1 < first + count:
                self.queue.pop(0)

        def run(step, carry):
            body(step)
            for index, names in steps.items():
                if names:

                    @pl.when(step == index)
                    def _(names=names):
                        for name in names:
                            self.call(name)

            return carry

        lax.fori_loop(first, first + count, run, 0)


def lanes_in_head(shape):
    return lax.broadcasted_iota(jnp.int32, shape, 1) & (HEAD - 1)


def low_head(shape):
    return lax.broadcasted_iota(jnp.int32, shape, 1) < HEAD


def two_parts(value):
    first = rounded(value)
    return first, value - first


def three_parts(value):
    first, rest = two_parts(value)
    second, third = two_parts(rest)
    return first, second, third


PARTS = 16


def query_codes(segment):
    lane = lanes_in_head((SEQ, 128)).astype(jnp.float32)
    return jnp.where(lane == upright(segment), 1.0, 0.0).astype(jnp.bfloat16)


def key_codes(live):
    lane = lanes_in_head((SEQ, 128))
    hidden = jnp.where(lane.astype(jnp.float32) == upright(live), 0.0, MASK_FILL)
    parts = jnp.where((lane >= PARTS) & (lane < PARTS + 3), 1.0, 0.0)
    return jnp.where(lane <= NPASS, hidden, parts).astype(jnp.bfloat16)


def attend_pair(r, p, qkv, context, codes, segments, keys):
    rows = part_of(r, SEQ)
    columns = pl.multiple_of(p * 128, 128)
    query = qkv[rows, pl.ds(columns, 128)]
    key = qkv[rows, pl.ds(columns + WIDTH, 128)]
    value = qkv[rows, pl.ds(columns + 2 * WIDTH, 128)]
    query_c, key_c = segments[rows, :], keys[rows, :]
    low = low_head((SEQ, 128))
    one = jnp.ones_like(value)
    outs, peaks = [], []
    for j in range(2):
        mine = low if j == 0 else ~low
        scores = dotted(jnp.where(mine, query, query_c), jnp.where(mine, key, key_c), 1, 1)
        peak = jnp.max(scores, -1, keepdims=True)
        shifted = jnp.exp2((scores - peak) * EXP2_SCALE).astype(jnp.bfloat16)
        outs.append(dotted(shifted, jnp.where(mine, value, one), 1, 0))
        peaks.append(peak)
    total = jnp.where(low, outs[1], outs[0])
    own = pltpu.roll(total, HEAD, 1)
    context[rows, pl.ds(columns, 128)] = (
        jnp.where(low, outs[0], outs[1]) * (1.0 / own)
    ).astype(jnp.bfloat16)
    logsum = jnp.where(low, peaks[1], peaks[0]) + jnp.log2(total) * (1.0 / EXP2_SCALE)
    first, second, third = three_parts(-logsum)
    lane = lanes_in_head((SEQ, 128))
    code = jnp.where(lane == PARTS + 2, third, query_c.astype(jnp.float32))
    code = jnp.where(lane == PARTS + 1, second, code)
    code = jnp.where(lane == PARTS, first, code)
    codes[rows, pl.ds(columns, 128)] = code.astype(jnp.bfloat16)


def dot_codes(p, context, d_context, codes):
    columns = part_of(p, 128)
    both = context[:, columns].astype(jnp.float32) * d_context[:, columns].astype(jnp.float32)
    first, second = two_parts(both)
    shape = (128, 128)
    other = low_head(shape) != (lax.broadcasted_iota(jnp.int32, shape, 0) < HEAD)
    other = jnp.where(other, -1.0, 0.0).astype(jnp.bfloat16)
    total = dotted(first.astype(jnp.bfloat16), other, 1, 0)
    total = total + dotted(second.astype(jnp.bfloat16), other, 1, 0)
    first, second = two_parts(total)
    lane = lanes_in_head(total.shape)
    code = jnp.where(lane == PARTS, first, jnp.where(lane == PARTS + 1, second, 0.0))
    codes[:, columns] = code.astype(jnp.bfloat16)


def pick_head(masks, j, value, code):
    return value * masks[j] + code * masks[1 - j]


def attend_back_pair(r, p, qkv, d_context, query_code, grad_code, key_code, value_code, lows):
    rows = part_of(r, SEQ)
    columns = pl.multiple_of(p * 128, 128)
    query = qkv[rows, pl.ds(columns, 128)]
    key = qkv[rows, pl.ds(columns + WIDTH, 128)]
    value = qkv[rows, pl.ds(columns + 2 * WIDTH, 128)]
    grad = d_context[rows, pl.ds(columns, 128)]
    query_c = query_code[rows, pl.ds(columns, 128)]
    grad_c = grad_code[rows, pl.ds(columns, 128)]
    key_c = key_code[rows, :]
    value_c = value_code[...]
    masks = (lows[0], lows[1])
    d_query, d_key, d_value = [], [], []
    for j in range(2):
        scores = dotted(pick_head(masks, j, key, key_c), pick_head(masks, j, query, query_c), 1, 1)
        chances = jnp.exp2(scores * EXP2_SCALE)
        d_chances = dotted(
            pick_head(masks, j, value, value_c), pick_head(masks, j, grad, grad_c), 1, 1
        )
        d_scores = (chances * d_chances).astype(jnp.bfloat16)
        d_value.append(dotted(chances.astype(jnp.bfloat16), grad, 1, 0))
        d_key.append(dotted(d_scores, query, 1, 0))
        d_query.append(dotted(d_scores, key, 0, 0))
    low = low_head((SEQ, 128))
    scale = 1.0 / math.sqrt(HEAD)
    low_type = jnp.bfloat16
    qkv[rows, pl.ds(columns, 128)] = (jnp.where(low, d_query[0], d_query[1]) * scale).astype(
        low_type
    )
    qkv[rows, pl.ds(columns + WIDTH, 128)] = (
        jnp.where(low, d_key[0], d_key[1]) * scale
    ).astype(low_type)
    qkv[rows, pl.ds(columns + 2 * WIDTH, 128)] = jnp.where(low, d_value[0], d_value[1]).astype(
        low_type
    )


def norm_parts(mixed):
    centred = mixed - jnp.mean(mixed, -1, keepdims=True)
    scaled = lax.rsqrt(jnp.mean(centred * centred, -1, keepdims=True) + NORM_EPS)
    return centred * scaled, scaled


def norm_back(grad_out, normed, scaled, gain):
    inner = grad_out * gain
    return scaled * (
        inner
        - jnp.mean(inner, -1, keepdims=True)
        - normed * jnp.mean(inner * normed, -1, keepdims=True)
    )


def halves(links, src, stage, sends, recvs, index):
    rows, width = src.shape
    columns = width // 2

    def ends():
        return src.at[:, part_of(1 - links.c, columns)], stage.at[part_of(links.c, rows), :]

    links.send(ends, lambda: (sends.at[index], recvs.at[index]), links.to_core)
    stage[part_of(links.c, rows), :] = src[:, part_of(links.c, columns)]


def passage_loss(similar, live, teacher_index, teacher_table):
    rows_dev = similar.shape[0] // QLEN
    scores = similar * (1.0 / SOFTNESS)
    inside, shares, student, teacher = [], [], [], []
    for p in range(NPASS):
        member = live == float(p + 1)
        masked = jnp.where(member, scores, MASK_FILL)
        peak = jnp.max(masked, -1, keepdims=True)
        shifted = jnp.exp(masked - peak)
        total = jnp.sum(shifted, -1, keepdims=True)
        inside.append(jnp.where(member, shifted, 0.0))
        shares.append(1.0 / total)
        sums = peak + jnp.log(total)
        student.append(
            [
                SOFTNESS * jnp.sum(sums[r * QLEN : (r + 1) * QLEN], axis=0, keepdims=True)
                for r in range(rows_dev)
            ]
        )
        teacher.append(
            [
                jnp.full((1, 1), teacher_table[teacher_index[r, p]], jnp.float32)
                for r in range(rows_dev)
            ]
        )

    def log_softmax(values):
        peak = functools.reduce(jnp.maximum, values)
        total = sum(jnp.exp(value - peak) for value in values)
        return [value - peak - jnp.log(total) for value in values]

    losses, slopes = [], []
    for r in range(rows_dev):
        ours = log_softmax([row[r] for row in student])
        theirs = log_softmax([row[r] for row in teacher])
        losses.append(sum(jnp.exp(t) * (t - s) for t, s in zip(theirs, ours)))
        slopes.append([jnp.broadcast_to(jnp.exp(s) - jnp.exp(t), (QLEN, 1)) for t, s in zip(theirs, ours)])
    d_similar = sum(
        part * (share * jnp.concatenate([row[p] for row in slopes], axis=0))
        for p, (part, share) in enumerate(zip(inside, shares))
    )
    return losses, d_similar


def first_kernel(*refs):
    given = refs[:18]
    row_lengths, teacher_index, teacher_table = refs[18:21]
    (
        losses,
        embeddings_hbm,
        attn_hbm,
        up_hbm,
        down_hbm,
        turned_hbm,
        qkv_hbm,
        context_hbm,
        low_one_hbm,
        normed_one_hbm,
        slope_hbm,
        d_mid_hbm,
        d_branch_hbm,
        grad_down_hbm,
        codes_hbm,
        scaled_one_hbm,
        vectors_hbm,
        grad_vectors_hbm,
        grad_proj_hbm,
    ) = refs[21:40]
    (
        attn_mat,
        up_mat,
        down_mat,
        turned,
        qkv,
        context,
        low_one,
        normed_one,
        slope,
        activated,
        d_mid,
        d_branch,
        grad_down,
        small_all,
        cat_attn,
        stage_attn,
        stage_out,
        stage_up,
        stage_down,
        proj,
        up_bias,
        scaled_two,
        d_raw,
        codes,
        segments,
        keys,
        sends,
        recvs,
        half_sends,
        half_recvs,
        local_sems,
        grad_sems,
        embeddings,
        scaled_one,
        vectors,
        grad_vectors,
        grad_proj,
        given_sems,
        *taken,
    ) = refs[40:]
    (
        tokens,
        w_query,
        w_key,
        w_value,
        w_out,
        w_up,
        w_down,
        w_proj,
        *vector_refs,
        b_up,
        segment_ids,
    ) = taken
    count = tokens.shape[0]
    rows_dev = count // SEQ
    links = Links()
    links.hail()
    loads = [
        pltpu.make_async_copy(src, dst, given_sems.at[index])
        for index, (src, dst) in enumerate(zip(given, taken))
    ]
    later = (0, len(loads) - 1)
    for index, load in enumerate(loads):
        if index not in later:
            load.start()
    for index in later:
        loads[index].start()

    def gather(kind, block, group, stage):
        return kind(links, block, sends, recvs, group).join_from(
            stage, half_sends, half_recvs, group
        )

    attn = gather(JoinedGather, grid_block(attn_mat, 1152), 0, stage_attn)
    out = gather(JoinedLevelGather, grid_block(attn_mat, 384, 3 * WIDTH), 1, stage_out)
    up = gather(JoinedGather, rows_block(up_mat, 48, 1536), 2, stage_up)
    down = gather(JoinedGather, rows_block(down_mat, 192, 384), 3, stage_down)
    tiny = LevelGather(links, lead_grid_block(small_all), sends, recvs, 4)
    own_chip = links.chip_own + links.z
    kept = []

    def keep(src, dst):
        copy = pltpu.make_async_copy(src, dst, local_sems.at[len(kept)])
        copy.start()
        kept.append(copy)

    for index, load in enumerate(loads):
        if index not in later:
            load.wait()
    for index, ref in enumerate((w_query, w_key, w_value)):
        cat_attn[:, index * WIDTH : (index + 1) * WIDTH] = ref[...]
    own_small = tiny.block(links.c, own_chip, 1)
    own_small[0:24, :] = w_proj[...]
    own_small[24:40, :] = jnp.zeros((16, 128), jnp.float32)
    for index, ref in enumerate(vector_refs):
        own_small[24 + index : 25 + index, 0:24] = ref[...].reshape(1, 24)
    own_small[32:33, 0:96] = b_up[...].reshape(1, 96)

    links.greet()
    halves(links, cat_attn, stage_attn, half_sends, half_recvs, 0)
    halves(links, w_out, stage_out, half_sends, half_recvs, 1)
    halves(links, w_up, stage_up, half_sends, half_recvs, 2)
    halves(links, w_down, stage_down, half_sends, half_recvs, 3)
    plan = Plan(FIRST_PLAN, {"a": attn, "o": out, "u": up, "d": down, "t": tiny, "l": links})
    plan.until("bias")
    for index in later:
        loads[index].wait()
    live_rows = []
    for r in range(rows_dev):
        segment, live = segment_forms(segment_ids, row_lengths, r)
        live_rows.append(live)
        keys[r * SEQ : (r + 1) * SEQ, :] = key_codes(live)
        segments[r * SEQ : (r + 1) * SEQ, :] = query_codes(segment)
    plan.until("turn")
    turned[...] = tokens[...].T
    keep(turned, turned_hbm)
    plan.until("vec")
    cores = [(i % 2, i // 8, i // 2 % 4) for i in range(SHARDS)]
    for index, tile in enumerate(spread_lanes([small_all[c, n, m, 24:32, :] for c, n, m in cores], 24)):
        vectors[:, index * 128 : (index + 1) * 128] = rounded(tile)
    for index, tile in enumerate(spread_lanes([small_all[c, n, m, 32:40, :] for c, n, m in cores], 96)):
        up_bias[:, index * 128 : (index + 1) * 128] = rounded(tile)
    for r in range(CHIPS):
        both = [small_all[c, r // 4, r % 4, 0:24, :] for c in range(2)]
        both = jnp.concatenate(both, axis=0)
        proj[r * 48 : (r + 1) * 48, :] = both.astype(jnp.bfloat16)
    keep(vectors, vectors_hbm)
    plan.until("project")

    def project(step):
        rows = part_of(step, CHUNK)
        weights = attn_mat[:, :, :, 0 : 3 * WIDTH].reshape(WIDTH, 3 * WIDTH)
        value = dotted(tokens[rows, :], weights, 1, 0)
        qkv[rows, 0:WIDTH] = (value[:, 0:WIDTH] + vectors[0:1, :]).astype(jnp.bfloat16)
        qkv[rows, WIDTH : 2 * WIDTH] = value[:, WIDTH : 2 * WIDTH].astype(jnp.bfloat16)
        qkv[rows, 2 * WIDTH :] = (value[:, 2 * WIDTH :] + vectors[1:2, :]).astype(jnp.bfloat16)

    plan.loop("p", 0, count // CHUNK, project)
    keep(qkv, qkv_hbm)
    plan.until("attend")

    def attend(item):
        r, p = lax.div(item, PAIRS), lax.rem(item, PAIRS)
        attend_pair(r, p, qkv, context, codes, segments, keys)

    plan.loop("a", 0, rows_dev * PAIRS, attend)
    keep(context, context_hbm)
    keep(codes, codes_hbm)
    plan.until("mix")
    keep(attn_mat, attn_hbm)

    def mix(step):
        rows = part_of(step, HALF)
        weights = attn_mat[:, :, :, 3 * WIDTH :].reshape(WIDTH, WIDTH)
        mixed = dotted(context[rows, :], weights, 1, 0) + vectors[2:3, :]
        normed, scaled = norm_parts(tokens[rows, :].astype(jnp.float32) + mixed)
        normed_one[rows, :] = normed
        scaled_one[rows, :] = jnp.broadcast_to(scaled, (HALF, 128))
        low_one[rows, :] = (normed * vectors[3:4, :] + vectors[4:5, :]).astype(jnp.bfloat16)

    plan.loop("m", 0, count // HALF, mix)
    keep(normed_one, normed_one_hbm)
    keep(scaled_one, scaled_one_hbm)
    keep(low_one, low_one_hbm)
    plan.until("widen")
    keep(up_mat, up_hbm)

    def widen(step):
        columns = part_of(step, CHUNK)
        upward = dotted(low_one[...], up_mat[:, columns], 1, 0) + up_bias[0:1, columns]
        chance = 0.5 * (1.0 + lax.erf(upward * ROOT_HALF))
        density = jnp.exp2(upward * upward * (-0.5 * LOG2_E)) * DENSITY_SCALE
        activated[:, columns] = (upward * chance).astype(jnp.bfloat16)
        slope[:, columns] = (chance + upward * density).astype(jnp.bfloat16)

    plan.loop("w", 0, HIDDEN // CHUNK, widen)
    keep(slope, slope_hbm)
    plan.until("narrow")
    keep(down_mat, down_hbm)

    grad_vectors[...] = jnp.zeros_like(grad_vectors)
    for r in range(rows_dev):
        rows = slice(r * SEQ, (r + 1) * SEQ)
        mixed = dotted(activated[rows, :], down_mat[...], 1, 0) + vectors[5:6, :]
        mixed = mixed + (normed_one[rows, :] * vectors[3:4, :] + vectors[4:5, :])
        normed, scaled = norm_parts(mixed)
        d_mid[rows, :] = normed
        scaled_two[rows, :] = jnp.broadcast_to(scaled, (SEQ, 128))
        d_branch[rows, :] = (normed * vectors[6:7, :] + vectors[7:8, :]).astype(jnp.bfloat16)
    raw = dotted(d_branch[...], proj[...], 1, 0)
    inverse = lax.rsqrt(jnp.sum(raw * raw, -1, keepdims=True) + UNIT_EPS)
    embedded = raw * inverse
    embeddings[...] = embedded.reshape(rows_dev, SEQ, EMBED)
    keep(embeddings, embeddings_hbm)
    low_embed = embedded.astype(jnp.bfloat16)
    starts = [r * SEQ for r in range(rows_dev)]
    heads = [low_embed[start : start + QLEN] for start in starts]
    wholes = [low_embed[start : start + SEQ] for start in starts]
    similar = jnp.concatenate([dotted(h, w, 1, 1) for h, w in zip(heads, wholes)], axis=0)
    live = jnp.concatenate([jnp.broadcast_to(row, (QLEN, SEQ)) for row in live_rows], axis=0)
    row_losses, d_similar = passage_loss(similar, live, teacher_index, teacher_table)
    for r in range(rows_dev):
        losses[r] = row_losses[r][0, 0]
    d_similar = d_similar.astype(jnp.bfloat16)
    d_parts = []
    for r in range(rows_dev):
        d_row = d_similar[r * QLEN : (r + 1) * QLEN]
        d_whole = dotted(d_row, heads[r], 0, 0)
        d_parts += [d_whole[0:QLEN] + dotted(d_row, wholes[r], 1, 0), d_whole[QLEN:]]
    d_embed = jnp.concatenate(d_parts, axis=0)
    along = jnp.sum(d_embed * embedded, -1, keepdims=True)
    d_raw[...] = (inverse * (d_embed - embedded * along)).astype(jnp.bfloat16)
    grad_proj[...] = dotted(d_branch[...], d_raw[...], 0, 0)
    keep(grad_proj, grad_proj_hbm)

    def unmix(step, carry):
        rows = part_of(step, CHUNK)
        d_hidden = dotted(d_raw[rows, :], proj[...], 1, 1)
        normed = d_mid[rows, :]
        d_mixed = norm_back(d_hidden, normed, scaled_two[rows, 0:1], vectors[6:7, :])
        low_mixed = d_mixed.astype(jnp.bfloat16)
        d_mid[rows, :] = d_mixed
        d_branch[rows, :] = low_mixed
        grad_vectors[5:6, :] += jnp.sum(low_mixed.astype(jnp.float32), 0, keepdims=True)
        grad_vectors[6:7, :] += jnp.sum(d_hidden * normed, 0, keepdims=True)
        grad_vectors[7:8, :] += jnp.sum(d_hidden, 0, keepdims=True)
        return carry

    lax.fori_loop(0, count // CHUNK, unmix, 0)
    keep(grad_vectors, grad_vectors_hbm)
    keep(d_mid, d_mid_hbm)
    keep(d_branch, d_branch_hbm)

    def grad_copy(step, slot):
        return pltpu.make_async_copy(
            grad_down.at[slot], grad_down_hbm.at[part_of(step, WIDTH), :], grad_sems.at[slot]
        )

    def weigh(step, carry):
        slot = lax.rem(step, 2)

        @pl.when(step >= 2)
        def _():
            grad_copy(step - 2, slot).wait()

        part = activated[:, part_of(step, WIDTH)]
        grad_down[slot] = dotted(part, d_branch[...], 0, 0).astype(jnp.bfloat16)
        grad_copy(step, slot).start()
        return carry

    steps = HIDDEN // WIDTH
    lax.fori_loop(0, steps, weigh, 0)
    links.finish()
    for step in (steps - 2, steps - 1):
        grad_copy(step, step % 2).wait()
    for copy in kept:
        copy.wait()


def run_first(tokens, weights, vectors, segment_ids, row_lengths, teacher_index, teacher_table):
    count = tokens.shape[0]
    rows_dev = count // SEQ
    smem = pl.BlockSpec(memory_space=pltpu.SMEM)
    anywhere = pl.BlockSpec(memory_space=pl.ANY)
    low = jnp.bfloat16
    wide = jnp.float32

    def array(kind, *shape):
        return jax.ShapeDtypeStruct(shape, kind)

    return pl.pallas_call(
        first_kernel,
        out_shape=[
            array(wide, rows_dev),
            array(wide, rows_dev, SEQ, EMBED),
            array(low, 4, 4, 48, HIDDEN),
            array(low, WIDTH, HIDDEN),
            array(low, HIDDEN, WIDTH),
            array(low, WIDTH, count),
            array(low, count, 3 * WIDTH),
            array(low, count, WIDTH),
            array(low, count, WIDTH),
            array(wide, count, WIDTH),
            array(low, count, HIDDEN),
            array(wide, count, WIDTH),
            array(low, count, WIDTH),
            array(low, HIDDEN, WIDTH),
            array(low, count, WIDTH),
            array(wide, count, 128),
            array(wide, 8, WIDTH),
            array(wide, 8, WIDTH),
            array(wide, WIDTH, EMBED),
        ],
        in_specs=[anywhere] * 18 + [smem] * 3,
        out_specs=[smem] + [anywhere] * 18,
        scratch_shapes=[
            pltpu.VMEM((4, 4, 48, HIDDEN), low),
            pltpu.VMEM((WIDTH, HIDDEN), low),
            pltpu.VMEM((HIDDEN, WIDTH), low),
            pltpu.VMEM((WIDTH, count), low),
            pltpu.VMEM((count, 3 * WIDTH), low),
            pltpu.VMEM((count, WIDTH), low),
            pltpu.VMEM((count, WIDTH), low),
            pltpu.VMEM((count, WIDTH), wide),
            pltpu.VMEM((count, HIDDEN), low),
            pltpu.VMEM((count, HIDDEN), low),
            pltpu.VMEM((count, WIDTH), wide),
            pltpu.VMEM((count, WIDTH), low),
            pltpu.VMEM((2, WIDTH, WIDTH), low),
            pltpu.VMEM((2, 4, 4, SMALL, 128), wide),
            pltpu.VMEM((24, 3 * WIDTH), wide),
            pltpu.VMEM((48, 3 * WIDTH // 2), wide),
            pltpu.VMEM((48, WIDTH // 2), wide),
            pltpu.VMEM((48, HIDDEN // 2), wide),
            pltpu.VMEM((192, WIDTH // 2), wide),
            pltpu.VMEM((WIDTH, EMBED), low),
            pltpu.VMEM((8, HIDDEN), wide),
            pltpu.VMEM((count, 128), wide),
            pltpu.VMEM((count, EMBED), low),
            pltpu.VMEM((count, WIDTH), low),
            pltpu.VMEM((count, 128), low),
            pltpu.VMEM((count, 128), low),
            pltpu.SemaphoreType.DMA((5, Gather.SEMS)),
            pltpu.SemaphoreType.DMA((5, Gather.SEMS)),
            pltpu.SemaphoreType.DMA((4,)),
            pltpu.SemaphoreType.DMA((4,)),
            pltpu.SemaphoreType.DMA((18,)),
            pltpu.SemaphoreType.DMA((2,)),
            pltpu.VMEM((rows_dev, SEQ, EMBED), wide),
            pltpu.VMEM((count, 128), wide),
            pltpu.VMEM((8, WIDTH), wide),
            pltpu.VMEM((8, WIDTH), wide),
            pltpu.VMEM((WIDTH, EMBED), wide),
            pltpu.SemaphoreType.DMA((18,)),
        ]
        + [pltpu.VMEM(a.shape, a.dtype) for a in (tokens, *weights, *vectors, segment_ids)],
        compiler_params=pltpu.CompilerParams(
            collective_id=0, has_side_effects=True, vmem_limit_bytes=62 * 2**20
        ),
        name="forward_gather",
    )(tokens, *weights, *vectors, segment_ids, row_lengths, teacher_index, teacher_table)


def last_kernel(*refs):
    (
        attn_hbm,
        up_hbm,
        down_hbm,
        turned_hbm,
        qkv_hbm,
        context_hbm,
        low_one_hbm,
        normed_one_hbm,
        slope_hbm,
        d_mid_hbm,
        d_branch_hbm,
        grad_down_hbm,
        codes_hbm,
        scaled_one_hbm,
        vectors_hbm,
        part_vectors_hbm,
        grad_proj_hbm,
        segment_ids_hbm,
        row_lengths,
    ) = refs[:19]
    (
        grad_tokens_hbm,
        own_rows_hbm,
        own_down_hbm,
        own_small_hbm,
    ) = refs[19:23]
    (
        attn_mat,
        grads,
        wide,
        low_one,
        d_branch,
        d_mid,
        part_down,
        small_all,
        grad_vectors,
        grad_up_bias,
        sends,
        recvs,
        local_sems,
        slope_sems,
        down_sems,
        qkv_sems,
        grad_sems,
        key_code,
        value_code,
        lows,
        scaled_one,
        vectors,
        grad_proj,
        segment_ids,
        own_rows,
        own_down,
        own_small,
        *rest,
    ) = refs[23:]
    held = [rest[6 * i : 6 * i + 6] for i in range(6)]
    fins = [rest[36 + 2 * i : 38 + 2 * i] for i in range(5)]
    count = d_mid.shape[0]
    rows_dev = count // SEQ
    links = Links()
    c = links.c

    def scatter(block, rows, group, deliver, mine=None):
        def own(chip, units):
            return block(c, chip, units)

        own = own if mine is None else mine
        fin = fins[group] if group < 5 else None
        return Scatter(
            links, block, own, rows, held[group], fin, deliver, sends, recvs, group, group in (2, 4, 5)
        )

    def down_mine(chip, units):
        return part_down.at[pl.ds(pl.multiple_of(chip * 192, 192), units * 192), :]

    def halves_to(ref, start, columns):
        def deliver(low, high):
            ref[:, start : start + columns] = low
            ref[:, start + columns : start + 2 * columns] = high

        return deliver

    def most_out(low, high):
        own_rows[:, 0:512] = low[:, 0:512]
        own_rows[:, 768:1024] = low[:, 512:768]
        own_rows[:, 1024:1280] = high[:, 0:256]
        own_rows[:, 1536:2048] = high[:, 256:768]

    def rest_out(low, high):
        own_rows[:, 512:768] = low[:, 0:256]
        own_rows[:, 1280:1408] = low[:, 256:384]
        own_rows[:, 1408:1536] = high[:, 0:128]
        own_rows[:, 2048:2304] = high[:, 128:384]

    def tiny_out(total):
        own_small[...] = total[0]

    down = scatter(rows_block(grad_down_hbm, 192, 384), 192, 0, halves_to(own_down, 0, WIDTH // 2), down_mine)
    up = scatter(rows_block(grads, 48, 1536), 48, 1, halves_to(own_rows, HIDDEN, HIDDEN // 2))
    out = scatter(rows_block(grads, 48, 384), 48, 2, halves_to(own_rows, 3 * WIDTH, WIDTH // 2))
    most = scatter(rows_block(grads, 48, 768, WIDTH), 48, 3, most_out)
    rest_of = scatter(rows_block(grads, 48, 384, 3 * WIDTH), 48, 4, rest_out)
    tiny = scatter(lead_block(small_all), 1, 5, tiny_out)

    def load(src, dst, index):
        return pltpu.make_async_copy(src, dst, local_sems.at[index])

    def start(copies):
        for copy in copies:
            copy.start()

    def wait(copies):
        for copy in copies:
            copy.wait()

    plan = Plan(
        LAST_PLAN,
        {"d": down, "u": up, "o": out, "m": most, "r": rest_of, "t": tiny, "l": links},
    )
    plan.until("pre")
    links.hail()
    first_loads = [
        load(d_branch_hbm, d_branch, 0),
        load(grad_down_hbm.at[:, part_of(c, WIDTH // 2)], part_down, 1),
    ]
    side_loads = [
        load(segment_ids_hbm, segment_ids, 11),
        load(grad_proj_hbm, grad_proj, 12),
        load(part_vectors_hbm, grad_vectors, 13),
        load(vectors_hbm, vectors, 14),
        load(scaled_one_hbm, scaled_one, 15),
    ]
    attn_load = load(attn_hbm, attn_mat, 3)
    start(first_loads + side_loads[:2])
    links.greet()
    wait(first_loads[1:])
    ones = jnp.ones((8, count), jnp.bfloat16)

    def slope_load(step):
        columns = part_of(step, WIDTH)
        return pltpu.make_async_copy(
            slope_hbm.at[:, columns], wide.at[:, columns], slope_sems.at[step]
        )

    def qkv_load(step):
        rows = part_of(step, HALF)
        return pltpu.make_async_copy(
            qkv_hbm.at[rows, :], wide.at[rows, 0 : 3 * WIDTH], qkv_sems.at[step]
        )

    def grad_store(step):
        rows = part_of(step, HALF)
        return pltpu.make_async_copy(
            d_mid.at[rows, :], grad_tokens_hbm.at[rows, :], grad_sems.at[step]
        )

    steps = count // HALF
    quarters = HIDDEN // WIDTH

    def weights(start, columns):
        return attn_mat[:, :, :, start : start + columns].reshape(WIDTH, columns)

    def feed_forward(up_mat, down_mat, normed_one):
        def down_load(step):
            rows = part_of(step, WIDTH)
            return pltpu.make_async_copy(
                down_hbm.at[rows, :], down_mat.at[rows, :], down_sems.at[step]
            )

        for step in range(quarters):
            down_load(step).start()
            slope_load(step).start()
        start(side_loads[2:])
        middle = [
            load(low_one_hbm, low_one, 6),
            load(up_hbm, up_mat, 7),
            load(d_mid_hbm, d_mid, 8),
            load(normed_one_hbm, normed_one, 9),
        ]
        plan.until("ld")
        wait(side_loads[:2])
        for r in range(rows_dev):
            _, live = segment_forms(segment_ids, row_lengths, r)
            key_code[r * SEQ : (r + 1) * SEQ, :] = key_codes(live)
        low = low_head((SEQ, 128))
        lows[0] = jnp.where(low, 1.0, 0.0).astype(jnp.bfloat16)
        lows[1] = jnp.where(low, 0.0, 1.0).astype(jnp.bfloat16)
        lane = lanes_in_head((SEQ, 128))
        parts = (lane == PARTS) | (lane == PARTS + 1)
        value_code[...] = jnp.where(parts, 1.0, 0.0).astype(jnp.bfloat16)
        for i in range(SHARDS):
            small_all[i % 2, i // 2, 0:24, :] = grad_proj[i * 24 : (i + 1) * 24, :]
        wait(first_loads[:1])

        def widen(step):
            columns = part_of(step, WIDTH)
            down_load(step).wait()
            slope_load(step).wait()
            grad = dotted(d_branch[...], down_mat[columns, :], 1, 1)
            wide[:, columns] = (grad * wide[:, columns].astype(jnp.float32)).astype(jnp.bfloat16)

            @pl.when(step == 0)
            def _():
                start(middle)

        plan.loop("w", 0, quarters, widen)
        wait(middle[:1])

        def weigh(step):
            rows = part_of(step, CHUNK)
            grads[rows, :] = dotted(low_one[:, rows], wide[...], 0, 0).astype(jnp.bfloat16)

        plan.loop("wu", 0, WIDTH // CHUNK, weigh)
        plan.until("bc")
        attn_load.start()
        for index in range(4):
            columns = slice(index * WIDTH, (index + 1) * WIDTH)
            grad_up_bias[:, columns] = dotted(ones, wide[:, columns], 1, 0)
        wait(middle[1:] + side_loads[2:])

        def narrow(step):
            rows = part_of(step, HALF)
            d_hidden = d_mid[rows, :] + dotted(wide[rows, :], up_mat[...], 1, 1)
            qkv_load(step).start()
            normed = normed_one[rows, :]
            d_mixed = norm_back(d_hidden, normed, scaled_one[rows, 0:1], vectors[3:4, :])
            d_mid[rows, :] = d_mixed
            d_branch[rows, :] = d_mixed.astype(jnp.bfloat16)
            grad_vectors[3:4, :] += jnp.sum(d_hidden * normed, 0, keepdims=True)
            grad_vectors[4:5, :] += jnp.sum(d_hidden, 0, keepdims=True)

        plan.loop("n", 0, steps, narrow)

    pl.run_scoped(
        feed_forward,
        pltpu.VMEM((WIDTH, HIDDEN), jnp.bfloat16),
        pltpu.VMEM((HIDDEN, WIDTH), jnp.bfloat16),
        pltpu.VMEM((count, WIDTH), jnp.float32),
    )

    def attention(d_context, context, codes, turned):
        loads = [
            load(context_hbm, context, 2),
            load(codes_hbm, codes, 4),
            load(turned_hbm, turned, 10),
        ]
        start(loads)
        plan.until("misc")
        grad_vectors[2:3, :] = dotted(ones, d_branch[...], 1, 0)[0:1]
        attn_load.wait()

        plan.until("g0")
        d_context[...] = dotted(d_branch[...], weights(3 * WIDTH, WIDTH), 1, 1).astype(jnp.bfloat16)
        plan.until("rd")

        wait(loads[:1])

        def gather_dots(p, carry):
            dot_codes(p, context, d_context, low_one)
            return carry

        lax.fori_loop(0, PAIRS, gather_dots, 0)
        up.settle()

        plan.until("wo0")
        grads[:, 0:WIDTH] = dotted(context[...], d_branch[...], 0, 0).astype(jnp.bfloat16)
        for step in range(steps):
            qkv_load(step).wait()

        wait(loads[1:])

        def attend(item):
            r = lax.rem(item, rows_dev)
            p = lax.div(item, rows_dev)
            attend_back_pair(
                r, p, wide, d_context, codes, low_one, key_code, value_code, lows
            )

        def weigh(first, pairs, base):
            def step(index):
                size = pairs * 128
                here = pl.ds(pl.multiple_of(index * WIDTH + first * 128, 128), size)
                there = pl.ds(pl.multiple_of(base + index * size, 128), size)
                grads[:, there] = dotted(turned[...], wide[:, here], 1, 0).astype(jnp.bfloat16)

            return step

        plan.loop("a", 0, 4 * rows_dev, attend)
        plan.loop("wm", 0, 3, weigh(0, 4, WIDTH))
        plan.loop("a", 4 * rows_dev, 2 * rows_dev, attend)
        plan.loop("wr", 0, 3, weigh(4, 2, 3 * WIDTH))

    pl.run_scoped(
        attention,
        pltpu.VMEM((count, WIDTH), jnp.bfloat16),
        pltpu.VMEM((count, WIDTH), jnp.bfloat16),
        pltpu.VMEM((count, WIDTH), jnp.bfloat16),
        pltpu.VMEM((WIDTH, count), jnp.bfloat16),
    )
    plan.until("vec")
    for index in (0, 2):
        total = dotted(ones, wide[:, index * WIDTH : (index + 1) * WIDTH], 1, 0)
        grad_vectors[index // 2 : index // 2 + 1, :] = total[0:1]
    tiles = [grad_vectors[:, i * 128 : (i + 1) * 128] for i in range(WIDTH // 128)]
    for i, part in enumerate(pick_lanes(tiles, 24, SHARDS)):
        small_all[i % 2, i // 2, 24:32, :] = part
    tiles = [grad_up_bias[:, i * 128 : (i + 1) * 128] for i in range(HIDDEN // 128)]
    for i, part in enumerate(pick_lanes(tiles, 96, SHARDS)):
        small_all[i % 2, i // 2, 32:40, :] = part

    def back(step):
        rows = part_of(step, HALF)
        value = dotted(wide[rows, 0 : 3 * WIDTH], weights(0, 3 * WIDTH), 1, 1)
        d_mid[rows, :] += value
        grad_store(step).start()

    plan.loop("b", 0, steps, back)
    plan.until("end")
    stores = [
        load(own_rows, own_rows_hbm, 16),
        load(own_down, own_down_hbm, 17),
        load(own_small, own_small_hbm, 18),
    ]
    start(stores)
    links.finish()
    for step in range(steps):
        grad_store(step).wait()
    wait(stores)


def run_last(kept, segment_ids, row_lengths):
    count = kept[9].shape[0]
    rows_dev = count // SEQ
    smem = pl.BlockSpec(memory_space=pltpu.SMEM)
    anywhere = pl.BlockSpec(memory_space=pl.ANY)
    low = jnp.bfloat16
    wide = jnp.float32

    def array(*shape):
        return jax.ShapeDtypeStruct(shape, wide)

    def held(unit, kind):
        return [pltpu.VMEM((n * unit[0],) + unit[1:], kind) for n in (16, 2, 2, 4, 4, 3)]

    blocks = ((192, 384), (48, 1536), (48, 384), (48, 768), (48, 384))
    buffers = []
    for block in blocks:
        buffers += held(block, low)
    buffers += held((1, SMALL, 128), wide)
    for rows, columns in blocks:
        buffers += [pltpu.VMEM((rows, columns), wide), pltpu.VMEM((rows // 2, columns), wide)]
    return pl.pallas_call(
        last_kernel,
        out_shape=[
            array(count, WIDTH),
            array(24, 2 * HIDDEN),
            array(96, WIDTH),
            array(SMALL, 128),
        ],
        in_specs=[anywhere] * 18 + [smem],
        out_specs=[anywhere] * 4,
        scratch_shapes=[
            pltpu.VMEM((4, 4, 48, HIDDEN), low),
            pltpu.VMEM((WIDTH, HIDDEN), low),
            pltpu.VMEM((count, HIDDEN), low),
            pltpu.VMEM((count, WIDTH), low),
            pltpu.VMEM((count, WIDTH), low),
            pltpu.VMEM((count, WIDTH), wide),
            pltpu.VMEM((HIDDEN, WIDTH // 2), low),
            pltpu.VMEM((2, CHIPS, SMALL, 128), wide),
            pltpu.VMEM((8, WIDTH), wide),
            pltpu.VMEM((8, HIDDEN), wide),
            pltpu.SemaphoreType.DMA((6, Scatter.SEMS)),
            pltpu.SemaphoreType.DMA((6, Scatter.SEMS)),
            pltpu.SemaphoreType.DMA((19,)),
            pltpu.SemaphoreType.DMA((HIDDEN // WIDTH,)),
            pltpu.SemaphoreType.DMA((HIDDEN // WIDTH,)),
            pltpu.SemaphoreType.DMA((count // HALF,)),
            pltpu.SemaphoreType.DMA((count // HALF,)),
            pltpu.VMEM((count, 128), low),
            pltpu.VMEM((SEQ, 128), low),
            pltpu.VMEM((2, SEQ, 128), low),
            pltpu.VMEM((count, 128), wide),
            pltpu.VMEM((8, WIDTH), wide),
            pltpu.VMEM((WIDTH, EMBED), wide),
            pltpu.VMEM((rows_dev, SEQ), jnp.int32),
            pltpu.VMEM((24, 2 * HIDDEN), wide),
            pltpu.VMEM((96, WIDTH), wide),
            pltpu.VMEM((SMALL, 128), wide),
        ]
        + buffers,
        compiler_params=pltpu.CompilerParams(
            collective_id=1, has_side_effects=True, vmem_limit_bytes=63 * 2**20
        ),
        name="backward_scatter",
    )(*kept, segment_ids, row_lengths)


def pass_kernel(*refs):
    sources, targets = refs[:6], refs[6:25]
    held, ready = refs[25:31], refs[31:40]
    in_sems, out_sems = refs[40:]
    grad_tokens, embeddings, query, key, value, out, up, down, proj = targets[:9]
    rows, down_in, small_in, losses_in = held[2:]
    pieces = 8
    through = []
    for src, mid, dst in zip(sources[:2], held[:2], (grad_tokens, embeddings)):
        size = src.shape[0] // pieces
        for piece in range(pieces):
            part = pl.ds(piece * size, size)
            index = len(through)
            through.append(
                (
                    pltpu.make_async_copy(src.at[part], mid.at[part], in_sems.at[index]),
                    pltpu.make_async_copy(mid.at[part], dst.at[part], out_sems.at[index]),
                )
            )
    small = [
        pltpu.make_async_copy(src, mid, in_sems.at[2 * pieces + index])
        for index, (src, mid) in enumerate(zip(sources[2:], held[2:]))
    ]
    for copy in small:
        copy.start()
    for here, _ in through:
        here.start()
    for copy in small:
        copy.wait()
    for index, ref in enumerate(ready[:8]):
        ref[...] = small_in[24 + index : 25 + index, 0:24].reshape(24)
    ready[8][...] = small_in[32:33, 0:96].reshape(96)
    made = [
        (rows.at[:, index * WIDTH : (index + 1) * WIDTH], ref)
        for index, ref in enumerate((query, key, value, out))
    ]
    made += [(rows.at[:, HIDDEN:], up), (down_in, down), (small_in.at[0:24, :], proj)]
    made += list(zip(ready, targets[9:18])) + [(losses_in, targets[18])]
    outs = [
        pltpu.make_async_copy(mid, dst, out_sems.at[2 * pieces + index])
        for index, (mid, dst) in enumerate(made)
    ]
    for copy in outs:
        copy.start()
    for here, there in through:
        here.wait()
        there.start()
    for copy in outs:
        copy.wait()
    for _, there in through:
        there.wait()


def run_pass(*arrays):
    anywhere = pl.BlockSpec(memory_space=pl.ANY)

    def array(*shape):
        return jax.ShapeDtypeStruct(shape, jnp.float32)

    whole = [array(*a.shape) for a in arrays]
    vectors = [array(24)] * 8 + [array(96)]
    return pl.pallas_call(
        pass_kernel,
        out_shape=whole[:2]
        + [array(24, WIDTH)] * 4
        + [array(24, HIDDEN), array(96, WIDTH), array(24, EMBED)]
        + vectors
        + [whole[-1]],
        in_specs=[anywhere] * 6,
        out_specs=[anywhere] * 19,
        scratch_shapes=[pltpu.VMEM(a.shape, a.dtype) for a in (*arrays, *vectors)]
        + [pltpu.SemaphoreType.DMA((20,)), pltpu.SemaphoreType.DMA((33,))],
        compiler_params=pltpu.CompilerParams(vmem_limit_bytes=62 * 2**20),
        name="hand_over",
    )(*arrays)


def body_tiles(
    tokens,
    w_query,
    b_query,
    w_key,
    w_value,
    b_value,
    w_out,
    b_out,
    gain_one,
    shift_one,
    w_up,
    b_up,
    w_down,
    b_down,
    gain_two,
    shift_two,
    w_proj,
    segment_ids,
    row_lengths,
    teacher_index,
    teacher_table,
):
    rows_dev, _, width = tokens.shape
    losses, embeddings, *kept = run_first(
        tokens.reshape(rows_dev * SEQ, width),
        (w_query, w_key, w_value, w_out, w_up, w_down, w_proj),
        (b_query, b_value, b_out, gain_one, shift_one, b_down, gain_two, shift_two, b_up),
        segment_ids,
        row_lengths,
        teacher_index,
        teacher_table,
    )
    grad_tokens, *small = run_last(kept, segment_ids, row_lengths)
    (
        grad_tokens,
        embeddings,
        grad_query,
        grad_key,
        grad_value,
        grad_out,
        grad_up,
        grad_down,
        grad_proj,
        grad_query_bias,
        grad_value_bias,
        grad_out_bias,
        grad_gain_first,
        grad_shift_first,
        grad_down_bias,
        grad_gain_second,
        grad_shift_second,
        grad_up_bias,
        losses,
    ) = run_pass(grad_tokens, embeddings.reshape(rows_dev * SEQ, EMBED), *small, losses)
    return (
        losses,
        embeddings.reshape(rows_dev, SEQ, EMBED),
        grad_tokens.reshape(rows_dev, SEQ, width),
        grad_query,
        grad_query_bias,
        grad_key,
        grad_value,
        grad_value_bias,
        grad_out,
        grad_out_bias,
        grad_gain_first,
        grad_shift_first,
        grad_up,
        grad_up_bias,
        grad_down,
        grad_down_bias,
        grad_gain_second,
        grad_shift_second,
        grad_proj,
    )


def solution(mesh):
    in_specs = (
        P(("dp", "fsdp"), None, None),
        P(("dp", "fsdp"), None),
        P(("dp", "fsdp")),
        P(("dp", "fsdp"), None),
        P(("dp", "fsdp"), None),
        P(("dp", "fsdp")),
        P(("dp", "fsdp"), None),
        P(("dp", "fsdp")),
        P(("dp", "fsdp")),
        P(("dp", "fsdp")),
        P(("dp", "fsdp"), None),
        P(("dp", "fsdp")),
        P(("dp", "fsdp"), None),
        P(("dp", "fsdp")),
        P(("dp", "fsdp")),
        P(("dp", "fsdp")),
        P(("dp", "fsdp"), None),
        P(("dp", "fsdp"), None),
        P(("dp", "fsdp")),
        P(("dp", "fsdp"), None),
        P(),
    )
    out_specs = (
        P(("dp", "fsdp")),
        P(("dp", "fsdp"), None, None),
        P(("dp", "fsdp"), None, None),
        P(("dp", "fsdp"), None),
        P(("dp", "fsdp")),
        P(("dp", "fsdp"), None),
        P(("dp", "fsdp"), None),
        P(("dp", "fsdp")),
        P(("dp", "fsdp"), None),
        P(("dp", "fsdp")),
        P(("dp", "fsdp")),
        P(("dp", "fsdp")),
        P(("dp", "fsdp"), None),
        P(("dp", "fsdp")),
        P(("dp", "fsdp"), None),
        P(("dp", "fsdp")),
        P(("dp", "fsdp")),
        P(("dp", "fsdp")),
        P(("dp", "fsdp"), None),
    )
    body = body_tiles if fits(mesh) else body_whole
    return jax.shard_map(body, mesh=mesh, in_specs=in_specs, out_specs=out_specs, check_vma=False)
```
